128 devices in a mesh: seq: 16 (over y, x_hi, core), batch: 4 (over z), mp: 2 (over x_lo).
Axes of the slice: x: 4 (x_hi: 2, x_lo: 2; x = x_hi * 2 + x_lo), y: 4, z: 4, core: 2. Of those that a mesh axis runs over, the one named last changes fastest.
Arguments:
- hidden: bfloat16 [24576, 7168], P(('seq', 'batch'), 'mp'), may hold values from -192 to 192
- kv_down: bfloat16 [7168, 576], P('mp', 'batch'), may hold values from -0.0625 to 0.0625
- kv_gain: float32 [512], replicated, may hold values from 0.1 to 1.9
- page_owner: int32 [1536, 1], P(('seq', 'batch')), may hold values from 0 to 3; in each aligned block of 24 rows (0 to 23, 24 to 47, ...) at most 12 rows name the same one
- page_request: int32 [1536], P(('seq', 'batch')), may hold values from 0 to 7
- queries: bfloat16 [4, 32, 128, 576], P(None, 'batch', 'mp'), may hold values from -6 to 6
- cache: bfloat16 [32, 8192, 576], P('batch', 'seq'), may hold values from -6 to 6
- lengths: int32 [32], P('batch'), may hold values from 1 to 8192
Outputs:
- attended: float32 [4, 32, 128, 512], P(None, 'batch', 'mp', 'seq')
The draws below stay inside these ranges and needn't reach their ends.
Inputs may be any that keep to these rules, and one draw needn't show every extreme that they name: `page_owner`: among the pages of one device, at most 12 share an owner.
All inputs are finite; a program needn't handle non-finite values.
Results may differ from the reference program's by a relative error of at most 0.0022.
Values may be sent and summed in bfloat16 or wider, within the bound.
A program may use at most 128 MiB of HBM per device.

```python
import math
import jax
import jax.numpy as jnp
import numpy as np
from jax import lax

D = 7168
LAT = 512
ROPE = 64
HEADS = 128
KV = 576
PAGE = 16
PAGES_DEV = 24
PTOK = 384
PAGES = 1536
PRE_TOK = 24576
CAP = 12
REQ_DEV = 8
REQS = 32
CTX = 8192
STEPS = 4
N_BATCH = 4


def anchor_pattern(key):
    magnitude = jax.random.uniform(jax.random.fold_in(key, 5), (REQS, LAT // 2), jnp.float32, 1.6, 2.0)
    signs = (2 * jax.random.randint(jax.random.fold_in(key, 7), (REQS, LAT), 0, 2) - 1).astype(jnp.float32)
    return (jnp.repeat(magnitude, 2, axis=1) * signs, signs)


def draw_hidden(key, part):
    key = jax.random.fold_in(key, 31)
    values = jnp.clip(jax.random.normal(jax.random.fold_in(key, 1), (PRE_TOK, D), jnp.float32), -6.0, 6.0)
    return values.astype(jnp.bfloat16)


def draw_cache(key, part):
    pattern, signs = anchor_pattern(key)
    key = jax.random.fold_in(key, 11)
    values = jnp.clip(jax.random.normal(jax.random.fold_in(key, 1), (REQS, CTX, KV), jnp.float32), -6.0, 6.0)
    pair_count = LAT // 2
    factor = jax.random.uniform(jax.random.fold_in(key, 2), (REQS, 1), jnp.float32, 1.4, 2.0)
    flipped_pair = jax.random.randint(jax.random.fold_in(key, 3), (REQS, 1), 0, pair_count)
    keep_pair = (jnp.arange(pair_count)[None, :] != flipped_pair).astype(jnp.float32)
    twist_one = jax.random.uniform(jax.random.fold_in(key, 4), (REQS, pair_count), jnp.float32, -2.0, 2.0) * keep_pair
    twist_two = jax.random.uniform(jax.random.fold_in(key, 6), (REQS, pair_count), jnp.float32, -2.0, 2.0) * keep_pair
    paired = signs.reshape(REQS, pair_count, 2)

    def across(twist):
        return jnp.stack([paired[:, :, 1] * twist, -paired[:, :, 0] * twist], axis=2).reshape(REQS, LAT)
    flip = jnp.where(jnp.arange(LAT)[None, :] == 2 * flipped_pair, -1.0, 1.0)
    first = factor * pattern + across(twist_one)
    second = factor * pattern * flip + across(twist_two)
    place_one = jax.random.randint(jax.random.fold_in(key, 8), (REQS, 1), 0, CTX)
    place_two = (place_one + 1 + jax.random.randint(jax.random.fold_in(key, 9), (REQS, 1), 0, CTX - 1)) % CTX
    places = jnp.arange(CTX)[None, :]
    latent = values[:, :, :LAT]
    latent = jnp.where((places == place_one)[:, :, None], first[:, None, :], latent)
    latent = jnp.where((places == place_two)[:, :, None], second[:, None, :], latent)
    values = jnp.concatenate([latent, values[:, :, LAT:]], axis=2)
    return values.astype(jnp.bfloat16)


def draw_queries(key, part):
    pattern, signs = anchor_pattern(key)
    key = jax.random.fold_in(key, 23)
    values = jnp.clip(jax.random.normal(jax.random.fold_in(key, 1), (STEPS, REQS, HEADS, KV), jnp.float32), -6.0, 6.0)
    order = jax.random.permutation(jax.random.fold_in(key, 2), HEADS)
    heavy = (order < HEADS // 4)[None, None, :, None]
    strength = jax.random.uniform(jax.random.fold_in(key, 3), (STEPS, REQS, HEADS, 1), jnp.float32, 2.0, 2.6)
    aligned = strength * pattern[None, :, None, :]
    latent = jnp.where(heavy, aligned, values[:, :, :, :LAT])
    rotary = jnp.where(heavy, 0.25 * values[:, :, :, LAT:], values[:, :, :, LAT:])
    values = jnp.concatenate([latent, rotary], axis=3)
    return values.astype(jnp.bfloat16)


def plant(drawn, stream_key, smallest, largest):
    longest = drawn.shape.index(max(drawn.shape))
    spots = []
    for shift in (0, 1):
        where = [jax.random.randint(jax.random.fold_in(stream_key, axis), (), 0, length) for axis, length in enumerate(drawn.shape)]
        where[longest] = (where[longest] + shift) % drawn.shape[longest]
        spots.append(tuple(where))
    return drawn.at[spots[0]].set(smallest).at[spots[1]].set(largest)


def block_scale(key, extent, cuts, smallest, largest):
    def one(axis_at, parts):
        draws = jax.random.uniform(jax.random.fold_in(jax.random.fold_in(key, 6), axis_at), (parts,), jnp.float32, smallest / len(cuts), largest / len(cuts))
        return jnp.repeat(jnp.exp(draws), extent[axis_at] // parts).reshape((-1,) + (1,) * (len(extent) - axis_at - 1))

    loudness = one(*cuts[0])
    for cut in cuts[1:]:
        loudness = loudness * one(*cut)
    return loudness


def routed_block(stream_key, own, number, rows, number_of, top, limit, lean):
    sequence = jax.random.permutation(stream_key, number_of)
    heavy_load, usual = load_shares(number_of, rows * top, limit, lean, True), load_shares(number_of, rows * top, limit, lean, False)
    places = jnp.arange(number_of)

    def named(sizes, offset_by):
        used = int((sizes > 0).sum())
        fixed = max(1, used // 4)
        shifted = fixed + (places - fixed + offset_by * (used - fixed)) % max(1, number_of - fixed)
        return jnp.zeros((number_of,), jnp.int32).at[sequence[jnp.where(places < fixed, places, shifted)]].set(jnp.asarray(sizes, jnp.int32))

    sizes = jnp.where(number % 4 == 0, named(heavy_load, number // 4), named(usual, number - number // 4 - 1))
    mixed = jax.random.permutation(jax.random.fold_in(own, 3), number_of)
    source_of, receiver = mixed[0:number_of // 2 * 2:2], mixed[1:number_of // 2 * 2:2]
    slack = jnp.minimum(sizes[source_of] - 1, limit - sizes[receiver]) // 2
    slack = jnp.where((source_of == sequence[0]) | (receiver == sequence[0]) | (sizes[receiver] == 0), 0, jnp.maximum(slack, 0))
    shifted = jax.random.randint(jax.random.fold_in(own, 4), (number_of // 2,), 0, 1 << 20) % (slack + 1)
    sizes = sizes.at[source_of].add(-shifted).at[receiver].add(shifted)
    items = jnp.searchsorted(jnp.cumsum(sizes), jnp.arange(rows * top), side="right").astype(jnp.int32)
    listing = items.reshape(top, rows).T
    listing = listing[jax.random.permutation(jax.random.fold_in(own, 1), rows)]
    offset_by = jax.random.randint(jax.random.fold_in(own, 2), (rows, 1), 0, top)
    return jnp.take_along_axis(listing, (jnp.arange(top)[None, :] + offset_by) % top, axis=1)


def load_shares(count, total, limit, skew, full):
    loads = [(1 << 20) // math.isqrt(grade ** skew) + 1 for grade in range(1, count + 1)]
    largest = limit if full else min(limit, max(-(-total // count), total * loads[0] // sum(loads)))
    least = 1 if total - largest >= count - 1 else 0
    holding, rest = [largest] + [least] * (count - 1), total - largest - least * (count - 1)
    while rest > 0:
        free = [i for i in range(1, count) if holding[i] < largest] or [i for i in range(1, count) if holding[i] < limit]
        pool, budget = sum([loads[i] for i in free]), rest
        for i in free:
            extra = min(limit - holding[i], max(1, budget * loads[i] // pool), rest)
            holding[i] = holding[i] + extra
            rest = rest - extra
    return np.array(holding)


def centred(stream_key, dims, scale, reach, cuts=(), kind=jnp.bfloat16):
    drawn = jax.random.normal(stream_key, dims, jnp.float32) * scale
    if len(cuts) > 0:
        drawn = block_scale(stream_key, dims, cuts, -0.22, 0.18) * drawn
    return jnp.clip(drawn, min=-reach, max=reach).astype(kind)


def setup_inputs(seed: int = 0) -> dict:
    key_of = jax.random.split(jax.random.key(seed), 9)
    hidden = draw_hidden(jax.random.fold_in(key_of[8], 71), 0)
    kv_down = centred(key_of[1], (D, KV), D ** -0.5, 0.0625, ((0, 2), (1, 4)))
    kv_gain = jnp.clip(1.0 + 0.18 * jax.random.normal(key_of[2], (LAT,), jnp.float32), 0.1, 1.9)
    page_owner_keys = jax.random.split(jax.random.fold_in(key_of[3], 1), PAGES // PAGES_DEV)
    page_owner_turns = jax.random.permutation(jax.random.fold_in(key_of[3], 3), PAGES // PAGES_DEV)
    page_owner = jax.vmap(lambda own, number: routed_block(jax.random.fold_in(key_of[3], 2), own, number, PAGES_DEV, N_BATCH, 1, CAP, 2))(page_owner_keys, page_owner_turns).reshape((PAGES, 1))
    page_request = plant(jax.random.randint(key_of[4], (PAGES,), 0, REQ_DEV), jax.random.fold_in(key_of[4], 1), 0, REQ_DEV - 1).astype(jnp.int32)
    queries = draw_queries(jax.random.fold_in(key_of[8], 71), 0)
    cache = draw_cache(jax.random.fold_in(key_of[8], 71), 0)
    lengths = plant(jax.random.randint(key_of[7], (REQS,), 1, CTX + 1), jax.random.fold_in(key_of[7], 1), 1, CTX).astype(jnp.int32)
    return {"hidden": hidden, "kv_down": kv_down, "kv_gain": kv_gain, "page_owner": page_owner, "page_request": page_request, "queries": queries, "cache": cache, "lengths": lengths}


eps_norm = 1e-06
score_scale = 192.0 ** (-0.5)
rope_base = 10000.0
masked_value = -1e+30

def finish_rows(portion, first_column, squares, gain, latent_width, rope_width, positions):
    breadth = portion.shape[1]
    columns = first_column + jnp.arange(breadth)
    inverse = lax.rsqrt(squares / latent_width + eps_norm)[:, None]
    gain_full = jnp.concatenate([gain, jnp.ones((rope_width,), gain.dtype)])
    scaling = lax.dynamic_slice_in_dim(gain_full, first_column, breadth)
    normed = portion * inverse * scaling[None, :]
    half_rope = rope_width // 2
    offsets = columns - latent_width
    pair_index = jnp.where(offsets >= 0, offsets % half_rope, 0)
    frequency = rope_base ** (-pair_index.astype(portion.dtype) / half_rope)
    angles = positions[:, None] * frequency[None, :]
    ahead = jnp.roll(portion, -half_rope, axis=1)
    behind = jnp.roll(portion, half_rope, axis=1)
    cosine = jnp.cos(angles)
    sine = jnp.sin(angles)
    rotated = jnp.where((offsets < half_rope)[None, :], portion * cosine - ahead * sine, portion * cosine + behind * sine)
    return jnp.where((columns >= latent_width)[None, :], rotated, normed).astype(jnp.bfloat16)

def reference(hidden, kv_down, kv_gain, page_owner, page_request, queries, cache, lengths):
    latent = jnp.dot(hidden, kv_down, preferred_element_type=jnp.float32)
    squares = lax.optimization_barrier(jnp.sum(latent[:, :LAT] * latent[:, :LAT], axis=1))
    positions = (jnp.arange(PRE_TOK) % PTOK).astype(jnp.float32)
    rows = finish_rows(latent, 0, squares, kv_gain, LAT, ROPE, positions)
    pages = rows.reshape(PAGES, PAGE, KV)
    page_target = (page_owner[:, 0] * REQ_DEV + page_request).astype(jnp.int32)
    query_rows = jnp.transpose(queries, (1, 0, 2, 3)).reshape(REQS, STEPS * HEADS, KV)
    cache_positions = jnp.arange(CTX)

    def resident_scores(request):
        scores = jnp.dot(query_rows[request], cache[request].T, preferred_element_type=jnp.float32) * score_scale
        live = (cache_positions < lengths[request])[None, :]
        return (scores, live)

    def resident_peak(request):
        scores, live = resident_scores(request)
        return lax.optimization_barrier(jnp.max(jnp.where(live, scores, masked_value), axis=1))
    peaks = lax.map(resident_peak, jnp.arange(REQS))

    def page_peak(carry, item):
        page, target = item
        scores = jnp.dot(query_rows[target], page.T, preferred_element_type=jnp.float32) * score_scale
        return (carry.at[target].max(lax.optimization_barrier(jnp.max(scores, axis=1))), None)
    peaks = lax.scan(page_peak, peaks, (pages, page_target))[0]

    def resident_sums(request):
        scores, live = resident_scores(request)
        weights = jnp.where(live, jnp.exp(jnp.where(live, scores, masked_value) - peaks[request][:, None]), 0.0)
        numerator = jnp.dot(weights.astype(jnp.bfloat16), cache[request][:, :LAT], preferred_element_type=jnp.float32)
        return (numerator, lax.optimization_barrier(jnp.sum(weights, axis=1)))
    numerators, totals = lax.map(resident_sums, jnp.arange(REQS))

    def page_sums(carry, item):
        page, target = item
        numerator, total = carry
        scores = jnp.dot(query_rows[target], page.T, preferred_element_type=jnp.float32) * score_scale
        weights = jnp.exp(scores - peaks[target][:, None])
        added = jnp.dot(weights.astype(jnp.bfloat16), page[:, :LAT], preferred_element_type=jnp.float32)
        return ((numerator.at[target].add(added), total.at[target].add(lax.optimization_barrier(jnp.sum(weights, axis=1)))), None)
    numerators, totals = lax.scan(page_sums, (numerators, totals), (pages, page_target))[0]
    attended = (numerators / totals[:, :, None]).reshape(REQS, STEPS, HEADS, LAT)
    return jnp.transpose(attended, (1, 0, 2, 3)).astype(jnp.float32)
```

```python
import jax
import jax.numpy as jnp
import numpy as np
from jax import lax
from jax.experimental import pallas as pl
from jax.experimental.pallas import tpu as pltpu
from jax.sharding import PartitionSpec as P

MESH = pl.DeviceIdType.MESH
F32, BF16, I32, I16 = jnp.float32, jnp.bfloat16, jnp.int32, jnp.int16

eps_norm = 1e-06
score_scale = 192.0 ** (-0.5)
log2_scale = score_scale * 1.4426950408889634
rope_base = 10000.0
masked_value = -1e30
floor_value = -1e29
code_top = 32767.0

TOK, HALF_D, KVW, LATW, ROPEW = 384, 3584, 576, 512, 64
LABELS = 64
KVX = KVW + LABELS
BLK = 144
SHARE, DIRECT = 256, 384
CAPTOK = 192
PAGES, PAGE, CAP = 24, 16, 12
QROWS = 256
CTXD = 512
NR = 4


def nt(a, b):
    return lax.dot_general(a, b, (((1,), (1,)), ((), ())), preferred_element_type=F32)


def nn(a, b):
    return jnp.dot(a, b, preferred_element_type=F32)


def kernel(
    hidden, kv_down, gain, owner, request, queries, cache, lengths, cosine, sine,
    out,
    hid, kvt, lat, mps, mpr, mss, msr, rows, packed, relay, arr, tok,
    qraw, qbuf, kbuf, acc, ms, ls, osend, ostat, ybuf, ystat, rsend, rstat, mbuf, mstat, xbuf, xstat, fin,
    loc, send, recv,
):
    s, b, p = lax.axis_index("seq"), lax.axis_index("batch"), lax.axis_index("mp")
    c = lax.rem(s, 2)
    sib = s + 1 - 2 * c
    y = lax.div(s, 4)
    in_y = lax.rem(s, 4)
    xh = lax.rem(lax.div(s, 2), 2)
    dev_zp = (s, lax.rem(b + 1, 4), p)
    dev_zm = (s, lax.rem(b + 3, 4), p)
    dev_zz = (s, lax.rem(b + 2, 4), p)
    dev_mp = (s, b, 1 - p)
    dev_sib = (sib, b, p)
    dev_yp = (lax.rem(y + 1, 4) * 4 + in_y, b, p)
    dev_ym = (lax.rem(y + 3, 4) * 4 + in_y, b, p)
    dev_x = (s + 2 - 4 * xh, b, p)

    used = [0]
    started = []

    def link(src, dst, dev):
        i = used[0]
        used[0] += 1
        return pltpu.make_async_remote_copy(
            src_ref=src, dst_ref=dst, send_sem=send.at[i], recv_sem=recv.at[i],
            device_id=dev, device_id_type=MESH,
        )

    def go(copy):
        copy.start()
        started.append(copy)

    def code(value, axis):
        most = jnp.max(jnp.abs(value), axis=axis, keepdims=True)
        return jnp.round(value * (code_top / jnp.maximum(most, 1e-30))), most * (1.0 / code_top)

    def to_code(value):
        return value.astype(I32).astype(I16)

    def from_code(coded):
        return coded.astype(I32).astype(F32)

    def go_pair(pair):
        go(pair[0])
        go(pair[1])

    def wait_pair(pair):
        pair[0].wait_recv()
        pair[1].wait_recv()

    load_kv = pltpu.make_async_copy(kv_down, kvt.at[0], loc.at[0])
    load_kv.start()
    load_hid = pltpu.make_async_copy(hidden, hid, loc.at[1])
    load_hid.start()
    load_q = []
    for step in range(4):
        load_q.append(pltpu.make_async_copy(queries.at[step, pl.ds(c * NR, NR)], qraw.at[:, step], loc.at[2 + step]))
        load_q[-1].start()
    load_cache = pltpu.make_async_copy(cache.at[pl.ds(c * NR, NR)], kbuf.at[0], loc.at[6])
    load_cache.start()

    barrier = pltpu.get_barrier_semaphore()
    for dev in (dev_zp, dev_zm, dev_zz, dev_mp, dev_sib, dev_yp, dev_ym, dev_x):
        pl.semaphore_signal(barrier, inc=1, device_id=dev, device_id_type=MESH)

    load_kv.wait()
    pl.semaphore_wait(barrier, 8)

    base = c * (HALF_D // 2)

    def lanes(start, size):
        return pl.ds(pl.multiple_of(base + start, 128), size)

    def kv_link(slot, to_slot, at, dev):
        return link(kvt.at[slot, :, at], kvt.at[to_slot, :, at], dev)

    def part_of(k, first=0, size=SHARE):
        return lanes(lax.rem(y + k, 4) * SHARE + first, size)

    low, high = lanes(4 * SHARE, DIRECT), lanes(4 * SHARE + DIRECT, DIRECT)
    mine = part_of(0)
    s_p, s_m = kv_link(0, 1, mine, dev_zp), kv_link(0, 2, mine, dev_zm)
    d_p0, d_m1 = kv_link(0, 1, low, dev_zp), kv_link(0, 2, high, dev_zm)
    d_p1, d_m0 = kv_link(0, 1, high, dev_zp), kv_link(0, 2, low, dev_zm)
    for copy in (s_p, s_m, d_p0, d_m1, d_p1, d_m0):
        go(copy)
    cache_out = link(cache.at[pl.ds((1 - c) * NR, NR)], kbuf.at[1], dev_sib)
    go(cache_out)
    sf_p, sf_m = (
        kv_link(1, 3, part_of(0, 0, SHARE // 2), dev_zp),
        kv_link(2, 3, part_of(0, SHARE // 2, SHARE // 2), dev_zm),
    )
    df_p, df_m = kv_link(1, 3, low, dev_zp), kv_link(2, 3, high, dev_zm)
    near_p = [None] + [kv_link(slot, slot, mine, dev_yp) for slot in (1, 2, 3)]
    near_m = [None] + [kv_link(slot, slot, mine, dev_ym) for slot in (1, 2, 3)]
    far = [
        None,
        [kv_link(1, 1, part_of(3), dev_yp)],
        [kv_link(2, 2, part_of(1), dev_ym)],
        [
            kv_link(3, 3, part_of(3, 0, SHARE // 2), dev_yp),
            kv_link(3, 3, part_of(1, SHARE // 2, SHARE // 2), dev_ym),
        ],
    ]
    share_s = [None] + [kv_link(slot, slot, lanes(0, 4 * SHARE), dev_sib) for slot in (1, 2, 3)]
    share_d = [None] + [kv_link(slot, slot, lanes(4 * SHARE, 2 * DIRECT), dev_sib) for slot in (1, 2, 3)]

    token = lax.broadcasted_iota(I32, (1, TOK), 1)
    token_page = lax.shift_right_logical(token, 4)
    dest = jnp.zeros((1, TOK), I32)
    asked = jnp.zeros((1, TOK), I32)
    counts = [jnp.int32(0)] * 4
    for page in range(PAGES):
        to = owner[0, page]
        rank = jnp.where(to == 0, counts[0], jnp.where(to == 1, counts[1], jnp.where(to == 2, counts[2], counts[3])))
        counts = [counts[o] + (to == o).astype(I32) for o in range(4)]
        dest = jnp.where(token_page == page, (to * CAP + rank) * PAGE, dest)
        asked = jnp.where(token_page == page, request[page] + 1, asked)
    dest = dest + lax.bitwise_and(token, 15)
    tok[...] = dest

    label_row = lax.broadcasted_iota(I32, (LABELS, TOK), 0)
    rows[KVW:, :] = (label_row == asked).astype(F32).astype(BF16)

    origin = [lax.rem(b + ahead, 4) for ahead in (0, 3, 1, 2)]
    m_copies = [
        (link(mps.at[slot], mpr.at[slot], dev_mp), link(mss.at[slot], msr.at[slot], dev_mp)) for slot in range(3)
    ]
    tails = (slice(0, 256), slice(256, TOK))
    for at in tails:
        at = pl.ds(at.start, at.stop - at.start)
        m_copies.append((
            link(mps.at[3, :, at], mpr.at[3, :, at], dev_mp), link(mss.at[3, :, at], msr.at[3, :, at], dev_mp),
        ))

    def send_part(slot, part, copies, at=slice(None)):
        lat[origin[slot], :, at] = part
        coded, scale = code(part, 0)
        mps[slot, :, at] = to_code(coded)
        mss[slot, :, at] = scale
        go_pair(copies)

    def weigh(score, top):
        return jnp.exp2(score * log2_scale - top * log2_scale)

    def fold(w):
        total = w[:, :128]
        for j in range(1, w.shape[1] // 128):
            total = total + w[:, j * 128:j * 128 + 128]
        return total

    def peak(score):
        most = score[:, :128]
        for j in range(1, score.shape[1] // 128):
            most = jnp.maximum(most, score[:, j * 128:j * 128 + 128])
        return most

    def resident(r, carry):
        q = qbuf[r, :, :KVW]
        length = lengths[c * NR + r]
        at = lax.broadcasted_iota(I32, (1, CTXD), 1)
        score0 = jnp.where(at + s * CTXD < length, nn(q, kbuf[0, r]), masked_value)
        score1 = jnp.where(at + sib * CTXD < length, nn(q, kbuf[1, r]), masked_value)
        top = jnp.max(jnp.maximum(peak(score0), peak(score1)), axis=1, keepdims=True)
        top = jnp.maximum(top, floor_value)
        w0 = weigh(score0, top)
        w1 = weigh(score1, top)
        acc[r] = nt(w0.astype(BF16), kbuf[0, r, :LATW, :]) + nt(w1.astype(BF16), kbuf[1, r, :LATW, :])
        ms[r] = jnp.broadcast_to(top, (QROWS, 128))
        ls[r] = fold(w0) + fold(w1)
        return carry

    load_hid.wait()
    s_p.wait_recv()
    go(sf_p)
    go(near_p[1])
    go(near_m[1])
    s_m.wait_recv()
    go(sf_m)
    go(near_p[2])
    go(near_m[2])
    send_part(0, nt(kvt[0], hid[...]), m_copies[0])

    near_p[1].wait_recv()
    go(far[1][0])
    near_m[2].wait_recv()
    go(far[2][0])
    d_p0.wait_recv()
    go(df_p)
    d_m1.wait_recv()
    go(df_m)
    sf_p.wait_recv()
    sf_m.wait_recv()
    go(near_p[3])
    go(near_m[3])

    for copy in load_q:
        copy.wait()
    load_cache.wait()
    cache_out.wait_recv()
    label_at = lax.broadcasted_iota(I32, (QROWS, LABELS), 1)
    for r in range(NR):
        qbuf[r, :, :KVW] = qraw[r].reshape(QROWS, KVW)
        qbuf[r, :, KVW:] = jnp.where(label_at == c * NR + r + 1, 0.0, masked_value).astype(BF16)
    lax.fori_loop(0, 1, resident, 0)

    d_p1.wait_recv()
    go(share_d[1])
    d_m0.wait_recv()
    go(share_d[2])
    near_m[1].wait_recv()
    far[1][0].wait_recv()
    go(share_s[1])
    near_p[2].wait_recv()
    far[2][0].wait_recv()
    go(share_s[2])
    near_p[3].wait_recv()
    go(far[3][0])
    near_m[3].wait_recv()
    go(far[3][1])
    lax.fori_loop(1, 2, resident, 0)

    df_p.wait_recv()
    df_m.wait_recv()
    go(share_d[3])
    for slot in (1, 2):
        share_d[slot].wait_recv()
        share_s[slot].wait_recv()
    both = nt(kvt[1:3].reshape(2 * BLK, HALF_D), hid[...])
    for slot in (1, 2):
        send_part(slot, both[(slot - 1) * BLK:slot * BLK], m_copies[slot])

    far[3][0].wait_recv()
    far[3][1].wait_recv()
    go(share_s[3])
    share_d[3].wait_recv()
    share_s[3].wait_recv()
    for i, at in enumerate(tails):
        send_part(3, nt(kvt[3], hid[at, :]), m_copies[3 + i], at)

    for slot in range(4):
        for pair in m_copies[slot:] if slot == 3 else m_copies[slot:slot + 1]:
            wait_pair(pair)
        lat[origin[slot]] = lat[origin[slot]] + from_code(mpr[slot]) * msr[slot]
    whole = lat[...].reshape(KVW, TOK)
    latent = whole[:LATW]
    inverse = lax.rsqrt(jnp.sum(latent * latent, axis=0, keepdims=True) / LATW + eps_norm)
    gain_cols = jnp.transpose(jnp.broadcast_to(gain[...], (128, LATW)))
    for j in range(TOK // 128):
        at = slice(j * 128, j * 128 + 128)
        rows[:LATW, at] = (latent[:, at] * inverse[:, at] * gain_cols).astype(BF16)
    first, second = whole[LATW:LATW + ROPEW // 2], whole[LATW + ROPEW // 2:]
    rows[LATW:LATW + ROPEW // 2, :] = (first * cosine[...] - second * sine[...]).astype(BF16)
    rows[LATW + ROPEW // 2:KVW, :] = (first * sine[...] + second * cosine[...]).astype(BF16)

    slot_at = lax.broadcasted_iota(I32, (CAPTOK, TOK), 0)

    def pack_for(to):
        chosen = ((slot_at + to * CAPTOK) == tok[...]).astype(F32)
        empty = jnp.sum(chosen, axis=1, keepdims=True) < 0.5
        page_rows = nt(chosen.astype(BF16), rows[...])
        column = lax.broadcasted_iota(I32, (CAPTOK, KVX), 1)
        return jnp.where((column == KVW) & empty, 1.0, page_rows).astype(BF16)

    half = CAPTOK // 2
    a_r0 = link(packed.at[2, pl.ds(0, half)], relay.at[0], dev_zp)
    a_r1 = link(packed.at[2, pl.ds(half, half)], relay.at[1], dev_zm)
    a_p = link(packed.at[0], arr.at[1, c], dev_zp)
    a_m = link(packed.at[1], arr.at[2, c], dev_zm)
    a_f0 = link(relay.at[0], arr.at[3, c, pl.ds(0, half)], dev_zp)
    a_f1 = link(relay.at[1], arr.at[3, c, pl.ds(half, half)], dev_zm)
    a_share = [link(arr.at[slot, c], arr.at[slot, c], dev_sib) for slot in range(3)]
    a_share3 = [
        link(arr.at[3, c, pl.ds(0, half)], arr.at[3, c, pl.ds(0, half)], dev_sib),
        link(arr.at[3, c, pl.ds(half, half)], arr.at[3, c, pl.ds(half, half)], dev_sib),
    ]
    packed[2] = pack_for(lax.rem(b + 2, 4))
    go(a_r0)
    go(a_r1)
    packed[0] = pack_for(lax.rem(b + 1, 4))
    go(a_p)
    packed[1] = pack_for(lax.rem(b + 3, 4))
    go(a_m)
    arr[0, c] = pack_for(b)
    go(a_share[0])

    def pages_step(r, slots):
        q = qbuf[r]
        old = ms[r][:, :1]
        scores = [nt(q, arr[slot].reshape(2 * CAPTOK, KVX)) for slot in slots]
        most = peak(scores[0])
        for score in scores[1:]:
            most = jnp.maximum(most, peak(score))
        top = jnp.maximum(old, jnp.max(most, axis=1, keepdims=True))
        shrink = jnp.exp2((old - top) * log2_scale)
        total = ls[r] * shrink
        value = acc[r] * shrink
        for slot, score in zip(slots, scores):
            w = weigh(score, top)
            total = total + fold(w)
            value = value + nn(w.astype(BF16), arr[slot].reshape(2 * CAPTOK, KVX)[:, :LATW])
        return value, jnp.broadcast_to(top, (QROWS, 128)), total

    def pages_of(slots):
        def body(r, carry):
            acc[r], ms[r], ls[r] = pages_step(r, slots)
            return carry

        return body

    a_r0.wait_recv()
    go(a_f0)
    a_r1.wait_recv()
    go(a_f1)
    lax.fori_loop(2, NR, resident, 0)
    a_share[0].wait_recv()
    lax.fori_loop(0, NR, pages_of((0,)), 0)
    a_p.wait_recv()
    go(a_share[1])
    a_m.wait_recv()
    go(a_share[2])
    a_share[1].wait_recv()
    a_share[2].wait_recv()
    lax.fori_loop(0, NR, pages_of((1, 2)), 0)
    a_f0.wait_recv()
    go(a_share3[0])
    a_f1.wait_recv()
    go(a_share3[1])
    a_share3[0].wait_recv()
    a_share3[1].wait_recv()

    def merge(parts):
        top = parts[0][1][0]
        for _, stat in parts[1:]:
            top = jnp.maximum(top, stat[0])
        value, total = 0.0, 0.0
        for coded, stat in parts:
            factor = jnp.exp2(stat[0] - top)
            value = value + from_code(coded) * (factor * stat[2])
            total = total + factor * stat[1]
        return value, top, total

    def put(coded_ref, stat_ref, value, top, total):
        coded, scale = code(value, 0)
        coded_ref[...] = to_code(coded)
        stat_ref[0] = top
        stat_ref[1] = total
        stat_ref[2] = scale

    yp, ym, yy = lax.rem(y + 1, 4), lax.rem(y + 3, 4), lax.rem(y + 2, 4)
    y_copies = []
    for r in range(NR):
        pairs = (
            (osend.at[r, yy, 0], ostat.at[r], 0, dev_yp),
            (osend.at[r, yy, 1], ostat.at[r], 1, dev_ym),
            (osend.at[r, yp, 1], ostat.at[r], 2, dev_yp),
            (osend.at[r, ym, 0], ostat.at[r], 3, dev_ym),
            (rsend.at[r, 0], rstat.at[r, 0], 4, dev_yp),
            (rsend.at[r, 1], rstat.at[r, 1], 5, dev_ym),
        )
        y_copies.append([
            (link(data, ybuf.at[r, k], dev), link(stat, ystat.at[r, k], dev)) for data, stat, k, dev in pairs
        ])

    lane = lax.broadcasted_iota(I32, (QROWS, 128), 1)
    for r in range(NR):
        value, top, total = pages_step(r, (3,))
        coded, scale = code(value, 1)
        osend[r] = to_code(jnp.transpose(coded)).reshape(4, 2, 64, QROWS)
        stat = jnp.transpose(jnp.where(lane == 0, top * log2_scale, scale))
        ostat[r, 0] = stat[0:1]
        ostat[r, 1] = jnp.sum(jnp.transpose(total), axis=0, keepdims=True)
        ostat[r, 2] = stat[1:2]
        for k in range(4):
            go_pair(y_copies[r][k])
    for r in range(NR):
        for k, to in ((0, yp), (1, ym)):
            wait_pair(y_copies[r][k])
            put(rsend.at[r, k], rstat.at[r, k], *merge([
                (osend[r, to, k], ostat[r]), (ybuf[r, k], ystat[r, k]),
            ]))
            go_pair(y_copies[r][4 + k])
    x_copies = []
    for r in range(NR):
        for k in range(2, 6):
            wait_pair(y_copies[r][k])
        for h, (one, two) in enumerate(((3, 4), (2, 5))):
            put(mbuf.at[r, h], mstat.at[r, h], *merge([
                (osend[r, y, h], ostat[r]), (ybuf[r, one], ystat[r, one]), (ybuf[r, two], ystat[r, two]),
            ]))
        x_copies.append((
            link(mbuf.at[r, 1 - xh], xbuf.at[r], dev_x), link(mstat.at[r, 1 - xh], xstat.at[r], dev_x),
        ))
        go_pair(x_copies[r])
    c_copies = []
    for r in range(NR):
        wait_pair(x_copies[r])
        value, _, total = merge([(mbuf[r, xh], mstat[r, xh]), (xbuf[r], xstat[r])])
        value = value / total
        for core in range(2):
            for step in range(4):
                fin[r, core, step] = value[32 * core:32 * core + 32, 64 * step:64 * step + 64]
        c_copies.append(link(fin.at[r, 1 - c], out.at[:, c * NR + r], dev_sib))
        go(c_copies[r])
        out[:, c * NR + r] = fin[r, c]
    for copy in c_copies:
        copy.wait_recv()
    for copy in started:
        copy.wait_send()


LINKS = 136


def tables():
    half = ROPEW // 2
    frequency = rope_base ** (-np.arange(half, dtype=np.float32) / np.float32(half))
    angles = np.arange(TOK, dtype=np.float32)[None, :] * frequency.astype(np.float32)[:, None]
    return np.cos(angles).astype(np.float32), np.sin(angles).astype(np.float32)


def on_device(hidden, kv_down, kv_gain, page_owner, page_request, queries, cache, lengths):
    cosine, sine = tables()
    anywhere = pl.BlockSpec(memory_space=pl.ANY)
    vmem = pl.BlockSpec(memory_space=pltpu.VMEM)
    smem = pl.BlockSpec(memory_space=pltpu.SMEM)
    sums = pl.pallas_call(
        kernel,
        out_shape=jax.ShapeDtypeStruct((4, 2 * NR, 32, 64), F32),
        in_specs=[anywhere, anywhere, vmem, smem, smem, anywhere, anywhere, smem, vmem, vmem],
        out_specs=vmem,
        scratch_shapes=[
            pltpu.VMEM((TOK, HALF_D), BF16),
            pltpu.VMEM((4, BLK, HALF_D), BF16),
            pltpu.VMEM((4, BLK, TOK), F32),
            pltpu.VMEM((4, BLK, TOK), I16),
            pltpu.VMEM((4, BLK, TOK), I16),
            pltpu.VMEM((4, 1, TOK), F32),
            pltpu.VMEM((4, 1, TOK), F32),
            pltpu.VMEM((KVX, TOK), BF16),
            pltpu.VMEM((3, CAPTOK, KVX), BF16),
            pltpu.VMEM((2, CAPTOK // 2, KVX), BF16),
            pltpu.VMEM((4, 2, CAPTOK, KVX), BF16),
            pltpu.VMEM((1, TOK), I32),
            pltpu.VMEM((NR, 4, 64, KVW), BF16),
            pltpu.VMEM((NR, QROWS, KVX), BF16),
            pltpu.VMEM((2, NR, KVW, CTXD), BF16),
            pltpu.VMEM((NR, QROWS, LATW), F32),
            pltpu.VMEM((NR, QROWS, 128), F32),
            pltpu.VMEM((NR, QROWS, 128), F32),
            pltpu.VMEM((NR, 4, 2, 64, QROWS), I16),
            pltpu.VMEM((NR, 3, 1, QROWS), F32),
            pltpu.VMEM((NR, 6, 64, QROWS), I16),
            pltpu.VMEM((NR, 6, 3, 1, QROWS), F32),
            pltpu.VMEM((NR, 2, 64, QROWS), I16),
            pltpu.VMEM((NR, 2, 3, 1, QROWS), F32),
            pltpu.VMEM((NR, 2, 64, QROWS), I16),
            pltpu.VMEM((NR, 2, 3, 1, QROWS), F32),
            pltpu.VMEM((NR, 64, QROWS), I16),
            pltpu.VMEM((NR, 3, 1, QROWS), F32),
            pltpu.VMEM((NR, 2, 4, 32, 64), F32),
            pltpu.SemaphoreType.DMA((7,)),
            pltpu.SemaphoreType.DMA((LINKS,)),
            pltpu.SemaphoreType.DMA((LINKS,)),
        ],
        compiler_params=pltpu.CompilerParams(
            collective_id=0, has_side_effects=True, vmem_limit_bytes=56 * 1024 * 1024
        ),
        cost_estimate=pl.CostEstimate(flops=7_500_000_000, bytes_accessed=12_000_000, transcendentals=3_000_000),
    )(
        hidden, kv_down.T, kv_gain.reshape(1, LATW), page_owner.T, page_request, queries, cache.transpose(0, 2, 1), lengths,
        jnp.asarray(cosine), jnp.asarray(sine),
    )
    return sums.transpose(0, 1, 3, 2)


def solution(mesh):
    return jax.shard_map(
        on_device,
        mesh=mesh,
        in_specs=(
            P(("seq", "batch"), "mp"),
            P("mp", "batch"),
            P(),
            P(("seq", "batch"), None),
            P(("seq", "batch")),
            P(None, "batch", "mp", None),
            P("batch", "seq", None),
            P("batch"),
        ),
        out_specs=P(None, "batch", "mp", "seq"),
        check_vma=False,
    )
```

```python
import jax
import jax.numpy as jnp
import numpy as np
from jax import lax
from jax.experimental import pallas as pl
from jax.experimental.pallas import tpu as pltpu
from jax.sharding import PartitionSpec as P

MESH = pl.DeviceIdType.MESH
F32, BF16, I32, I16 = jnp.float32, jnp.bfloat16, jnp.int32, jnp.int16

eps_norm = 1e-06
score_scale = 192.0 ** (-0.5)
log2_e = 1.4426950408889634
log2_scale = score_scale * log2_e
rope_base = 10000.0
masked_value = -1e30
floor_value = -1e29
code_top = 32767.0

TOK, HALF_D, KVW, LATW, ROPEW = 384, 3584, 576, 512, 64
LABELS = 64
KVX = KVW + LABELS
BLK = 144
SHARE, DIRECT = 256, 384
CAPTOK = 192
PAGES, PAGE, CAP = 24, 16, 12
QROWS = 256
CTXD = 512
NR = 4
PAIRS = ((0, 1), (2, 3))


def nt(a, b):
    return lax.dot_general(a, b, (((1,), (1,)), ((), ())), preferred_element_type=F32)


def nn(a, b):
    return jnp.dot(a, b, preferred_element_type=F32)


def kernel(
    hidden, kv_down, gain, owner, request, queries, cache, lengths, cosine, sine,
    out,
    hid, kvt, lat, mps, mpr, mss, msr, rows, packed, relay, arr, tok,
    qraw, qbuf, kbuf, esend, estat, ebuf, efrom, acc, ms, ls, osend, ostat, ybuf, ystat, rsend, rstat, mbuf, mstat, fbuf, fstat,
    loc, send, recv,
):
    s, b, p = lax.axis_index("seq"), lax.axis_index("batch"), lax.axis_index("mp")
    c = lax.rem(s, 2)
    sib = s + 1 - 2 * c
    y = lax.div(s, 4)
    in_y = lax.rem(s, 4)
    xh = lax.rem(lax.div(s, 2), 2)
    dev_zp = (s, lax.rem(b + 1, 4), p)
    dev_zm = (s, lax.rem(b + 3, 4), p)
    dev_zz = (s, lax.rem(b + 2, 4), p)
    dev_mp = (s, b, 1 - p)
    dev_sib = (sib, b, p)
    dev_yp = (lax.rem(y + 1, 4) * 4 + in_y, b, p)
    dev_ym = (lax.rem(y + 3, 4) * 4 + in_y, b, p)
    dev_x = (s + 2 - 4 * xh, b, p)
    dev_x_sib = (sib + 2 - 4 * xh, b, p)

    used = [0]
    started = []

    def link(src, dst, dev):
        used[0] += 1
        return link_at(used[0] - 1, src, dst, dev)

    def link_at(i, src, dst, dev):
        return pltpu.make_async_remote_copy(
            src_ref=src, dst_ref=dst, send_sem=send.at[i], recv_sem=recv.at[i],
            device_id=dev, device_id_type=MESH,
        )

    def go(copy):
        copy.start()
        started.append(copy)

    def code(value, axis):
        most = jnp.max(jnp.abs(value), axis=axis, keepdims=True)
        most = jnp.maximum(most, 1e-25)
        return jnp.round(value * (code_top / most)), most * (1.0 / code_top)

    def to_code(value):
        return value.astype(I32).astype(I16)

    def from_code(coded):
        return coded.astype(I32).astype(F32)

    def go_pair(pair):
        go(pair[0])
        go(pair[1])

    def wait_pair(pair):
        pair[0].wait_recv()
        pair[1].wait_recv()

    load_kv = pltpu.make_async_copy(kv_down, kvt.at[0], loc.at[0])
    load_kv.start()
    load_hid = pltpu.make_async_copy(hidden, hid, loc.at[1])
    load_hid.start()
    load_q = []
    for step in range(4):
        load_q.append(pltpu.make_async_copy(queries.at[step], qraw.at[:, step], loc.at[2 + step]))
        load_q[-1].start()
    load_cache = pltpu.make_async_copy(cache, kbuf, loc.at[6])
    load_cache.start()

    barrier = pltpu.get_barrier_semaphore()
    for dev in (dev_zp, dev_zm, dev_zz, dev_mp, dev_sib, dev_yp, dev_ym, dev_x, dev_x_sib):
        pl.semaphore_signal(barrier, inc=1, device_id=dev, device_id_type=MESH)

    pl.semaphore_wait(barrier, 9)

    base = c * (HALF_D // 2)

    def lanes(start, size):
        return pl.ds(pl.multiple_of(base + start, 128), size)

    def kv_link(slot, to_slot, at, dev):
        return link(kvt.at[slot, :, at], kvt.at[to_slot, :, at], dev)

    def first_link(to_slot, at, dev):
        return link(kv_down.at[:, at], kvt.at[to_slot, :, at], dev)

    def part_of(k, first=0, size=SHARE):
        return lanes(lax.rem(y + k, 4) * SHARE + first, size)

    low, high = lanes(4 * SHARE, DIRECT), lanes(4 * SHARE + DIRECT, DIRECT)
    mine = part_of(0)
    s_p, s_m = first_link(1, mine, dev_zp), first_link(2, mine, dev_zm)
    d_p0, d_m1 = first_link(1, low, dev_zp), first_link(2, high, dev_zm)
    d_p1, d_m0 = first_link(1, high, dev_zp), first_link(2, low, dev_zm)
    for copy in (s_p, s_m, d_p0, d_m1):
        go(copy)
    sf_p, sf_m = (
        kv_link(1, 3, part_of(0, 0, SHARE // 2), dev_zp),
        kv_link(2, 3, part_of(0, SHARE // 2, SHARE // 2), dev_zm),
    )
    df_p, df_m = kv_link(1, 3, low, dev_zp), kv_link(2, 3, high, dev_zm)
    near_p = [None] + [kv_link(slot, slot, mine, dev_yp) for slot in (1, 2, 3)]
    near_m = [None] + [kv_link(slot, slot, mine, dev_ym) for slot in (1, 2, 3)]
    far = [None] + [
        (
            kv_link(slot, slot, part_of(3, 0, SHARE // 2), dev_yp),
            kv_link(slot, slot, part_of(1, SHARE // 2, SHARE // 2), dev_ym),
        )
        for slot in (1, 2, 3)
    ]
    share_s = [None] + [kv_link(slot, slot, lanes(0, 4 * SHARE), dev_sib) for slot in (1, 2, 3)]
    share_d = [None] + [kv_link(slot, slot, lanes(4 * SHARE, 2 * DIRECT), dev_sib) for slot in (1, 2, 3)]

    token = lax.broadcasted_iota(I32, (1, TOK), 1)
    token_page = lax.shift_right_logical(token, 4)
    dest = jnp.zeros((1, TOK), I32)
    asked = jnp.zeros((1, TOK), I32)
    counts = [jnp.int32(0)] * 4
    for page in range(PAGES):
        to = owner[0, page]
        rank = jnp.where(to == 0, counts[0], jnp.where(to == 1, counts[1], jnp.where(to == 2, counts[2], counts[3])))
        counts = [counts[o] + (to == o).astype(I32) for o in range(4)]
        dest = jnp.where(token_page == page, (to * CAP + rank) * PAGE, dest)
        asked = jnp.where(token_page == page, request[page] + 1, asked)
    dest = dest + lax.bitwise_and(token, 15)
    tok[...] = dest

    label_row = lax.broadcasted_iota(I32, (LABELS, TOK), 0)
    rows[KVW:, :] = (label_row == asked).astype(F32).astype(BF16)

    origin = [lax.rem(b + ahead, 4) for ahead in (0, 3, 1, 2)]
    m_copies = [
        (link(mps.at[slot], mpr.at[slot], dev_mp), link(mss.at[slot], msr.at[slot], dev_mp)) for slot in range(3)
    ]
    tails = (slice(0, 256), slice(256, TOK))
    for at in tails:
        at = pl.ds(at.start, at.stop - at.start)
        m_copies.append((
            link(mps.at[3, :, at], mpr.at[3, :, at], dev_mp), link(mss.at[3, :, at], msr.at[3, :, at], dev_mp),
        ))

    def send_part(slot, part, copies, at=slice(None)):
        lat[origin[slot], :, at] = part
        coded, scale = code(part, 0)
        mps[slot, :, at] = to_code(coded)
        mss[slot, :, at] = scale
        go_pair(copies)

    def weigh(score, top):
        return jnp.exp2(score * log2_scale - top * log2_scale)

    def fold(w):
        total = w[:, :128]
        for j in range(1, w.shape[1] // 128):
            total = total + w[:, j * 128:j * 128 + 128]
        return total

    def peak(score):
        most = score[:, :128]
        for j in range(1, score.shape[1] // 128):
            most = jnp.maximum(most, score[:, j * 128:j * 128 + 128])
        return most

    lane = lax.broadcasted_iota(I32, (QROWS, 128), 1)

    def put_columns(stat_ref, top, total, scale):
        stat = jnp.transpose(jnp.where(lane == 0, top * log2_scale, scale))
        stat_ref[0] = stat[0:1]
        stat_ref[1] = jnp.sum(jnp.transpose(total), axis=0, keepdims=True)
        stat_ref[2] = stat[1:2]

    def resident(pair, half):
        at = lax.broadcasted_iota(I32, (1, CTXD), 1) + s * CTXD
        scores = [
            jnp.where(at < lengths[half * NR + r], nn(qbuf[half * NR + r, :, :KVW], kbuf[half * NR + r]), masked_value)
            for r in pair
        ]
        weights = []
        for score in scores:
            top = jnp.maximum(jnp.max(peak(score), axis=1, keepdims=True), floor_value)
            w = weigh(score, top)
            weights.append((w.astype(BF16), jnp.broadcast_to(top, (QROWS, 128)), fold(w)))
        return [
            (nt(w, kbuf[half * NR + r, :LATW, :]), top, total) for r, (w, top, total) in zip(pair, weights)
        ]

    def resident_own(i, carry):
        for r, state in zip((2 * i, 2 * i + 1), resident((2 * i, 2 * i + 1), c)):
            acc[r], ms[r], ls[r] = state
        return carry

    def add_other(r, carry):
        row = lax.broadcasted_iota(I32, (128, QROWS), 0)
        stat = jnp.where(row == 0, efrom[r, 0], jnp.where(row == 1, efrom[r, 1], efrom[r, 2]))
        stat = jnp.transpose(stat)
        top2, total2, scale2 = stat[:, 0:1] * (1.0 / log2_scale), stat[:, 1:2], stat[:, 2:3]
        old = ms[r][:, :1]
        top = jnp.maximum(old, top2)
        keep, gain2 = jnp.exp2((old - top) * log2_scale), jnp.exp2((top2 - top) * log2_scale)
        acc[r] = acc[r] * keep + from_code(ebuf[r]) * (gain2 * scale2)
        ms[r] = jnp.broadcast_to(top, (QROWS, 128))
        ls[r] = ls[r] * keep + jnp.where(lane == 0, gain2 * total2, 0.0)
        return carry

    load_hid.wait()
    load_kv.wait()
    s_p.wait_recv()
    go(sf_p)
    go(near_p[1])
    go(near_m[1])
    s_m.wait_recv()
    go(sf_m)
    go(near_p[2])
    go(near_m[2])
    go(d_p1)
    go(d_m0)
    send_part(0, nt(kvt[0], hid[...]), m_copies[0])

    d_p0.wait_recv()
    go(df_p)
    d_m1.wait_recv()
    go(df_m)

    def pass_on(slot):
        near_p[slot].wait_recv()
        go(far[slot][0])
        near_m[slot].wait_recv()
        go(far[slot][1])

    def swap_shared(slot):
        far[slot][0].wait_recv()
        far[slot][1].wait_recv()
        go(share_s[slot])

    pass_on(1)
    sf_p.wait_recv()
    sf_m.wait_recv()
    go(near_p[3])
    go(near_m[3])

    for copy in load_q:
        copy.wait()
    load_cache.wait()
    label_at = lax.broadcasted_iota(I32, (QROWS, LABELS), 1)

    def fill(r, carry):
        qbuf[r, :, :KVW] = qraw[r].reshape(QROWS, KVW)
        qbuf[r, :, KVW:] = jnp.where(label_at == r + 1, 0.0, masked_value).astype(BF16)
        return carry

    def resident_other(i, carry):
        for r, (value, top, total) in zip((2 * i, 2 * i + 1), resident((2 * i, 2 * i + 1), 1 - c)):
            coded, scale = code(value, 1)
            esend[r] = to_code(coded)
            put_columns(estat.at[r], top, total, scale)
        return carry

    lax.fori_loop(0, 2 * NR, fill, 0)
    lax.fori_loop(0, 1, resident_other, 0)

    pass_on(2)
    d_p1.wait_recv()
    go(share_d[1])
    d_m0.wait_recv()
    go(share_d[2])
    swap_shared(1)
    swap_shared(2)

    def over_lanes(slots, starts, size, at):
        keys = slice(slots[0], slots[-1] + 1)
        rows_at = len(slots) * BLK
        return sum(
            nt(kvt[keys, :, start:start + size].reshape(rows_at, size), hid[at, start:start + size]) for start in starts
        )

    direct_at = ((4 * SHARE, HALF_D // 2 + 4 * SHARE), 2 * DIRECT)
    shared_at = ((0, HALF_D // 2), 4 * SHARE)
    whole_at = slice(None)
    share_d[1].wait_recv()
    share_d[2].wait_recv()
    both = over_lanes((1, 2), *direct_at, whole_at)
    lat[origin[1]] = both[:BLK]
    lat[origin[2]] = both[BLK:]
    pass_on(3)
    for slot in (1, 2):
        share_s[slot].wait_recv()
        send_part(slot, lat[origin[slot]] + over_lanes((slot,), *shared_at, whole_at), m_copies[slot])
    df_p.wait_recv()
    df_m.wait_recv()
    go(share_d[3])
    swap_shared(3)
    share_d[3].wait_recv()
    lat[origin[3]] = over_lanes((3,), *direct_at, whole_at)
    share_s[3].wait_recv()
    for i, at in enumerate(tails):
        send_part(3, lat[origin[3], :, at] + over_lanes((3,), *shared_at, at), m_copies[3 + i], at)

    lax.fori_loop(1, 2, resident_other, 0)
    e_copies = [
        (link(esend.at[r], ebuf.at[r], dev_sib), link(estat.at[r], efrom.at[r], dev_sib)) for r in range(NR)
    ]
    for pair in e_copies:
        go_pair(pair)
    lax.fori_loop(0, 2, resident_own, 0)
    for pair in e_copies:
        wait_pair(pair)
    lax.fori_loop(0, NR, add_other, 0)

    for slot in range(4):
        for pair in m_copies[slot:] if slot == 3 else m_copies[slot:slot + 1]:
            wait_pair(pair)
        lat[origin[slot]] = lat[origin[slot]] + from_code(mpr[slot]) * msr[slot]
    whole = lat[...].reshape(KVW, TOK)
    latent = whole[:LATW]
    inverse = lax.rsqrt(jnp.sum(latent * latent, axis=0, keepdims=True) / LATW + eps_norm)
    gain_cols = jnp.transpose(jnp.broadcast_to(gain[...], (128, LATW)))
    for j in range(TOK // 128):
        at = slice(j * 128, j * 128 + 128)
        rows[:LATW, at] = (latent[:, at] * inverse[:, at] * gain_cols).astype(BF16)
    first, second = whole[LATW:LATW + ROPEW // 2], whole[LATW + ROPEW // 2:]
    rows[LATW:LATW + ROPEW // 2, :] = (first * cosine[...] - second * sine[...]).astype(BF16)
    rows[LATW + ROPEW // 2:KVW, :] = (first * sine[...] + second * cosine[...]).astype(BF16)

    slot_at = lax.broadcasted_iota(I32, (CAPTOK, TOK), 0)

    def pack_for(to):
        chosen = ((slot_at + to * CAPTOK) == tok[...]).astype(F32)
        empty = jnp.sum(chosen, axis=1, keepdims=True) < 0.5
        page_rows = nt(chosen.astype(BF16), rows[...])
        column = lax.broadcasted_iota(I32, (CAPTOK, KVX), 1)
        return jnp.where((column == KVW) & empty, 1.0, page_rows).astype(BF16)

    half = CAPTOK // 2
    a_r0 = link(packed.at[2, pl.ds(0, half)], relay.at[0], dev_zp)
    a_r1 = link(packed.at[2, pl.ds(half, half)], relay.at[1], dev_zm)
    a_p = link(packed.at[0], arr.at[1, c], dev_zp)
    a_m = link(packed.at[1], arr.at[2, c], dev_zm)
    a_f0 = link(relay.at[0], arr.at[3, c, pl.ds(0, half)], dev_zp)
    a_f1 = link(relay.at[1], arr.at[3, c, pl.ds(half, half)], dev_zm)
    a_share = [link(arr.at[slot, c], arr.at[slot, c], dev_sib) for slot in range(3)]
    a_share3 = [
        link(arr.at[3, c, pl.ds(0, half)], arr.at[3, c, pl.ds(0, half)], dev_sib),
        link(arr.at[3, c, pl.ds(half, half)], arr.at[3, c, pl.ds(half, half)], dev_sib),
    ]
    packed[2] = pack_for(lax.rem(b + 2, 4))
    go(a_r0)
    go(a_r1)
    packed[0] = pack_for(lax.rem(b + 1, 4))
    go(a_p)
    packed[1] = pack_for(lax.rem(b + 3, 4))
    go(a_m)
    arr[0, c] = pack_for(b)
    go(a_share[0])

    def pages_step(pair, first, last):
        keys = arr[first:last + 1].reshape((last + 1 - first) * 2 * CAPTOK, KVX)
        scores = [nt(qbuf[c * NR + r], keys) for r in pair]
        weights = []
        for r, score in zip(pair, scores):
            old = ms[r][:, :1]
            top = jnp.maximum(old, jnp.max(peak(score), axis=1, keepdims=True))
            shrink = jnp.exp2((old - top) * log2_scale)
            w = weigh(score, top)
            weights.append((w.astype(BF16), shrink, top, ls[r] * shrink + fold(w)))
        return [
            (acc[r] * shrink + nn(w, keys[:, :LATW]), jnp.broadcast_to(top, (QROWS, 128)), total)
            for r, (w, shrink, top, total) in zip(pair, weights)
        ]

    def pages_of(first, last):
        def body(i, carry):
            pair = (2 * i, 2 * i + 1)
            for r, state in zip(pair, pages_step(pair, first, last)):
                acc[r], ms[r], ls[r] = state
            return carry

        lax.fori_loop(0, 2, body, 0)

    a_r0.wait_recv()
    go(a_f0)
    a_r1.wait_recv()
    go(a_f1)
    a_share[0].wait_recv()
    pages_of(0, 0)
    a_p.wait_recv()
    go(a_share[1])
    a_m.wait_recv()
    go(a_share[2])
    a_share[1].wait_recv()
    a_share[2].wait_recv()
    pages_of(1, 2)
    a_f0.wait_recv()
    go(a_share3[0])
    a_f1.wait_recv()
    go(a_share3[1])
    a_share3[0].wait_recv()
    a_share3[1].wait_recv()

    def merge(parts):
        top = parts[0][1][0]
        for _, stat in parts[1:]:
            top = jnp.maximum(top, stat[0])
        value, total = 0.0, 0.0
        for coded, stat in parts:
            factor = jnp.exp2(stat[0] - top)
            value = value + from_code(coded) * factor
            total = total + factor * stat[1]
        return value, top, total

    def put(coded_ref, stat_ref, value, top, total):
        coded, scale = code(value, 0)
        coded_ref[...] = to_code(coded).reshape(coded_ref.shape)
        stat_ref[0] = top + jnp.log(scale) * log2_e
        stat_ref[1] = total / scale

    yp, ym, yy = lax.rem(y + 1, 4), lax.rem(y + 3, 4), lax.rem(y + 2, 4)
    first_y = used[0]

    def y_pair(r, k):
        pairs = (
            (osend.at[r, yy, 0], ostat.at[r], 0, dev_yp),
            (osend.at[r, yy, 1], ostat.at[r], 1, dev_ym),
            (osend.at[r, yp, 1], ostat.at[r], 2, dev_yp),
            (osend.at[r, ym, 0], ostat.at[r], 3, dev_ym),
            (rsend.at[r, 0], rstat.at[r, 0], 4, dev_yp),
            (rsend.at[r, 1], rstat.at[r, 1], 5, dev_ym),
        )
        data, stat, _, dev = pairs[k]
        return (
            link_at(first_y + 18 * r + 2 * k, data, ybuf.at[r, k], dev),
            link_at(first_y + 18 * r + 2 * k + 1, stat, ystat.at[r, k], dev),
        )

    def last_pair(r, k):
        half, core, dev = ((1 - xh, c, dev_x), (1 - xh, 1 - c, dev_x_sib), (xh, 1 - c, dev_sib))[k]
        return (
            link_at(first_y + 18 * r + 12 + 2 * k, mbuf.at[r, half, core], fbuf.at[r, k], dev),
            link_at(first_y + 18 * r + 13 + 2 * k, mstat.at[r, half], fstat.at[r, k], dev),
        )

    def start_pair(pair):
        pair[0].start()
        pair[1].start()

    for r in range(NR):
        value, top, total = pages_step((r,), 3, 3)[0]
        coded, scale = code(value, 1)
        osend[r] = to_code(jnp.transpose(coded)).reshape(4, 2, 64, QROWS)
        stat = jnp.transpose(jnp.where(lane == 0, top * log2_scale + jnp.log(scale) * log2_e, 1.0 / scale))
        ostat[r, 0] = stat[0:1]
        ostat[r, 1] = jnp.sum(jnp.transpose(total), axis=0, keepdims=True) * stat[1:2]
        for k in range(4):
            start_pair(y_pair(r, k))

    def relay_sums(r, carry):
        for k, to in ((0, yp), (1, ym)):
            wait_pair(y_pair(r, k))
            put(rsend.at[r, k], rstat.at[r, k], *merge([
                (osend[r, to, k], ostat[r]), (ybuf[r, k], ystat[r, k]),
            ]))
            start_pair(y_pair(r, 4 + k))
        return carry

    def sums_over_y(r, carry):
        for k in range(2, 6):
            wait_pair(y_pair(r, k))
        for h, (one, two) in enumerate(((3, 4), (2, 5))):
            put(mbuf.at[r, h], mstat.at[r, h], *merge([
                (osend[r, y, h], ostat[r]), (ybuf[r, one], ystat[r, one]), (ybuf[r, two], ystat[r, two]),
            ]))
        for k in (1, 0, 2):
            start_pair(last_pair(r, k))
        return carry

    def last_sums(r, carry):
        for k in range(3):
            wait_pair(last_pair(r, k))
        own, other = c * NR + r, (1 - c) * NR + r
        for request, parts in (
            (own, [(mbuf[r, xh, c], mstat[r, xh]), (fbuf[r, 0], fstat[r, 0])]),
            (other, [(fbuf[r, 2], fstat[r, 2]), (fbuf[r, 1], fstat[r, 1])]),
        ):
            value, _, total = merge(parts)
            value = value / total
            for step in range(4):
                out[step, request] = value[:, 64 * step:64 * step + 64]
        return carry

    def finish(r, carry):
        for pair in [y_pair(r, k) for k in range(6)] + [last_pair(r, k) for k in range(3)]:
            pair[0].wait_send()
            pair[1].wait_send()
        return carry

    for stage in (relay_sums, sums_over_y, last_sums, finish):
        lax.fori_loop(0, NR, stage, 0)
    for copy in started:
        copy.wait_send()


LINKS = 144


def tables():
    half = ROPEW // 2
    frequency = rope_base ** (-np.arange(half, dtype=np.float32) / np.float32(half))
    angles = np.arange(TOK, dtype=np.float32)[None, :] * frequency.astype(np.float32)[:, None]
    return np.cos(angles).astype(np.float32), np.sin(angles).astype(np.float32)


def on_device(hidden, kv_down, kv_gain, page_owner, page_request, queries, cache, lengths):
    cosine, sine = tables()
    anywhere = pl.BlockSpec(memory_space=pl.ANY)
    vmem = pl.BlockSpec(memory_space=pltpu.VMEM)
    smem = pl.BlockSpec(memory_space=pltpu.SMEM)
    sums = pl.pallas_call(
        kernel,
        out_shape=jax.ShapeDtypeStruct((4, 2 * NR, 32, 64), F32),
        in_specs=[anywhere, anywhere, vmem, smem, smem, anywhere, anywhere, smem, vmem, vmem],
        out_specs=vmem,
        scratch_shapes=[
            pltpu.VMEM((TOK, HALF_D), BF16),
            pltpu.VMEM((4, BLK, HALF_D), BF16),
            pltpu.VMEM((4, BLK, TOK), F32),
            pltpu.VMEM((4, BLK, TOK), I16),
            pltpu.VMEM((4, BLK, TOK), I16),
            pltpu.VMEM((4, 1, TOK), F32),
            pltpu.VMEM((4, 1, TOK), F32),
            pltpu.VMEM((KVX, TOK), BF16),
            pltpu.VMEM((3, CAPTOK, KVX), BF16),
            pltpu.VMEM((2, CAPTOK // 2, KVX), BF16),
            pltpu.VMEM((4, 2, CAPTOK, KVX), BF16),
            pltpu.VMEM((1, TOK), I32),
            pltpu.VMEM((2 * NR, 4, 64, KVW), BF16),
            pltpu.VMEM((2 * NR, QROWS, KVX), BF16),
            pltpu.VMEM((2 * NR, KVW, CTXD), BF16),
            pltpu.VMEM((NR, QROWS, LATW), I16),
            pltpu.VMEM((NR, 3, 1, QROWS), F32),
            pltpu.VMEM((NR, QROWS, LATW), I16),
            pltpu.VMEM((NR, 3, 1, QROWS), F32),
            pltpu.VMEM((NR, QROWS, LATW), F32),
            pltpu.VMEM((NR, QROWS, 128), F32),
            pltpu.VMEM((NR, QROWS, 128), F32),
            pltpu.VMEM((NR, 4, 2, 64, QROWS), I16),
            pltpu.VMEM((NR, 2, 1, QROWS), F32),
            pltpu.VMEM((NR, 6, 64, QROWS), I16),
            pltpu.VMEM((NR, 6, 2, 1, QROWS), F32),
            pltpu.VMEM((NR, 2, 64, QROWS), I16),
            pltpu.VMEM((NR, 2, 2, 1, QROWS), F32),
            pltpu.VMEM((NR, 2, 2, 32, QROWS), I16),
            pltpu.VMEM((NR, 2, 2, 1, QROWS), F32),
            pltpu.VMEM((NR, 3, 32, QROWS), I16),
            pltpu.VMEM((NR, 3, 2, 1, QROWS), F32),
            pltpu.SemaphoreType.DMA((7,)),
            pltpu.SemaphoreType.DMA((LINKS,)),
            pltpu.SemaphoreType.DMA((LINKS,)),
        ],
        compiler_params=pltpu.CompilerParams(
            collective_id=0, has_side_effects=True, vmem_limit_bytes=56 * 1024 * 1024
        ),
        cost_estimate=pl.CostEstimate(flops=7_500_000_000, bytes_accessed=12_000_000, transcendentals=3_000_000),
    )(
        hidden, kv_down.T, kv_gain.reshape(1, LATW), page_owner.T, page_request, queries, cache.transpose(0, 2, 1), lengths,
        jnp.asarray(cosine), jnp.asarray(sine),
    )
    return sums.transpose(0, 1, 3, 2)


def solution(mesh):
    return jax.shard_map(
        on_device,
        mesh=mesh,
        in_specs=(
            P(("seq", "batch"), "mp"),
            P("mp", "batch"),
            P(),
            P(("seq", "batch"), None),
            P(("seq", "batch")),
            P(None, "batch", "mp", None),
            P("batch", "seq", None),
            P("batch"),
        ),
        out_specs=P(None, "batch", "mp", "seq"),
        check_vma=False,
    )
```

```python
import jax
import jax.numpy as jnp
import numpy as np
from jax import lax
from jax.experimental import pallas as pl
from jax.experimental.pallas import tpu as pltpu
from jax.sharding import PartitionSpec as P

MESH = pl.DeviceIdType.MESH
F32, BF16, I32, I16 = jnp.float32, jnp.bfloat16, jnp.int32, jnp.int16

eps_norm = 1e-06
score_scale = 192.0 ** (-0.5)
log2_e = 1.4426950408889634
log2_scale = score_scale * log2_e
rope_base = 10000.0
masked_value = -1e30
floor_value = -1e29
code_top = 32767.0

TOK, HALF_D, KVW, LATW, ROPEW = 384, 3584, 576, 512, 64
LABELS = 64
KVX = KVW + LABELS
BLK = 144
SHARE, DIRECT = 256, 384
CAPTOK = 192
PAGES, PAGE, CAP = 24, 16, 12
QROWS = 256
CTXD = 512
NR = 4
PAIRS = ((0, 1), (2, 3))


def nt(a, b):
    return lax.dot_general(a, b, (((1,), (1,)), ((), ())), preferred_element_type=F32)


def nn(a, b):
    return jnp.dot(a, b, preferred_element_type=F32)


def kernel(
    hidden, kv_down, gain, owner, request, queries, cache, lengths, cosine, sine,
    out,
    hid, kvt, lat, mps, mpr, mss, msr, rows, packed, relay, arr, tok,
    qraw, qbuf, kbuf, esend, estat, ebuf, efrom, acc, ms, ls, osend, ostat, ybuf, ystat, rsend, rstat, mbuf, mstat, fbuf, fstat,
    loc, send, recv,
):
    s, b, p = lax.axis_index("seq"), lax.axis_index("batch"), lax.axis_index("mp")
    c = lax.rem(s, 2)
    sib = s + 1 - 2 * c
    y = lax.div(s, 4)
    in_y = lax.rem(s, 4)
    xh = lax.rem(lax.div(s, 2), 2)
    dev_zp = (s, lax.rem(b + 1, 4), p)
    dev_zm = (s, lax.rem(b + 3, 4), p)
    dev_zz = (s, lax.rem(b + 2, 4), p)
    dev_mp = (s, b, 1 - p)
    dev_sib = (sib, b, p)
    dev_yp = (lax.rem(y + 1, 4) * 4 + in_y, b, p)
    dev_ym = (lax.rem(y + 3, 4) * 4 + in_y, b, p)
    dev_x = (s + 2 - 4 * xh, b, p)
    dev_x_sib = (sib + 2 - 4 * xh, b, p)

    used = [0]
    started = []

    def link(src, dst, dev):
        used[0] += 1
        return link_at(used[0] - 1, src, dst, dev)

    def link_at(i, src, dst, dev):
        return pltpu.make_async_remote_copy(
            src_ref=src, dst_ref=dst, send_sem=send.at[i], recv_sem=recv.at[i],
            device_id=dev, device_id_type=MESH,
        )

    def go(copy):
        copy.start()
        started.append(copy)

    def code(value, axis):
        most = jnp.max(jnp.abs(value), axis=axis, keepdims=True)
        most = jnp.maximum(most, 1e-25)
        return jnp.round(value * (code_top / most)), most * (1.0 / code_top)

    def to_code(value):
        return value.astype(I32).astype(I16)

    def from_code(coded):
        return coded.astype(I32).astype(F32)

    def go_pair(pair):
        go(pair[0])
        go(pair[1])

    def wait_pair(pair):
        pair[0].wait_recv()
        pair[1].wait_recv()

    load_kv = pltpu.make_async_copy(kv_down, kvt.at[0], loc.at[0])
    load_kv.start()
    load_hid = pltpu.make_async_copy(hidden, hid, loc.at[1])
    load_hid.start()
    load_q = []
    for step in range(4):
        load_q.append(pltpu.make_async_copy(queries.at[step], qraw.at[:, step], loc.at[2 + step]))
        load_q[-1].start()
    load_cache = pltpu.make_async_copy(cache, kbuf, loc.at[6])
    load_cache.start()

    barrier = pltpu.get_barrier_semaphore()
    for dev in (dev_zp, dev_zm, dev_zz, dev_mp, dev_sib, dev_yp, dev_ym, dev_x, dev_x_sib):
        pl.semaphore_signal(barrier, inc=1, device_id=dev, device_id_type=MESH)

    pl.semaphore_wait(barrier, 9)

    base = c * (HALF_D // 2)

    def lanes(start, size):
        return pl.ds(pl.multiple_of(base + start, 128), size)

    def kv_link(slot, to_slot, at, dev):
        return link(kvt.at[slot, :, at], kvt.at[to_slot, :, at], dev)

    def first_link(to_slot, at, dev):
        return link(kv_down.at[:, at], kvt.at[to_slot, :, at], dev)

    def part_of(k, first=0, size=SHARE):
        return lanes(lax.rem(y + k, 4) * SHARE + first, size)

    low, high = lanes(4 * SHARE, DIRECT), lanes(4 * SHARE + DIRECT, DIRECT)
    mine = part_of(0)
    s_p, s_m = first_link(1, mine, dev_zp), first_link(2, mine, dev_zm)
    d_p0, d_m1 = first_link(1, low, dev_zp), first_link(2, high, dev_zm)
    d_p1, d_m0 = first_link(1, high, dev_zp), first_link(2, low, dev_zm)
    for copy in (s_p, s_m, d_p0, d_m1):
        go(copy)
    sf_p, sf_m = (
        kv_link(1, 3, part_of(0, 0, SHARE // 2), dev_zp),
        kv_link(2, 3, part_of(0, SHARE // 2, SHARE // 2), dev_zm),
    )
    df_p, df_m = kv_link(1, 3, low, dev_zp), kv_link(2, 3, high, dev_zm)
    near_p = [None] + [kv_link(slot, slot, mine, dev_yp) for slot in (1, 2, 3)]
    near_m = [None] + [kv_link(slot, slot, mine, dev_ym) for slot in (1, 2, 3)]
    far = [None] + [
        (
            kv_link(slot, slot, part_of(3, 0, SHARE // 2), dev_yp),
            kv_link(slot, slot, part_of(1, SHARE // 2, SHARE // 2), dev_ym),
        )
        for slot in (1, 2, 3)
    ]
    share_s = [None] + [kv_link(slot, slot, lanes(0, 4 * SHARE), dev_sib) for slot in (1, 2, 3)]
    share_d = [None] + [kv_link(slot, slot, lanes(4 * SHARE, 2 * DIRECT), dev_sib) for slot in (1, 2, 3)]

    token = lax.broadcasted_iota(I32, (1, TOK), 1)
    token_page = lax.shift_right_logical(token, 4)
    dest = jnp.zeros((1, TOK), I32)
    asked = jnp.zeros((1, TOK), I32)
    counts = [jnp.int32(0)] * 4
    for page in range(PAGES):
        to = owner[0, page]
        rank = jnp.where(to == 0, counts[0], jnp.where(to == 1, counts[1], jnp.where(to == 2, counts[2], counts[3])))
        counts = [counts[o] + (to == o).astype(I32) for o in range(4)]
        dest = jnp.where(token_page == page, (to * CAP + rank) * PAGE, dest)
        asked = jnp.where(token_page == page, request[page] + 1, asked)
    dest = dest + lax.bitwise_and(token, 15)
    tok[...] = dest

    label_row = lax.broadcasted_iota(I32, (LABELS, TOK), 0)
    rows[KVW:, :] = (label_row == asked).astype(F32).astype(BF16)

    origin = [lax.rem(b + ahead, 4) for ahead in (0, 3, 1, 2)]
    m_copies = [
        (link(mps.at[slot], mpr.at[slot], dev_mp), link(mss.at[slot], msr.at[slot], dev_mp)) for slot in range(3)
    ]
    tails = (slice(0, 256), slice(256, TOK))
    for at in tails:
        at = pl.ds(at.start, at.stop - at.start)
        m_copies.append((
            link(mps.at[3, :, at], mpr.at[3, :, at], dev_mp), link(mss.at[3, :, at], msr.at[3, :, at], dev_mp),
        ))

    def send_part(slot, part, copies, at=slice(None)):
        lat[origin[slot], :, at] = part
        coded, scale = code(part, 0)
        mps[slot, :, at] = to_code(coded)
        mss[slot, :, at] = scale
        go_pair(copies)

    def weigh(score, top):
        return jnp.exp2(score * log2_scale - top * log2_scale)

    def fold(w):
        total = w[:, :128]
        for j in range(1, w.shape[1] // 128):
            total = total + w[:, j * 128:j * 128 + 128]
        return total

    def peak(score):
        most = score[:, :128]
        for j in range(1, score.shape[1] // 128):
            most = jnp.maximum(most, score[:, j * 128:j * 128 + 128])
        return most

    lane = lax.broadcasted_iota(I32, (QROWS, 128), 1)

    def put_columns(stat_ref, top, total, scale):
        stat = jnp.transpose(jnp.where(lane == 0, top * log2_scale, scale))
        stat_ref[0] = stat[0:1]
        stat_ref[1] = jnp.sum(jnp.transpose(total), axis=0, keepdims=True)
        stat_ref[2] = stat[1:2]

    def resident(pair, half):
        at = lax.broadcasted_iota(I32, (1, CTXD), 1) + s * CTXD
        scores = [
            jnp.where(at < lengths[half * NR + r], nn(qbuf[half * NR + r, :, :KVW], kbuf[half * NR + r]), masked_value)
            for r in pair
        ]
        weights = []
        for score in scores:
            top = jnp.maximum(jnp.max(peak(score), axis=1, keepdims=True), floor_value)
            w = weigh(score, top)
            weights.append((w.astype(BF16), jnp.broadcast_to(top, (QROWS, 128)), fold(w)))
        return [
            (nt(w, kbuf[half * NR + r, :LATW, :]), top, total) for r, (w, top, total) in zip(pair, weights)
        ]

    def resident_own(i, carry):
        for r, state in zip((2 * i, 2 * i + 1), resident((2 * i, 2 * i + 1), c)):
            acc[r], ms[r], ls[r] = state
        return carry

    def add_other(r, carry):
        row = lax.broadcasted_iota(I32, (128, QROWS), 0)
        stat = jnp.where(row == 0, efrom[r, 0], jnp.where(row == 1, efrom[r, 1], efrom[r, 2]))
        stat = jnp.transpose(stat)
        top2, total2, scale2 = stat[:, 0:1] * (1.0 / log2_scale), stat[:, 1:2], stat[:, 2:3]
        old = ms[r][:, :1]
        top = jnp.maximum(old, top2)
        keep, gain2 = jnp.exp2((old - top) * log2_scale), jnp.exp2((top2 - top) * log2_scale)
        acc[r] = acc[r] * keep + from_code(ebuf[r]) * (gain2 * scale2)
        ms[r] = jnp.broadcast_to(top, (QROWS, 128))
        ls[r] = ls[r] * keep + jnp.where(lane == 0, gain2 * total2, 0.0)
        return carry

    load_hid.wait()
    load_kv.wait()
    s_p.wait_recv()
    go(sf_p)
    go(near_p[1])
    go(near_m[1])
    s_m.wait_recv()
    go(sf_m)
    go(near_p[2])
    go(near_m[2])
    go(d_p1)
    go(d_m0)
    send_part(0, jnp.transpose(nt(hid[...], kvt[0])), m_copies[0])

    d_p0.wait_recv()
    go(df_p)
    d_m1.wait_recv()
    go(df_m)

    def pass_on(slot):
        near_p[slot].wait_recv()
        go(far[slot][0])
        near_m[slot].wait_recv()
        go(far[slot][1])

    def swap_shared(slot):
        far[slot][0].wait_recv()
        far[slot][1].wait_recv()
        go(share_s[slot])

    pass_on(1)
    sf_p.wait_recv()
    sf_m.wait_recv()
    go(near_p[3])
    go(near_m[3])

    for copy in load_q:
        copy.wait()
    load_cache.wait()
    label_at = lax.broadcasted_iota(I32, (QROWS, LABELS), 1)

    def fill(r, carry):
        qbuf[r, :, :KVW] = qraw[r].reshape(QROWS, KVW)
        qbuf[r, :, KVW:] = jnp.where(label_at == r + 1, 0.0, masked_value).astype(BF16)
        return carry

    def resident_other(i, carry):
        for r, (value, top, total) in zip((2 * i, 2 * i + 1), resident((2 * i, 2 * i + 1), 1 - c)):
            coded, scale = code(value, 1)
            esend[r] = to_code(coded)
            put_columns(estat.at[r], top, total, scale)
        return carry

    lax.fori_loop(0, 2 * NR, fill, 0)
    lax.fori_loop(0, 1, resident_other, 0)

    pass_on(2)
    d_p1.wait_recv()
    go(share_d[1])
    d_m0.wait_recv()
    go(share_d[2])
    swap_shared(1)
    swap_shared(2)

    for slot in (1, 2):
        share_d[slot].wait_recv()
        share_s[slot].wait_recv()
        send_part(slot, jnp.transpose(nt(hid[...], kvt[slot])), m_copies[slot])
        if slot == 1:
            pass_on(3)

    def over_lanes(starts, size, at):
        part = sum(nt(hid[at, start:start + size], kvt[3, :, start:start + size]) for start in starts)
        return jnp.transpose(part)

    direct_at = ((4 * SHARE, HALF_D // 2 + 4 * SHARE), 2 * DIRECT)
    shared_at = ((0, HALF_D // 2), 4 * SHARE)
    df_p.wait_recv()
    df_m.wait_recv()
    go(share_d[3])
    swap_shared(3)
    share_d[3].wait_recv()
    lat[origin[3]] = over_lanes(*direct_at, slice(None))
    share_s[3].wait_recv()
    for i, at in enumerate(tails):
        send_part(3, lat[origin[3], :, at] + over_lanes(*shared_at, at), m_copies[3 + i], at)

    lax.fori_loop(1, 2, resident_other, 0)
    e_copies = [
        (link(esend.at[r], ebuf.at[r], dev_sib), link(estat.at[r], efrom.at[r], dev_sib)) for r in range(NR)
    ]
    for pair in e_copies:
        go_pair(pair)
    lax.fori_loop(0, 2, resident_own, 0)
    for pair in e_copies:
        wait_pair(pair)
    lax.fori_loop(0, NR, add_other, 0)

    for slot in range(4):
        for pair in m_copies[slot:] if slot == 3 else m_copies[slot:slot + 1]:
            wait_pair(pair)
        lat[origin[slot]] = lat[origin[slot]] + from_code(mpr[slot]) * msr[slot]
    whole = lat[...].reshape(KVW, TOK)
    latent = whole[:LATW]
    inverse = lax.rsqrt(jnp.sum(latent * latent, axis=0, keepdims=True) / LATW + eps_norm)
    gain_cols = jnp.transpose(jnp.broadcast_to(gain[...], (128, LATW)))
    for j in range(TOK // 128):
        at = slice(j * 128, j * 128 + 128)
        rows[:LATW, at] = (latent[:, at] * inverse[:, at] * gain_cols).astype(BF16)
    first, second = whole[LATW:LATW + ROPEW // 2], whole[LATW + ROPEW // 2:]
    rows[LATW:LATW + ROPEW // 2, :] = (first * cosine[...] - second * sine[...]).astype(BF16)
    rows[LATW + ROPEW // 2:KVW, :] = (first * sine[...] + second * cosine[...]).astype(BF16)

    slot_at = lax.broadcasted_iota(I32, (CAPTOK, TOK), 0)

    def pack_for(to):
        chosen = ((slot_at + to * CAPTOK) == tok[...]).astype(F32)
        empty = jnp.sum(chosen, axis=1, keepdims=True) < 0.5
        page_rows = nt(chosen.astype(BF16), rows[...])
        column = lax.broadcasted_iota(I32, (CAPTOK, KVX), 1)
        return jnp.where((column == KVW) & empty, 1.0, page_rows).astype(BF16)

    half = CAPTOK // 2
    a_r0 = link(packed.at[2, pl.ds(0, half)], relay.at[0], dev_zp)
    a_r1 = link(packed.at[2, pl.ds(half, half)], relay.at[1], dev_zm)
    a_p = link(packed.at[0], arr.at[1, c], dev_zp)
    a_m = link(packed.at[1], arr.at[2, c], dev_zm)
    a_f0 = link(relay.at[0], arr.at[3, c, pl.ds(0, half)], dev_zp)
    a_f1 = link(relay.at[1], arr.at[3, c, pl.ds(half, half)], dev_zm)
    a_share = [link(arr.at[slot, c], arr.at[slot, c], dev_sib) for slot in range(3)]
    a_share3 = [
        link(arr.at[3, c, pl.ds(0, half)], arr.at[3, c, pl.ds(0, half)], dev_sib),
        link(arr.at[3, c, pl.ds(half, half)], arr.at[3, c, pl.ds(half, half)], dev_sib),
    ]
    packed[2] = pack_for(lax.rem(b + 2, 4))
    go(a_r0)
    go(a_r1)
    packed[0] = pack_for(lax.rem(b + 1, 4))
    go(a_p)
    packed[1] = pack_for(lax.rem(b + 3, 4))
    go(a_m)
    arr[0, c] = pack_for(b)
    go(a_share[0])

    def pages_step(pair, first, last):
        keys = arr[first:last + 1].reshape((last + 1 - first) * 2 * CAPTOK, KVX)
        scores = [nt(qbuf[c * NR + r], keys) for r in pair]
        weights = []
        for r, score in zip(pair, scores):
            old = ms[r][:, :1]
            top = jnp.maximum(old, jnp.max(peak(score), axis=1, keepdims=True))
            shrink = jnp.exp2((old - top) * log2_scale)
            w = weigh(score, top)
            weights.append((w.astype(BF16), shrink, top, ls[r] * shrink + fold(w)))
        return [
            (acc[r] * shrink + nn(w, keys[:, :LATW]), jnp.broadcast_to(top, (QROWS, 128)), total)
            for r, (w, shrink, top, total) in zip(pair, weights)
        ]

    def pages_of(first, last):
        def body(i, carry):
            pair = (2 * i, 2 * i + 1)
            for r, state in zip(pair, pages_step(pair, first, last)):
                acc[r], ms[r], ls[r] = state
            return carry

        lax.fori_loop(0, 2, body, 0)

    a_r0.wait_recv()
    go(a_f0)
    a_r1.wait_recv()
    go(a_f1)
    a_share[0].wait_recv()
    pages_of(0, 0)
    a_p.wait_recv()
    go(a_share[1])
    a_m.wait_recv()
    go(a_share[2])
    a_share[1].wait_recv()
    a_share[2].wait_recv()
    pages_of(1, 2)
    a_f0.wait_recv()
    go(a_share3[0])
    a_f1.wait_recv()
    go(a_share3[1])
    a_share3[0].wait_recv()
    a_share3[1].wait_recv()

    def merge(parts):
        top = parts[0][1][0]
        for _, stat in parts[1:]:
            top = jnp.maximum(top, stat[0])
        value, total = 0.0, 0.0
        for coded, stat in parts:
            factor = jnp.exp2(stat[0] - top)
            value = value + from_code(coded) * factor
            total = total + factor * stat[1]
        return value, top, total

    def put(coded_ref, stat_ref, value, top, total):
        coded, scale = code(value, 0)
        coded_ref[...] = to_code(coded).reshape(coded_ref.shape)
        stat_ref[0] = top + jnp.log(scale) * log2_e
        stat_ref[1] = total / scale

    yp, ym, yy = lax.rem(y + 1, 4), lax.rem(y + 3, 4), lax.rem(y + 2, 4)
    first_y = used[0]

    def y_pair(r, k):
        pairs = (
            (osend.at[r, yy, 0], ostat.at[r], 0, dev_yp),
            (osend.at[r, yy, 1], ostat.at[r], 1, dev_ym),
            (osend.at[r, yp, 1], ostat.at[r], 2, dev_yp),
            (osend.at[r, ym, 0], ostat.at[r], 3, dev_ym),
            (rsend.at[r, 0], rstat.at[r, 0], 4, dev_yp),
            (rsend.at[r, 1], rstat.at[r, 1], 5, dev_ym),
        )
        data, stat, _, dev = pairs[k]
        return (
            link_at(first_y + 18 * r + 2 * k, data, ybuf.at[r, k], dev),
            link_at(first_y + 18 * r + 2 * k + 1, stat, ystat.at[r, k], dev),
        )

    def last_pair(r, k):
        half, core, dev = ((1 - xh, c, dev_x), (1 - xh, 1 - c, dev_x_sib), (xh, 1 - c, dev_sib))[k]
        return (
            link_at(first_y + 18 * r + 12 + 2 * k, mbuf.at[r, half, core], fbuf.at[r, k], dev),
            link_at(first_y + 18 * r + 13 + 2 * k, mstat.at[r, half], fstat.at[r, k], dev),
        )

    def start_pair(pair):
        pair[0].start()
        pair[1].start()

    for r in range(NR):
        value, top, total = pages_step((r,), 3, 3)[0]
        coded, scale = code(value, 1)
        osend[r] = to_code(jnp.transpose(coded)).reshape(4, 2, 64, QROWS)
        stat = jnp.transpose(jnp.where(lane == 0, top * log2_scale + jnp.log(scale) * log2_e, 1.0 / scale))
        ostat[r, 0] = stat[0:1]
        ostat[r, 1] = jnp.sum(jnp.transpose(total), axis=0, keepdims=True) * stat[1:2]
        for k in range(4):
            start_pair(y_pair(r, k))

    def relay_sums(r, carry):
        for k, to in ((0, yp), (1, ym)):
            wait_pair(y_pair(r, k))
            put(rsend.at[r, k], rstat.at[r, k], *merge([
                (osend[r, to, k], ostat[r]), (ybuf[r, k], ystat[r, k]),
            ]))
            start_pair(y_pair(r, 4 + k))
        return carry

    def sums_over_y(r, carry):
        for k in range(2, 6):
            wait_pair(y_pair(r, k))
        for h, (one, two) in enumerate(((3, 4), (2, 5))):
            put(mbuf.at[r, h], mstat.at[r, h], *merge([
                (osend[r, y, h], ostat[r]), (ybuf[r, one], ystat[r, one]), (ybuf[r, two], ystat[r, two]),
            ]))
        for k in (1, 0, 2):
            start_pair(last_pair(r, k))
        return carry

    def last_sums(r, carry):
        for k in range(3):
            wait_pair(last_pair(r, k))
        own, other = c * NR + r, (1 - c) * NR + r
        for request, parts in (
            (own, [(mbuf[r, xh, c], mstat[r, xh]), (fbuf[r, 0], fstat[r, 0])]),
            (other, [(fbuf[r, 2], fstat[r, 2]), (fbuf[r, 1], fstat[r, 1])]),
        ):
            value, _, total = merge(parts)
            value = value / total
            for step in range(4):
                out[step, request] = value[:, 64 * step:64 * step + 64]
        return carry

    def finish(r, carry):
        for pair in [y_pair(r, k) for k in range(6)] + [last_pair(r, k) for k in range(3)]:
            pair[0].wait_send()
            pair[1].wait_send()
        return carry

    for stage in (relay_sums, sums_over_y, last_sums, finish):
        lax.fori_loop(0, NR, stage, 0)
    for copy in started:
        copy.wait_send()


LINKS = 144


def tables():
    half = ROPEW // 2
    frequency = rope_base ** (-np.arange(half, dtype=np.float32) / np.float32(half))
    angles = np.arange(TOK, dtype=np.float32)[None, :] * frequency.astype(np.float32)[:, None]
    return np.cos(angles).astype(np.float32), np.sin(angles).astype(np.float32)


def on_device(hidden, kv_down, kv_gain, page_owner, page_request, queries, cache, lengths):
    cosine, sine = tables()
    anywhere = pl.BlockSpec(memory_space=pl.ANY)
    vmem = pl.BlockSpec(memory_space=pltpu.VMEM)
    smem = pl.BlockSpec(memory_space=pltpu.SMEM)
    sums = pl.pallas_call(
        kernel,
        out_shape=jax.ShapeDtypeStruct((4, 2 * NR, 32, 64), F32),
        in_specs=[anywhere, anywhere, vmem, smem, smem, anywhere, anywhere, smem, vmem, vmem],
        out_specs=vmem,
        scratch_shapes=[
            pltpu.VMEM((TOK, HALF_D), BF16),
            pltpu.VMEM((4, BLK, HALF_D), BF16),
            pltpu.VMEM((4, BLK, TOK), F32),
            pltpu.VMEM((4, BLK, TOK), I16),
            pltpu.VMEM((4, BLK, TOK), I16),
            pltpu.VMEM((4, 1, TOK), F32),
            pltpu.VMEM((4, 1, TOK), F32),
            pltpu.VMEM((KVX, TOK), BF16),
            pltpu.VMEM((3, CAPTOK, KVX), BF16),
            pltpu.VMEM((2, CAPTOK // 2, KVX), BF16),
            pltpu.VMEM((4, 2, CAPTOK, KVX), BF16),
            pltpu.VMEM((1, TOK), I32),
            pltpu.VMEM((2 * NR, 4, 64, KVW), BF16),
            pltpu.VMEM((2 * NR, QROWS, KVX), BF16),
            pltpu.VMEM((2 * NR, KVW, CTXD), BF16),
            pltpu.VMEM((NR, QROWS, LATW), I16),
            pltpu.VMEM((NR, 3, 1, QROWS), F32),
            pltpu.VMEM((NR, QROWS, LATW), I16),
            pltpu.VMEM((NR, 3, 1, QROWS), F32),
            pltpu.VMEM((NR, QROWS, LATW), F32),
            pltpu.VMEM((NR, QROWS, 128), F32),
            pltpu.VMEM((NR, QROWS, 128), F32),
            pltpu.VMEM((NR, 4, 2, 64, QROWS), I16),
            pltpu.VMEM((NR, 2, 1, QROWS), F32),
            pltpu.VMEM((NR, 6, 64, QROWS), I16),
            pltpu.VMEM((NR, 6, 2, 1, QROWS), F32),
            pltpu.VMEM((NR, 2, 64, QROWS), I16),
            pltpu.VMEM((NR, 2, 2, 1, QROWS), F32),
            pltpu.VMEM((NR, 2, 2, 32, QROWS), I16),
            pltpu.VMEM((NR, 2, 2, 1, QROWS), F32),
            pltpu.VMEM((NR, 3, 32, QROWS), I16),
            pltpu.VMEM((NR, 3, 2, 1, QROWS), F32),
            pltpu.SemaphoreType.DMA((7,)),
            pltpu.SemaphoreType.DMA((LINKS,)),
            pltpu.SemaphoreType.DMA((LINKS,)),
        ],
        compiler_params=pltpu.CompilerParams(
            collective_id=0, has_side_effects=True, vmem_limit_bytes=56 * 1024 * 1024
        ),
        cost_estimate=pl.CostEstimate(flops=7_500_000_000, bytes_accessed=12_000_000, transcendentals=3_000_000),
    )(
        hidden, kv_down.T, kv_gain.reshape(1, LATW), page_owner.T, page_request, queries, cache.transpose(0, 2, 1), lengths,
        jnp.asarray(cosine), jnp.asarray(sine),
    )
    return sums.transpose(0, 1, 3, 2)


def solution(mesh):
    return jax.shard_map(
        on_device,
        mesh=mesh,
        in_specs=(
            P(("seq", "batch"), "mp"),
            P("mp", "batch"),
            P(),
            P(("seq", "batch"), None),
            P(("seq", "batch")),
            P(None, "batch", "mp", None),
            P("batch", "seq", None),
            P("batch"),
        ),
        out_specs=P(None, "batch", "mp", "seq"),
        check_vma=False,
    )
```

```python
import jax
import jax.numpy as jnp
import numpy as np
from jax import lax
from jax.experimental import pallas as pl
from jax.experimental.pallas import tpu as pltpu
from jax.sharding import PartitionSpec as P

MESH = pl.DeviceIdType.MESH
F32, BF16, I32, I16 = jnp.float32, jnp.bfloat16, jnp.int32, jnp.int16

eps_norm = 1e-06
score_scale = 192.0 ** (-0.5)
log2_e = 1.4426950408889634
log2_scale = score_scale * log2_e
rope_base = 10000.0
masked_value = -1e30
floor_value = -1e29
code_top = 32767.0

TOK, HALF_D, KVW, LATW, ROPEW = 384, 3584, 576, 512, 64
LABELS = 64
KVX = KVW + LABELS
BLK = 144
SHARE, DIRECT = 256, 384
CAPTOK = 192
PAGES, PAGE, CAP = 24, 16, 12
QROWS = 256
CTXD = 512
NR = 4
PAIRS = ((0, 1), (2, 3))


def nt(a, b):
    return lax.dot_general(a, b, (((1,), (1,)), ((), ())), preferred_element_type=F32)


def nn(a, b):
    return jnp.dot(a, b, preferred_element_type=F32)


def kernel(
    hidden, kv_down, gain, owner, request, queries, cache, lengths, cosine, sine,
    out,
    hid, hidt, keyst, kvt, lat, mps, mpr, mss, msr, rows, packed, relay, arr, tok,
    qraw, qbuf, kbuf, esend, estat, ebuf, efrom, acc, ms, ls, osend, ostat, ybuf, ystat, rsend, rstat, mbuf, mstat, fbuf, fstat,
    loc, send, recv,
):
    s, b, p = lax.axis_index("seq"), lax.axis_index("batch"), lax.axis_index("mp")
    c = lax.rem(s, 2)
    sib = s + 1 - 2 * c
    y = lax.div(s, 4)
    in_y = lax.rem(s, 4)
    xh = lax.rem(lax.div(s, 2), 2)
    dev_zp = (s, lax.rem(b + 1, 4), p)
    dev_zm = (s, lax.rem(b + 3, 4), p)
    dev_zz = (s, lax.rem(b + 2, 4), p)
    dev_mp = (s, b, 1 - p)
    dev_sib = (sib, b, p)
    dev_yp = (lax.rem(y + 1, 4) * 4 + in_y, b, p)
    dev_ym = (lax.rem(y + 3, 4) * 4 + in_y, b, p)
    dev_x = (s + 2 - 4 * xh, b, p)
    dev_x_sib = (sib + 2 - 4 * xh, b, p)

    used = [0]
    started = []

    def link(src, dst, dev):
        used[0] += 1
        return link_at(used[0] - 1, src, dst, dev)

    def link_at(i, src, dst, dev):
        return pltpu.make_async_remote_copy(
            src_ref=src, dst_ref=dst, send_sem=send.at[i], recv_sem=recv.at[i],
            device_id=dev, device_id_type=MESH,
        )

    def go(copy):
        copy.start()
        started.append(copy)

    def code(value, axis):
        most = jnp.max(jnp.abs(value), axis=axis, keepdims=True)
        most = jnp.maximum(most, 1e-25)
        return jnp.round(value * (code_top / most)), most * (1.0 / code_top)

    def to_code(value):
        return value.astype(I32).astype(I16)

    def from_code(coded):
        return coded.astype(I32).astype(F32)

    def go_pair(pair):
        go(pair[0])
        go(pair[1])

    def wait_pair(pair):
        pair[0].wait_recv()
        pair[1].wait_recv()

    load_kv = pltpu.make_async_copy(kv_down, kvt.at[0], loc.at[0])
    load_kv.start()
    load_hid = pltpu.make_async_copy(hidden, hid, loc.at[1])
    load_hid.start()
    load_q = []
    for step in range(4):
        load_q.append(pltpu.make_async_copy(queries.at[step], qraw.at[:, step], loc.at[2 + step]))
        load_q[-1].start()
    load_cache = pltpu.make_async_copy(cache, kbuf, loc.at[6])
    load_cache.start()

    barrier = pltpu.get_barrier_semaphore()
    for dev in (dev_zp, dev_zm, dev_zz, dev_mp, dev_sib, dev_yp, dev_ym, dev_x, dev_x_sib):
        pl.semaphore_signal(barrier, inc=1, device_id=dev, device_id_type=MESH)

    pl.semaphore_wait(barrier, 9)

    base = c * (HALF_D // 2)

    def lanes(start, size):
        return pl.ds(pl.multiple_of(base + start, 128), size)

    def kv_link(slot, to_slot, at, dev):
        return link(kvt.at[slot, :, at], kvt.at[to_slot, :, at], dev)

    def first_link(to_slot, at, dev):
        return link(kv_down.at[:, at], kvt.at[to_slot, :, at], dev)

    def part_of(k, first=0, size=SHARE):
        return lanes(lax.rem(y + k, 4) * SHARE + first, size)

    low, high = lanes(4 * SHARE, DIRECT), lanes(4 * SHARE + DIRECT, DIRECT)
    mine = part_of(0)
    s_p, s_m = first_link(1, mine, dev_zp), first_link(2, mine, dev_zm)
    d_p0, d_m1 = first_link(1, low, dev_zp), first_link(2, high, dev_zm)
    d_p1, d_m0 = first_link(1, high, dev_zp), first_link(2, low, dev_zm)
    for copy in (s_p, s_m, d_p0, d_m1):
        go(copy)
    sf_p, sf_m = (
        kv_link(1, 3, part_of(0, 0, SHARE // 2), dev_zp),
        kv_link(2, 3, part_of(0, SHARE // 2, SHARE // 2), dev_zm),
    )
    df_p, df_m = kv_link(1, 3, low, dev_zp), kv_link(2, 3, high, dev_zm)
    near_p = [None] + [kv_link(slot, slot, mine, dev_yp) for slot in (1, 2, 3)]
    near_m = [None] + [kv_link(slot, slot, mine, dev_ym) for slot in (1, 2, 3)]
    far = [
        None,
        [kv_link(1, 1, part_of(3), dev_yp)],
        [kv_link(2, 2, part_of(1), dev_ym)],
        [
            kv_link(3, 3, part_of(3, 0, SHARE // 2), dev_yp),
            kv_link(3, 3, part_of(1, SHARE // 2, SHARE // 2), dev_ym),
        ],
    ]
    share_s = [None] + [kv_link(slot, slot, lanes(0, 4 * SHARE), dev_sib) for slot in (1, 2, 3)]
    share_d = [None] + [kv_link(slot, slot, lanes(4 * SHARE, 2 * DIRECT), dev_sib) for slot in (1, 2, 3)]

    token = lax.broadcasted_iota(I32, (1, TOK), 1)
    token_page = lax.shift_right_logical(token, 4)
    dest = jnp.zeros((1, TOK), I32)
    asked = jnp.zeros((1, TOK), I32)
    counts = [jnp.int32(0)] * 4
    for page in range(PAGES):
        to = owner[0, page]
        rank = jnp.where(to == 0, counts[0], jnp.where(to == 1, counts[1], jnp.where(to == 2, counts[2], counts[3])))
        counts = [counts[o] + (to == o).astype(I32) for o in range(4)]
        dest = jnp.where(token_page == page, (to * CAP + rank) * PAGE, dest)
        asked = jnp.where(token_page == page, request[page] + 1, asked)
    dest = dest + lax.bitwise_and(token, 15)
    tok[...] = dest

    label_row = lax.broadcasted_iota(I32, (LABELS, TOK), 0)
    rows[KVW:, :] = (label_row == asked).astype(F32).astype(BF16)

    origin = [lax.rem(b + ahead, 4) for ahead in (0, 3, 1, 2)]
    m_copies = [
        (link(mps.at[slot], mpr.at[slot], dev_mp), link(mss.at[slot], msr.at[slot], dev_mp)) for slot in range(3)
    ]
    tails = (slice(0, 256), slice(256, TOK))
    for at in tails:
        at = pl.ds(at.start, at.stop - at.start)
        m_copies.append((
            link(mps.at[3, :, at], mpr.at[3, :, at], dev_mp), link(mss.at[3, :, at], msr.at[3, :, at], dev_mp),
        ))

    def send_part(slot, part, copies, at=slice(None)):
        lat[origin[slot], :, at] = part
        coded, scale = code(part, 0)
        mps[slot, :, at] = to_code(coded)
        mss[slot, :, at] = scale
        go_pair(copies)

    def weigh(score, top):
        return jnp.exp2(score * log2_scale - top * log2_scale)

    def fold(w):
        total = w[:, :128]
        for j in range(1, w.shape[1] // 128):
            total = total + w[:, j * 128:j * 128 + 128]
        return total

    def peak(score):
        most = score[:, :128]
        for j in range(1, score.shape[1] // 128):
            most = jnp.maximum(most, score[:, j * 128:j * 128 + 128])
        return most

    lane = lax.broadcasted_iota(I32, (QROWS, 128), 1)

    def put_columns(stat_ref, top, total, scale):
        stat = jnp.transpose(jnp.where(lane == 0, top * log2_scale, scale))
        stat_ref[0] = stat[0:1]
        stat_ref[1] = jnp.sum(jnp.transpose(total), axis=0, keepdims=True)
        stat_ref[2] = stat[1:2]

    def resident(pair, half):
        at = lax.broadcasted_iota(I32, (1, CTXD), 1) + s * CTXD
        scores = [
            jnp.where(at < lengths[half * NR + r], nn(qbuf[half * NR + r, :, :KVW], kbuf[half * NR + r]), masked_value)
            for r in pair
        ]
        weights = []
        for score in scores:
            top = jnp.maximum(jnp.max(peak(score), axis=1, keepdims=True), floor_value)
            w = weigh(score, top)
            weights.append((w.astype(BF16), jnp.broadcast_to(top, (QROWS, 128)), fold(w)))
        return [
            (nt(w, kbuf[half * NR + r, :LATW, :]), top, total) for r, (w, top, total) in zip(pair, weights)
        ]

    def resident_own(i, carry):
        for r, state in zip((2 * i, 2 * i + 1), resident((2 * i, 2 * i + 1), c)):
            acc[r], ms[r], ls[r] = state
        return carry

    def add_other(r, carry):
        row = lax.broadcasted_iota(I32, (128, QROWS), 0)
        stat = jnp.where(row == 0, efrom[r, 0], jnp.where(row == 1, efrom[r, 1], efrom[r, 2]))
        stat = jnp.transpose(stat)
        top2, total2, scale2 = stat[:, 0:1] * (1.0 / log2_scale), stat[:, 1:2], stat[:, 2:3]
        old = ms[r][:, :1]
        top = jnp.maximum(old, top2)
        keep, gain2 = jnp.exp2((old - top) * log2_scale), jnp.exp2((top2 - top) * log2_scale)
        acc[r] = acc[r] * keep + from_code(ebuf[r]) * (gain2 * scale2)
        ms[r] = jnp.broadcast_to(top, (QROWS, 128))
        ls[r] = ls[r] * keep + jnp.where(lane == 0, gain2 * total2, 0.0)
        return carry

    load_hid.wait()

    def turn(j, carry):
        at = pl.ds(pl.multiple_of(j * 512, 512), 512)
        hidt[at, :] = jnp.transpose(hid[:, at])
        return carry

    lax.fori_loop(0, HALF_D // 512, turn, 0)
    load_kv.wait()
    s_p.wait_recv()
    go(sf_p)
    go(near_p[1])
    go(near_m[1])
    s_m.wait_recv()
    go(sf_m)
    go(near_p[2])
    go(near_m[2])
    go(d_p1)
    go(d_m0)
    send_part(0, nn(kvt[0], hidt[...]), m_copies[0])

    near_p[1].wait_recv()
    go(far[1][0])
    near_m[2].wait_recv()
    go(far[2][0])
    d_p0.wait_recv()
    go(df_p)
    d_m1.wait_recv()
    go(df_m)
    sf_p.wait_recv()
    sf_m.wait_recv()
    go(near_p[3])
    go(near_m[3])

    for copy in load_q:
        copy.wait()
    load_cache.wait()
    label_at = lax.broadcasted_iota(I32, (QROWS, LABELS), 1)

    def fill(r, carry):
        qbuf[r, :, :KVW] = qraw[r].reshape(QROWS, KVW)
        qbuf[r, :, KVW:] = jnp.where(label_at == r + 1, 0.0, masked_value).astype(BF16)
        return carry

    lax.fori_loop(0, 2 * NR, fill, 0)

    def resident_other(i, carry):
        for r, (value, top, total) in zip((2 * i, 2 * i + 1), resident((2 * i, 2 * i + 1), 1 - c)):
            coded, scale = code(value, 1)
            esend[r] = to_code(coded)
            put_columns(estat.at[r], top, total, scale)
        return carry

    lax.fori_loop(0, 2, resident_other, 0)
    e_copies = [
        (link(esend.at[r], ebuf.at[r], dev_sib), link(estat.at[r], efrom.at[r], dev_sib)) for r in range(NR)
    ]
    for pair in e_copies:
        go_pair(pair)

    d_p1.wait_recv()
    go(share_d[1])
    d_m0.wait_recv()
    go(share_d[2])
    near_m[1].wait_recv()
    far[1][0].wait_recv()
    go(share_s[1])
    near_p[2].wait_recv()
    far[2][0].wait_recv()
    go(share_s[2])
    near_p[3].wait_recv()
    go(far[3][0])
    near_m[3].wait_recv()
    go(far[3][1])

    df_p.wait_recv()
    df_m.wait_recv()
    go(share_d[3])
    share_d[1].wait_recv()
    share_s[1].wait_recv()
    send_part(1, nn(kvt[1], hidt[...]), m_copies[1])
    far[3][0].wait_recv()
    far[3][1].wait_recv()
    go(share_s[3])
    share_d[2].wait_recv()
    share_s[2].wait_recv()
    send_part(2, nn(kvt[2], hidt[...]), m_copies[2])

    def over_lanes(starts, size, at):
        return sum(nn(kvt[3, :, start:start + size], hidt[start:start + size, at]) for start in starts)

    share_d[3].wait_recv()
    lat[origin[3]] = over_lanes((4 * SHARE, HALF_D // 2 + 4 * SHARE), 2 * DIRECT, slice(None))
    share_s[3].wait_recv()
    for i, at in enumerate(tails):
        send_part(
            3, lat[origin[3], :, at] + over_lanes((0, HALF_D // 2), 4 * SHARE, at), m_copies[3 + i], at
        )
    lax.fori_loop(0, 2, resident_own, 0)
    for pair in e_copies:
        wait_pair(pair)
    lax.fori_loop(0, NR, add_other, 0)

    for slot in range(4):
        for pair in m_copies[slot:] if slot == 3 else m_copies[slot:slot + 1]:
            wait_pair(pair)
        lat[origin[slot]] = lat[origin[slot]] + from_code(mpr[slot]) * msr[slot]
    whole = lat[...].reshape(KVW, TOK)
    latent = whole[:LATW]
    inverse = lax.rsqrt(jnp.sum(latent * latent, axis=0, keepdims=True) / LATW + eps_norm)
    gain_cols = jnp.transpose(jnp.broadcast_to(gain[...], (128, LATW)))
    for j in range(TOK // 128):
        at = slice(j * 128, j * 128 + 128)
        rows[:LATW, at] = (latent[:, at] * inverse[:, at] * gain_cols).astype(BF16)
    first, second = whole[LATW:LATW + ROPEW // 2], whole[LATW + ROPEW // 2:]
    rows[LATW:LATW + ROPEW // 2, :] = (first * cosine[...] - second * sine[...]).astype(BF16)
    rows[LATW + ROPEW // 2:KVW, :] = (first * sine[...] + second * cosine[...]).astype(BF16)

    slot_at = lax.broadcasted_iota(I32, (CAPTOK, TOK), 0)

    def pack_for(to):
        chosen = ((slot_at + to * CAPTOK) == tok[...]).astype(F32)
        empty = jnp.sum(chosen, axis=1, keepdims=True) < 0.5
        page_rows = nt(chosen.astype(BF16), rows[...])
        column = lax.broadcasted_iota(I32, (CAPTOK, KVX), 1)
        return jnp.where((column == KVW) & empty, 1.0, page_rows).astype(BF16)

    half = CAPTOK // 2
    a_r0 = link(packed.at[2, pl.ds(0, half)], relay.at[0], dev_zp)
    a_r1 = link(packed.at[2, pl.ds(half, half)], relay.at[1], dev_zm)
    a_p = link(packed.at[0], arr.at[1, c], dev_zp)
    a_m = link(packed.at[1], arr.at[2, c], dev_zm)
    a_f0 = link(relay.at[0], arr.at[3, c, pl.ds(0, half)], dev_zp)
    a_f1 = link(relay.at[1], arr.at[3, c, pl.ds(half, half)], dev_zm)
    a_share = [link(arr.at[slot, c], arr.at[slot, c], dev_sib) for slot in range(3)]
    a_share3 = [
        link(arr.at[3, c, pl.ds(0, half)], arr.at[3, c, pl.ds(0, half)], dev_sib),
        link(arr.at[3, c, pl.ds(half, half)], arr.at[3, c, pl.ds(half, half)], dev_sib),
    ]
    packed[2] = pack_for(lax.rem(b + 2, 4))
    go(a_r0)
    go(a_r1)
    packed[0] = pack_for(lax.rem(b + 1, 4))
    go(a_p)
    packed[1] = pack_for(lax.rem(b + 3, 4))
    go(a_m)
    arr[0, c] = pack_for(b)
    go(a_share[0])

    def pages_step(pair, first, last):
        keys = arr[first:last + 1].reshape((last + 1 - first) * 2 * CAPTOK, KVX)
        scores = [nn(qbuf[c * NR + r], keyst[:, :keys.shape[0]]) for r in pair]
        weights = []
        for r, score in zip(pair, scores):
            old = ms[r][:, :1]
            top = jnp.maximum(old, jnp.max(peak(score), axis=1, keepdims=True))
            shrink = jnp.exp2((old - top) * log2_scale)
            w = weigh(score, top)
            weights.append((w.astype(BF16), shrink, top, ls[r] * shrink + fold(w)))
        return [
            (acc[r] * shrink + nn(w, keys[:, :LATW]), jnp.broadcast_to(top, (QROWS, 128)), total)
            for r, (w, shrink, top, total) in zip(pair, weights)
        ]

    def turn_keys(first, last):
        count = (last + 1 - first) * 2 * CAPTOK
        keyst[:, :count] = jnp.transpose(arr[first:last + 1].reshape(count, KVX))

    def pages_of(first, last):
        turn_keys(first, last)

        def body(i, carry):
            pair = (2 * i, 2 * i + 1)
            for r, state in zip(pair, pages_step(pair, first, last)):
                acc[r], ms[r], ls[r] = state
            return carry

        lax.fori_loop(0, 2, body, 0)

    a_r0.wait_recv()
    go(a_f0)
    a_r1.wait_recv()
    go(a_f1)
    a_share[0].wait_recv()
    pages_of(0, 0)
    a_p.wait_recv()
    go(a_share[1])
    a_m.wait_recv()
    go(a_share[2])
    a_share[1].wait_recv()
    a_share[2].wait_recv()
    pages_of(1, 2)
    a_f0.wait_recv()
    go(a_share3[0])
    a_f1.wait_recv()
    go(a_share3[1])
    a_share3[0].wait_recv()
    a_share3[1].wait_recv()

    def merge(parts):
        top = parts[0][1][0]
        for _, stat in parts[1:]:
            top = jnp.maximum(top, stat[0])
        value, total = 0.0, 0.0
        for coded, stat in parts:
            factor = jnp.exp2(stat[0] - top)
            value = value + from_code(coded) * factor
            total = total + factor * stat[1]
        return value, top, total

    def put(coded_ref, stat_ref, value, top, total):
        coded, scale = code(value, 0)
        coded_ref[...] = to_code(coded).reshape(coded_ref.shape)
        stat_ref[0] = top + jnp.log(scale) * log2_e
        stat_ref[1] = total / scale

    yp, ym, yy = lax.rem(y + 1, 4), lax.rem(y + 3, 4), lax.rem(y + 2, 4)
    first_y = used[0]

    def y_pair(r, k):
        pairs = (
            (osend.at[r, yy, 0], ostat.at[r], 0, dev_yp),
            (osend.at[r, yy, 1], ostat.at[r], 1, dev_ym),
            (osend.at[r, yp, 1], ostat.at[r], 2, dev_yp),
            (osend.at[r, ym, 0], ostat.at[r], 3, dev_ym),
            (rsend.at[r, 0], rstat.at[r, 0], 4, dev_yp),
            (rsend.at[r, 1], rstat.at[r, 1], 5, dev_ym),
        )
        data, stat, _, dev = pairs[k]
        return (
            link_at(first_y + 18 * r + 2 * k, data, ybuf.at[r, k], dev),
            link_at(first_y + 18 * r + 2 * k + 1, stat, ystat.at[r, k], dev),
        )

    def last_pair(r, k):
        half, core, dev = ((1 - xh, c, dev_x), (1 - xh, 1 - c, dev_x_sib), (xh, 1 - c, dev_sib))[k]
        return (
            link_at(first_y + 18 * r + 12 + 2 * k, mbuf.at[r, half, core], fbuf.at[r, k], dev),
            link_at(first_y + 18 * r + 13 + 2 * k, mstat.at[r, half], fstat.at[r, k], dev),
        )

    def start_pair(pair):
        pair[0].start()
        pair[1].start()

    turn_keys(3, 3)
    for r in range(NR):
        value, top, total = pages_step((r,), 3, 3)[0]
        coded, scale = code(value, 1)
        osend[r] = to_code(jnp.transpose(coded)).reshape(4, 2, 64, QROWS)
        stat = jnp.transpose(jnp.where(lane == 0, top * log2_scale + jnp.log(scale) * log2_e, 1.0 / scale))
        ostat[r, 0] = stat[0:1]
        ostat[r, 1] = jnp.sum(jnp.transpose(total), axis=0, keepdims=True) * stat[1:2]
        for k in range(4):
            start_pair(y_pair(r, k))

    def relay_sums(r, carry):
        for k, to in ((0, yp), (1, ym)):
            wait_pair(y_pair(r, k))
            put(rsend.at[r, k], rstat.at[r, k], *merge([
                (osend[r, to, k], ostat[r]), (ybuf[r, k], ystat[r, k]),
            ]))
            start_pair(y_pair(r, 4 + k))
        return carry

    def sums_over_y(r, carry):
        for k in range(2, 6):
            wait_pair(y_pair(r, k))
        for h, (one, two) in enumerate(((3, 4), (2, 5))):
            put(mbuf.at[r, h], mstat.at[r, h], *merge([
                (osend[r, y, h], ostat[r]), (ybuf[r, one], ystat[r, one]), (ybuf[r, two], ystat[r, two]),
            ]))
        for k in (1, 0, 2):
            start_pair(last_pair(r, k))
        return carry

    def last_sums(r, carry):
        for k in range(3):
            wait_pair(last_pair(r, k))
        own, other = c * NR + r, (1 - c) * NR + r
        for request, parts in (
            (own, [(mbuf[r, xh, c], mstat[r, xh]), (fbuf[r, 0], fstat[r, 0])]),
            (other, [(fbuf[r, 2], fstat[r, 2]), (fbuf[r, 1], fstat[r, 1])]),
        ):
            value, _, total = merge(parts)
            value = value / total
            for step in range(4):
                out[step, request] = value[:, 64 * step:64 * step + 64]
        return carry

    def finish(r, carry):
        for pair in [y_pair(r, k) for k in range(6)] + [last_pair(r, k) for k in range(3)]:
            pair[0].wait_send()
            pair[1].wait_send()
        return carry

    for stage in (relay_sums, sums_over_y, last_sums, finish):
        lax.fori_loop(0, NR, stage, 0)
    for copy in started:
        copy.wait_send()


LINKS = 144


def tables():
    half = ROPEW // 2
    frequency = rope_base ** (-np.arange(half, dtype=np.float32) / np.float32(half))
    angles = np.arange(TOK, dtype=np.float32)[None, :] * frequency.astype(np.float32)[:, None]
    return np.cos(angles).astype(np.float32), np.sin(angles).astype(np.float32)


def on_device(hidden, kv_down, kv_gain, page_owner, page_request, queries, cache, lengths):
    cosine, sine = tables()
    anywhere = pl.BlockSpec(memory_space=pl.ANY)
    vmem = pl.BlockSpec(memory_space=pltpu.VMEM)
    smem = pl.BlockSpec(memory_space=pltpu.SMEM)
    sums = pl.pallas_call(
        kernel,
        out_shape=jax.ShapeDtypeStruct((4, 2 * NR, 32, 64), F32),
        in_specs=[anywhere, anywhere, vmem, smem, smem, anywhere, anywhere, smem, vmem, vmem],
        out_specs=vmem,
        scratch_shapes=[
            pltpu.VMEM((TOK, HALF_D), BF16),
            pltpu.VMEM((HALF_D, TOK), BF16),
            pltpu.VMEM((KVX, 4 * CAPTOK), BF16),
            pltpu.VMEM((4, BLK, HALF_D), BF16),
            pltpu.VMEM((4, BLK, TOK), F32),
            pltpu.VMEM((4, BLK, TOK), I16),
            pltpu.VMEM((4, BLK, TOK), I16),
            pltpu.VMEM((4, 1, TOK), F32),
            pltpu.VMEM((4, 1, TOK), F32),
            pltpu.VMEM((KVX, TOK), BF16),
            pltpu.VMEM((3, CAPTOK, KVX), BF16),
            pltpu.VMEM((2, CAPTOK // 2, KVX), BF16),
            pltpu.VMEM((4, 2, CAPTOK, KVX), BF16),
            pltpu.VMEM((1, TOK), I32),
            pltpu.VMEM((2 * NR, 4, 64, KVW), BF16),
            pltpu.VMEM((2 * NR, QROWS, KVX), BF16),
            pltpu.VMEM((2 * NR, KVW, CTXD), BF16),
            pltpu.VMEM((NR, QROWS, LATW), I16),
            pltpu.VMEM((NR, 3, 1, QROWS), F32),
            pltpu.VMEM((NR, QROWS, LATW), I16),
            pltpu.VMEM((NR, 3, 1, QROWS), F32),
            pltpu.VMEM((NR, QROWS, LATW), F32),
            pltpu.VMEM((NR, QROWS, 128), F32),
            pltpu.VMEM((NR, QROWS, 128), F32),
            pltpu.VMEM((NR, 4, 2, 64, QROWS), I16),
            pltpu.VMEM((NR, 2, 1, QROWS), F32),
            pltpu.VMEM((NR, 6, 64, QROWS), I16),
            pltpu.VMEM((NR, 6, 2, 1, QROWS), F32),
            pltpu.VMEM((NR, 2, 64, QROWS), I16),
            pltpu.VMEM((NR, 2, 2, 1, QROWS), F32),
            pltpu.VMEM((NR, 2, 2, 32, QROWS), I16),
            pltpu.VMEM((NR, 2, 2, 1, QROWS), F32),
            pltpu.VMEM((NR, 3, 32, QROWS), I16),
            pltpu.VMEM((NR, 3, 2, 1, QROWS), F32),
            pltpu.SemaphoreType.DMA((7,)),
            pltpu.SemaphoreType.DMA((LINKS,)),
            pltpu.SemaphoreType.DMA((LINKS,)),
        ],
        compiler_params=pltpu.CompilerParams(
            collective_id=0, has_side_effects=True, vmem_limit_bytes=56 * 1024 * 1024
        ),
        cost_estimate=pl.CostEstimate(flops=7_500_000_000, bytes_accessed=12_000_000, transcendentals=3_000_000),
    )(
        hidden, kv_down.T, kv_gain.reshape(1, LATW), page_owner.T, page_request, queries, cache.transpose(0, 2, 1), lengths,
        jnp.asarray(cosine), jnp.asarray(sine),
    )
    return sums.transpose(0, 1, 3, 2)


def solution(mesh):
    return jax.shard_map(
        on_device,
        mesh=mesh,
        in_specs=(
            P(("seq", "batch"), "mp"),
            P("mp", "batch"),
            P(),
            P(("seq", "batch"), None),
            P(("seq", "batch")),
            P(None, "batch", "mp", None),
            P("batch", "seq", None),
            P("batch"),
        ),
        out_specs=P(None, "batch", "mp", "seq"),
        check_vma=False,
    )
```

```python
import jax
import jax.numpy as jnp
import numpy as np
from jax import lax
from jax.experimental import pallas as pl
from jax.experimental.pallas import tpu as pltpu
from jax.sharding import PartitionSpec as P

MESH = pl.DeviceIdType.MESH
F32, BF16, I32, I16 = jnp.float32, jnp.bfloat16, jnp.int32, jnp.int16

eps_norm = 1e-06
score_scale = 192.0 ** (-0.5)
log2_e = 1.4426950408889634
log2_scale = score_scale * log2_e
rope_base = 10000.0
masked_value = -1e30
floor_value = -1e29
code_top = 32767.0

TOK, HALF_D, KVW, LATW, ROPEW = 384, 3584, 576, 512, 64
LABELS = 64
KVX = KVW + LABELS
BLK = 144
SHARE, DIRECT = 256, 384
CAPTOK = 192
HALF = CAPTOK // 2
PAGES, PAGE, CAP = 24, 16, 12
QROWS = 256
CTXD = 512
NR = 4
PAIRS = ((0, 1), (2, 3))


def nt(a, b):
    return lax.dot_general(a, b, (((1,), (1,)), ((), ())), preferred_element_type=F32)


def nn(a, b):
    return jnp.dot(a, b, preferred_element_type=F32)


def kernel(
    hidden, kv_down, gain, owner, request, queries, cache, lengths, cosine, sine,
    out,
    hid, kvt, lat, mps, mpr, mss, msr, rows, packed, relay, arr, tok,
    qraw, qbuf, kbuf, esend, estat, ebuf, efrom, acc, ms, ls, osend, ostat, ybuf, ystat, rsend, rstat, mbuf, mstat, fbuf, fstat,
    loc, send, recv,
):
    s, b, p = lax.axis_index("seq"), lax.axis_index("batch"), lax.axis_index("mp")
    c = lax.rem(s, 2)
    sib = s + 1 - 2 * c
    y = lax.div(s, 4)
    in_y = lax.rem(s, 4)
    xh = lax.rem(lax.div(s, 2), 2)
    dev_zp = (s, lax.rem(b + 1, 4), p)
    dev_zm = (s, lax.rem(b + 3, 4), p)
    dev_zz = (s, lax.rem(b + 2, 4), p)
    dev_mp = (s, b, 1 - p)
    dev_sib = (sib, b, p)
    dev_yp = (lax.rem(y + 1, 4) * 4 + in_y, b, p)
    dev_ym = (lax.rem(y + 3, 4) * 4 + in_y, b, p)
    dev_x = (s + 2 - 4 * xh, b, p)
    dev_x_sib = (sib + 2 - 4 * xh, b, p)

    used = [0]
    started = []

    def link(src, dst, dev):
        used[0] += 1
        return link_at(used[0] - 1, src, dst, dev)

    def link_at(i, src, dst, dev):
        return pltpu.make_async_remote_copy(
            src_ref=src, dst_ref=dst, send_sem=send.at[i], recv_sem=recv.at[i],
            device_id=dev, device_id_type=MESH,
        )

    def go(copy):
        copy.start()
        started.append(copy)

    def code(value, axis):
        most = jnp.max(jnp.abs(value), axis=axis, keepdims=True)
        most = jnp.maximum(most, 1e-25)
        return jnp.round(value * (code_top / most)), most * (1.0 / code_top)

    def to_code(value):
        return value.astype(I32).astype(I16)

    def from_code(coded):
        return coded.astype(I32).astype(F32)

    def go_pair(pair):
        go(pair[0])
        go(pair[1])

    def wait_pair(pair):
        pair[0].wait_recv()
        pair[1].wait_recv()

    load_kv = pltpu.make_async_copy(kv_down, kvt.at[0], loc.at[0])
    load_kv.start()
    load_hid = pltpu.make_async_copy(hidden, hid, loc.at[1])
    load_hid.start()
    load_q = []
    for step in range(4):
        load_q.append(pltpu.make_async_copy(queries.at[step], qraw.at[:, step], loc.at[2 + step]))
        load_q[-1].start()
    load_cache = pltpu.make_async_copy(cache, kbuf, loc.at[6])
    load_cache.start()

    barrier = pltpu.get_barrier_semaphore()
    for dev in (dev_zp, dev_zm, dev_zz, dev_mp, dev_sib, dev_yp, dev_ym, dev_x, dev_x_sib):
        pl.semaphore_signal(barrier, inc=1, device_id=dev, device_id_type=MESH)

    pl.semaphore_wait(barrier, 9)

    base = c * (HALF_D // 2)

    def lanes(start, size):
        return pl.ds(pl.multiple_of(base + start, 128), size)

    def kv_link(slot, to_slot, at, dev):
        return link(kvt.at[slot, :, at], kvt.at[to_slot, :, at], dev)

    def first_link(to_slot, at, dev):
        return link(kv_down.at[:, at], kvt.at[to_slot, :, at], dev)

    def part_of(k, first=0, size=SHARE):
        return lanes(lax.rem(y + k, 4) * SHARE + first, size)

    low, high = lanes(4 * SHARE, DIRECT), lanes(4 * SHARE + DIRECT, DIRECT)
    mine = part_of(0)
    s_p, s_m = first_link(1, mine, dev_zp), first_link(2, mine, dev_zm)
    d_p0, d_m1 = first_link(1, low, dev_zp), first_link(2, high, dev_zm)
    d_p1, d_m0 = first_link(1, high, dev_zp), first_link(2, low, dev_zm)
    for copy in (s_p, s_m, d_p0, d_m1):
        go(copy)
    sf_p, sf_m = (
        kv_link(1, 3, part_of(0, 0, SHARE // 2), dev_zp),
        kv_link(2, 3, part_of(0, SHARE // 2, SHARE // 2), dev_zm),
    )
    df_p, df_m = kv_link(1, 3, low, dev_zp), kv_link(2, 3, high, dev_zm)
    near_p = [None] + [kv_link(slot, slot, mine, dev_yp) for slot in (1, 2, 3)]
    near_m = [None] + [kv_link(slot, slot, mine, dev_ym) for slot in (1, 2, 3)]
    far = [None] + [
        (
            kv_link(slot, slot, part_of(3, 0, SHARE // 2), dev_yp),
            kv_link(slot, slot, part_of(1, SHARE // 2, SHARE // 2), dev_ym),
        )
        for slot in (1, 2, 3)
    ]
    share_s = [None] + [kv_link(slot, slot, lanes(0, 4 * SHARE), dev_sib) for slot in (1, 2, 3)]
    share_d = [None] + [kv_link(slot, slot, lanes(4 * SHARE, 2 * DIRECT), dev_sib) for slot in (1, 2, 3)]

    token = lax.broadcasted_iota(I32, (1, TOK), 1)
    token_page = lax.shift_right_logical(token, 4)
    dest = jnp.zeros((1, TOK), I32)
    asked = jnp.zeros((1, TOK), I32)
    counts = [jnp.int32(0)] * 4
    for page in range(PAGES):
        to = owner[0, page]
        rank = jnp.where(to == 0, counts[0], jnp.where(to == 1, counts[1], jnp.where(to == 2, counts[2], counts[3])))
        counts = [counts[o] + (to == o).astype(I32) for o in range(4)]
        dest = jnp.where(token_page == page, (to * CAP + rank) * PAGE, dest)
        asked = jnp.where(token_page == page, request[page] + 1, asked)
    dest = dest + lax.bitwise_and(token, 15)
    tok[...] = dest

    label_row = lax.broadcasted_iota(I32, (LABELS, TOK), 0)
    rows[KVW:, :] = (label_row == asked).astype(F32).astype(BF16)

    origin = [lax.rem(b + ahead, 4) for ahead in (0, 3, 1, 2)]
    m_copies = [
        (link(mps.at[slot], mpr.at[slot], dev_mp), link(mss.at[slot], msr.at[slot], dev_mp)) for slot in range(3)
    ]
    tails = (slice(0, 256), slice(256, TOK))
    for at in tails:
        at = pl.ds(at.start, at.stop - at.start)
        m_copies.append((
            link(mps.at[3, :, at], mpr.at[3, :, at], dev_mp), link(mss.at[3, :, at], msr.at[3, :, at], dev_mp),
        ))

    def send_part(slot, part, copies, at=slice(None)):
        lat[origin[slot], :, at] = part
        coded, scale = code(part, 0)
        mps[slot, :, at] = to_code(coded)
        mss[slot, :, at] = scale
        go_pair(copies)

    def weigh(score, top):
        return jnp.exp2(score * log2_scale - top * log2_scale)

    def fold(w):
        total = w[:, :128]
        for j in range(1, w.shape[1] // 128):
            total = total + w[:, j * 128:j * 128 + 128]
        return total

    def peak(score):
        most = score[:, :128]
        for j in range(1, score.shape[1] // 128):
            most = jnp.maximum(most, score[:, j * 128:j * 128 + 128])
        return most

    lane = lax.broadcasted_iota(I32, (QROWS, 128), 1)

    def put_columns(stat_ref, top, total, scale):
        stat = jnp.transpose(jnp.where(lane == 0, top * log2_scale, scale))
        stat_ref[0] = stat[0:1]
        stat_ref[1] = jnp.sum(jnp.transpose(total), axis=0, keepdims=True)
        stat_ref[2] = stat[1:2]

    def resident(pair, half):
        at = lax.broadcasted_iota(I32, (1, CTXD), 1) + s * CTXD
        scores = [
            jnp.where(at < lengths[half * NR + r], nn(qbuf[half * NR + r, :, :KVW], kbuf[half * NR + r]), masked_value)
            for r in pair
        ]
        weights = []
        for score in scores:
            top = jnp.maximum(jnp.max(peak(score), axis=1, keepdims=True), floor_value)
            w = weigh(score, top)
            weights.append((w.astype(BF16), jnp.broadcast_to(top, (QROWS, 128)), fold(w)))
        return [
            (nt(w, kbuf[half * NR + r, :LATW, :]), top, total) for r, (w, top, total) in zip(pair, weights)
        ]

    def resident_own(i, carry):
        for r, state in zip((2 * i, 2 * i + 1), resident((2 * i, 2 * i + 1), c)):
            acc[r], ms[r], ls[r] = state
        return carry

    def add_other(r, carry):
        row = lax.broadcasted_iota(I32, (128, QROWS), 0)
        stat = jnp.where(row == 0, efrom[r, 0], jnp.where(row == 1, efrom[r, 1], efrom[r, 2]))
        stat = jnp.transpose(stat)
        top2, total2, scale2 = stat[:, 0:1] * (1.0 / log2_scale), stat[:, 1:2], stat[:, 2:3]
        old = ms[r][:, :1]
        top = jnp.maximum(old, top2)
        keep, gain2 = jnp.exp2((old - top) * log2_scale), jnp.exp2((top2 - top) * log2_scale)
        acc[r] = acc[r] * keep + from_code(ebuf[r]) * (gain2 * scale2)
        ms[r] = jnp.broadcast_to(top, (QROWS, 128))
        ls[r] = ls[r] * keep + jnp.where(lane == 0, gain2 * total2, 0.0)
        return carry

    load_hid.wait()
    load_kv.wait()
    s_p.wait_recv()
    go(sf_p)
    go(near_p[1])
    go(near_m[1])
    s_m.wait_recv()
    go(sf_m)
    go(near_p[2])
    go(near_m[2])
    go(d_p1)
    go(d_m0)
    send_part(0, nt(kvt[0], hid[...]), m_copies[0])

    d_p0.wait_recv()
    go(df_p)
    d_m1.wait_recv()
    go(df_m)

    def pass_on(slot):
        near_p[slot].wait_recv()
        go(far[slot][0])
        near_m[slot].wait_recv()
        go(far[slot][1])

    def swap_shared(slot):
        far[slot][0].wait_recv()
        far[slot][1].wait_recv()
        go(share_s[slot])

    pass_on(1)
    sf_p.wait_recv()
    sf_m.wait_recv()
    go(near_p[3])
    go(near_m[3])

    for copy in load_q:
        copy.wait()
    load_cache.wait()
    label_at = lax.broadcasted_iota(I32, (QROWS, LABELS), 1)

    def fill(r, carry):
        qbuf[r, :, :KVW] = qraw[r].reshape(QROWS, KVW)
        qbuf[r, :, KVW:] = jnp.where(label_at == r + 1, 0.0, masked_value).astype(BF16)
        return carry

    def resident_other(pair):
        for r, (value, top, total) in zip(pair, resident(pair, 1 - c)):
            coded, scale = code(value, 1)
            esend[r] = to_code(coded)
            put_columns(estat.at[r], top, total, scale)
            go_pair(e_copies[r])

    e_copies = [
        (link(esend.at[r], ebuf.at[r], dev_sib), link(estat.at[r], efrom.at[r], dev_sib)) for r in range(NR)
    ]
    lax.fori_loop(0, 2 * NR, fill, 0)
    resident_other(PAIRS[0])

    pass_on(2)
    d_p1.wait_recv()
    go(share_d[1])
    d_m0.wait_recv()
    go(share_d[2])
    swap_shared(1)
    resident_other(PAIRS[1])

    pass_on(3)
    swap_shared(2)
    share_d[1].wait_recv()
    share_s[1].wait_recv()
    send_part(1, nt(kvt[1], hid[...]), m_copies[1])
    df_p.wait_recv()
    df_m.wait_recv()
    go(share_d[3])
    swap_shared(3)
    share_d[2].wait_recv()
    share_s[2].wait_recv()
    send_part(2, nt(kvt[2], hid[...]), m_copies[2])

    def over_lanes(starts, size, at):
        return sum(nt(kvt[3, :, start:start + size], hid[at, start:start + size]) for start in starts)

    share_d[3].wait_recv()
    lat[origin[3]] = over_lanes((4 * SHARE, HALF_D // 2 + 4 * SHARE), 2 * DIRECT, slice(None))
    share_s[3].wait_recv()
    for i, at in enumerate(tails):
        send_part(
            3, lat[origin[3], :, at] + over_lanes((0, HALF_D // 2), 4 * SHARE, at), m_copies[3 + i], at
        )
    lax.fori_loop(0, 2, resident_own, 0)

    for slot in range(4):
        for pair in m_copies[slot:] if slot == 3 else m_copies[slot:slot + 1]:
            wait_pair(pair)
        lat[origin[slot]] = lat[origin[slot]] + from_code(mpr[slot]) * msr[slot]
    whole = lat[...].reshape(KVW, TOK)
    latent = whole[:LATW]
    inverse = lax.rsqrt(jnp.sum(latent * latent, axis=0, keepdims=True) / LATW + eps_norm)
    gain_cols = jnp.transpose(jnp.broadcast_to(gain[...], (128, LATW)))
    for j in range(TOK // 128):
        at = slice(j * 128, j * 128 + 128)
        rows[:LATW, at] = (latent[:, at] * inverse[:, at] * gain_cols).astype(BF16)
    first, second = whole[LATW:LATW + ROPEW // 2], whole[LATW + ROPEW // 2:]
    rows[LATW:LATW + ROPEW // 2, :] = (first * cosine[...] - second * sine[...]).astype(BF16)
    rows[LATW + ROPEW // 2:KVW, :] = (first * sine[...] + second * cosine[...]).astype(BF16)

    slot_at = lax.broadcasted_iota(I32, (CAPTOK, TOK), 0)

    def pack_for(to):
        chosen = ((slot_at + to * CAPTOK) == tok[...]).astype(F32)
        empty = jnp.sum(chosen, axis=1, keepdims=True) < 0.5
        page_rows = nt(chosen.astype(BF16), rows[...])
        column = lax.broadcasted_iota(I32, (CAPTOK, KVX), 1)
        return jnp.where((column == KVW) & empty, 1.0, page_rows).astype(BF16)

    first, second = pl.ds(0, HALF), pl.ds(HALF, HALF)
    a_p = [link(packed.at[0, at], arr.at[part, c], dev_zp) for at, part in ((first, 2), (second, 4))]
    a_m = [link(packed.at[1, at], arr.at[part, c], dev_zm) for at, part in ((first, 3), (second, 5))]
    a_r0 = link(packed.at[2, first], relay.at[0], dev_zp)
    a_r1 = link(packed.at[2, second], relay.at[1], dev_zm)
    a_f0 = link(relay.at[0], arr.at[6, c], dev_zp)
    a_f1 = link(relay.at[1], arr.at[7, c], dev_zm)
    a_share = [link(arr.at[part, c], arr.at[part, c], dev_sib) for part in range(8)]
    packed[0] = pack_for(lax.rem(b + 1, 4))
    go(a_p[0])
    packed[1] = pack_for(lax.rem(b + 3, 4))
    go(a_m[0])
    packed[2] = pack_for(lax.rem(b + 2, 4))
    go(a_r0)
    go(a_r1)
    go(a_p[1])
    go(a_m[1])
    own_pages = pack_for(b)
    arr[0, c] = own_pages[:HALF]
    go(a_share[0])
    arr[1, c] = own_pages[HALF:]
    go(a_share[1])

    def swap(copies, parts):
        for copy, part in zip(copies, parts):
            copy.wait_recv()
            go(a_share[part])

    def ready(parts):
        for part in parts:
            a_share[part].wait_recv()

    def pages_step(pair, first, last):
        keys = arr[first:last + 1].reshape((last + 1 - first) * CAPTOK, KVX)
        scores = [nt(qbuf[c * NR + r], keys) for r in pair]
        weights = []
        for r, score in zip(pair, scores):
            old = ms[r][:, :1]
            top = jnp.maximum(old, jnp.max(peak(score), axis=1, keepdims=True))
            shrink = jnp.exp2((old - top) * log2_scale)
            w = weigh(score, top)
            weights.append((w.astype(BF16), shrink, top, ls[r] * shrink + fold(w)))
        return [
            (acc[r] * shrink + nn(w, keys[:, :LATW]), jnp.broadcast_to(top, (QROWS, 128)), total)
            for r, (w, shrink, top, total) in zip(pair, weights)
        ]

    def pages_of(pair, first, last):
        for r, state in zip(pair, pages_step(pair, first, last)):
            acc[r], ms[r], ls[r] = state

    for pair in e_copies:
        wait_pair(pair)
    lax.fori_loop(0, NR, add_other, 0)
    ready((0, 1))
    pages_of(PAIRS[0], 0, 1)
    swap((a_p[0], a_m[0]), (2, 3))
    pages_of(PAIRS[1], 0, 1)
    a_r0.wait_recv()
    go(a_f0)
    a_r1.wait_recv()
    go(a_f1)
    ready((2, 3))
    pages_of(PAIRS[0], 2, 3)
    swap((a_p[1], a_m[1]), (4, 5))
    pages_of(PAIRS[1], 2, 3)
    ready((4, 5))
    pages_of((0,), 4, 5)
    swap((a_f0, a_f1), (6, 7))
    pages_of((1,), 4, 5)
    ready((6, 7))

    def merge(parts):
        top = parts[0][1][0]
        for _, stat in parts[1:]:
            top = jnp.maximum(top, stat[0])
        value, total = 0.0, 0.0
        for coded, stat in parts:
            factor = jnp.exp2(stat[0] - top)
            value = value + from_code(coded) * factor
            total = total + factor * stat[1]
        return value, top, total

    def put(coded_ref, stat_ref, value, top, total):
        coded, scale = code(value, 0)
        coded_ref[...] = to_code(coded).reshape(coded_ref.shape)
        stat_ref[0] = top + jnp.log(scale) * log2_e
        stat_ref[1] = total / scale

    yp, ym, yy = lax.rem(y + 1, 4), lax.rem(y + 3, 4), lax.rem(y + 2, 4)
    first_y = used[0]

    def y_pair(r, k):
        pairs = (
            (osend.at[r, yy, 0], ostat.at[r], 0, dev_yp),
            (osend.at[r, yy, 1], ostat.at[r], 1, dev_ym),
            (osend.at[r, yp, 1], ostat.at[r], 2, dev_yp),
            (osend.at[r, ym, 0], ostat.at[r], 3, dev_ym),
            (rsend.at[r, 0], rstat.at[r, 0], 4, dev_yp),
            (rsend.at[r, 1], rstat.at[r, 1], 5, dev_ym),
        )
        data, stat, _, dev = pairs[k]
        return (
            link_at(first_y + 18 * r + 2 * k, data, ybuf.at[r, k], dev),
            link_at(first_y + 18 * r + 2 * k + 1, stat, ystat.at[r, k], dev),
        )

    def last_pair(r, k):
        half, core, dev = ((1 - xh, c, dev_x), (1 - xh, 1 - c, dev_x_sib), (xh, 1 - c, dev_sib))[k]
        return (
            link_at(first_y + 18 * r + 12 + 2 * k, mbuf.at[r, half, core], fbuf.at[r, k], dev),
            link_at(first_y + 18 * r + 13 + 2 * k, mstat.at[r, half], fstat.at[r, k], dev),
        )

    def start_pair(pair):
        pair[0].start()
        pair[1].start()

    def relay_sums(r, carry):
        for k, to in ((0, yp), (1, ym)):
            wait_pair(y_pair(r, k))
            put(rsend.at[r, k], rstat.at[r, k], *merge([
                (osend[r, to, k], ostat[r]), (ybuf[r, k], ystat[r, k]),
            ]))
            start_pair(y_pair(r, 4 + k))
        return carry

    for r in range(NR):
        value, top, total = pages_step((r,), 6 if r < 2 else 4, 7)[0]
        coded, scale = code(value, 1)
        osend[r] = to_code(jnp.transpose(coded)).reshape(4, 2, 64, QROWS)
        stat = jnp.transpose(jnp.where(lane == 0, top * log2_scale + jnp.log(scale) * log2_e, 1.0 / scale))
        ostat[r, 0] = stat[0:1]
        ostat[r, 1] = jnp.sum(jnp.transpose(total), axis=0, keepdims=True) * stat[1:2]
        for k in range(4):
            start_pair(y_pair(r, k))
        if r >= 2:
            relay_sums(r - 2, 0)

    def sums_over_y(r, carry):
        for k in range(2, 6):
            wait_pair(y_pair(r, k))
        for h, (one, two) in enumerate(((3, 4), (2, 5))):
            put(mbuf.at[r, h], mstat.at[r, h], *merge([
                (osend[r, y, h], ostat[r]), (ybuf[r, one], ystat[r, one]), (ybuf[r, two], ystat[r, two]),
            ]))
        for k in (1, 0, 2):
            start_pair(last_pair(r, k))
        return carry

    def last_sums(r, carry):
        for k in range(3):
            wait_pair(last_pair(r, k))
        own, other = c * NR + r, (1 - c) * NR + r
        for request, parts in (
            (own, [(mbuf[r, xh, c], mstat[r, xh]), (fbuf[r, 0], fstat[r, 0])]),
            (other, [(fbuf[r, 2], fstat[r, 2]), (fbuf[r, 1], fstat[r, 1])]),
        ):
            value, _, total = merge(parts)
            value = value / total
            for step in range(4):
                out[step, request] = value[:, 64 * step:64 * step + 64]
        return carry

    def finish(r, carry):
        for pair in [y_pair(r, k) for k in range(6)] + [last_pair(r, k) for k in range(3)]:
            pair[0].wait_send()
            pair[1].wait_send()
        return carry

    lax.fori_loop(2, NR, relay_sums, 0)
    for stage in (sums_over_y, last_sums, finish):
        lax.fori_loop(0, NR, stage, 0)
    for copy in started:
        copy.wait_send()


LINKS = 144


def tables():
    half = ROPEW // 2
    frequency = rope_base ** (-np.arange(half, dtype=np.float32) / np.float32(half))
    angles = np.arange(TOK, dtype=np.float32)[None, :] * frequency.astype(np.float32)[:, None]
    return np.cos(angles).astype(np.float32), np.sin(angles).astype(np.float32)


def on_device(hidden, kv_down, kv_gain, page_owner, page_request, queries, cache, lengths):
    cosine, sine = tables()
    anywhere = pl.BlockSpec(memory_space=pl.ANY)
    vmem = pl.BlockSpec(memory_space=pltpu.VMEM)
    smem = pl.BlockSpec(memory_space=pltpu.SMEM)
    sums = pl.pallas_call(
        kernel,
        out_shape=jax.ShapeDtypeStruct((4, 2 * NR, 32, 64), F32),
        in_specs=[anywhere, anywhere, vmem, smem, smem, anywhere, anywhere, smem, vmem, vmem],
        out_specs=vmem,
        scratch_shapes=[
            pltpu.VMEM((TOK, HALF_D), BF16),
            pltpu.VMEM((4, BLK, HALF_D), BF16),
            pltpu.VMEM((4, BLK, TOK), F32),
            pltpu.VMEM((4, BLK, TOK), I16),
            pltpu.VMEM((4, BLK, TOK), I16),
            pltpu.VMEM((4, 1, TOK), F32),
            pltpu.VMEM((4, 1, TOK), F32),
            pltpu.VMEM((KVX, TOK), BF16),
            pltpu.VMEM((3, CAPTOK, KVX), BF16),
            pltpu.VMEM((2, HALF, KVX), BF16),
            pltpu.VMEM((8, 2, HALF, KVX), BF16),
            pltpu.VMEM((1, TOK), I32),
            pltpu.VMEM((2 * NR, 4, 64, KVW), BF16),
            pltpu.VMEM((2 * NR, QROWS, KVX), BF16),
            pltpu.VMEM((2 * NR, KVW, CTXD), BF16),
            pltpu.VMEM((NR, QROWS, LATW), I16),
            pltpu.VMEM((NR, 3, 1, QROWS), F32),
            pltpu.VMEM((NR, QROWS, LATW), I16),
            pltpu.VMEM((NR, 3, 1, QROWS), F32),
            pltpu.VMEM((NR, QROWS, LATW), F32),
            pltpu.VMEM((NR, QROWS, 128), F32),
            pltpu.VMEM((NR, QROWS, 128), F32),
            pltpu.VMEM((NR, 4, 2, 64, QROWS), I16),
            pltpu.VMEM((NR, 2, 1, QROWS), F32),
            pltpu.VMEM((NR, 6, 64, QROWS), I16),
            pltpu.VMEM((NR, 6, 2, 1, QROWS), F32),
            pltpu.VMEM((NR, 2, 64, QROWS), I16),
            pltpu.VMEM((NR, 2, 2, 1, QROWS), F32),
            pltpu.VMEM((NR, 2, 2, 32, QROWS), I16),
            pltpu.VMEM((NR, 2, 2, 1, QROWS), F32),
            pltpu.VMEM((NR, 3, 32, QROWS), I16),
            pltpu.VMEM((NR, 3, 2, 1, QROWS), F32),
            pltpu.SemaphoreType.DMA((7,)),
            pltpu.SemaphoreType.DMA((LINKS,)),
            pltpu.SemaphoreType.DMA((LINKS,)),
        ],
        compiler_params=pltpu.CompilerParams(
            collective_id=0, has_side_effects=True, vmem_limit_bytes=56 * 1024 * 1024
        ),
        cost_estimate=pl.CostEstimate(flops=7_500_000_000, bytes_accessed=12_000_000, transcendentals=3_000_000),
    )(
        hidden, kv_down.T, kv_gain.reshape(1, LATW), page_owner.T, page_request, queries, cache.transpose(0, 2, 1), lengths,
        jnp.asarray(cosine), jnp.asarray(sine),
    )
    return sums.transpose(0, 1, 3, 2)


def solution(mesh):
    return jax.shard_map(
        on_device,
        mesh=mesh,
        in_specs=(
            P(("seq", "batch"), "mp"),
            P("mp", "batch"),
            P(),
            P(("seq", "batch"), None),
            P(("seq", "batch")),
            P(None, "batch", "mp", None),
            P("batch", "seq", None),
            P("batch"),
        ),
        out_specs=P(None, "batch", "mp", "seq"),
        check_vma=False,
    )
```

```python
import jax
import jax.numpy as jnp
import numpy as np
from jax import lax
from jax.experimental import pallas as pl
from jax.experimental.pallas import tpu as pltpu
from jax.sharding import PartitionSpec as P

MESH = pl.DeviceIdType.MESH
F32, BF16, I32, I16 = jnp.float32, jnp.bfloat16, jnp.int32, jnp.int16

eps_norm = 1e-06
score_scale = 192.0 ** (-0.5)
log2_e = 1.4426950408889634
log2_scale = score_scale * log2_e
rope_base = 10000.0
masked_value = -1e30
floor_value = -1e29
code_top = 32767.0

TOK, HALF_D, KVW, LATW, ROPEW = 384, 3584, 576, 512, 64
LABELS = 64
KVX = KVW + LABELS
BLK = 144
SHARE, DIRECT = 256, 384
CAPTOK = 192
HALF = CAPTOK // 2
PAGES, PAGE, CAP = 24, 16, 12
QROWS = 256
CTXD = 512
NR = 4
PAIRS = ((0, 1), (2, 3))


def nt(a, b):
    return lax.dot_general(a, b, (((1,), (1,)), ((), ())), preferred_element_type=F32)


def nn(a, b):
    return jnp.dot(a, b, preferred_element_type=F32)


def kernel(
    hidden, kv_down, gain, owner, request, queries, cache, lengths, cosine, sine,
    out,
    hid, kvt, lat, mps, mpr, mss, msr, rows, packed, relay, arr, tok,
    vt, qraw, qbuf, kbuf, esend, estat, ebuf, efrom, acc, ms, ls, osend, ostat, ybuf, ystat, rsend, rstat, mbuf, mstat, fbuf, fstat,
    loc, send, recv,
):
    s, b, p = lax.axis_index("seq"), lax.axis_index("batch"), lax.axis_index("mp")
    c = lax.rem(s, 2)
    sib = s + 1 - 2 * c
    y = lax.div(s, 4)
    in_y = lax.rem(s, 4)
    xh = lax.rem(lax.div(s, 2), 2)
    dev_zp = (s, lax.rem(b + 1, 4), p)
    dev_zm = (s, lax.rem(b + 3, 4), p)
    dev_zz = (s, lax.rem(b + 2, 4), p)
    dev_mp = (s, b, 1 - p)
    dev_sib = (sib, b, p)
    dev_yp = (lax.rem(y + 1, 4) * 4 + in_y, b, p)
    dev_ym = (lax.rem(y + 3, 4) * 4 + in_y, b, p)
    dev_x = (s + 2 - 4 * xh, b, p)
    dev_x_sib = (sib + 2 - 4 * xh, b, p)

    used = [0]
    started = []

    def link(src, dst, dev):
        used[0] += 1
        return link_at(used[0] - 1, src, dst, dev)

    def link_at(i, src, dst, dev):
        return pltpu.make_async_remote_copy(
            src_ref=src, dst_ref=dst, send_sem=send.at[i], recv_sem=recv.at[i],
            device_id=dev, device_id_type=MESH,
        )

    def go(copy):
        copy.start()
        started.append(copy)

    def code(value, axis):
        most = jnp.max(jnp.abs(value), axis=axis, keepdims=True)
        most = jnp.maximum(most, 1e-25)
        return jnp.round(value * (code_top / most)), most * (1.0 / code_top)

    def to_code(value):
        return value.astype(I32).astype(I16)

    def from_code(coded):
        return coded.astype(I32).astype(F32)

    def go_pair(pair):
        go(pair[0])
        go(pair[1])

    def wait_pair(pair):
        pair[0].wait_recv()
        pair[1].wait_recv()

    load_kv = pltpu.make_async_copy(kv_down, kvt.at[0], loc.at[0])
    load_kv.start()
    load_hid = pltpu.make_async_copy(hidden, hid, loc.at[1])
    load_hid.start()
    load_q = []
    for step in range(4):
        load_q.append(pltpu.make_async_copy(queries.at[step], qraw.at[:, step], loc.at[2 + step]))
        load_q[-1].start()
    load_cache = pltpu.make_async_copy(cache, kbuf, loc.at[6])
    load_cache.start()

    barrier = pltpu.get_barrier_semaphore()
    for dev in (dev_zp, dev_zm, dev_zz, dev_mp, dev_sib, dev_yp, dev_ym, dev_x, dev_x_sib):
        pl.semaphore_signal(barrier, inc=1, device_id=dev, device_id_type=MESH)

    pl.semaphore_wait(barrier, 9)

    base = c * (HALF_D // 2)

    def lanes(start, size):
        return pl.ds(pl.multiple_of(base + start, 128), size)

    def kv_link(slot, to_slot, at, dev):
        return link(kvt.at[slot, :, at], kvt.at[to_slot, :, at], dev)

    def first_link(to_slot, at, dev):
        return link(kv_down.at[:, at], kvt.at[to_slot, :, at], dev)

    def part_of(k, first=0, size=SHARE):
        return lanes(lax.rem(y + k, 4) * SHARE + first, size)

    low, high = lanes(4 * SHARE, DIRECT), lanes(4 * SHARE + DIRECT, DIRECT)
    mine = part_of(0)
    s_p, s_m = first_link(1, mine, dev_zp), first_link(2, mine, dev_zm)
    d_p0, d_m1 = first_link(1, low, dev_zp), first_link(2, high, dev_zm)
    d_p1, d_m0 = first_link(1, high, dev_zp), first_link(2, low, dev_zm)
    for copy in (s_p, s_m, d_p0, d_m1):
        go(copy)
    sf_p, sf_m = (
        kv_link(1, 3, part_of(0, 0, SHARE // 2), dev_zp),
        kv_link(2, 3, part_of(0, SHARE // 2, SHARE // 2), dev_zm),
    )
    df_p, df_m = kv_link(1, 3, low, dev_zp), kv_link(2, 3, high, dev_zm)
    near_p = [None] + [kv_link(slot, slot, mine, dev_yp) for slot in (1, 2, 3)]
    near_m = [None] + [kv_link(slot, slot, mine, dev_ym) for slot in (1, 2, 3)]
    far = [None] + [
        (
            kv_link(slot, slot, part_of(3, 0, SHARE // 2), dev_yp),
            kv_link(slot, slot, part_of(1, SHARE // 2, SHARE // 2), dev_ym),
        )
        for slot in (1, 2, 3)
    ]
    share_s = [None] + [kv_link(slot, slot, lanes(0, 4 * SHARE), dev_sib) for slot in (1, 2, 3)]
    share_d = [None] + [kv_link(slot, slot, lanes(4 * SHARE, 2 * DIRECT), dev_sib) for slot in (1, 2, 3)]

    token = lax.broadcasted_iota(I32, (1, TOK), 1)
    token_page = lax.shift_right_logical(token, 4)
    dest = jnp.zeros((1, TOK), I32)
    asked = jnp.zeros((1, TOK), I32)
    counts = [jnp.int32(0)] * 4
    for page in range(PAGES):
        to = owner[0, page]
        rank = jnp.where(to == 0, counts[0], jnp.where(to == 1, counts[1], jnp.where(to == 2, counts[2], counts[3])))
        counts = [counts[o] + (to == o).astype(I32) for o in range(4)]
        dest = jnp.where(token_page == page, (to * CAP + rank) * PAGE, dest)
        asked = jnp.where(token_page == page, request[page] + 1, asked)
    dest = dest + lax.bitwise_and(token, 15)
    tok[...] = dest

    label_row = lax.broadcasted_iota(I32, (LABELS, TOK), 0)
    rows[KVW:, :] = (label_row == asked).astype(F32).astype(BF16)

    origin = [lax.rem(b + ahead, 4) for ahead in (0, 3, 1, 2)]
    m_copies = [
        (link(mps.at[slot], mpr.at[slot], dev_mp), link(mss.at[slot], msr.at[slot], dev_mp)) for slot in range(3)
    ]
    tails = (slice(0, 256), slice(256, TOK))
    for at in tails:
        at = pl.ds(at.start, at.stop - at.start)
        m_copies.append((
            link(mps.at[3, :, at], mpr.at[3, :, at], dev_mp), link(mss.at[3, :, at], msr.at[3, :, at], dev_mp),
        ))

    def send_part(slot, part, copies, at=slice(None)):
        lat[origin[slot], :, at] = part
        coded, scale = code(part, 0)
        mps[slot, :, at] = to_code(coded)
        mss[slot, :, at] = scale
        go_pair(copies)

    def weigh(score, top):
        return jnp.exp2(score * log2_scale - top * log2_scale)

    def fold(w):
        total = w[:, :128]
        for j in range(1, w.shape[1] // 128):
            total = total + w[:, j * 128:j * 128 + 128]
        return total

    def peak(score):
        most = score[:, :128]
        for j in range(1, score.shape[1] // 128):
            most = jnp.maximum(most, score[:, j * 128:j * 128 + 128])
        return most

    def resident(pair, half):
        at = lax.broadcasted_iota(I32, (1, CTXD), 1) + s * CTXD
        scores = [
            jnp.where(at < lengths[half * NR + r], nn(qbuf[half * NR + r, :, :KVW], kbuf[half * NR + r]), masked_value)
            for r in pair
        ]
        weights = []
        for score in scores:
            top = jnp.maximum(jnp.max(peak(score), axis=1, keepdims=True), floor_value)
            w = weigh(score, top)
            top = jnp.transpose(jnp.broadcast_to(top, (QROWS, 128)))[0:1]
            weights.append((w.astype(BF16), top, jnp.sum(jnp.transpose(fold(w)), axis=0, keepdims=True)))
        return [
            (nt(kbuf[half * NR + r, :LATW, :], w), top, total) for r, (w, top, total) in zip(pair, weights)
        ]

    def columns(first, count=1):
        return slice(first * QROWS, (first + count) * QROWS)

    def resident_own(pair):
        for r, (value, top, total) in zip(pair, resident(pair, c)):
            acc[:, columns(r)], ms[:, columns(r)], ls[:, columns(r)] = value, top, total

    def add_other(r):
        at = columns(r)
        old, top2 = ms[:, at], efrom[r, 0]
        top = jnp.maximum(old, top2)
        keep, gain2 = jnp.exp2((old - top) * log2_scale), jnp.exp2((top2 - top) * log2_scale)
        acc[:, at] = acc[:, at] * keep + from_code(ebuf[r]) * (gain2 * efrom[r, 2])
        ls[:, at] = ls[:, at] * keep + gain2 * efrom[r, 1]
        ms[:, at] = top

    load_hid.wait()
    load_kv.wait()
    s_p.wait_recv()
    go(sf_p)
    go(near_p[1])
    go(near_m[1])
    s_m.wait_recv()
    go(sf_m)
    go(near_p[2])
    go(near_m[2])
    go(d_p1)
    go(d_m0)
    send_part(0, nt(kvt[0], hid[...]), m_copies[0])

    d_p0.wait_recv()
    go(df_p)
    d_m1.wait_recv()
    go(df_m)

    def pass_on(slot):
        near_p[slot].wait_recv()
        go(far[slot][0])
        near_m[slot].wait_recv()
        go(far[slot][1])

    def swap_shared(slot):
        far[slot][0].wait_recv()
        far[slot][1].wait_recv()
        go(share_s[slot])

    pass_on(1)
    sf_p.wait_recv()
    sf_m.wait_recv()
    go(near_p[3])
    go(near_m[3])

    for copy in load_q:
        copy.wait()
    load_cache.wait()
    label_at = lax.broadcasted_iota(I32, (QROWS, LABELS), 1)

    def fill(r, carry):
        qbuf[r, :, :KVW] = qraw[r].reshape(QROWS, KVW)
        qbuf[r, :, KVW:] = jnp.where(label_at == r + 1, 0.0, masked_value).astype(BF16)
        return carry

    def resident_other(pair):
        for r, (value, top, total) in zip(pair, resident(pair, 1 - c)):
            coded, scale = code(value, 0)
            esend[r] = to_code(coded)
            for k, row in enumerate((top, total, scale)):
                estat[r, k] = row
            go_pair(e_copies[r])

    e_copies = [
        (link(esend.at[r], ebuf.at[r], dev_sib), link(estat.at[r], efrom.at[r], dev_sib)) for r in range(NR)
    ]
    lax.fori_loop(0, 2 * NR, fill, 0)
    resident_other(PAIRS[0])

    pass_on(2)
    d_p1.wait_recv()
    go(share_d[1])
    d_m0.wait_recv()
    go(share_d[2])
    swap_shared(1)
    resident_other(PAIRS[1])

    pass_on(3)
    swap_shared(2)
    share_d[1].wait_recv()
    share_s[1].wait_recv()
    send_part(1, nt(kvt[1], hid[...]), m_copies[1])
    df_p.wait_recv()
    df_m.wait_recv()
    go(share_d[3])
    swap_shared(3)
    share_d[2].wait_recv()
    share_s[2].wait_recv()
    send_part(2, nt(kvt[2], hid[...]), m_copies[2])

    def over_lanes(starts, size, at):
        return sum(nt(kvt[3, :, start:start + size], hid[at, start:start + size]) for start in starts)

    share_d[3].wait_recv()
    lat[origin[3]] = over_lanes((4 * SHARE, HALF_D // 2 + 4 * SHARE), 2 * DIRECT, slice(None))
    share_s[3].wait_recv()
    for i, at in enumerate(tails):
        send_part(
            3, lat[origin[3], :, at] + over_lanes((0, HALF_D // 2), 4 * SHARE, at), m_copies[3 + i], at
        )
    for pair in PAIRS:
        resident_own(pair)

    for slot in range(4):
        for pair in m_copies[slot:] if slot == 3 else m_copies[slot:slot + 1]:
            wait_pair(pair)
        lat[origin[slot]] = lat[origin[slot]] + from_code(mpr[slot]) * msr[slot]
    whole = lat[...].reshape(KVW, TOK)
    latent = whole[:LATW]
    inverse = lax.rsqrt(jnp.sum(latent * latent, axis=0, keepdims=True) / LATW + eps_norm)
    gain_cols = jnp.transpose(jnp.broadcast_to(gain[...], (128, LATW)))
    for j in range(TOK // 128):
        at = slice(j * 128, j * 128 + 128)
        rows[:LATW, at] = (latent[:, at] * inverse[:, at] * gain_cols).astype(BF16)
    first, second = whole[LATW:LATW + ROPEW // 2], whole[LATW + ROPEW // 2:]
    rows[LATW:LATW + ROPEW // 2, :] = (first * cosine[...] - second * sine[...]).astype(BF16)
    rows[LATW + ROPEW // 2:KVW, :] = (first * sine[...] + second * cosine[...]).astype(BF16)

    slot_at = lax.broadcasted_iota(I32, (CAPTOK, TOK), 0)

    def pack_for(to):
        chosen = ((slot_at + to * CAPTOK) == tok[...]).astype(F32)
        empty = jnp.sum(chosen, axis=1, keepdims=True) < 0.5
        page_rows = nt(chosen.astype(BF16), rows[...])
        column = lax.broadcasted_iota(I32, (CAPTOK, KVX), 1)
        return jnp.where((column == KVW) & empty, 1.0, page_rows).astype(BF16)

    first, second = pl.ds(0, HALF), pl.ds(HALF, HALF)
    a_p = [link(packed.at[0, at], arr.at[part, c], dev_zp) for at, part in ((first, 2), (second, 4))]
    a_m = [link(packed.at[1, at], arr.at[part, c], dev_zm) for at, part in ((first, 3), (second, 5))]
    a_r0 = link(packed.at[2, first], relay.at[0], dev_zp)
    a_r1 = link(packed.at[2, second], relay.at[1], dev_zm)
    a_f0 = link(relay.at[0], arr.at[6, c], dev_zp)
    a_f1 = link(relay.at[1], arr.at[7, c], dev_zm)
    a_share = [link(arr.at[part, c], arr.at[part, c], dev_sib) for part in range(8)]
    packed[0] = pack_for(lax.rem(b + 1, 4))
    go(a_p[0])
    packed[1] = pack_for(lax.rem(b + 3, 4))
    go(a_m[0])
    packed[2] = pack_for(lax.rem(b + 2, 4))
    go(a_r0)
    go(a_r1)
    go(a_p[1])
    go(a_m[1])
    own_pages = pack_for(b)
    arr[0, c] = own_pages[:HALF]
    go(a_share[0])
    arr[1, c] = own_pages[HALF:]
    go(a_share[1])

    def swap(copies, parts):
        for copy, part in zip(copies, parts):
            copy.wait_recv()
            go(a_share[part])

    def ready(parts):
        for part in parts:
            a_share[part].wait_recv()

    def turn_values(first, last):
        size = (last + 1 - first) * CAPTOK
        values = arr[first:last + 1].reshape(size, KVX)[:, :LATW]
        vt[:, first * CAPTOK:first * CAPTOK + size] = jnp.transpose(values)

    def pages_step(request, count, first, last):
        size, at = (last + 1 - first) * CAPTOK, columns(request, count)
        keys = arr[first:last + 1].reshape(size, KVX)
        score = nt(keys, qbuf[pl.ds(c * NR + request, count)].reshape(count * QROWS, KVX))
        old = ms[:, at]
        top = jnp.maximum(old, jnp.max(score, axis=0, keepdims=True))
        shrink = jnp.exp2((old - top) * log2_scale)
        w = weigh(score, top)
        total = ls[:, at] * shrink + jnp.sum(w, axis=0, keepdims=True)
        value = acc[:, at] * shrink + nn(vt[:, first * CAPTOK:first * CAPTOK + size], w.astype(BF16))
        return value, top, total

    def pages_of(request, count, first, last):
        at = columns(request, count)
        acc[:, at], ms[:, at], ls[:, at] = pages_step(request, count, first, last)

    for pair in e_copies:
        wait_pair(pair)
    for r in range(NR):
        add_other(r)
    ready((0, 1))
    turn_values(0, 1)
    pages_of(0, 2, 0, 1)
    swap((a_p[0], a_m[0]), (2, 3))
    pages_of(2, 2, 0, 1)
    a_r0.wait_recv()
    go(a_f0)
    a_r1.wait_recv()
    go(a_f1)
    ready((2, 3))
    turn_values(2, 3)
    pages_of(0, 2, 2, 3)
    swap((a_p[1], a_m[1]), (4, 5))
    pages_of(2, 2, 2, 3)
    ready((4, 5))
    turn_values(4, 5)
    swap((a_f0, a_f1), (6, 7))
    pages_of(0, 2, 4, 5)
    ready((6, 7))
    turn_values(6, 7)

    def merge(parts):
        top = parts[0][1][0]
        for _, stat in parts[1:]:
            top = jnp.maximum(top, stat[0])
        value, total = 0.0, 0.0
        for coded, stat in parts:
            factor = jnp.exp2(stat[0] - top)
            value = value + from_code(coded) * factor
            total = total + factor * stat[1]
        return value, top, total

    def put(coded_ref, stat_ref, value, top, total):
        coded, scale = code(value, 0)
        coded_ref[...] = to_code(coded).reshape(coded_ref.shape)
        stat_ref[0] = top + jnp.log(scale) * log2_e
        stat_ref[1] = total / scale

    yp, ym, yy = lax.rem(y + 1, 4), lax.rem(y + 3, 4), lax.rem(y + 2, 4)
    first_y = used[0]

    def y_pair(r, k):
        pairs = (
            (osend.at[r, yy, 0], ostat.at[r], 0, dev_yp),
            (osend.at[r, yy, 1], ostat.at[r], 1, dev_ym),
            (osend.at[r, yp, 1], ostat.at[r], 2, dev_yp),
            (osend.at[r, ym, 0], ostat.at[r], 3, dev_ym),
            (rsend.at[r, 0], rstat.at[r, 0], 4, dev_yp),
            (rsend.at[r, 1], rstat.at[r, 1], 5, dev_ym),
        )
        data, stat, _, dev = pairs[k]
        return (
            link_at(first_y + 18 * r + 2 * k, data, ybuf.at[r, k], dev),
            link_at(first_y + 18 * r + 2 * k + 1, stat, ystat.at[r, k], dev),
        )

    def last_pair(r, k):
        half, core, dev = ((1 - xh, c, dev_x), (1 - xh, 1 - c, dev_x_sib), (xh, 1 - c, dev_sib))[k]
        return (
            link_at(first_y + 18 * r + 12 + 2 * k, mbuf.at[r, half, core], fbuf.at[r, k], dev),
            link_at(first_y + 18 * r + 13 + 2 * k, mstat.at[r, half], fstat.at[r, k], dev),
        )

    def start_pair(pair):
        pair[0].start()
        pair[1].start()

    def relay_sums(r, carry):
        for k, to in ((0, yp), (1, ym)):
            wait_pair(y_pair(r, k))
            put(rsend.at[r, k], rstat.at[r, k], *merge([
                (osend[r, to, k], ostat[r]), (ybuf[r, k], ystat[r, k]),
            ]))
            start_pair(y_pair(r, 4 + k))
        return carry

    for request, first in ((0, 6), (2, 4)):
        value, top, total = pages_step(request, 2, first, 7)
        coded, scale = code(value, 0)
        coded, top, total = to_code(coded), top * log2_scale + jnp.log(scale) * log2_e, total / scale
        for r in (request, request + 1):
            at = columns(r - request)
            osend[r] = coded[:, at].reshape(4, 2, 64, QROWS)
            ostat[r, 0] = top[:, at]
            ostat[r, 1] = total[:, at]
            for k in range(4):
                start_pair(y_pair(r, k))

    def sums_over_y(r, carry):
        for k in range(2, 6):
            wait_pair(y_pair(r, k))
        for h, (one, two) in enumerate(((3, 4), (2, 5))):
            put(mbuf.at[r, h], mstat.at[r, h], *merge([
                (osend[r, y, h], ostat[r]), (ybuf[r, one], ystat[r, one]), (ybuf[r, two], ystat[r, two]),
            ]))
        for k in (1, 0, 2):
            start_pair(last_pair(r, k))
        return carry

    def last_sums(r, carry):
        for k in range(3):
            wait_pair(last_pair(r, k))
        own, other = c * NR + r, (1 - c) * NR + r
        for request, parts in (
            (own, [(mbuf[r, xh, c], mstat[r, xh]), (fbuf[r, 0], fstat[r, 0])]),
            (other, [(fbuf[r, 2], fstat[r, 2]), (fbuf[r, 1], fstat[r, 1])]),
        ):
            value, _, total = merge(parts)
            value = value / total
            for step in range(4):
                out[step, request] = value[:, 64 * step:64 * step + 64]
        return carry

    def finish(r, carry):
        for pair in [y_pair(r, k) for k in range(6)] + [last_pair(r, k) for k in range(3)]:
            pair[0].wait_send()
            pair[1].wait_send()
        return carry

    lax.fori_loop(0, NR, relay_sums, 0)
    for stage in (sums_over_y, last_sums, finish):
        lax.fori_loop(0, NR, stage, 0)
    for copy in started:
        copy.wait_send()


LINKS = 144


def tables():
    half = ROPEW // 2
    frequency = rope_base ** (-np.arange(half, dtype=np.float32) / np.float32(half))
    angles = np.arange(TOK, dtype=np.float32)[None, :] * frequency.astype(np.float32)[:, None]
    return np.cos(angles).astype(np.float32), np.sin(angles).astype(np.float32)


def on_device(hidden, kv_down, kv_gain, page_owner, page_request, queries, cache, lengths):
    cosine, sine = tables()
    anywhere = pl.BlockSpec(memory_space=pl.ANY)
    vmem = pl.BlockSpec(memory_space=pltpu.VMEM)
    smem = pl.BlockSpec(memory_space=pltpu.SMEM)
    sums = pl.pallas_call(
        kernel,
        out_shape=jax.ShapeDtypeStruct((4, 2 * NR, 32, 64), F32),
        in_specs=[anywhere, anywhere, vmem, smem, smem, anywhere, anywhere, smem, vmem, vmem],
        out_specs=vmem,
        scratch_shapes=[
            pltpu.VMEM((TOK, HALF_D), BF16),
            pltpu.VMEM((4, BLK, HALF_D), BF16),
            pltpu.VMEM((4, BLK, TOK), F32),
            pltpu.VMEM((4, BLK, TOK), I16),
            pltpu.VMEM((4, BLK, TOK), I16),
            pltpu.VMEM((4, 1, TOK), F32),
            pltpu.VMEM((4, 1, TOK), F32),
            pltpu.VMEM((KVX, TOK), BF16),
            pltpu.VMEM((3, CAPTOK, KVX), BF16),
            pltpu.VMEM((2, HALF, KVX), BF16),
            pltpu.VMEM((8, 2, HALF, KVX), BF16),
            pltpu.VMEM((1, TOK), I32),
            pltpu.VMEM((LATW, 8 * CAPTOK), BF16),
            pltpu.VMEM((2 * NR, 4, 64, KVW), BF16),
            pltpu.VMEM((2 * NR, QROWS, KVX), BF16),
            pltpu.VMEM((2 * NR, KVW, CTXD), BF16),
            pltpu.VMEM((NR, LATW, QROWS), I16),
            pltpu.VMEM((NR, 3, 1, QROWS), F32),
            pltpu.VMEM((NR, LATW, QROWS), I16),
            pltpu.VMEM((NR, 3, 1, QROWS), F32),
            pltpu.VMEM((LATW, NR * QROWS), F32),
            pltpu.VMEM((1, NR * QROWS), F32),
            pltpu.VMEM((1, NR * QROWS), F32),
            pltpu.VMEM((NR, 4, 2, 64, QROWS), I16),
            pltpu.VMEM((NR, 2, 1, QROWS), F32),
            pltpu.VMEM((NR, 6, 64, QROWS), I16),
            pltpu.VMEM((NR, 6, 2, 1, QROWS), F32),
            pltpu.VMEM((NR, 2, 64, QROWS), I16),
            pltpu.VMEM((NR, 2, 2, 1, QROWS), F32),
            pltpu.VMEM((NR, 2, 2, 32, QROWS), I16),
            pltpu.VMEM((NR, 2, 2, 1, QROWS), F32),
            pltpu.VMEM((NR, 3, 32, QROWS), I16),
            pltpu.VMEM((NR, 3, 2, 1, QROWS), F32),
            pltpu.SemaphoreType.DMA((7,)),
            pltpu.SemaphoreType.DMA((LINKS,)),
            pltpu.SemaphoreType.DMA((LINKS,)),
        ],
        compiler_params=pltpu.CompilerParams(
            collective_id=0, has_side_effects=True, vmem_limit_bytes=56 * 1024 * 1024
        ),
        cost_estimate=pl.CostEstimate(flops=7_500_000_000, bytes_accessed=12_000_000, transcendentals=3_000_000),
    )(
        hidden, kv_down.T, kv_gain.reshape(1, LATW), page_owner.T, page_request, queries, cache.transpose(0, 2, 1), lengths,
        jnp.asarray(cosine), jnp.asarray(sine),
    )
    return sums.transpose(0, 1, 3, 2)


def solution(mesh):
    return jax.shard_map(
        on_device,
        mesh=mesh,
        in_specs=(
            P(("seq", "batch"), "mp"),
            P("mp", "batch"),
            P(),
            P(("seq", "batch"), None),
            P(("seq", "batch")),
            P(None, "batch", "mp", None),
            P("batch", "seq", None),
            P("batch"),
        ),
        out_specs=P(None, "batch", "mp", "seq"),
        check_vma=False,
    )
```

```python
import jax
import jax.numpy as jnp
import numpy as np
from jax import lax
from jax.experimental import pallas as pl
from jax.experimental.pallas import tpu as pltpu
from jax.sharding import PartitionSpec as P

MESH = pl.DeviceIdType.MESH
F32, BF16, I32, I16 = jnp.float32, jnp.bfloat16, jnp.int32, jnp.int16

eps_norm = 1e-06
score_scale = 192.0 ** (-0.5)
log2_e = 1.4426950408889634
log2_scale = score_scale * log2_e
rope_base = 10000.0
masked_value = -1e30
floor_value = -1e29
code_top = 32767.0

TOK, HALF_D, KVW, LATW, ROPEW = 384, 3584, 576, 512, 64
LABELS = 64
KVX = KVW + LABELS
BLK = 144
SHARE, DIRECT = 256, 384
CAPTOK = 192
HALF = CAPTOK // 2
PAGES, PAGE, CAP = 24, 16, 12
QROWS = 256
CTXD = 512
NR = 4
PAIRS = ((0, 1), (2, 3))


def nt(a, b):
    return lax.dot_general(a, b, (((1,), (1,)), ((), ())), preferred_element_type=F32)


def nn(a, b):
    return jnp.dot(a, b, preferred_element_type=F32)


def kernel(
    hidden, kv_down, gain_in, owner_in, request_in, queries, cache, lengths_in, cosine_in, sine_in,
    out_hbm,
    gain, owner, request, lengths, cosine, sine, out,
    hid, kvt, lat, mps, mpr, mss, msr, rows, packed, relay, arr, tok,
    vt, qraw, qbuf, kbuf, esend, estat, ebuf, efrom, acc, ms, ls, osend, ostat, ybuf, ystat, rsend, rstat, mbuf, mstat, fbuf, fstat,
    loc, send, recv,
):
    s, b, p = lax.axis_index("seq"), lax.axis_index("batch"), lax.axis_index("mp")
    c = lax.rem(s, 2)
    sib = s + 1 - 2 * c
    y = lax.div(s, 4)
    in_y = lax.rem(s, 4)
    xh = lax.rem(lax.div(s, 2), 2)
    dev_zp = (s, lax.rem(b + 1, 4), p)
    dev_zm = (s, lax.rem(b + 3, 4), p)
    dev_zz = (s, lax.rem(b + 2, 4), p)
    dev_mp = (s, b, 1 - p)
    dev_sib = (sib, b, p)
    dev_yp = (lax.rem(y + 1, 4) * 4 + in_y, b, p)
    dev_ym = (lax.rem(y + 3, 4) * 4 + in_y, b, p)
    dev_x = (s + 2 - 4 * xh, b, p)
    dev_x_sib = (sib + 2 - 4 * xh, b, p)

    used = [0]
    started = []

    def link(src, dst, dev):
        used[0] += 1
        return link_at(used[0] - 1, src, dst, dev)

    def link_at(i, src, dst, dev):
        return pltpu.make_async_remote_copy(
            src_ref=src, dst_ref=dst, send_sem=send.at[i], recv_sem=recv.at[i],
            device_id=dev, device_id_type=MESH,
        )

    def go(copy):
        copy.start()
        started.append(copy)

    def code(value, axis):
        most = jnp.max(jnp.abs(value), axis=axis, keepdims=True)
        most = jnp.maximum(most, 1e-25)
        return jnp.round(value * (code_top / most)), most * (1.0 / code_top)

    def to_code(value):
        return value.astype(I32).astype(I16)

    def from_code(coded):
        return coded.astype(I32).astype(F32)

    def go_pair(pair):
        go(pair[0])
        go(pair[1])

    def wait_pair(pair):
        pair[0].wait_recv()
        pair[1].wait_recv()

    barrier = pltpu.get_barrier_semaphore()
    for dev in (dev_zp, dev_zm, dev_zz, dev_mp, dev_sib, dev_yp, dev_ym, dev_x, dev_x_sib):
        pl.semaphore_signal(barrier, inc=1, device_id=dev, device_id_type=MESH)

    small = [
        pltpu.make_async_copy(src, dst, loc.at[7 + i])
        for i, (src, dst) in enumerate((
            (owner_in, owner), (request_in, request), (lengths_in, lengths), (gain_in, gain), (cosine_in, cosine),
            (sine_in, sine),
        ))
    ]
    load_kv = pltpu.make_async_copy(kv_down, kvt.at[0], loc.at[0])
    load_hid = pltpu.make_async_copy(hidden, hid, loc.at[1])
    load_q = [pltpu.make_async_copy(queries.at[step], qraw.at[:, step], loc.at[2 + step]) for step in range(4)]
    load_cache = pltpu.make_async_copy(cache, kbuf, loc.at[6])
    for copy in [load_hid, load_kv] + small:
        copy.start()

    pl.semaphore_wait(barrier, 9)

    base = c * (HALF_D // 2)

    def lanes(start, size):
        return pl.ds(pl.multiple_of(base + start, 128), size)

    def kv_link(slot, to_slot, at, dev):
        return link(kvt.at[slot, :, at], kvt.at[to_slot, :, at], dev)

    def first_link(to_slot, at, dev):
        return link(kv_down.at[:, at], kvt.at[to_slot, :, at], dev)

    def part_of(k, first=0, size=SHARE):
        return lanes(lax.rem(y + k, 4) * SHARE + first, size)

    low, high = lanes(4 * SHARE, DIRECT), lanes(4 * SHARE + DIRECT, DIRECT)
    mine = part_of(0)
    s_p, s_m = first_link(1, mine, dev_zp), first_link(2, mine, dev_zm)
    d_p0, d_m1 = first_link(1, low, dev_zp), first_link(2, high, dev_zm)
    d_p1, d_m0 = first_link(1, high, dev_zp), first_link(2, low, dev_zm)
    for copy in (s_p, s_m, d_p0, d_m1):
        go(copy)
    for copy in load_q + [load_cache]:
        copy.start()
    sf_p, sf_m = (
        kv_link(1, 3, part_of(0, 0, SHARE // 2), dev_zp),
        kv_link(2, 3, part_of(0, SHARE // 2, SHARE // 2), dev_zm),
    )
    df_p, df_m = kv_link(1, 3, low, dev_zp), kv_link(2, 3, high, dev_zm)
    near_p = [None] + [kv_link(slot, slot, mine, dev_yp) for slot in (1, 2, 3)]
    near_m = [None] + [kv_link(slot, slot, mine, dev_ym) for slot in (1, 2, 3)]
    far = [None] + [
        (
            kv_link(slot, slot, part_of(3, 0, SHARE // 2), dev_yp),
            kv_link(slot, slot, part_of(1, SHARE // 2, SHARE // 2), dev_ym),
        )
        for slot in (1, 2, 3)
    ]
    share_s = [None] + [kv_link(slot, slot, lanes(0, 4 * SHARE), dev_sib) for slot in (1, 2, 3)]
    share_d = [None] + [kv_link(slot, slot, lanes(4 * SHARE, 2 * DIRECT), dev_sib) for slot in (1, 2, 3)]

    origin = [lax.rem(b + ahead, 4) for ahead in (0, 3, 1, 2)]
    m_copies = [
        (link(mps.at[slot], mpr.at[slot], dev_mp), link(mss.at[slot], msr.at[slot], dev_mp)) for slot in range(3)
    ]
    tails = (slice(0, 256), slice(256, TOK))
    for at in tails:
        at = pl.ds(at.start, at.stop - at.start)
        m_copies.append((
            link(mps.at[3, :, at], mpr.at[3, :, at], dev_mp), link(mss.at[3, :, at], msr.at[3, :, at], dev_mp),
        ))

    def send_part(slot, part, copies, at=slice(None)):
        lat[origin[slot], :, at] = part
        coded, scale = code(part, 0)
        mps[slot, :, at] = to_code(coded)
        mss[slot, :, at] = scale
        go_pair(copies)

    def weigh(score, top):
        return jnp.exp2(score * log2_scale - top * log2_scale)

    def fold(w):
        total = w[:, :128]
        for j in range(1, w.shape[1] // 128):
            total = total + w[:, j * 128:j * 128 + 128]
        return total

    def peak(score):
        most = score[:, :128]
        for j in range(1, score.shape[1] // 128):
            most = jnp.maximum(most, score[:, j * 128:j * 128 + 128])
        return most

    def resident(pair, half):
        at = lax.broadcasted_iota(I32, (1, CTXD), 1) + s * CTXD
        scores = [
            jnp.where(at < lengths[half * NR + r], nn(qbuf[half * NR + r, :, :KVW], kbuf[half * NR + r]), masked_value)
            for r in pair
        ]
        weights = []
        for score in scores:
            top = jnp.maximum(jnp.max(peak(score), axis=1, keepdims=True), floor_value)
            w = weigh(score, top)
            top = jnp.transpose(jnp.broadcast_to(top, (QROWS, 128)))[0:1]
            weights.append((w.astype(BF16), top, jnp.sum(jnp.transpose(fold(w)), axis=0, keepdims=True)))
        return [
            (nt(kbuf[half * NR + r, :LATW, :], w), top, total) for r, (w, top, total) in zip(pair, weights)
        ]

    def columns(first, count=1):
        return slice(first * QROWS, (first + count) * QROWS)

    def resident_own(pair):
        for r, (value, top, total) in zip(pair, resident(pair, c)):
            acc[:, columns(r)], ms[:, columns(r)], ls[:, columns(r)] = value, top, total

    def add_other(r):
        at = columns(r)
        old, top2 = ms[:, at], efrom[r, 0]
        top = jnp.maximum(old, top2)
        keep, gain2 = jnp.exp2((old - top) * log2_scale), jnp.exp2((top2 - top) * log2_scale)
        acc[:, at] = acc[:, at] * keep + from_code(ebuf[r]) * (gain2 * efrom[r, 2])
        ls[:, at] = ls[:, at] * keep + gain2 * efrom[r, 1]
        ms[:, at] = top

    load_hid.wait()
    load_kv.wait()
    send_part(0, nt(kvt[0], hid[...]), m_copies[0])
    s_p.wait_recv()
    go(sf_p)
    go(near_p[1])
    go(near_m[1])
    s_m.wait_recv()
    go(sf_m)
    go(near_p[2])
    go(near_m[2])
    go(d_p1)
    go(d_m0)

    for copy in small:
        copy.wait()
    token = lax.broadcasted_iota(I32, (1, TOK), 1)
    token_page = lax.shift_right_logical(token, 4)
    dest = jnp.zeros((1, TOK), I32)
    asked = jnp.zeros((1, TOK), I32)
    counts = [jnp.int32(0)] * 4
    for page in range(PAGES):
        to = owner[0, page]
        rank = jnp.where(to == 0, counts[0], jnp.where(to == 1, counts[1], jnp.where(to == 2, counts[2], counts[3])))
        counts = [counts[o] + (to == o).astype(I32) for o in range(4)]
        dest = jnp.where(token_page == page, (to * CAP + rank) * PAGE, dest)
        asked = jnp.where(token_page == page, request[page] + 1, asked)
    dest = dest + lax.bitwise_and(token, 15)
    tok[...] = dest

    label_row = lax.broadcasted_iota(I32, (LABELS, TOK), 0)
    rows[KVW:, :] = (label_row == asked).astype(F32).astype(BF16)

    d_p0.wait_recv()
    go(df_p)
    d_m1.wait_recv()
    go(df_m)

    def pass_on(slot):
        near_p[slot].wait_recv()
        go(far[slot][0])
        near_m[slot].wait_recv()
        go(far[slot][1])

    def swap_shared(slot):
        far[slot][0].wait_recv()
        far[slot][1].wait_recv()
        go(share_s[slot])

    pass_on(1)
    sf_p.wait_recv()
    sf_m.wait_recv()
    go(near_p[3])
    go(near_m[3])

    for copy in load_q:
        copy.wait()
    load_cache.wait()
    label_at = lax.broadcasted_iota(I32, (QROWS, LABELS), 1)

    def fill(r, carry):
        qbuf[r, :, :KVW] = qraw[r].reshape(QROWS, KVW)
        qbuf[r, :, KVW:] = jnp.where(label_at == r + 1, 0.0, masked_value).astype(BF16)
        return carry

    def resident_other(pair):
        for r, (value, top, total) in zip(pair, resident(pair, 1 - c)):
            coded, scale = code(value, 0)
            esend[r] = to_code(coded)
            for k, row in enumerate((top, total, scale)):
                estat[r, k] = row
            go_pair(e_copies[r])

    e_copies = [
        (link(esend.at[r], ebuf.at[r], dev_sib), link(estat.at[r], efrom.at[r], dev_sib)) for r in range(NR)
    ]
    lax.fori_loop(0, 2 * NR, fill, 0)
    resident_other(PAIRS[0])

    pass_on(2)
    d_p1.wait_recv()
    go(share_d[1])
    d_m0.wait_recv()
    go(share_d[2])
    swap_shared(1)
    resident_other(PAIRS[1])

    pass_on(3)
    swap_shared(2)
    share_d[1].wait_recv()
    share_s[1].wait_recv()
    send_part(1, nt(kvt[1], hid[...]), m_copies[1])
    df_p.wait_recv()
    df_m.wait_recv()
    go(share_d[3])
    swap_shared(3)
    share_d[2].wait_recv()
    share_s[2].wait_recv()
    send_part(2, nt(kvt[2], hid[...]), m_copies[2])

    def over_lanes(starts, size, at):
        return sum(nt(kvt[3, :, start:start + size], hid[at, start:start + size]) for start in starts)

    share_d[3].wait_recv()
    lat[origin[3]] = over_lanes((4 * SHARE, HALF_D // 2 + 4 * SHARE), 2 * DIRECT, slice(None))
    share_s[3].wait_recv()
    for i, at in enumerate(tails):
        send_part(
            3, lat[origin[3], :, at] + over_lanes((0, HALF_D // 2), 4 * SHARE, at), m_copies[3 + i], at
        )
    for pair in PAIRS:
        resident_own(pair)

    for slot in range(4):
        for pair in m_copies[slot:] if slot == 3 else m_copies[slot:slot + 1]:
            wait_pair(pair)
        lat[origin[slot]] = lat[origin[slot]] + from_code(mpr[slot]) * msr[slot]
    whole = lat[...].reshape(KVW, TOK)
    latent = whole[:LATW]
    inverse = lax.rsqrt(jnp.sum(latent * latent, axis=0, keepdims=True) / LATW + eps_norm)
    gain_cols = jnp.transpose(jnp.broadcast_to(gain[...], (128, LATW)))
    for j in range(TOK // 128):
        at = slice(j * 128, j * 128 + 128)
        rows[:LATW, at] = (latent[:, at] * inverse[:, at] * gain_cols).astype(BF16)
    first, second = whole[LATW:LATW + ROPEW // 2], whole[LATW + ROPEW // 2:]
    rows[LATW:LATW + ROPEW // 2, :] = (first * cosine[...] - second * sine[...]).astype(BF16)
    rows[LATW + ROPEW // 2:KVW, :] = (first * sine[...] + second * cosine[...]).astype(BF16)

    slot_at = lax.broadcasted_iota(I32, (CAPTOK, TOK), 0)

    def pack_for(to):
        chosen = ((slot_at + to * CAPTOK) == tok[...]).astype(F32)
        empty = jnp.sum(chosen, axis=1, keepdims=True) < 0.5
        page_rows = nt(chosen.astype(BF16), rows[...])
        column = lax.broadcasted_iota(I32, (CAPTOK, KVX), 1)
        return jnp.where((column == KVW) & empty, 1.0, page_rows).astype(BF16)

    first, second = pl.ds(0, HALF), pl.ds(HALF, HALF)
    a_p = [link(packed.at[0, at], arr.at[part, c], dev_zp) for at, part in ((first, 2), (second, 4))]
    a_m = [link(packed.at[1, at], arr.at[part, c], dev_zm) for at, part in ((first, 3), (second, 5))]
    a_r0 = link(packed.at[2, first], relay.at[0], dev_zp)
    a_r1 = link(packed.at[2, second], relay.at[1], dev_zm)
    a_f0 = link(relay.at[0], arr.at[6, c], dev_zp)
    a_f1 = link(relay.at[1], arr.at[7, c], dev_zm)
    a_share = [link(arr.at[part, c], arr.at[part, c], dev_sib) for part in range(8)]
    packed[0] = pack_for(lax.rem(b + 1, 4))
    go(a_p[0])
    packed[1] = pack_for(lax.rem(b + 3, 4))
    go(a_m[0])
    packed[2] = pack_for(lax.rem(b + 2, 4))
    go(a_r0)
    go(a_r1)
    go(a_p[1])
    go(a_m[1])
    own_pages = pack_for(b)
    arr[0, c] = own_pages[:HALF]
    go(a_share[0])
    arr[1, c] = own_pages[HALF:]
    go(a_share[1])

    def swap(copies, parts):
        for copy, part in zip(copies, parts):
            copy.wait_recv()
            go(a_share[part])

    def ready(parts):
        for part in parts:
            a_share[part].wait_recv()

    def turn_values(first, last):
        size = (last + 1 - first) * CAPTOK
        values = arr[first:last + 1].reshape(size, KVX)[:, :LATW]
        vt[:, first * CAPTOK:first * CAPTOK + size] = jnp.transpose(values)

    def pages_step(request, count, first, last):
        size, at = (last + 1 - first) * CAPTOK, columns(request, count)
        keys = arr[first:last + 1].reshape(size, KVX)
        score = nt(keys, qbuf[pl.ds(c * NR + request, count)].reshape(count * QROWS, KVX))
        old = ms[:, at]
        top = jnp.maximum(old, jnp.max(score, axis=0, keepdims=True))
        shrink = jnp.exp2((old - top) * log2_scale)
        w = weigh(score, top)
        total = ls[:, at] * shrink + jnp.sum(w, axis=0, keepdims=True)
        value = acc[:, at] * shrink + nn(vt[:, first * CAPTOK:first * CAPTOK + size], w.astype(BF16))
        return value, top, total

    def pages_of(request, count, first, last):
        at = columns(request, count)
        acc[:, at], ms[:, at], ls[:, at] = pages_step(request, count, first, last)

    for pair in e_copies:
        wait_pair(pair)
    for r in range(NR):
        add_other(r)
    ready((0, 1))
    turn_values(0, 1)
    pages_of(0, 2, 0, 1)
    swap((a_p[0], a_m[0]), (2, 3))
    pages_of(2, 2, 0, 1)
    a_r0.wait_recv()
    go(a_f0)
    a_r1.wait_recv()
    go(a_f1)
    ready((2, 3))
    turn_values(2, 3)
    pages_of(0, 2, 2, 3)
    swap((a_p[1], a_m[1]), (4, 5))
    pages_of(2, 2, 2, 3)
    ready((4, 5))
    turn_values(4, 5)
    swap((a_f0, a_f1), (6, 7))
    pages_of(0, 2, 4, 5)
    ready((6, 7))
    turn_values(6, 7)

    def merge(parts):
        top = parts[0][1][0]
        for _, stat in parts[1:]:
            top = jnp.maximum(top, stat[0])
        value, total = 0.0, 0.0
        for coded, stat in parts:
            factor = jnp.exp2(stat[0] - top)
            value = value + from_code(coded) * factor
            total = total + factor * stat[1]
        return value, top, total

    def put(coded_ref, stat_ref, value, top, total):
        coded, scale = code(value, 0)
        coded_ref[...] = to_code(coded).reshape(coded_ref.shape)
        stat_ref[0] = top + jnp.log(scale) * log2_e
        stat_ref[1] = total / scale

    yp, ym, yy = lax.rem(y + 1, 4), lax.rem(y + 3, 4), lax.rem(y + 2, 4)
    first_y = used[0]

    def y_pair(r, k):
        pairs = (
            (osend.at[r, yy, 0], ostat.at[r], 0, dev_yp),
            (osend.at[r, yy, 1], ostat.at[r], 1, dev_ym),
            (osend.at[r, yp, 1], ostat.at[r], 2, dev_yp),
            (osend.at[r, ym, 0], ostat.at[r], 3, dev_ym),
            (rsend.at[r, 0], rstat.at[r, 0], 4, dev_yp),
            (rsend.at[r, 1], rstat.at[r, 1], 5, dev_ym),
        )
        data, stat, _, dev = pairs[k]
        return (
            link_at(first_y + 18 * r + 2 * k, data, ybuf.at[r, k], dev),
            link_at(first_y + 18 * r + 2 * k + 1, stat, ystat.at[r, k], dev),
        )

    def last_pair(r, k):
        half, core, dev = ((1 - xh, c, dev_x), (1 - xh, 1 - c, dev_x_sib), (xh, 1 - c, dev_sib))[k]
        return (
            link_at(first_y + 18 * r + 12 + 2 * k, mbuf.at[r, half, core], fbuf.at[r, k], dev),
            link_at(first_y + 18 * r + 13 + 2 * k, mstat.at[r, half], fstat.at[r, k], dev),
        )

    def start_pair(pair):
        pair[0].start()
        pair[1].start()

    def relay_sums(r, carry):
        for k, to in ((0, yp), (1, ym)):
            wait_pair(y_pair(r, k))
            put(rsend.at[r, k], rstat.at[r, k], *merge([
                (osend[r, to, k], ostat[r]), (ybuf[r, k], ystat[r, k]),
            ]))
            start_pair(y_pair(r, 4 + k))
        return carry

    for first_request, count, first in ((0, 1, 6), (1, 1, 6), (2, 2, 4)):
        value, top, total = pages_step(first_request, count, first, 7)
        coded, scale = code(value, 0)
        coded, top, total = to_code(coded), top * log2_scale + jnp.log(scale) * log2_e, total / scale
        for r in range(first_request, first_request + count):
            at = columns(r - first_request)
            osend[r] = coded[:, at].reshape(4, 2, 64, QROWS)
            ostat[r, 0] = top[:, at]
            ostat[r, 1] = total[:, at]
            for k in range(4):
                start_pair(y_pair(r, k))

    def sums_over_y(r, carry):
        for k in range(2, 6):
            wait_pair(y_pair(r, k))
        for h, (one, two) in enumerate(((3, 4), (2, 5))):
            put(mbuf.at[r, h], mstat.at[r, h], *merge([
                (osend[r, y, h], ostat[r]), (ybuf[r, one], ystat[r, one]), (ybuf[r, two], ystat[r, two]),
            ]))
        for k in (1, 0, 2):
            start_pair(last_pair(r, k))
        return carry

    def out_copy(wanted):
        return pltpu.make_async_copy(out.at[:, wanted], out_hbm.at[:, wanted], loc.at[13 + wanted])

    def last_sums(r, carry):
        for k in range(3):
            wait_pair(last_pair(r, k))
        own, other = c * NR + r, (1 - c) * NR + r
        for wanted, parts in (
            (own, [(mbuf[r, xh, c], mstat[r, xh]), (fbuf[r, 0], fstat[r, 0])]),
            (other, [(fbuf[r, 2], fstat[r, 2]), (fbuf[r, 1], fstat[r, 1])]),
        ):
            value, _, total = merge(parts)
            value = value / total
            for step in range(4):
                out[step, wanted] = value[:, 64 * step:64 * step + 64]
            out_copy(wanted).start()
        return carry

    def finish(r, carry):
        for pair in [y_pair(r, k) for k in range(6)] + [last_pair(r, k) for k in range(3)]:
            pair[0].wait_send()
            pair[1].wait_send()
        return carry

    lax.fori_loop(0, NR, relay_sums, 0)
    for stage in (sums_over_y, last_sums, finish):
        lax.fori_loop(0, NR, stage, 0)
    for wanted in range(2 * NR):
        out_copy(wanted).wait()
    for copy in started:
        copy.wait_send()


LINKS = 144


def tables():
    half = ROPEW // 2
    frequency = rope_base ** (-np.arange(half, dtype=np.float32) / np.float32(half))
    angles = np.arange(TOK, dtype=np.float32)[None, :] * frequency.astype(np.float32)[:, None]
    return np.cos(angles).astype(np.float32), np.sin(angles).astype(np.float32)


def on_device(hidden, kv_down, kv_gain, page_owner, page_request, queries, cache, lengths):
    cosine, sine = tables()
    anywhere = pl.BlockSpec(memory_space=pl.ANY)
    sums = pl.pallas_call(
        kernel,
        out_shape=jax.ShapeDtypeStruct((4, 2 * NR, 32, 64), F32),
        in_specs=[anywhere] * 10,
        out_specs=anywhere,
        scratch_shapes=[
            pltpu.VMEM((1, LATW), F32),
            pltpu.SMEM((1, PAGES), I32),
            pltpu.SMEM((PAGES,), I32),
            pltpu.SMEM((2 * NR,), I32),
            pltpu.VMEM((ROPEW // 2, TOK), F32),
            pltpu.VMEM((ROPEW // 2, TOK), F32),
            pltpu.VMEM((4, 2 * NR, 32, 64), F32),
            pltpu.VMEM((TOK, HALF_D), BF16),
            pltpu.VMEM((4, BLK, HALF_D), BF16),
            pltpu.VMEM((4, BLK, TOK), F32),
            pltpu.VMEM((4, BLK, TOK), I16),
            pltpu.VMEM((4, BLK, TOK), I16),
            pltpu.VMEM((4, 1, TOK), F32),
            pltpu.VMEM((4, 1, TOK), F32),
            pltpu.VMEM((KVX, TOK), BF16),
            pltpu.VMEM((3, CAPTOK, KVX), BF16),
            pltpu.VMEM((2, HALF, KVX), BF16),
            pltpu.VMEM((8, 2, HALF, KVX), BF16),
            pltpu.VMEM((1, TOK), I32),
            pltpu.VMEM((LATW, 8 * CAPTOK), BF16),
            pltpu.VMEM((2 * NR, 4, 64, KVW), BF16),
            pltpu.VMEM((2 * NR, QROWS, KVX), BF16),
            pltpu.VMEM((2 * NR, KVW, CTXD), BF16),
            pltpu.VMEM((NR, LATW, QROWS), I16),
            pltpu.VMEM((NR, 3, 1, QROWS), F32),
            pltpu.VMEM((NR, LATW, QROWS), I16),
            pltpu.VMEM((NR, 3, 1, QROWS), F32),
            pltpu.VMEM((LATW, NR * QROWS), F32),
            pltpu.VMEM((1, NR * QROWS), F32),
            pltpu.VMEM((1, NR * QROWS), F32),
            pltpu.VMEM((NR, 4, 2, 64, QROWS), I16),
            pltpu.VMEM((NR, 2, 1, QROWS), F32),
            pltpu.VMEM((NR, 6, 64, QROWS), I16),
            pltpu.VMEM((NR, 6, 2, 1, QROWS), F32),
            pltpu.VMEM((NR, 2, 64, QROWS), I16),
            pltpu.VMEM((NR, 2, 2, 1, QROWS), F32),
            pltpu.VMEM((NR, 2, 2, 32, QROWS), I16),
            pltpu.VMEM((NR, 2, 2, 1, QROWS), F32),
            pltpu.VMEM((NR, 3, 32, QROWS), I16),
            pltpu.VMEM((NR, 3, 2, 1, QROWS), F32),
            pltpu.SemaphoreType.DMA((13 + 2 * NR,)),
            pltpu.SemaphoreType.DMA((LINKS,)),
            pltpu.SemaphoreType.DMA((LINKS,)),
        ],
        compiler_params=pltpu.CompilerParams(
            collective_id=0, has_side_effects=True, vmem_limit_bytes=56 * 1024 * 1024
        ),
        cost_estimate=pl.CostEstimate(flops=7_500_000_000, bytes_accessed=12_000_000, transcendentals=3_000_000),
    )(
        hidden, kv_down.T, kv_gain.reshape(1, LATW), page_owner.T, page_request, queries, cache.transpose(0, 2, 1), lengths,
        jnp.asarray(cosine), jnp.asarray(sine),
    )
    return sums.transpose(0, 1, 3, 2)


def solution(mesh):
    return jax.shard_map(
        on_device,
        mesh=mesh,
        in_specs=(
            P(("seq", "batch"), "mp"),
            P("mp", "batch"),
            P(),
            P(("seq", "batch"), None),
            P(("seq", "batch")),
            P(None, "batch", "mp", None),
            P("batch", "seq", None),
            P("batch"),
        ),
        out_specs=P(None, "batch", "mp", "seq"),
        check_vma=False,
    )
```

```python
import jax
import jax.numpy as jnp
import numpy as np
from jax import lax
from jax.experimental import pallas as pl
from jax.experimental.pallas import tpu as pltpu
from jax.sharding import PartitionSpec as P

MESH = pl.DeviceIdType.MESH
F32, BF16, I32, I16 = jnp.float32, jnp.bfloat16, jnp.int32, jnp.int16

eps_norm = 1e-06
score_scale = 192.0 ** (-0.5)
log2_e = 1.4426950408889634
log2_scale = score_scale * log2_e
rope_base = 10000.0
masked_value = -1e30
floor_value = -1e29
code_top = 32767.0

TOK, HALF_D, KVW, LATW, ROPEW = 384, 3584, 576, 512, 64
LABELS = 64
KVX = KVW + LABELS
BLK = 144
SHARE, DIRECT = 256, 384
CAPTOK = 192
HALF = CAPTOK // 2
PAGES, PAGE, CAP = 24, 16, 12
QROWS = 256
CTXD = 512
NR = 4
PAIRS = ((0, 1), (2, 3))


def nt(a, b):
    return lax.dot_general(a, b, (((1,), (1,)), ((), ())), preferred_element_type=F32)


def nn(a, b):
    return jnp.dot(a, b, preferred_element_type=F32)


def kernel(
    hidden, kv_down, gain_in, owner_in, request_in, queries, cache, lengths_in, cosine_in, sine_in,
    out_hbm,
    gain, owner, request, lengths, cosine, sine, out,
    hid, kvt, lat, mps, mpr, mss, msr, rows, packed, relay, arr, tok,
    vt, qraw, qbuf, kbuf, esend, estat, ebuf, efrom, acc, ms, ls, osend, ostat, ybuf, ystat, rsend, rstat, mbuf, mstat, fbuf, fstat,
    loc, send, recv,
):
    s, b, p = lax.axis_index("seq"), lax.axis_index("batch"), lax.axis_index("mp")
    c = lax.rem(s, 2)
    sib = s + 1 - 2 * c
    y = lax.div(s, 4)
    in_y = lax.rem(s, 4)
    xh = lax.rem(lax.div(s, 2), 2)
    dev_zp = (s, lax.rem(b + 1, 4), p)
    dev_zm = (s, lax.rem(b + 3, 4), p)
    dev_zz = (s, lax.rem(b + 2, 4), p)
    dev_mp = (s, b, 1 - p)
    dev_sib = (sib, b, p)
    dev_yp = (lax.rem(y + 1, 4) * 4 + in_y, b, p)
    dev_ym = (lax.rem(y + 3, 4) * 4 + in_y, b, p)
    dev_x = (s + 2 - 4 * xh, b, p)
    dev_x_sib = (sib + 2 - 4 * xh, b, p)

    used = [0]
    started = []

    def link(src, dst, dev):
        used[0] += 1
        return link_at(used[0] - 1, src, dst, dev)

    def link_at(i, src, dst, dev):
        return pltpu.make_async_remote_copy(
            src_ref=src, dst_ref=dst, send_sem=send.at[i], recv_sem=recv.at[i],
            device_id=dev, device_id_type=MESH,
        )

    def go(copy):
        copy.start()
        started.append(copy)

    def code(value, axis):
        most = jnp.max(jnp.abs(value), axis=axis, keepdims=True)
        most = jnp.maximum(most, 1e-25)
        return jnp.round(value * (code_top / most)), most * (1.0 / code_top)

    def to_code(value):
        return value.astype(I32).astype(I16)

    def from_code(coded):
        return coded.astype(I32).astype(F32)

    def go_pair(pair):
        go(pair[0])
        go(pair[1])

    def wait_pair(pair):
        pair[0].wait_recv()
        pair[1].wait_recv()

    barrier = pltpu.get_barrier_semaphore()
    for dev in (dev_zp, dev_zm, dev_zz, dev_mp, dev_sib, dev_yp, dev_ym, dev_x, dev_x_sib):
        pl.semaphore_signal(barrier, inc=1, device_id=dev, device_id_type=MESH)

    small = [
        pltpu.make_async_copy(src, dst, loc.at[7 + i])
        for i, (src, dst) in enumerate((
            (owner_in, owner), (request_in, request), (lengths_in, lengths), (gain_in, gain), (cosine_in, cosine),
            (sine_in, sine),
        ))
    ]
    load_kv = pltpu.make_async_copy(kv_down, kvt.at[0], loc.at[0])
    load_hid = pltpu.make_async_copy(hidden, hid, loc.at[1])
    load_q = [pltpu.make_async_copy(queries.at[step], qraw.at[:, step], loc.at[2 + step]) for step in range(4)]
    load_cache = pltpu.make_async_copy(cache, kbuf, loc.at[6])
    for copy in [load_hid, load_kv] + small:
        copy.start()

    pl.semaphore_wait(barrier, 9)

    base = c * (HALF_D // 2)

    def lanes(start, size):
        return pl.ds(pl.multiple_of(base + start, 128), size)

    def kv_link(slot, to_slot, at, dev):
        return link(kvt.at[slot, :, at], kvt.at[to_slot, :, at], dev)

    def first_link(to_slot, at, dev):
        return link(kv_down.at[:, at], kvt.at[to_slot, :, at], dev)

    def part_of(k, first=0, size=SHARE):
        return lanes(lax.rem(y + k, 4) * SHARE + first, size)

    low, high = lanes(4 * SHARE, DIRECT), lanes(4 * SHARE + DIRECT, DIRECT)
    mine = part_of(0)
    s_p, s_m = first_link(1, mine, dev_zp), first_link(2, mine, dev_zm)
    d_p0, d_m1 = first_link(1, low, dev_zp), first_link(2, high, dev_zm)
    d_p1, d_m0 = first_link(1, high, dev_zp), first_link(2, low, dev_zm)
    for copy in (s_p, s_m, d_p0, d_m1):
        go(copy)
    for copy in load_q + [load_cache]:
        copy.start()
    sf_p, sf_m = (
        kv_link(1, 3, part_of(0, 0, SHARE // 2), dev_zp),
        kv_link(2, 3, part_of(0, SHARE // 2, SHARE // 2), dev_zm),
    )
    df_p, df_m = kv_link(1, 3, low, dev_zp), kv_link(2, 3, high, dev_zm)
    near_p = [None] + [kv_link(slot, slot, mine, dev_yp) for slot in (1, 2, 3)]
    near_m = [None] + [kv_link(slot, slot, mine, dev_ym) for slot in (1, 2, 3)]
    far = [None] + [
        (
            kv_link(slot, slot, part_of(3, 0, SHARE // 2), dev_yp),
            kv_link(slot, slot, part_of(1, SHARE // 2, SHARE // 2), dev_ym),
        )
        for slot in (1, 2, 3)
    ]
    share_s = [None] + [kv_link(slot, slot, lanes(0, 4 * SHARE), dev_sib) for slot in (1, 2, 3)]
    share_d = [None] + [kv_link(slot, slot, lanes(4 * SHARE, 2 * DIRECT), dev_sib) for slot in (1, 2, 3)]

    origin = [lax.rem(b + ahead, 4) for ahead in (0, 3, 1, 2)]
    m_copies = [
        (link(mps.at[slot], mpr.at[slot], dev_mp), link(mss.at[slot], msr.at[slot], dev_mp)) for slot in range(3)
    ]
    tails = (slice(0, 256), slice(256, TOK))
    for at in tails:
        at = pl.ds(at.start, at.stop - at.start)
        m_copies.append((
            link(mps.at[3, :, at], mpr.at[3, :, at], dev_mp), link(mss.at[3, :, at], msr.at[3, :, at], dev_mp),
        ))

    def send_part(slot, part, copies, at=slice(None)):
        lat[origin[slot], :, at] = part
        coded, scale = code(part, 0)
        mps[slot, :, at] = to_code(coded)
        mss[slot, :, at] = scale
        go_pair(copies)

    def weigh(score, top):
        return jnp.exp2(score * log2_scale - top * log2_scale)

    def fold(w):
        total = w[:, :128]
        for j in range(1, w.shape[1] // 128):
            total = total + w[:, j * 128:j * 128 + 128]
        return total

    def peak(score):
        most = score[:, :128]
        for j in range(1, score.shape[1] // 128):
            most = jnp.maximum(most, score[:, j * 128:j * 128 + 128])
        return most

    def resident(pair, half):
        at = lax.broadcasted_iota(I32, (1, CTXD), 1) + s * CTXD
        scores = [
            jnp.where(at < lengths[half * NR + r], nn(qbuf[half * NR + r, :, :KVW], kbuf[half * NR + r]), masked_value)
            for r in pair
        ]
        weights = []
        for score in scores:
            top = jnp.maximum(jnp.max(peak(score), axis=1, keepdims=True), floor_value)
            w = weigh(score, top)
            top = jnp.transpose(jnp.broadcast_to(top, (QROWS, 128)))[0:1]
            weights.append((w.astype(BF16), top, jnp.sum(jnp.transpose(fold(w)), axis=0, keepdims=True)))
        return [
            (nt(kbuf[half * NR + r, :LATW, :], w), top, total) for r, (w, top, total) in zip(pair, weights)
        ]

    def columns(first, count=1):
        return slice(first * QROWS, (first + count) * QROWS)

    def resident_own(pair):
        for r, (value, top, total) in zip(pair, resident(pair, c)):
            acc[:, columns(r)], ms[:, columns(r)], ls[:, columns(r)] = value, top, total

    def add_other(r):
        at = columns(r)
        old, top2 = ms[:, at], efrom[r, 0]
        top = jnp.maximum(old, top2)
        keep, gain2 = jnp.exp2((old - top) * log2_scale), jnp.exp2((top2 - top) * log2_scale)
        acc[:, at] = acc[:, at] * keep + from_code(ebuf[r]) * (gain2 * efrom[r, 2])
        ls[:, at] = ls[:, at] * keep + gain2 * efrom[r, 1]
        ms[:, at] = top

    load_hid.wait()
    load_kv.wait()
    send_part(0, nt(kvt[0], hid[...]), m_copies[0])
    s_p.wait_recv()
    go(sf_p)
    go(near_p[1])
    go(near_m[1])
    s_m.wait_recv()
    go(sf_m)
    go(near_p[2])
    go(near_m[2])
    go(d_p1)
    go(d_m0)

    for copy in small:
        copy.wait()
    token = lax.broadcasted_iota(I32, (1, TOK), 1)
    token_page = lax.shift_right_logical(token, 4)
    dest = jnp.zeros((1, TOK), I32)
    asked = jnp.zeros((1, TOK), I32)
    counts = [jnp.int32(0)] * 4
    for page in range(PAGES):
        to = owner[0, page]
        rank = jnp.where(to == 0, counts[0], jnp.where(to == 1, counts[1], jnp.where(to == 2, counts[2], counts[3])))
        counts = [counts[o] + (to == o).astype(I32) for o in range(4)]
        dest = jnp.where(token_page == page, (to * CAP + rank) * PAGE, dest)
        asked = jnp.where(token_page == page, request[page] + 1, asked)
    dest = dest + lax.bitwise_and(token, 15)
    tok[...] = dest

    label_row = lax.broadcasted_iota(I32, (LABELS, TOK), 0)
    rows[KVW:, :] = (label_row == asked).astype(F32).astype(BF16)

    d_p0.wait_recv()
    go(df_p)
    d_m1.wait_recv()
    go(df_m)

    def pass_on(slot):
        near_p[slot].wait_recv()
        go(far[slot][0])
        near_m[slot].wait_recv()
        go(far[slot][1])

    def swap_shared(slot):
        far[slot][0].wait_recv()
        far[slot][1].wait_recv()
        go(share_s[slot])

    pass_on(1)
    sf_p.wait_recv()
    sf_m.wait_recv()
    go(near_p[3])
    go(near_m[3])

    for copy in load_q:
        copy.wait()
    load_cache.wait()
    label_at = lax.broadcasted_iota(I32, (QROWS, LABELS), 1)

    def fill(r, carry):
        qbuf[r, :, :KVW] = qraw[r].reshape(QROWS, KVW)
        qbuf[r, :, KVW:] = jnp.where(label_at == r + 1, 0.0, masked_value).astype(BF16)
        return carry

    def resident_other(pair):
        for r, (value, top, total) in zip(pair, resident(pair, 1 - c)):
            coded, scale = code(value, 0)
            esend[r] = to_code(coded)
            for k, row in enumerate((top, total, scale)):
                estat[r, k] = row
            go_pair(e_copies[r])

    e_copies = [
        (link(esend.at[r], ebuf.at[r], dev_sib), link(estat.at[r], efrom.at[r], dev_sib)) for r in range(NR)
    ]
    lax.fori_loop(0, 2 * NR, fill, 0)
    resident_other(PAIRS[0])

    pass_on(2)
    d_p1.wait_recv()
    go(share_d[1])
    d_m0.wait_recv()
    go(share_d[2])
    swap_shared(1)
    resident_other(PAIRS[1])

    pass_on(3)
    swap_shared(2)
    share_d[1].wait_recv()
    share_s[1].wait_recv()
    send_part(1, nt(kvt[1], hid[...]), m_copies[1])
    df_p.wait_recv()
    df_m.wait_recv()
    go(share_d[3])
    swap_shared(3)
    share_d[2].wait_recv()
    share_s[2].wait_recv()
    send_part(2, nt(kvt[2], hid[...]), m_copies[2])

    def over_lanes(starts, size, at):
        return sum(nt(kvt[3, :, start:start + size], hid[at, start:start + size]) for start in starts)

    share_d[3].wait_recv()
    lat[origin[3]] = over_lanes((4 * SHARE, HALF_D // 2 + 4 * SHARE), 2 * DIRECT, slice(None))
    share_s[3].wait_recv()
    for i, at in enumerate(tails):
        send_part(
            3, lat[origin[3], :, at] + over_lanes((0, HALF_D // 2), 4 * SHARE, at), m_copies[3 + i], at
        )
    for pair in PAIRS:
        resident_own(pair)

    for slot in range(4):
        for pair in m_copies[slot:] if slot == 3 else m_copies[slot:slot + 1]:
            wait_pair(pair)
        lat[origin[slot]] = lat[origin[slot]] + from_code(mpr[slot]) * msr[slot]
    whole = lat[...].reshape(KVW, TOK)
    latent = whole[:LATW]
    inverse = lax.rsqrt(jnp.sum(latent * latent, axis=0, keepdims=True) / LATW + eps_norm)
    gain_cols = jnp.transpose(jnp.broadcast_to(gain[...], (128, LATW)))
    for j in range(TOK // 128):
        at = slice(j * 128, j * 128 + 128)
        rows[:LATW, at] = (latent[:, at] * inverse[:, at] * gain_cols).astype(BF16)
    first, second = whole[LATW:LATW + ROPEW // 2], whole[LATW + ROPEW // 2:]
    rows[LATW:LATW + ROPEW // 2, :] = (first * cosine[...] - second * sine[...]).astype(BF16)
    rows[LATW + ROPEW // 2:KVW, :] = (first * sine[...] + second * cosine[...]).astype(BF16)

    slot_at = lax.broadcasted_iota(I32, (CAPTOK, TOK), 0)

    def pack_for(to):
        chosen = ((slot_at + to * CAPTOK) == tok[...]).astype(F32)
        empty = jnp.sum(chosen, axis=1, keepdims=True) < 0.5
        page_rows = nt(chosen.astype(BF16), rows[...])
        column = lax.broadcasted_iota(I32, (CAPTOK, KVX), 1)
        return jnp.where((column == KVW) & empty, 1.0, page_rows).astype(BF16)

    first, second = pl.ds(0, HALF), pl.ds(HALF, HALF)
    mine_at = pl.ds(p * HALF, HALF)
    here, there = 2 + 2 * p, 4 - 2 * p
    a_p = link(packed.at[0, mine_at], arr.at[here, c], dev_zp)
    a_m = link(packed.at[1, mine_at], arr.at[here + 1, c], dev_zm)
    a_x = [link(arr.at[here + i, c], arr.at[here + i, c], dev_mp) for i in range(2)]
    a_r0 = link(packed.at[2, first], relay.at[0], dev_zp)
    a_r1 = link(packed.at[2, second], relay.at[1], dev_zm)
    a_f0 = link(relay.at[0], arr.at[6, c], dev_zp)
    a_f1 = link(relay.at[1], arr.at[7, c], dev_zm)
    a_share = [
        link(arr.at[part, c], arr.at[part, c], dev_sib) for part in (0, 1, here, here + 1, there, there + 1, 6, 7)
    ]
    packed[0] = pack_for(lax.rem(b + 1, 4))
    go(a_p)
    packed[1] = pack_for(lax.rem(b + 3, 4))
    go(a_m)
    packed[2] = pack_for(lax.rem(b + 2, 4))
    go(a_r0)
    go(a_r1)
    own_pages = pack_for(b)
    arr[0, c] = own_pages[:HALF]
    go(a_share[0])
    arr[1, c] = own_pages[HALF:]
    go(a_share[1])

    def swap(copies, parts):
        for copy, part in zip(copies, parts):
            copy.wait_recv()
            go(a_share[part])

    def ready(parts):
        for part in parts:
            a_share[part].wait_recv()

    starts = (0, here, there, 6)

    def turn_values(group):
        size = 2 * CAPTOK
        values = arr[pl.ds(starts[group], 2)].reshape(size, KVX)[:, :LATW]
        vt[:, group * size:(group + 1) * size] = jnp.transpose(values)

    def pages_step(request, count, group, groups=1):
        size, at = 2 * CAPTOK, columns(request, count)
        q = qbuf[pl.ds(c * NR + request, count)].reshape(count * QROWS, KVX)
        score = jnp.concatenate([
            nt(arr[pl.ds(starts[g], 2)].reshape(size, KVX), q) for g in range(group, group + groups)
        ])
        old = ms[:, at]
        top = jnp.maximum(old, jnp.max(score, axis=0, keepdims=True))
        shrink = jnp.exp2((old - top) * log2_scale)
        w = weigh(score, top)
        total = ls[:, at] * shrink + jnp.sum(w, axis=0, keepdims=True)
        value = acc[:, at] * shrink + nn(vt[:, group * size:(group + groups) * size], w.astype(BF16))
        return value, top, total

    def pages_of(request, count, group):
        at = columns(request, count)
        acc[:, at], ms[:, at], ls[:, at] = pages_step(request, count, group)

    for pair in e_copies:
        wait_pair(pair)
    for r in range(NR):
        add_other(r)
    ready((0, 1))
    turn_values(0)
    pages_of(0, 2, 0)
    a_p.wait_recv()
    go(a_x[0])
    go(a_share[2])
    a_m.wait_recv()
    go(a_x[1])
    go(a_share[3])
    pages_of(2, 2, 0)
    a_r0.wait_recv()
    go(a_f0)
    a_r1.wait_recv()
    go(a_f1)
    ready((2, 3))
    turn_values(1)
    pages_of(0, 2, 1)
    swap(a_x, (4, 5))
    pages_of(2, 2, 1)
    swap((a_f0, a_f1), (6, 7))
    ready((4, 5))
    turn_values(2)
    pages_of(0, 2, 2)
    ready((6, 7))
    turn_values(3)

    def merge(parts):
        top = parts[0][1][0]
        for _, stat in parts[1:]:
            top = jnp.maximum(top, stat[0])
        value, total = 0.0, 0.0
        for coded, stat in parts:
            factor = jnp.exp2(stat[0] - top)
            value = value + from_code(coded) * factor
            total = total + factor * stat[1]
        return value, top, total

    def put(coded_ref, stat_ref, value, top, total):
        coded, scale = code(value, 0)
        coded_ref[...] = to_code(coded).reshape(coded_ref.shape)
        stat_ref[0] = top + jnp.log(scale) * log2_e
        stat_ref[1] = total / scale

    yp, ym, yy = lax.rem(y + 1, 4), lax.rem(y + 3, 4), lax.rem(y + 2, 4)
    first_y = used[0]

    def y_pair(r, k):
        pairs = (
            (osend.at[r, yy, 0], ostat.at[r], 0, dev_yp),
            (osend.at[r, yy, 1], ostat.at[r], 1, dev_ym),
            (osend.at[r, yp, 1], ostat.at[r], 2, dev_yp),
            (osend.at[r, ym, 0], ostat.at[r], 3, dev_ym),
            (rsend.at[r, 0], rstat.at[r, 0], 4, dev_yp),
            (rsend.at[r, 1], rstat.at[r, 1], 5, dev_ym),
        )
        data, stat, _, dev = pairs[k]
        return (
            link_at(first_y + 18 * r + 2 * k, data, ybuf.at[r, k], dev),
            link_at(first_y + 18 * r + 2 * k + 1, stat, ystat.at[r, k], dev),
        )

    def last_pair(r, k):
        half, core, dev = ((1 - xh, c, dev_x), (1 - xh, 1 - c, dev_x_sib), (xh, 1 - c, dev_sib))[k]
        return (
            link_at(first_y + 18 * r + 12 + 2 * k, mbuf.at[r, half, core], fbuf.at[r, k], dev),
            link_at(first_y + 18 * r + 13 + 2 * k, mstat.at[r, half], fstat.at[r, k], dev),
        )

    def start_pair(pair):
        pair[0].start()
        pair[1].start()

    def relay_sums(r, carry):
        for k, to in ((0, yp), (1, ym)):
            wait_pair(y_pair(r, k))
            put(rsend.at[r, k], rstat.at[r, k], *merge([
                (osend[r, to, k], ostat[r]), (ybuf[r, k], ystat[r, k]),
            ]))
            start_pair(y_pair(r, 4 + k))
        return carry

    for r in range(NR):
        value, top, total = pages_step(r, 1, 3) if r < 2 else pages_step(r, 1, 2, 2)
        coded, scale = code(value, 0)
        osend[r] = to_code(coded).reshape(4, 2, 64, QROWS)
        ostat[r, 0] = top * log2_scale + jnp.log(scale) * log2_e
        ostat[r, 1] = total / scale
        for k in range(4):
            start_pair(y_pair(r, k))
        if r == 2:
            lax.fori_loop(0, 2, relay_sums, 0)

    def sums_over_y(r, carry):
        for k in range(2, 6):
            wait_pair(y_pair(r, k))
        for h, (one, two) in enumerate(((3, 4), (2, 5))):
            put(mbuf.at[r, h], mstat.at[r, h], *merge([
                (osend[r, y, h], ostat[r]), (ybuf[r, one], ystat[r, one]), (ybuf[r, two], ystat[r, two]),
            ]))
        for k in (1, 0, 2):
            start_pair(last_pair(r, k))
        return carry

    def out_copy(wanted):
        return pltpu.make_async_copy(out.at[:, wanted], out_hbm.at[:, wanted], loc.at[13 + wanted])

    def last_sums(r, carry):
        for k in range(3):
            wait_pair(last_pair(r, k))
        own, other = c * NR + r, (1 - c) * NR + r
        for wanted, parts in (
            (own, [(mbuf[r, xh, c], mstat[r, xh]), (fbuf[r, 0], fstat[r, 0])]),
            (other, [(fbuf[r, 2], fstat[r, 2]), (fbuf[r, 1], fstat[r, 1])]),
        ):
            value, _, total = merge(parts)
            value = value / total
            for step in range(4):
                out[step, wanted] = value[:, 64 * step:64 * step + 64]
            out_copy(wanted).start()
        return carry

    def finish(r, carry):
        for pair in [y_pair(r, k) for k in range(6)] + [last_pair(r, k) for k in range(3)]:
            pair[0].wait_send()
            pair[1].wait_send()
        return carry

    lax.fori_loop(2, NR, relay_sums, 0)
    for stage in (sums_over_y, last_sums, finish):
        lax.fori_loop(0, NR, stage, 0)
    for wanted in range(2 * NR):
        out_copy(wanted).wait()
    for copy in started:
        copy.wait_send()


LINKS = 144


def tables():
    half = ROPEW // 2
    frequency = rope_base ** (-np.arange(half, dtype=np.float32) / np.float32(half))
    angles = np.arange(TOK, dtype=np.float32)[None, :] * frequency.astype(np.float32)[:, None]
    return np.cos(angles).astype(np.float32), np.sin(angles).astype(np.float32)


def on_device(hidden, kv_down, kv_gain, page_owner, page_request, queries, cache, lengths):
    cosine, sine = tables()
    anywhere = pl.BlockSpec(memory_space=pl.ANY)
    sums = pl.pallas_call(
        kernel,
        out_shape=jax.ShapeDtypeStruct((4, 2 * NR, 32, 64), F32),
        in_specs=[anywhere] * 10,
        out_specs=anywhere,
        scratch_shapes=[
            pltpu.VMEM((1, LATW), F32),
            pltpu.SMEM((1, PAGES), I32),
            pltpu.SMEM((PAGES,), I32),
            pltpu.SMEM((2 * NR,), I32),
            pltpu.VMEM((ROPEW // 2, TOK), F32),
            pltpu.VMEM((ROPEW // 2, TOK), F32),
            pltpu.VMEM((4, 2 * NR, 32, 64), F32),
            pltpu.VMEM((TOK, HALF_D), BF16),
            pltpu.VMEM((4, BLK, HALF_D), BF16),
            pltpu.VMEM((4, BLK, TOK), F32),
            pltpu.VMEM((4, BLK, TOK), I16),
            pltpu.VMEM((4, BLK, TOK), I16),
            pltpu.VMEM((4, 1, TOK), F32),
            pltpu.VMEM((4, 1, TOK), F32),
            pltpu.VMEM((KVX, TOK), BF16),
            pltpu.VMEM((3, CAPTOK, KVX), BF16),
            pltpu.VMEM((2, HALF, KVX), BF16),
            pltpu.VMEM((8, 2, HALF, KVX), BF16),
            pltpu.VMEM((1, TOK), I32),
            pltpu.VMEM((LATW, 8 * CAPTOK), BF16),
            pltpu.VMEM((2 * NR, 4, 64, KVW), BF16),
            pltpu.VMEM((2 * NR, QROWS, KVX), BF16),
            pltpu.VMEM((2 * NR, KVW, CTXD), BF16),
            pltpu.VMEM((NR, LATW, QROWS), I16),
            pltpu.VMEM((NR, 3, 1, QROWS), F32),
            pltpu.VMEM((NR, LATW, QROWS), I16),
            pltpu.VMEM((NR, 3, 1, QROWS), F32),
            pltpu.VMEM((LATW, NR * QROWS), F32),
            pltpu.VMEM((1, NR * QROWS), F32),
            pltpu.VMEM((1, NR * QROWS), F32),
            pltpu.VMEM((NR, 4, 2, 64, QROWS), I16),
            pltpu.VMEM((NR, 2, 1, QROWS), F32),
            pltpu.VMEM((NR, 6, 64, QROWS), I16),
            pltpu.VMEM((NR, 6, 2, 1, QROWS), F32),
            pltpu.VMEM((NR, 2, 64, QROWS), I16),
            pltpu.VMEM((NR, 2, 2, 1, QROWS), F32),
            pltpu.VMEM((NR, 2, 2, 32, QROWS), I16),
            pltpu.VMEM((NR, 2, 2, 1, QROWS), F32),
            pltpu.VMEM((NR, 3, 32, QROWS), I16),
            pltpu.VMEM((NR, 3, 2, 1, QROWS), F32),
            pltpu.SemaphoreType.DMA((13 + 2 * NR,)),
            pltpu.SemaphoreType.DMA((LINKS,)),
            pltpu.SemaphoreType.DMA((LINKS,)),
        ],
        compiler_params=pltpu.CompilerParams(
            collective_id=0, has_side_effects=True, vmem_limit_bytes=56 * 1024 * 1024
        ),
        cost_estimate=pl.CostEstimate(flops=7_500_000_000, bytes_accessed=12_000_000, transcendentals=3_000_000),
    )(
        hidden, kv_down.T, kv_gain.reshape(1, LATW), page_owner.T, page_request, queries, cache.transpose(0, 2, 1), lengths,
        jnp.asarray(cosine), jnp.asarray(sine),
    )
    return sums.transpose(0, 1, 3, 2)


def solution(mesh):
    return jax.shard_map(
        on_device,
        mesh=mesh,
        in_specs=(
            P(("seq", "batch"), "mp"),
            P("mp", "batch"),
            P(),
            P(("seq", "batch"), None),
            P(("seq", "batch")),
            P(None, "batch", "mp", None),
            P("batch", "seq", None),
            P("batch"),
        ),
        out_specs=P(None, "batch", "mp", "seq"),
        check_vma=False,
    )
```

```python
import jax
import jax.numpy as jnp
import numpy as np
from jax import lax
from jax.experimental import pallas as pl
from jax.experimental.pallas import tpu as pltpu
from jax.sharding import PartitionSpec as P

MESH = pl.DeviceIdType.MESH
F32, BF16, I32, I16 = jnp.float32, jnp.bfloat16, jnp.int32, jnp.int16

eps_norm = 1e-06
score_scale = 192.0 ** (-0.5)
log2_e = 1.4426950408889634
log2_scale = score_scale * log2_e
rope_base = 10000.0
masked_value = -1e30
floor_value = -1e29
code_top = 32767.0

TOK, HALF_D, KVW, LATW, ROPEW = 384, 3584, 576, 512, 64
USED = 16
LABELS = 64
KVX = KVW + LABELS
BLK = 144
SHARE, DIRECT = 256, 384
CAPTOK = 192
HALF = CAPTOK // 2
PAGES, PAGE, CAP = 24, 16, 12
QROWS = 256
CTXD = 512
NR = 4


def nt(a, b):
    return lax.dot_general(a, b, (((1,), (1,)), ((), ())), preferred_element_type=F32)


def nn(a, b):
    return jnp.dot(a, b, preferred_element_type=F32)


def kernel(
    hidden, kv_down, gain_in, owner_in, request_in, queries, cache, lengths_in, cosine_in, sine_in,
    out_hbm,
    gain, owner, request, lengths, cosine, sine, out,
    hid, kvt, lat, mps, mpr, mss, msr, rows, packed, relay, arr, tok,
    vt, qraw, qbuf, kbuf, acc, ms, ls, osend, ostat, ybuf, ystat, rsend, rstat, mbuf, mstat, fbuf, fstat,
    loc, send, recv,
):
    s, b, p = lax.axis_index("seq"), lax.axis_index("batch"), lax.axis_index("mp")
    c = lax.rem(s, 2)
    sib = s + 1 - 2 * c
    y = lax.div(s, 4)
    in_y = lax.rem(s, 4)
    xh = lax.rem(lax.div(s, 2), 2)
    dev_zp = (s, lax.rem(b + 1, 4), p)
    dev_zm = (s, lax.rem(b + 3, 4), p)
    dev_zz = (s, lax.rem(b + 2, 4), p)
    dev_mp = (s, b, 1 - p)
    dev_sib = (sib, b, p)
    dev_yp = (lax.rem(y + 1, 4) * 4 + in_y, b, p)
    dev_ym = (lax.rem(y + 3, 4) * 4 + in_y, b, p)
    dev_x = (s + 2 - 4 * xh, b, p)
    dev_x_sib = (sib + 2 - 4 * xh, b, p)

    used = [0]
    started = []

    def link(src, dst, dev):
        used[0] += 1
        return link_at(used[0] - 1, src, dst, dev)

    def link_at(i, src, dst, dev):
        return pltpu.make_async_remote_copy(
            src_ref=src, dst_ref=dst, send_sem=send.at[i], recv_sem=recv.at[i],
            device_id=dev, device_id_type=MESH,
        )

    def go(copy):
        copy.start()
        started.append(copy)

    def code(value, axis):
        most = jnp.max(jnp.abs(value), axis=axis, keepdims=True)
        most = jnp.maximum(most, 1e-25)
        return jnp.round(value * (code_top / most)), most * (1.0 / code_top)

    def to_code(value):
        return value.astype(I32).astype(I16)

    def from_code(coded):
        return coded.astype(I32).astype(F32)

    def go_pair(pair):
        go(pair[0])
        go(pair[1])

    def wait_pair(pair):
        pair[0].wait_recv()
        pair[1].wait_recv()

    barrier = pltpu.get_barrier_semaphore()
    for dev in (dev_zp, dev_zm, dev_zz, dev_mp, dev_sib, dev_yp, dev_ym, dev_x, dev_x_sib):
        pl.semaphore_signal(barrier, inc=1, device_id=dev, device_id_type=MESH)

    small = [
        pltpu.make_async_copy(src, dst, loc.at[7 + i])
        for i, (src, dst) in enumerate((
            (owner_in, owner), (request_in, request), (lengths_in, lengths), (gain_in, gain), (cosine_in, cosine),
            (sine_in, sine),
        ))
    ]
    load_kv = pltpu.make_async_copy(kv_down, kvt.at[0], loc.at[0])
    load_hid = pltpu.make_async_copy(hidden, hid, loc.at[1])
    load_q = [pltpu.make_async_copy(queries.at[step, pl.ds(c * NR, NR)], qraw.at[:, step], loc.at[2 + step]) for step in range(4)]
    load_cache = pltpu.make_async_copy(cache.at[pl.ds(c * NR, NR)], kbuf.at[0], loc.at[6])
    for copy in [load_hid, load_kv] + small:
        copy.start()

    pl.semaphore_wait(barrier, 9)

    base = c * (HALF_D // 2)

    def lanes(start, size):
        return pl.ds(pl.multiple_of(base + start, 128), size)

    def kv_link(slot, to_slot, at, dev):
        return link(kvt.at[slot, :, at], kvt.at[to_slot, :, at], dev)

    def first_link(to_slot, at, dev):
        return link(kv_down.at[:, at], kvt.at[to_slot, :, at], dev)

    def part_of(k, first=0, size=SHARE):
        return lanes(lax.rem(y + k, 4) * SHARE + first, size)

    low, high = lanes(4 * SHARE, DIRECT), lanes(4 * SHARE + DIRECT, DIRECT)
    mine = part_of(0)
    s_p, s_m = first_link(1, mine, dev_zp), first_link(2, mine, dev_zm)
    d_p0, d_m1 = first_link(1, low, dev_zp), first_link(2, high, dev_zm)
    d_p1, d_m0 = first_link(1, high, dev_zp), first_link(2, low, dev_zm)
    for copy in (s_p, s_m, d_p0, d_m1):
        go(copy)
    for copy in load_q + [load_cache]:
        copy.start()
    cache_out = link(cache.at[pl.ds((1 - c) * NR, NR)], kbuf.at[1], dev_sib)
    go(cache_out)
    sf_p, sf_m = (
        kv_link(1, 3, part_of(0, 0, SHARE // 2), dev_zp),
        kv_link(2, 3, part_of(0, SHARE // 2, SHARE // 2), dev_zm),
    )
    df_p, df_m = kv_link(1, 3, low, dev_zp), kv_link(2, 3, high, dev_zm)
    near_p = [None] + [kv_link(slot, slot, mine, dev_yp) for slot in (1, 2, 3)]
    near_m = [None] + [kv_link(slot, slot, mine, dev_ym) for slot in (1, 2, 3)]
    far = [None] + [
        (
            kv_link(slot, slot, part_of(3, 0, SHARE // 2), dev_yp),
            kv_link(slot, slot, part_of(1, SHARE // 2, SHARE // 2), dev_ym),
        )
        for slot in (1, 2, 3)
    ]
    share_s = [None] + [kv_link(slot, slot, lanes(0, 4 * SHARE), dev_sib) for slot in (1, 2, 3)]
    share_d = [None] + [kv_link(slot, slot, lanes(4 * SHARE, 2 * DIRECT), dev_sib) for slot in (1, 2, 3)]

    origin = [lax.rem(b + ahead, 4) for ahead in (0, 3, 1, 2)]
    m_copies = [
        (link(mps.at[slot], mpr.at[slot], dev_mp), link(mss.at[slot], msr.at[slot], dev_mp)) for slot in range(3)
    ]
    tails = (slice(0, 256), slice(256, TOK))
    for at in tails:
        at = pl.ds(at.start, at.stop - at.start)
        m_copies.append((
            link(mps.at[3, :, at], mpr.at[3, :, at], dev_mp), link(mss.at[3, :, at], msr.at[3, :, at], dev_mp),
        ))

    def send_part(slot, part, copies, at=slice(None)):
        lat[origin[slot], :, at] = part
        coded, scale = code(part, 0)
        mps[slot, :, at] = to_code(coded)
        mss[slot, :, at] = scale
        go_pair(copies)

    def weigh(score, top):
        return jnp.exp2(score * log2_scale - top * log2_scale)

    def fold(w):
        total = w[:, :128]
        for j in range(1, w.shape[1] // 128):
            total = total + w[:, j * 128:j * 128 + 128]
        return total

    def peak(score):
        most = score[:, :128]
        for j in range(1, score.shape[1] // 128):
            most = jnp.maximum(most, score[:, j * 128:j * 128 + 128])
        return most

    def columns(first, count=1):
        return slice(first * QROWS, (first + count) * QROWS)

    def resident(requests):
        at = lax.broadcasted_iota(I32, (1, CTXD), 1)
        scores = [
            [
                jnp.where(at + place * CTXD < lengths[c * NR + r], nn(qbuf[r, :, :KVW], kbuf[part, r]), masked_value)
                for part, place in enumerate((s, sib))
            ]
            for r in requests
        ]
        weights = []
        for r, (score0, score1) in zip(requests, scores):
            top = jnp.max(jnp.maximum(peak(score0), peak(score1)), axis=1, keepdims=True)
            top = jnp.maximum(top, floor_value)
            w0, w1 = weigh(score0, top), weigh(score1, top)
            ms[:, columns(r)] = jnp.transpose(jnp.broadcast_to(top, (QROWS, 128)))[0:1]
            ls[:, columns(r)] = jnp.sum(jnp.transpose(fold(w0) + fold(w1)), axis=0, keepdims=True)
            weights.append((w0.astype(BF16), w1.astype(BF16)))
        for r, (w0, w1) in zip(requests, weights):
            acc[:, columns(r)] = nt(kbuf[0, r, :LATW, :], w0) + nt(kbuf[1, r, :LATW, :], w1)

    load_hid.wait()
    load_kv.wait()
    send_part(0, nt(kvt[0], hid[...]), m_copies[0])
    s_p.wait_recv()
    go(sf_p)
    go(near_p[1])
    go(near_m[1])
    s_m.wait_recv()
    go(sf_m)
    go(near_p[2])
    go(near_m[2])
    go(d_p1)
    go(d_m0)

    for copy in small:
        copy.wait()
    token = lax.broadcasted_iota(I32, (1, TOK), 1)
    token_page = lax.shift_right_logical(token, 4)
    dest = jnp.zeros((1, TOK), I32)
    asked = jnp.zeros((1, TOK), I32)
    counts = [jnp.int32(0)] * 4
    for page in range(PAGES):
        to = owner[0, page]
        rank = jnp.where(to == 0, counts[0], jnp.where(to == 1, counts[1], jnp.where(to == 2, counts[2], counts[3])))
        counts = [counts[o] + (to == o).astype(I32) for o in range(4)]
        dest = jnp.where(token_page == page, (to * CAP + rank) * PAGE, dest)
        asked = jnp.where(token_page == page, request[page] + 1, asked)
    dest = dest + lax.bitwise_and(token, 15)
    tok[...] = dest

    label_row = lax.broadcasted_iota(I32, (LABELS, TOK), 0)
    rows[KVW:, :] = ((label_row == asked) | (label_row == USED)).astype(F32).astype(BF16)

    d_p0.wait_recv()
    go(df_p)
    d_m1.wait_recv()
    go(df_m)

    def pass_on(slot):
        near_p[slot].wait_recv()
        go(far[slot][0])
        near_m[slot].wait_recv()
        go(far[slot][1])

    def swap_shared(slot):
        far[slot][0].wait_recv()
        far[slot][1].wait_recv()
        go(share_s[slot])

    pass_on(1)
    sf_p.wait_recv()
    sf_m.wait_recv()
    go(near_p[3])
    go(near_m[3])

    for copy in load_q:
        copy.wait()
    load_cache.wait()
    label_at = lax.broadcasted_iota(I32, (QROWS, LABELS), 1)

    def fill(r, carry):
        qbuf[r, :, :KVW] = qraw[r].reshape(QROWS, KVW)
        opened = (label_at == c * NR + r + 1) | (label_at == USED)
        qbuf[r, :, KVW:] = jnp.where(opened, 0.0, masked_value).astype(BF16)
        return carry

    lax.fori_loop(0, NR, fill, 0)
    cache_out.wait_recv()
    resident((0,))

    pass_on(2)
    d_p1.wait_recv()
    go(share_d[1])
    d_m0.wait_recv()
    go(share_d[2])
    swap_shared(1)
    resident((1,))

    pass_on(3)
    swap_shared(2)
    share_d[1].wait_recv()
    share_s[1].wait_recv()
    send_part(1, nt(kvt[1], hid[...]), m_copies[1])
    df_p.wait_recv()
    df_m.wait_recv()
    go(share_d[3])
    swap_shared(3)
    share_d[2].wait_recv()
    share_s[2].wait_recv()
    send_part(2, nt(kvt[2], hid[...]), m_copies[2])

    def over_lanes(starts, size, at):
        return sum(nt(kvt[3, :, start:start + size], hid[at, start:start + size]) for start in starts)

    share_d[3].wait_recv()
    lat[origin[3]] = over_lanes((4 * SHARE, HALF_D // 2 + 4 * SHARE), 2 * DIRECT, slice(None))
    share_s[3].wait_recv()
    for i, at in enumerate(tails):
        send_part(
            3, lat[origin[3], :, at] + over_lanes((0, HALF_D // 2), 4 * SHARE, at), m_copies[3 + i], at
        )
    resident((2, 3))

    for slot in range(4):
        for pair in m_copies[slot:] if slot == 3 else m_copies[slot:slot + 1]:
            wait_pair(pair)
        lat[origin[slot]] = lat[origin[slot]] + from_code(mpr[slot]) * msr[slot]
    whole = lat[...].reshape(KVW, TOK)
    latent = whole[:LATW]
    inverse = lax.rsqrt(jnp.sum(latent * latent, axis=0, keepdims=True) / LATW + eps_norm)
    gain_cols = jnp.transpose(jnp.broadcast_to(gain[...], (128, LATW)))
    for j in range(TOK // 128):
        at = slice(j * 128, j * 128 + 128)
        rows[:LATW, at] = (latent[:, at] * inverse[:, at] * gain_cols).astype(BF16)
    first, second = whole[LATW:LATW + ROPEW // 2], whole[LATW + ROPEW // 2:]
    rows[LATW:LATW + ROPEW // 2, :] = (first * cosine[...] - second * sine[...]).astype(BF16)
    rows[LATW + ROPEW // 2:KVW, :] = (first * sine[...] + second * cosine[...]).astype(BF16)

    slot_at = lax.broadcasted_iota(I32, (CAPTOK, TOK), 0)

    def pack_for(to):
        chosen = ((slot_at + to * CAPTOK) == tok[...]).astype(F32).astype(BF16)
        page_rows = nt(chosen, rows[...])
        empty = page_rows[:, KVW + USED:KVW + USED + 1] < 0.5
        column = lax.broadcasted_iota(I32, (CAPTOK, KVX), 1)
        return jnp.where((column == KVW) & empty, 1.0, page_rows).astype(BF16)

    first, second = pl.ds(0, HALF), pl.ds(HALF, HALF)
    a_p = [link(packed.at[0, at], arr.at[part, c], dev_zp) for at, part in ((first, 2), (second, 4))]
    a_m = [link(packed.at[1, at], arr.at[part, c], dev_zm) for at, part in ((first, 3), (second, 5))]
    a_r0 = link(packed.at[2, first], relay.at[0], dev_zp)
    a_r1 = link(packed.at[2, second], relay.at[1], dev_zm)
    a_f0 = link(relay.at[0], arr.at[6, c], dev_zp)
    a_f1 = link(relay.at[1], arr.at[7, c], dev_zm)
    a_share = [link(arr.at[part, c], arr.at[part, c], dev_sib) for part in range(8)]
    packed[0] = pack_for(lax.rem(b + 1, 4))
    go(a_p[0])
    packed[1] = pack_for(lax.rem(b + 3, 4))
    go(a_m[0])
    packed[2] = pack_for(lax.rem(b + 2, 4))
    go(a_r0)
    go(a_r1)
    go(a_p[1])
    go(a_m[1])
    own_pages = pack_for(b)
    arr[0, c] = own_pages[:HALF]
    go(a_share[0])
    arr[1, c] = own_pages[HALF:]
    go(a_share[1])

    def swap(copies, parts):
        for copy, part in zip(copies, parts):
            copy.wait_recv()
            go(a_share[part])

    def ready(parts):
        for part in parts:
            a_share[part].wait_recv()

    def turn_values(first, last):
        size = (last + 1 - first) * CAPTOK
        values = arr[first:last + 1].reshape(size, KVX)[:, :LATW]
        vt[:, first * CAPTOK:first * CAPTOK + size] = jnp.transpose(values)

    def pages_step(request, count, first, last):
        size, at = (last + 1 - first) * CAPTOK, columns(request, count)
        keys = arr[first:last + 1].reshape(size, KVX)
        score = nt(keys, qbuf[request:request + count].reshape(count * QROWS, KVX))
        old = ms[:, at]
        top = jnp.maximum(old, jnp.max(score, axis=0, keepdims=True))
        shrink = jnp.exp2((old - top) * log2_scale)
        w = weigh(score, top)
        total = ls[:, at] * shrink + jnp.sum(w, axis=0, keepdims=True)
        value = acc[:, at] * shrink + nn(vt[:, first * CAPTOK:first * CAPTOK + size], w.astype(BF16))
        return value, top, total

    def pages_of(request, count, first, last):
        at = columns(request, count)
        acc[:, at], ms[:, at], ls[:, at] = pages_step(request, count, first, last)

    ready((0, 1))
    turn_values(0, 1)
    pages_of(0, 4, 0, 1)
    swap((a_p[0], a_m[0]), (2, 3))
    a_r0.wait_recv()
    go(a_f0)
    a_r1.wait_recv()
    go(a_f1)
    ready((2, 3))
    turn_values(2, 3)
    pages_of(0, 4, 2, 3)
    swap((a_p[1], a_m[1]), (4, 5))
    ready((4, 5))
    turn_values(4, 5)
    swap((a_f0, a_f1), (6, 7))
    pages_of(0, 2, 4, 5)
    ready((6, 7))
    turn_values(6, 7)

    def merge(parts):
        top = parts[0][1][0]
        for _, stat in parts[1:]:
            top = jnp.maximum(top, stat[0])
        value, total = 0.0, 0.0
        for coded, stat in parts:
            factor = jnp.exp2(stat[0] - top)
            value = value + from_code(coded) * factor
            total = total + factor * stat[1]
        return value, top, total

    def put(coded_ref, stat_ref, value, top, total):
        coded, scale = code(value, 0)
        coded_ref[...] = to_code(coded).reshape(coded_ref.shape)
        stat_ref[0] = top + jnp.log(scale) * log2_e
        stat_ref[1] = total / scale

    yp, ym, yy = lax.rem(y + 1, 4), lax.rem(y + 3, 4), lax.rem(y + 2, 4)
    first_y = used[0]

    def y_pair(r, k):
        pairs = (
            (osend.at[r, yy, 0], ostat.at[r], 0, dev_yp),
            (osend.at[r, yy, 1], ostat.at[r], 1, dev_ym),
            (osend.at[r, yp, 1], ostat.at[r], 2, dev_yp),
            (osend.at[r, ym, 0], ostat.at[r], 3, dev_ym),
            (rsend.at[r, 0], rstat.at[r, 0], 4, dev_yp),
            (rsend.at[r, 1], rstat.at[r, 1], 5, dev_ym),
        )
        data, stat, _, dev = pairs[k]
        return (
            link_at(first_y + 18 * r + 2 * k, data, ybuf.at[r, k], dev),
            link_at(first_y + 18 * r + 2 * k + 1, stat, ystat.at[r, k], dev),
        )

    def last_pair(r, k):
        half, core, dev = ((1 - xh, c, dev_x), (1 - xh, 1 - c, dev_x_sib), (xh, 1 - c, dev_sib))[k]
        return (
            link_at(first_y + 18 * r + 12 + 2 * k, mbuf.at[r, half, core], fbuf.at[r, k], dev),
            link_at(first_y + 18 * r + 13 + 2 * k, mstat.at[r, half], fstat.at[r, k], dev),
        )

    def start_pair(pair):
        pair[0].start()
        pair[1].start()

    def relay_sums(r, carry):
        for k, to in ((0, yp), (1, ym)):
            wait_pair(y_pair(r, k))
            put(rsend.at[r, k], rstat.at[r, k], *merge([
                (osend[r, to, k], ostat[r]), (ybuf[r, k], ystat[r, k]),
            ]))
            start_pair(y_pair(r, 4 + k))
        return carry

    for first_request, count, first in ((0, 1, 6), (1, 1, 6), (2, 2, 4)):
        value, top, total = pages_step(first_request, count, first, 7)
        coded, scale = code(value, 0)
        coded, top, total = to_code(coded), top * log2_scale + jnp.log(scale) * log2_e, total / scale
        for r in range(first_request, first_request + count):
            at = columns(r - first_request)
            osend[r] = coded[:, at].reshape(4, 2, 64, QROWS)
            ostat[r, 0] = top[:, at]
            ostat[r, 1] = total[:, at]
            for k in range(4):
                start_pair(y_pair(r, k))

    def sums_over_y(r, carry):
        for k in range(2, 6):
            wait_pair(y_pair(r, k))
        for h, (one, two) in enumerate(((3, 4), (2, 5))):
            put(mbuf.at[r, h], mstat.at[r, h], *merge([
                (osend[r, y, h], ostat[r]), (ybuf[r, one], ystat[r, one]), (ybuf[r, two], ystat[r, two]),
            ]))
        for k in (1, 0, 2):
            start_pair(last_pair(r, k))
        return carry

    def out_copy(wanted):
        return pltpu.make_async_copy(out.at[:, wanted], out_hbm.at[:, wanted], loc.at[13 + wanted])

    def last_sums(r, carry):
        for k in range(3):
            wait_pair(last_pair(r, k))
        own, other = c * NR + r, (1 - c) * NR + r
        for wanted, parts in (
            (own, [(mbuf[r, xh, c], mstat[r, xh]), (fbuf[r, 0], fstat[r, 0])]),
            (other, [(fbuf[r, 2], fstat[r, 2]), (fbuf[r, 1], fstat[r, 1])]),
        ):
            value, _, total = merge(parts)
            value = value / total
            for step in range(4):
                out[step, wanted] = value[:, 64 * step:64 * step + 64]
            out_copy(wanted).start()
        return carry

    def finish(r, carry):
        for pair in [y_pair(r, k) for k in range(6)] + [last_pair(r, k) for k in range(3)]:
            pair[0].wait_send()
            pair[1].wait_send()
        return carry

    lax.fori_loop(0, NR, relay_sums, 0)
    for stage in (sums_over_y, last_sums, finish):
        lax.fori_loop(0, NR, stage, 0)
    for wanted in range(2 * NR):
        out_copy(wanted).wait()
    for copy in started:
        copy.wait_send()


LINKS = 144


def tables():
    half = ROPEW // 2
    frequency = rope_base ** (-np.arange(half, dtype=np.float32) / np.float32(half))
    angles = np.arange(TOK, dtype=np.float32)[None, :] * frequency.astype(np.float32)[:, None]
    return np.cos(angles).astype(np.float32), np.sin(angles).astype(np.float32)


def on_device(hidden, kv_down, kv_gain, page_owner, page_request, queries, cache, lengths):
    cosine, sine = tables()
    anywhere = pl.BlockSpec(memory_space=pl.ANY)
    sums = pl.pallas_call(
        kernel,
        out_shape=jax.ShapeDtypeStruct((4, 2 * NR, 32, 64), F32),
        in_specs=[anywhere] * 10,
        out_specs=anywhere,
        scratch_shapes=[
            pltpu.VMEM((1, LATW), F32),
            pltpu.SMEM((1, PAGES), I32),
            pltpu.SMEM((PAGES,), I32),
            pltpu.SMEM((2 * NR,), I32),
            pltpu.VMEM((ROPEW // 2, TOK), F32),
            pltpu.VMEM((ROPEW // 2, TOK), F32),
            pltpu.VMEM((4, 2 * NR, 32, 64), F32),
            pltpu.VMEM((TOK, HALF_D), BF16),
            pltpu.VMEM((4, BLK, HALF_D), BF16),
            pltpu.VMEM((4, BLK, TOK), F32),
            pltpu.VMEM((4, BLK, TOK), I16),
            pltpu.VMEM((4, BLK, TOK), I16),
            pltpu.VMEM((4, 1, TOK), F32),
            pltpu.VMEM((4, 1, TOK), F32),
            pltpu.VMEM((KVX, TOK), BF16),
            pltpu.VMEM((3, CAPTOK, KVX), BF16),
            pltpu.VMEM((2, HALF, KVX), BF16),
            pltpu.VMEM((8, 2, HALF, KVX), BF16),
            pltpu.VMEM((1, TOK), I32),
            pltpu.VMEM((LATW, 8 * CAPTOK), BF16),
            pltpu.VMEM((NR, 4, 64, KVW), BF16),
            pltpu.VMEM((NR, QROWS, KVX), BF16),
            pltpu.VMEM((2, NR, KVW, CTXD), BF16),
            pltpu.VMEM((LATW, NR * QROWS), F32),
            pltpu.VMEM((1, NR * QROWS), F32),
            pltpu.VMEM((1, NR * QROWS), F32),
            pltpu.VMEM((NR, 4, 2, 64, QROWS), I16),
            pltpu.VMEM((NR, 2, 1, QROWS), F32),
            pltpu.VMEM((NR, 6, 64, QROWS), I16),
            pltpu.VMEM((NR, 6, 2, 1, QROWS), F32),
            pltpu.VMEM((NR, 2, 64, QROWS), I16),
            pltpu.VMEM((NR, 2, 2, 1, QROWS), F32),
            pltpu.VMEM((NR, 2, 2, 32, QROWS), I16),
            pltpu.VMEM((NR, 2, 2, 1, QROWS), F32),
            pltpu.VMEM((NR, 3, 32, QROWS), I16),
            pltpu.VMEM((NR, 3, 2, 1, QROWS), F32),
            pltpu.SemaphoreType.DMA((13 + 2 * NR,)),
            pltpu.SemaphoreType.DMA((LINKS,)),
            pltpu.SemaphoreType.DMA((LINKS,)),
        ],
        compiler_params=pltpu.CompilerParams(
            collective_id=0, has_side_effects=True, vmem_limit_bytes=56 * 1024 * 1024
        ),
        cost_estimate=pl.CostEstimate(flops=7_500_000_000, bytes_accessed=12_000_000, transcendentals=3_000_000),
    )(
        hidden, kv_down.T, kv_gain.reshape(1, LATW), page_owner.T, page_request, queries, cache.transpose(0, 2, 1), lengths,
        jnp.asarray(cosine), jnp.asarray(sine),
    )
    return sums.transpose(0, 1, 3, 2)


def solution(mesh):
    return jax.shard_map(
        on_device,
        mesh=mesh,
        in_specs=(
            P(("seq", "batch"), "mp"),
            P("mp", "batch"),
            P(),
            P(("seq", "batch"), None),
            P(("seq", "batch")),
            P(None, "batch", "mp", None),
            P("batch", "seq", None),
            P("batch"),
        ),
        out_specs=P(None, "batch", "mp", "seq"),
        check_vma=False,
    )
```

```python
import jax
import jax.numpy as jnp
import numpy as np
from jax import lax
from jax.experimental import pallas as pl
from jax.experimental.pallas import tpu as pltpu
from jax.sharding import PartitionSpec as P

MESH = pl.DeviceIdType.MESH
F32, BF16, I32, I16 = jnp.float32, jnp.bfloat16, jnp.int32, jnp.int16

eps_norm = 1e-06
score_scale = 192.0 ** (-0.5)
log2_e = 1.4426950408889634
log2_scale = score_scale * log2_e
rope_base = 10000.0
masked_value = -1e30
floor_value = -1e29
code_top = 32767.0

TOK, HALF_D, KVW, LATW, ROPEW = 384, 3584, 576, 512, 64
USED = 16
LABELS = 64
KVX = KVW + LABELS
BLK = 144
SHARE, DIRECT = 256, 384
CAPTOK = 192
HALF = CAPTOK // 2
PAGES, PAGE, CAP = 24, 16, 12
QROWS = 256
CTXD = 512
NR = 4


def nt(a, b):
    return lax.dot_general(a, b, (((1,), (1,)), ((), ())), preferred_element_type=F32)


def nn(a, b):
    return jnp.dot(a, b, preferred_element_type=F32)


def kernel(
    hidden, kv_down, gain_in, owner_in, request_in, queries, cache, lengths_in, cosine_in, sine_in,
    out_hbm,
    gain, owner, request, lengths, cosine, sine, out,
    hid, kvt, lat, mps, mpr, mss, msr, rows, packed, relay, arr, tok,
    vt, qraw, qbuf, kbuf, acc, ms, ls, osend, ostat, yfirst, yfstat, rsend, rstat, yrelay, yrstat, mbuf, mstat, fbuf, fstat,
    loc, send, recv,
):
    s, b, p = lax.axis_index("seq"), lax.axis_index("batch"), lax.axis_index("mp")
    c = lax.rem(s, 2)
    sib = s + 1 - 2 * c
    y = lax.div(s, 4)
    in_y = lax.rem(s, 4)
    xh = lax.rem(lax.div(s, 2), 2)
    dev_zp = (s, lax.rem(b + 1, 4), p)
    dev_zm = (s, lax.rem(b + 3, 4), p)
    dev_zz = (s, lax.rem(b + 2, 4), p)
    dev_mp = (s, b, 1 - p)
    dev_sib = (sib, b, p)
    dev_yp = (lax.rem(y + 1, 4) * 4 + in_y, b, p)
    dev_ym = (lax.rem(y + 3, 4) * 4 + in_y, b, p)
    dev_x = (s + 2 - 4 * xh, b, p)
    dev_x_sib = (sib + 2 - 4 * xh, b, p)

    used = [0]
    started = []

    def link(src, dst, dev):
        used[0] += 1
        return link_at(used[0] - 1, src, dst, dev)

    def link_at(i, src, dst, dev):
        return pltpu.make_async_remote_copy(
            src_ref=src, dst_ref=dst, send_sem=send.at[i], recv_sem=recv.at[i],
            device_id=dev, device_id_type=MESH,
        )

    def go(copy):
        copy.start()
        started.append(copy)

    def code(value, axis):
        most = jnp.max(jnp.abs(value), axis=axis, keepdims=True)
        most = jnp.maximum(most, 1e-25)
        return jnp.round(value * (code_top / most)), most * (1.0 / code_top)

    def to_code(value):
        return value.astype(I32).astype(I16)

    def from_code(coded):
        return coded.astype(I32).astype(F32)

    def go_pair(pair):
        go(pair[0])
        go(pair[1])

    def wait_pair(pair):
        pair[0].wait_recv()
        pair[1].wait_recv()

    barrier = pltpu.get_barrier_semaphore()
    for dev in (dev_zp, dev_zm, dev_zz, dev_mp, dev_sib, dev_yp, dev_ym, dev_x, dev_x_sib):
        pl.semaphore_signal(barrier, inc=1, device_id=dev, device_id_type=MESH)

    small = [
        pltpu.make_async_copy(src, dst, loc.at[7 + i])
        for i, (src, dst) in enumerate((
            (owner_in, owner), (request_in, request), (lengths_in, lengths), (gain_in, gain), (cosine_in, cosine),
            (sine_in, sine),
        ))
    ]
    load_kv = pltpu.make_async_copy(kv_down, kvt.at[0], loc.at[0])
    load_hid = pltpu.make_async_copy(hidden, hid, loc.at[1])
    load_q = [pltpu.make_async_copy(queries.at[step, pl.ds(c * NR, NR)], qraw.at[:, step], loc.at[2 + step]) for step in range(4)]
    load_cache = pltpu.make_async_copy(cache.at[pl.ds(c * NR, NR)], kbuf.at[0], loc.at[6])
    for copy in [load_hid, load_kv] + small:
        copy.start()

    pl.semaphore_wait(barrier, 9)

    base = c * (HALF_D // 2)

    def lanes(start, size):
        return pl.ds(pl.multiple_of(base + start, 128), size)

    def kv_link(slot, to_slot, at, dev):
        return link(kvt.at[slot, :, at], kvt.at[to_slot, :, at], dev)

    def first_link(to_slot, at, dev):
        return link(kv_down.at[:, at], kvt.at[to_slot, :, at], dev)

    def part_of(k, first=0, size=SHARE):
        return lanes(lax.rem(y + k, 4) * SHARE + first, size)

    low, high = lanes(4 * SHARE, DIRECT), lanes(4 * SHARE + DIRECT, DIRECT)
    mine = part_of(0)
    s_p, s_m = first_link(1, mine, dev_zp), first_link(2, mine, dev_zm)
    d_p0, d_m1 = first_link(1, low, dev_zp), first_link(2, high, dev_zm)
    d_p1, d_m0 = first_link(1, high, dev_zp), first_link(2, low, dev_zm)
    for copy in (s_p, s_m, d_p0, d_m1):
        go(copy)
    for copy in load_q + [load_cache]:
        copy.start()
    cache_out = link(cache.at[pl.ds((1 - c) * NR, NR)], kbuf.at[1], dev_sib)
    go(cache_out)
    sf_p, sf_m = (
        kv_link(1, 3, part_of(0, 0, SHARE // 2), dev_zp),
        kv_link(2, 3, part_of(0, SHARE // 2, SHARE // 2), dev_zm),
    )
    df_p, df_m = kv_link(1, 3, low, dev_zp), kv_link(2, 3, high, dev_zm)
    near_p = [None] + [kv_link(slot, slot, mine, dev_yp) for slot in (1, 2, 3)]
    near_m = [None] + [kv_link(slot, slot, mine, dev_ym) for slot in (1, 2, 3)]
    far = [None] + [
        (
            kv_link(slot, slot, part_of(3, 0, SHARE // 2), dev_yp),
            kv_link(slot, slot, part_of(1, SHARE // 2, SHARE // 2), dev_ym),
        )
        for slot in (1, 2, 3)
    ]
    share_s = [None] + [kv_link(slot, slot, lanes(0, 4 * SHARE), dev_sib) for slot in (1, 2, 3)]
    share_d = [None] + [kv_link(slot, slot, lanes(4 * SHARE, 2 * DIRECT), dev_sib) for slot in (1, 2, 3)]

    origin = [lax.rem(b + ahead, 4) for ahead in (0, 3, 1, 2)]
    m_copies = [
        (link(mps.at[slot], mpr.at[slot], dev_mp), link(mss.at[slot], msr.at[slot], dev_mp)) for slot in range(3)
    ]
    tails = (slice(0, 256), slice(256, TOK))
    for at in tails:
        at = pl.ds(at.start, at.stop - at.start)
        m_copies.append((
            link(mps.at[3, :, at], mpr.at[3, :, at], dev_mp), link(mss.at[3, :, at], msr.at[3, :, at], dev_mp),
        ))

    def send_part(slot, part, copies, at=slice(None)):
        lat[origin[slot], :, at] = part
        coded, scale = code(part, 0)
        mps[slot, :, at] = to_code(coded)
        mss[slot, :, at] = scale
        go_pair(copies)

    def weigh(score, top):
        return jnp.exp2(score * log2_scale - top * log2_scale)

    def fold(w):
        total = w[:, :128]
        for j in range(1, w.shape[1] // 128):
            total = total + w[:, j * 128:j * 128 + 128]
        return total

    def peak(score):
        most = score[:, :128]
        for j in range(1, score.shape[1] // 128):
            most = jnp.maximum(most, score[:, j * 128:j * 128 + 128])
        return most

    def columns(first, count=1):
        return slice(first * QROWS, (first + count) * QROWS)

    def resident(requests):
        at = lax.broadcasted_iota(I32, (1, CTXD), 1)
        scores = [
            [
                jnp.where(at + place * CTXD < lengths[c * NR + r], nn(qbuf[r, :, :KVW], kbuf[part, r]), masked_value)
                for part, place in enumerate((s, sib))
            ]
            for r in requests
        ]
        weights = []
        for r, (score0, score1) in zip(requests, scores):
            top = jnp.max(jnp.maximum(peak(score0), peak(score1)), axis=1, keepdims=True)
            top = jnp.maximum(top, floor_value)
            w0, w1 = weigh(score0, top), weigh(score1, top)
            ms[:, columns(r)] = jnp.transpose(jnp.broadcast_to(top, (QROWS, 128)))[0:1]
            ls[:, columns(r)] = jnp.sum(jnp.transpose(fold(w0) + fold(w1)), axis=0, keepdims=True)
            weights.append((w0.astype(BF16), w1.astype(BF16)))
        for r, (w0, w1) in zip(requests, weights):
            acc[:, columns(r)] = nt(kbuf[0, r, :LATW, :], w0) + nt(kbuf[1, r, :LATW, :], w1)

    load_hid.wait()
    load_kv.wait()
    send_part(0, nt(kvt[0], hid[...]), m_copies[0])
    s_p.wait_recv()
    go(sf_p)
    go(near_p[1])
    go(near_m[1])
    s_m.wait_recv()
    go(sf_m)
    go(near_p[2])
    go(near_m[2])
    go(d_p1)
    go(d_m0)

    for copy in small:
        copy.wait()
    token = lax.broadcasted_iota(I32, (1, TOK), 1)
    token_page = lax.shift_right_logical(token, 4)
    dest = jnp.zeros((1, TOK), I32)
    asked = jnp.zeros((1, TOK), I32)
    counts = [jnp.int32(0)] * 4
    for page in range(PAGES):
        to = owner[0, page]
        rank = jnp.where(to == 0, counts[0], jnp.where(to == 1, counts[1], jnp.where(to == 2, counts[2], counts[3])))
        counts = [counts[o] + (to == o).astype(I32) for o in range(4)]
        dest = jnp.where(token_page == page, (to * CAP + rank) * PAGE, dest)
        asked = jnp.where(token_page == page, request[page] + 1, asked)
    dest = dest + lax.bitwise_and(token, 15)
    tok[...] = dest

    label_row = lax.broadcasted_iota(I32, (LABELS, TOK), 0)
    rows[KVW:, :] = ((label_row == asked) | (label_row == USED)).astype(F32).astype(BF16)

    d_p0.wait_recv()
    go(df_p)
    d_m1.wait_recv()
    go(df_m)

    def pass_on(slot):
        near_p[slot].wait_recv()
        go(far[slot][0])
        near_m[slot].wait_recv()
        go(far[slot][1])

    def swap_shared(slot):
        far[slot][0].wait_recv()
        far[slot][1].wait_recv()
        go(share_s[slot])

    pass_on(1)
    sf_p.wait_recv()
    sf_m.wait_recv()
    go(near_p[3])
    go(near_m[3])

    for copy in load_q:
        copy.wait()
    load_cache.wait()
    label_at = lax.broadcasted_iota(I32, (QROWS, LABELS), 1)

    def fill(r, carry):
        qbuf[r, :, :KVW] = qraw[r].reshape(QROWS, KVW)
        opened = (label_at == c * NR + r + 1) | (label_at == USED)
        qbuf[r, :, KVW:] = jnp.where(opened, 0.0, masked_value).astype(BF16)
        return carry

    lax.fori_loop(0, NR, fill, 0)
    cache_out.wait_recv()
    resident((0,))

    pass_on(2)
    d_p1.wait_recv()
    go(share_d[1])
    d_m0.wait_recv()
    go(share_d[2])
    swap_shared(1)
    resident((1,))

    pass_on(3)
    swap_shared(2)
    share_d[1].wait_recv()
    share_s[1].wait_recv()
    send_part(1, nt(kvt[1], hid[...]), m_copies[1])
    df_p.wait_recv()
    df_m.wait_recv()
    go(share_d[3])
    swap_shared(3)
    share_d[2].wait_recv()
    share_s[2].wait_recv()
    send_part(2, nt(kvt[2], hid[...]), m_copies[2])

    def over_lanes(starts, size, at):
        return sum(nt(kvt[3, :, start:start + size], hid[at, start:start + size]) for start in starts)

    share_d[3].wait_recv()
    lat[origin[3]] = over_lanes((4 * SHARE, HALF_D // 2 + 4 * SHARE), 2 * DIRECT, slice(None))
    share_s[3].wait_recv()
    for i, at in enumerate(tails):
        send_part(
            3, lat[origin[3], :, at] + over_lanes((0, HALF_D // 2), 4 * SHARE, at), m_copies[3 + i], at
        )
    resident((2, 3))

    for slot in range(4):
        for pair in m_copies[slot:] if slot == 3 else m_copies[slot:slot + 1]:
            wait_pair(pair)
        lat[origin[slot]] = lat[origin[slot]] + from_code(mpr[slot]) * msr[slot]
    whole = lat[...].reshape(KVW, TOK)
    latent = whole[:LATW]
    inverse = lax.rsqrt(jnp.sum(latent * latent, axis=0, keepdims=True) / LATW + eps_norm)
    gain_cols = jnp.transpose(jnp.broadcast_to(gain[...], (128, LATW)))
    for j in range(TOK // 128):
        at = slice(j * 128, j * 128 + 128)
        rows[:LATW, at] = (latent[:, at] * inverse[:, at] * gain_cols).astype(BF16)
    first, second = whole[LATW:LATW + ROPEW // 2], whole[LATW + ROPEW // 2:]
    rows[LATW:LATW + ROPEW // 2, :] = (first * cosine[...] - second * sine[...]).astype(BF16)
    rows[LATW + ROPEW // 2:KVW, :] = (first * sine[...] + second * cosine[...]).astype(BF16)

    slot_at = lax.broadcasted_iota(I32, (CAPTOK, TOK), 0)

    def pack_for(to):
        chosen = ((slot_at + to * CAPTOK) == tok[...]).astype(F32).astype(BF16)
        page_rows = nt(chosen, rows[...])
        empty = page_rows[:, KVW + USED:KVW + USED + 1] < 0.5
        column = lax.broadcasted_iota(I32, (CAPTOK, KVX), 1)
        return jnp.where((column == KVW) & empty, 1.0, page_rows).astype(BF16)

    first, second = pl.ds(0, HALF), pl.ds(HALF, HALF)
    a_p = [link(packed.at[0, at], arr.at[part, c], dev_zp) for at, part in ((first, 2), (second, 4))]
    a_m = [link(packed.at[1, at], arr.at[part, c], dev_zm) for at, part in ((first, 3), (second, 5))]
    a_r0 = link(packed.at[2, first], relay.at[0], dev_zp)
    a_r1 = link(packed.at[2, second], relay.at[1], dev_zm)
    a_f0 = link(relay.at[0], arr.at[6, c], dev_zp)
    a_f1 = link(relay.at[1], arr.at[7, c], dev_zm)
    a_share = [link(arr.at[pl.ds(part, 2), c], arr.at[pl.ds(part, 2), c], dev_sib) for part in (0, 2, 4, 6)]
    packed[0] = pack_for(lax.rem(b + 1, 4))
    go(a_p[0])
    packed[1] = pack_for(lax.rem(b + 3, 4))
    go(a_m[0])
    packed[2] = pack_for(lax.rem(b + 2, 4))
    go(a_r0)
    go(a_r1)
    go(a_p[1])
    go(a_m[1])
    own_pages = pack_for(b)
    arr[0, c] = own_pages[:HALF]
    arr[1, c] = own_pages[HALF:]
    go(a_share[0])

    def swap(copies, group):
        for copy in copies:
            copy.wait_recv()
        go(a_share[group])

    def turn_values(first, last):
        size = (last + 1 - first) * CAPTOK
        values = arr[first:last + 1].reshape(size, KVX)[:, :LATW]
        vt[:, first * CAPTOK:first * CAPTOK + size] = jnp.transpose(values)

    def pages_step(request, count, first, last):
        size, at = (last + 1 - first) * CAPTOK, columns(request, count)
        keys = arr[first:last + 1].reshape(size, KVX)
        score = nt(keys, qbuf[request:request + count].reshape(count * QROWS, KVX))
        old = ms[:, at]
        top = jnp.maximum(old, jnp.max(score, axis=0, keepdims=True))
        shrink = jnp.exp2((old - top) * log2_scale)
        w = weigh(score, top)
        total = ls[:, at] * shrink + jnp.sum(w, axis=0, keepdims=True)
        value = acc[:, at] * shrink + nn(vt[:, first * CAPTOK:first * CAPTOK + size], w.astype(BF16))
        return value, top, total

    def pages_of(request, count, first, last):
        at = columns(request, count)
        acc[:, at], ms[:, at], ls[:, at] = pages_step(request, count, first, last)

    a_share[0].wait_recv()
    turn_values(0, 1)
    pages_of(0, 4, 0, 1)
    swap((a_p[0], a_m[0]), 1)
    a_r0.wait_recv()
    go(a_f0)
    a_r1.wait_recv()
    go(a_f1)
    a_share[1].wait_recv()
    turn_values(2, 3)
    pages_of(0, 4, 2, 3)
    swap((a_p[1], a_m[1]), 2)
    a_share[2].wait_recv()
    turn_values(4, 5)
    swap((a_f0, a_f1), 3)
    pages_of(0, 2, 4, 5)
    a_share[3].wait_recv()
    turn_values(6, 7)

    def merge(parts):
        top = parts[0][1][0]
        for _, stat in parts[1:]:
            top = jnp.maximum(top, stat[0])
        value, total = 0.0, 0.0
        for coded, stat in parts:
            factor = jnp.exp2(stat[0] - top)
            value = value + from_code(coded) * factor
            total = total + factor * stat[1]
        return value, top, total

    def put(coded_ref, stat_ref, value, top, total):
        coded, scale = code(value, 0)
        coded_ref[...] = to_code(coded).reshape(coded_ref.shape)
        stat_ref[0] = top + jnp.log(scale) * log2_e
        stat_ref[1] = total / scale

    def both(data, stat, data_to, stat_to, dev):
        return link(data, data_to, dev), link(stat, stat_to, dev)

    first_copies, relay_copies, last_copies = [], [], []
    for i in range(2):
        first_copies.append([
            both(osend.at[i, pl.ds(3 + 2 * k, 2)], ostat.at[i], yfirst.at[i, k], yfstat.at[i, k], dev)
            for k, dev in enumerate((dev_yp, dev_ym))
        ])
        relay_copies.append([
            both(rsend.at[i, k], rstat.at[i, k], yrelay.at[i, k], yrstat.at[i, k], dev)
            for k, dev in enumerate((dev_yp, dev_ym))
        ])
        last_copies.append([
            both(mbuf.at[i, half, core], mstat.at[i, half], fbuf.at[i, k], fstat.at[i, k], dev)
            for k, (half, core, dev) in enumerate((
                (1 - xh, c, dev_x), (1 - xh, 1 - c, dev_x_sib), (xh, 1 - c, dev_sib),
            ))
        ])

    def relay_sums(i):
        for k, (own, far) in enumerate(((2, 1), (7, 0))):
            wait_pair(first_copies[i][k])
            put(rsend.at[i, k], rstat.at[i, k], *merge([
                (osend[i, own], ostat[i]), (yfirst[i, k, far], yfstat[i, k]),
            ]))
            go_pair(relay_copies[i][k])

    def sums_over_y(i):
        for half in range(2):
            wait_pair(relay_copies[i][half])
            near = 1 - half
            put(mbuf.at[i, half], mstat.at[i, half], *merge([
                (osend[i, half], ostat[i]), (yfirst[i, near, near], yfstat[i, near]), (yrelay[i, half], yrstat[i, half]),
            ]))
        for k in (1, 0, 2):
            go_pair(last_copies[i][k])

    def out_copy(wanted):
        return pltpu.make_async_copy(out.at[:, wanted], out_hbm.at[:, wanted], loc.at[13 + wanted])

    def last_sums(i):
        for pair in last_copies[i]:
            wait_pair(pair)
        for core, parts in (
            (c, [(mbuf[i, xh, c], mstat[i, xh]), (fbuf[i, 0], fstat[i, 0])]),
            (1 - c, [(fbuf[i, 2], fstat[i, 2]), (fbuf[i, 1], fstat[i, 1])]),
        ):
            value, _, total = merge(parts)
            value = value / total
            for j in range(2):
                wanted = core * NR + 2 * i + j
                for step in range(4):
                    at = QROWS * j + 64 * step
                    out[step, wanted] = value[:, at:at + 64]
                out_copy(wanted).start()

    for i, first in enumerate((6, 4)):
        value, top, total = pages_step(2 * i, 2, first, 7)
        coded, scale = code(value, 0)
        blocks = to_code(coded).reshape(4, 2, 64, 2 * QROWS)
        for chip in range(4):
            osend[i, pl.ds(2 * lax.rem(chip - y + 4, 4), 2)] = blocks[chip]
        ostat[i, 0] = top * log2_scale + jnp.log(scale) * log2_e
        ostat[i, 1] = total / scale
        for pair in first_copies[i]:
            go_pair(pair)
    for stage in (relay_sums, sums_over_y, last_sums):
        for i in range(2):
            stage(i)
    for wanted in range(2 * NR):
        out_copy(wanted).wait()
    for copy in started:
        copy.wait_send()


LINKS = 144


def tables():
    half = ROPEW // 2
    frequency = rope_base ** (-np.arange(half, dtype=np.float32) / np.float32(half))
    angles = np.arange(TOK, dtype=np.float32)[None, :] * frequency.astype(np.float32)[:, None]
    return np.cos(angles).astype(np.float32), np.sin(angles).astype(np.float32)


def on_device(hidden, kv_down, kv_gain, page_owner, page_request, queries, cache, lengths):
    cosine, sine = tables()
    anywhere = pl.BlockSpec(memory_space=pl.ANY)
    sums = pl.pallas_call(
        kernel,
        out_shape=jax.ShapeDtypeStruct((4, 2 * NR, 32, 64), F32),
        in_specs=[anywhere] * 10,
        out_specs=anywhere,
        scratch_shapes=[
            pltpu.VMEM((1, LATW), F32),
            pltpu.SMEM((1, PAGES), I32),
            pltpu.SMEM((PAGES,), I32),
            pltpu.SMEM((2 * NR,), I32),
            pltpu.VMEM((ROPEW // 2, TOK), F32),
            pltpu.VMEM((ROPEW // 2, TOK), F32),
            pltpu.VMEM((4, 2 * NR, 32, 64), F32),
            pltpu.VMEM((TOK, HALF_D), BF16),
            pltpu.VMEM((4, BLK, HALF_D), BF16),
            pltpu.VMEM((4, BLK, TOK), F32),
            pltpu.VMEM((4, BLK, TOK), I16),
            pltpu.VMEM((4, BLK, TOK), I16),
            pltpu.VMEM((4, 1, TOK), F32),
            pltpu.VMEM((4, 1, TOK), F32),
            pltpu.VMEM((KVX, TOK), BF16),
            pltpu.VMEM((3, CAPTOK, KVX), BF16),
            pltpu.VMEM((2, HALF, KVX), BF16),
            pltpu.VMEM((8, 2, HALF, KVX), BF16),
            pltpu.VMEM((1, TOK), I32),
            pltpu.VMEM((LATW, 8 * CAPTOK), BF16),
            pltpu.VMEM((NR, 4, 64, KVW), BF16),
            pltpu.VMEM((NR, QROWS, KVX), BF16),
            pltpu.VMEM((2, NR, KVW, CTXD), BF16),
            pltpu.VMEM((LATW, NR * QROWS), F32),
            pltpu.VMEM((1, NR * QROWS), F32),
            pltpu.VMEM((1, NR * QROWS), F32),
            pltpu.VMEM((2, 8, 64, 2 * QROWS), I16),
            pltpu.VMEM((2, 2, 1, 2 * QROWS), F32),
            pltpu.VMEM((2, 2, 2, 64, 2 * QROWS), I16),
            pltpu.VMEM((2, 2, 2, 1, 2 * QROWS), F32),
            pltpu.VMEM((2, 2, 64, 2 * QROWS), I16),
            pltpu.VMEM((2, 2, 2, 1, 2 * QROWS), F32),
            pltpu.VMEM((2, 2, 64, 2 * QROWS), I16),
            pltpu.VMEM((2, 2, 2, 1, 2 * QROWS), F32),
            pltpu.VMEM((2, 2, 2, 32, 2 * QROWS), I16),
            pltpu.VMEM((2, 2, 2, 1, 2 * QROWS), F32),
            pltpu.VMEM((2, 3, 32, 2 * QROWS), I16),
            pltpu.VMEM((2, 3, 2, 1, 2 * QROWS), F32),
            pltpu.SemaphoreType.DMA((13 + 2 * NR,)),
            pltpu.SemaphoreType.DMA((LINKS,)),
            pltpu.SemaphoreType.DMA((LINKS,)),
        ],
        compiler_params=pltpu.CompilerParams(
            collective_id=0, has_side_effects=True, vmem_limit_bytes=56 * 1024 * 1024
        ),
        cost_estimate=pl.CostEstimate(flops=7_500_000_000, bytes_accessed=12_000_000, transcendentals=3_000_000),
    )(
        hidden, kv_down.T, kv_gain.reshape(1, LATW), page_owner.T, page_request, queries, cache.transpose(0, 2, 1), lengths,
        jnp.asarray(cosine), jnp.asarray(sine),
    )
    return sums.transpose(0, 1, 3, 2)


def solution(mesh):
    return jax.shard_map(
        on_device,
        mesh=mesh,
        in_specs=(
            P(("seq", "batch"), "mp"),
            P("mp", "batch"),
            P(),
            P(("seq", "batch"), None),
            P(("seq", "batch")),
            P(None, "batch", "mp", None),
            P("batch", "seq", None),
            P("batch"),
        ),
        out_specs=P(None, "batch", "mp", "seq"),
        check_vma=False,
    )
```

```python
import jax
import jax.numpy as jnp
import numpy as np
from jax import lax
from jax.experimental import pallas as pl
from jax.experimental.pallas import tpu as pltpu
from jax.sharding import PartitionSpec as P

MESH = pl.DeviceIdType.MESH
F32, BF16, I32, I16 = jnp.float32, jnp.bfloat16, jnp.int32, jnp.int16

eps_norm = 1e-06
score_scale = 192.0 ** (-0.5)
log2_e = 1.4426950408889634
log2_scale = score_scale * log2_e
rope_base = 10000.0
masked_value = -1e30
floor_value = -1e29
code_top = 32767.0

TOK, HALF_D, KVW, LATW, ROPEW = 384, 3584, 576, 512, 64
USED = 16
LABELS = 64
KVX = KVW + LABELS
BLK = 144
SHARE, DIRECT = 256, 384
CAPTOK = 192
HALF = CAPTOK // 2
PAGES, PAGE, CAP = 24, 16, 12
QROWS = 256
CTXD = 512
NR = 4


def nt(a, b):
    return lax.dot_general(a, b, (((1,), (1,)), ((), ())), preferred_element_type=F32)


def nn(a, b):
    return jnp.dot(a, b, preferred_element_type=F32)


def kernel(
    hidden, kv_down, gain_in, owner_in, request_in, queries, cache, lengths_in, cosine_in, sine_in,
    out_hbm,
    gain, owner, request, lengths, cosine, sine, out,
    hid, kvt, lat, mps, mpr, mss, msr, rows, packed, relay, arr, tok,
    vt, qraw, qbuf, kbuf, acc, ms, ls, osend, ostat, ybuf, ystat, rsend, rstat, mbuf, mstat, fbuf, fstat,
    loc, send, recv,
):
    s, b, p = lax.axis_index("seq"), lax.axis_index("batch"), lax.axis_index("mp")
    c = lax.rem(s, 2)
    sib = s + 1 - 2 * c
    y = lax.div(s, 4)
    in_y = lax.rem(s, 4)
    xh = lax.rem(lax.div(s, 2), 2)
    dev_zp = (s, lax.rem(b + 1, 4), p)
    dev_zm = (s, lax.rem(b + 3, 4), p)
    dev_zz = (s, lax.rem(b + 2, 4), p)
    dev_mp = (s, b, 1 - p)
    dev_sib = (sib, b, p)
    dev_yp = (lax.rem(y + 1, 4) * 4 + in_y, b, p)
    dev_ym = (lax.rem(y + 3, 4) * 4 + in_y, b, p)
    dev_x = (s + 2 - 4 * xh, b, p)
    dev_x_sib = (sib + 2 - 4 * xh, b, p)

    used = [0]
    started = []

    def link(src, dst, dev):
        used[0] += 1
        return link_at(used[0] - 1, src, dst, dev)

    def link_at(i, src, dst, dev):
        return pltpu.make_async_remote_copy(
            src_ref=src, dst_ref=dst, send_sem=send.at[i], recv_sem=recv.at[i],
            device_id=dev, device_id_type=MESH,
        )

    def go(copy):
        copy.start()
        started.append(copy)

    def code(value, axis):
        most = jnp.max(jnp.abs(value), axis=axis, keepdims=True)
        most = jnp.maximum(most, 1e-25)
        return jnp.round(value * (code_top / most)), most * (1.0 / code_top)

    def to_code(value):
        return value.astype(I32).astype(I16)

    def from_code(coded):
        return coded.astype(I32).astype(F32)

    def go_pair(pair):
        go(pair[0])
        go(pair[1])

    def wait_pair(pair):
        pair[0].wait_recv()
        pair[1].wait_recv()

    barrier = pltpu.get_barrier_semaphore()
    for dev in (dev_zp, dev_zm, dev_zz, dev_mp, dev_sib, dev_yp, dev_ym, dev_x, dev_x_sib):
        pl.semaphore_signal(barrier, inc=1, device_id=dev, device_id_type=MESH)

    small = [
        pltpu.make_async_copy(src, dst, loc.at[7 + i])
        for i, (src, dst) in enumerate((
            (owner_in, owner), (request_in, request), (lengths_in, lengths), (gain_in, gain), (cosine_in, cosine),
            (sine_in, sine),
        ))
    ]
    load_kv = pltpu.make_async_copy(kv_down, kvt.at[0], loc.at[0])
    load_hid = pltpu.make_async_copy(hidden, hid, loc.at[1])
    load_q = [pltpu.make_async_copy(queries.at[step, pl.ds(c * NR, NR)], qraw.at[:, step], loc.at[2 + step]) for step in range(4)]
    load_cache = pltpu.make_async_copy(cache.at[pl.ds(c * NR, NR)], kbuf.at[0], loc.at[6])
    for copy in [load_hid, load_kv] + small:
        copy.start()

    pl.semaphore_wait(barrier, 9)

    base = c * (HALF_D // 2)

    def lanes(start, size):
        return pl.ds(pl.multiple_of(base + start, 128), size)

    def kv_link(slot, to_slot, at, dev):
        return link(kvt.at[slot, :, at], kvt.at[to_slot, :, at], dev)

    def first_link(to_slot, at, dev):
        return link(kv_down.at[:, at], kvt.at[to_slot, :, at], dev)

    def part_of(k, first=0, size=SHARE):
        return lanes(lax.rem(y + k, 4) * SHARE + first, size)

    low, high = lanes(4 * SHARE, DIRECT), lanes(4 * SHARE + DIRECT, DIRECT)
    mine = part_of(0)
    s_p, s_m = first_link(1, mine, dev_zp), first_link(2, mine, dev_zm)
    d_p0, d_m1 = first_link(1, low, dev_zp), first_link(2, high, dev_zm)
    d_p1, d_m0 = first_link(1, high, dev_zp), first_link(2, low, dev_zm)
    for copy in (s_p, s_m, d_p0, d_m1):
        go(copy)
    for copy in load_q + [load_cache]:
        copy.start()
    cache_out = link(cache.at[pl.ds((1 - c) * NR, NR)], kbuf.at[1], dev_sib)
    go(cache_out)
    sf_p, sf_m = (
        kv_link(1, 3, part_of(0, 0, SHARE // 2), dev_zp),
        kv_link(2, 3, part_of(0, SHARE // 2, SHARE // 2), dev_zm),
    )
    df_p, df_m = kv_link(1, 3, low, dev_zp), kv_link(2, 3, high, dev_zm)
    near_p = [None] + [kv_link(slot, slot, mine, dev_yp) for slot in (1, 2, 3)]
    near_m = [None] + [kv_link(slot, slot, mine, dev_ym) for slot in (1, 2, 3)]
    far = [None] + [
        (
            kv_link(slot, slot, part_of(3, 0, SHARE // 2), dev_yp),
            kv_link(slot, slot, part_of(1, SHARE // 2, SHARE // 2), dev_ym),
        )
        for slot in (1, 2, 3)
    ]
    share_s = [None] + [kv_link(slot, slot, lanes(0, 4 * SHARE), dev_sib) for slot in (1, 2, 3)]
    share_d = [None] + [kv_link(slot, slot, lanes(4 * SHARE, 2 * DIRECT), dev_sib) for slot in (1, 2, 3)]

    origin = [lax.rem(b + ahead, 4) for ahead in (0, 3, 1, 2)]
    m_copies = [
        (link(mps.at[slot], mpr.at[slot], dev_mp), link(mss.at[slot], msr.at[slot], dev_mp)) for slot in range(3)
    ]
    tails = (slice(0, 256), slice(256, TOK))
    for at in tails:
        at = pl.ds(at.start, at.stop - at.start)
        m_copies.append((
            link(mps.at[3, :, at], mpr.at[3, :, at], dev_mp), link(mss.at[3, :, at], msr.at[3, :, at], dev_mp),
        ))

    def send_part(slot, part, copies, at=slice(None)):
        lat[origin[slot], :, at] = part
        coded, scale = code(part, 0)
        mps[slot, :, at] = to_code(coded)
        mss[slot, :, at] = scale
        go_pair(copies)

    def weigh(score, top):
        return jnp.exp2(score * log2_scale - top * log2_scale)

    def fold(w):
        total = w[:, :128]
        for j in range(1, w.shape[1] // 128):
            total = total + w[:, j * 128:j * 128 + 128]
        return total

    def peak(score):
        most = score[:, :128]
        for j in range(1, score.shape[1] // 128):
            most = jnp.maximum(most, score[:, j * 128:j * 128 + 128])
        return most

    def columns(first, count=1):
        return slice(first * QROWS, (first + count) * QROWS)

    def resident(requests):
        at = lax.broadcasted_iota(I32, (1, CTXD), 1)
        scores = [
            [
                jnp.where(at + place * CTXD < lengths[c * NR + r], nn(qbuf[r, :, :KVW], kbuf[part, r]), masked_value)
                for part, place in enumerate((s, sib))
            ]
            for r in requests
        ]
        weights = []
        for r, (score0, score1) in zip(requests, scores):
            top = jnp.max(jnp.maximum(peak(score0), peak(score1)), axis=1, keepdims=True)
            top = jnp.maximum(top, floor_value)
            w0, w1 = weigh(score0, top), weigh(score1, top)
            ms[:, columns(r)] = jnp.transpose(jnp.broadcast_to(top, (QROWS, 128)))[0:1]
            ls[:, columns(r)] = jnp.sum(jnp.transpose(fold(w0) + fold(w1)), axis=0, keepdims=True)
            weights.append((w0.astype(BF16), w1.astype(BF16)))
        for r, (w0, w1) in zip(requests, weights):
            acc[:, columns(r)] = nt(kbuf[0, r, :LATW, :], w0) + nt(kbuf[1, r, :LATW, :], w1)

    load_hid.wait()
    load_kv.wait()
    send_part(0, nt(kvt[0], hid[...]), m_copies[0])
    s_p.wait_recv()
    go(sf_p)
    go(near_p[1])
    go(near_m[1])
    s_m.wait_recv()
    go(sf_m)
    go(near_p[2])
    go(near_m[2])
    go(d_p1)
    go(d_m0)

    for copy in small:
        copy.wait()
    token = lax.broadcasted_iota(I32, (1, TOK), 1)
    token_page = lax.shift_right_logical(token, 4)
    dest = jnp.zeros((1, TOK), I32)
    asked = jnp.zeros((1, TOK), I32)
    counts = [jnp.int32(0)] * 4
    for page in range(PAGES):
        to = owner[0, page]
        rank = jnp.where(to == 0, counts[0], jnp.where(to == 1, counts[1], jnp.where(to == 2, counts[2], counts[3])))
        counts = [counts[o] + (to == o).astype(I32) for o in range(4)]
        dest = jnp.where(token_page == page, (to * CAP + rank) * PAGE, dest)
        asked = jnp.where(token_page == page, request[page] + 1, asked)
    dest = dest + lax.bitwise_and(token, 15)
    tok[...] = dest

    label_row = lax.broadcasted_iota(I32, (LABELS, TOK), 0)
    rows[KVW:, :] = ((label_row == asked) | (label_row == USED)).astype(F32).astype(BF16)

    d_p0.wait_recv()
    go(df_p)
    d_m1.wait_recv()
    go(df_m)

    def pass_on(slot):
        near_p[slot].wait_recv()
        go(far[slot][0])
        near_m[slot].wait_recv()
        go(far[slot][1])

    def swap_shared(slot):
        far[slot][0].wait_recv()
        far[slot][1].wait_recv()
        go(share_s[slot])

    pass_on(1)
    sf_p.wait_recv()
    sf_m.wait_recv()
    go(near_p[3])
    go(near_m[3])

    for copy in load_q:
        copy.wait()
    load_cache.wait()
    label_at = lax.broadcasted_iota(I32, (QROWS, LABELS), 1)

    def fill(r, carry):
        qbuf[r, :, :KVW] = qraw[r].reshape(QROWS, KVW)
        opened = (label_at == c * NR + r + 1) | (label_at == USED)
        qbuf[r, :, KVW:] = jnp.where(opened, 0.0, masked_value).astype(BF16)
        return carry

    lax.fori_loop(0, NR, fill, 0)
    cache_out.wait_recv()
    resident((0,))

    pass_on(2)
    d_p1.wait_recv()
    go(share_d[1])
    d_m0.wait_recv()
    go(share_d[2])
    swap_shared(1)
    resident((1,))

    pass_on(3)
    swap_shared(2)
    share_d[1].wait_recv()
    share_s[1].wait_recv()
    send_part(1, nt(kvt[1], hid[...]), m_copies[1])
    df_p.wait_recv()
    df_m.wait_recv()
    go(share_d[3])
    swap_shared(3)
    share_d[2].wait_recv()
    share_s[2].wait_recv()
    send_part(2, nt(kvt[2], hid[...]), m_copies[2])

    def over_lanes(starts, size, at):
        return sum(nt(kvt[3, :, start:start + size], hid[at, start:start + size]) for start in starts)

    share_d[3].wait_recv()
    lat[origin[3]] = over_lanes((4 * SHARE, HALF_D // 2 + 4 * SHARE), 2 * DIRECT, slice(None))
    share_s[3].wait_recv()
    for i, at in enumerate(tails):
        send_part(
            3, lat[origin[3], :, at] + over_lanes((0, HALF_D // 2), 4 * SHARE, at), m_copies[3 + i], at
        )
    resident((2, 3))

    for slot in range(4):
        for pair in m_copies[slot:] if slot == 3 else m_copies[slot:slot + 1]:
            wait_pair(pair)
        lat[origin[slot]] = lat[origin[slot]] + from_code(mpr[slot]) * msr[slot]
    whole = lat[...].reshape(KVW, TOK)
    latent = whole[:LATW]
    inverse = lax.rsqrt(jnp.sum(latent * latent, axis=0, keepdims=True) / LATW + eps_norm)
    gain_cols = jnp.transpose(jnp.broadcast_to(gain[...], (128, LATW)))
    for j in range(TOK // 128):
        at = slice(j * 128, j * 128 + 128)
        rows[:LATW, at] = (latent[:, at] * inverse[:, at] * gain_cols).astype(BF16)
    first, second = whole[LATW:LATW + ROPEW // 2], whole[LATW + ROPEW // 2:]
    rows[LATW:LATW + ROPEW // 2, :] = (first * cosine[...] - second * sine[...]).astype(BF16)
    rows[LATW + ROPEW // 2:KVW, :] = (first * sine[...] + second * cosine[...]).astype(BF16)

    slot_at = lax.broadcasted_iota(I32, (CAPTOK, TOK), 0)

    def pack_for(to):
        chosen = ((slot_at + to * CAPTOK) == tok[...]).astype(F32).astype(BF16)
        page_rows = nt(chosen, rows[...])
        empty = page_rows[:, KVW + USED:KVW + USED + 1] < 0.5
        column = lax.broadcasted_iota(I32, (CAPTOK, KVX), 1)
        return jnp.where((column == KVW) & empty, 1.0, page_rows).astype(BF16)

    first, second = pl.ds(0, HALF), pl.ds(HALF, HALF)
    a_p = [link(packed.at[0, at], arr.at[part, c], dev_zp) for at, part in ((first, 2), (second, 4))]
    a_m = [link(packed.at[1, at], arr.at[part, c], dev_zm) for at, part in ((first, 3), (second, 5))]
    a_r0 = link(packed.at[2, first], relay.at[0], dev_zp)
    a_r1 = link(packed.at[2, second], relay.at[1], dev_zm)
    a_f0 = link(relay.at[0], arr.at[6, c], dev_zp)
    a_f1 = link(relay.at[1], arr.at[7, c], dev_zm)
    a_share = [link(arr.at[part, c], arr.at[part, c], dev_sib) for part in range(8)]
    packed[0] = pack_for(lax.rem(b + 1, 4))
    go(a_p[0])
    packed[1] = pack_for(lax.rem(b + 3, 4))
    go(a_m[0])
    packed[2] = pack_for(lax.rem(b + 2, 4))
    go(a_r0)
    go(a_r1)
    go(a_p[1])
    go(a_m[1])
    own_pages = pack_for(b)
    arr[0, c] = own_pages[:HALF]
    go(a_share[0])
    arr[1, c] = own_pages[HALF:]
    go(a_share[1])

    def swap(copies, parts):
        for copy, part in zip(copies, parts):
            copy.wait_recv()
            go(a_share[part])

    def ready(parts):
        for part in parts:
            a_share[part].wait_recv()

    def turn_values(first, last):
        size = (last + 1 - first) * CAPTOK
        values = arr[first:last + 1].reshape(size, KVX)[:, :LATW]
        vt[:, first * CAPTOK:first * CAPTOK + size] = jnp.transpose(values)

    def pages_step(request, count, first, last):
        size, at = (last + 1 - first) * CAPTOK, columns(request, count)
        keys = arr[first:last + 1].reshape(size, KVX)
        score = nt(keys, qbuf[request:request + count].reshape(count * QROWS, KVX))
        old = ms[:, at]
        top = jnp.maximum(old, jnp.max(score, axis=0, keepdims=True))
        shrink = jnp.exp2((old - top) * log2_scale)
        w = weigh(score, top)
        total = ls[:, at] * shrink + jnp.sum(w, axis=0, keepdims=True)
        value = acc[:, at] * shrink + nn(vt[:, first * CAPTOK:first * CAPTOK + size], w.astype(BF16))
        return value, top, total

    def pages_of(request, count, first, last):
        at = columns(request, count)
        acc[:, at], ms[:, at], ls[:, at] = pages_step(request, count, first, last)

    ready((0, 1))
    turn_values(0, 1)
    pages_of(0, 4, 0, 1)
    swap((a_p[0], a_m[0]), (2, 3))
    a_r0.wait_recv()
    go(a_f0)
    a_r1.wait_recv()
    go(a_f1)
    ready((2, 3))
    turn_values(2, 3)
    pages_of(0, 4, 2, 3)
    swap((a_p[1], a_m[1]), (4, 5))
    ready((4, 5))
    turn_values(4, 5)
    swap((a_f0, a_f1), (6, 7))
    pages_of(0, 4, 4, 5)
    ready((6, 7))
    turn_values(6, 7)

    def merge(parts):
        top = parts[0][1][0]
        for _, stat in parts[1:]:
            top = jnp.maximum(top, stat[0])
        value, total = 0.0, 0.0
        for coded, stat in parts:
            factor = jnp.exp2(stat[0] - top)
            value = value + from_code(coded) * factor
            total = total + factor * stat[1]
        return value, top, total

    def put(coded_ref, stat_ref, value, top, total):
        coded, scale = code(value, 0)
        coded_ref[...] = to_code(coded).reshape(coded_ref.shape)
        stat_ref[0] = top + jnp.log(scale) * log2_e
        stat_ref[1] = total / scale

    yp, ym, yy = lax.rem(y + 1, 4), lax.rem(y + 3, 4), lax.rem(y + 2, 4)
    first_y = used[0]

    def y_pair(r, k):
        pairs = (
            (osend.at[r, yy, 0], ostat.at[r], 0, dev_yp),
            (osend.at[r, yy, 1], ostat.at[r], 1, dev_ym),
            (osend.at[r, yp, 1], ostat.at[r], 2, dev_yp),
            (osend.at[r, ym, 0], ostat.at[r], 3, dev_ym),
            (rsend.at[r, 0], rstat.at[r, 0], 4, dev_yp),
            (rsend.at[r, 1], rstat.at[r, 1], 5, dev_ym),
        )
        data, stat, _, dev = pairs[k]
        return (
            link_at(first_y + 18 * r + 2 * k, data, ybuf.at[r, k], dev),
            link_at(first_y + 18 * r + 2 * k + 1, stat, ystat.at[r, k], dev),
        )

    def last_pair(r, k):
        half, core, dev = ((1 - xh, c, dev_x), (1 - xh, 1 - c, dev_x_sib), (xh, 1 - c, dev_sib))[k]
        return (
            link_at(first_y + 18 * r + 12 + 2 * k, mbuf.at[r, half, core], fbuf.at[r, k], dev),
            link_at(first_y + 18 * r + 13 + 2 * k, mstat.at[r, half], fstat.at[r, k], dev),
        )

    def start_pair(pair):
        pair[0].start()
        pair[1].start()

    def relay_sums(r, carry):
        for k, to in ((0, yp), (1, ym)):
            wait_pair(y_pair(r, k))
            put(rsend.at[r, k], rstat.at[r, k], *merge([
                (osend[r, to, k], ostat[r]), (ybuf[r, k], ystat[r, k]),
            ]))
            start_pair(y_pair(r, 4 + k))
        return carry

    for r in range(NR):
        value, top, total = pages_step(r, 1, 6, 7)
        coded, scale = code(value, 0)
        osend[r] = to_code(coded).reshape(4, 2, 64, QROWS)
        ostat[r, 0] = top * log2_scale + jnp.log(scale) * log2_e
        ostat[r, 1] = total / scale
        for k in (0, 1):
            start_pair(y_pair(r, k))
        if r >= 1:
            for k in (2, 3):
                start_pair(y_pair(r - 1, k))
        if r >= 2:
            lax.fori_loop(r - 2, r - 1, relay_sums, 0)
    for k in (2, 3):
        start_pair(y_pair(NR - 1, k))

    def sums_over_y(r, carry):
        for k in range(2, 6):
            wait_pair(y_pair(r, k))
        for h, (one, two) in enumerate(((3, 4), (2, 5))):
            put(mbuf.at[r, h], mstat.at[r, h], *merge([
                (osend[r, y, h], ostat[r]), (ybuf[r, one], ystat[r, one]), (ybuf[r, two], ystat[r, two]),
            ]))
        for k in (1, 0, 2):
            start_pair(last_pair(r, k))
        return carry

    def out_copy(wanted):
        return pltpu.make_async_copy(out.at[:, wanted], out_hbm.at[:, wanted], loc.at[13 + wanted])

    def last_sums(r, carry):
        for k in range(3):
            wait_pair(last_pair(r, k))
        own, other = c * NR + r, (1 - c) * NR + r
        for wanted, parts in (
            (own, [(mbuf[r, xh, c], mstat[r, xh]), (fbuf[r, 0], fstat[r, 0])]),
            (other, [(fbuf[r, 2], fstat[r, 2]), (fbuf[r, 1], fstat[r, 1])]),
        ):
            value, _, total = merge(parts)
            value = value / total
            for step in range(4):
                out[step, wanted] = value[:, 64 * step:64 * step + 64]
            out_copy(wanted).start()
        return carry

    def finish(r, carry):
        for pair in [y_pair(r, k) for k in range(6)] + [last_pair(r, k) for k in range(3)]:
            pair[0].wait_send()
            pair[1].wait_send()
        return carry

    lax.fori_loop(2, NR, relay_sums, 0)
    for stage in (sums_over_y, last_sums, finish):
        lax.fori_loop(0, NR, stage, 0)
    for wanted in range(2 * NR):
        out_copy(wanted).wait()
    for copy in started:
        copy.wait_send()


LINKS = 144


def tables():
    half = ROPEW // 2
    frequency = rope_base ** (-np.arange(half, dtype=np.float32) / np.float32(half))
    angles = np.arange(TOK, dtype=np.float32)[None, :] * frequency.astype(np.float32)[:, None]
    return np.cos(angles).astype(np.float32), np.sin(angles).astype(np.float32)


def on_device(hidden, kv_down, kv_gain, page_owner, page_request, queries, cache, lengths):
    cosine, sine = tables()
    anywhere = pl.BlockSpec(memory_space=pl.ANY)
    sums = pl.pallas_call(
        kernel,
        out_shape=jax.ShapeDtypeStruct((4, 2 * NR, 32, 64), F32),
        in_specs=[anywhere] * 10,
        out_specs=anywhere,
        scratch_shapes=[
            pltpu.VMEM((1, LATW), F32),
            pltpu.SMEM((1, PAGES), I32),
            pltpu.SMEM((PAGES,), I32),
            pltpu.SMEM((2 * NR,), I32),
            pltpu.VMEM((ROPEW // 2, TOK), F32),
            pltpu.VMEM((ROPEW // 2, TOK), F32),
            pltpu.VMEM((4, 2 * NR, 32, 64), F32),
            pltpu.VMEM((TOK, HALF_D), BF16),
            pltpu.VMEM((4, BLK, HALF_D), BF16),
            pltpu.VMEM((4, BLK, TOK), F32),
            pltpu.VMEM((4, BLK, TOK), I16),
            pltpu.VMEM((4, BLK, TOK), I16),
            pltpu.VMEM((4, 1, TOK), F32),
            pltpu.VMEM((4, 1, TOK), F32),
            pltpu.VMEM((KVX, TOK), BF16),
            pltpu.VMEM((3, CAPTOK, KVX), BF16),
            pltpu.VMEM((2, HALF, KVX), BF16),
            pltpu.VMEM((8, 2, HALF, KVX), BF16),
            pltpu.VMEM((1, TOK), I32),
            pltpu.VMEM((LATW, 8 * CAPTOK), BF16),
            pltpu.VMEM((NR, 4, 64, KVW), BF16),
            pltpu.VMEM((NR, QROWS, KVX), BF16),
            pltpu.VMEM((2, NR, KVW, CTXD), BF16),
            pltpu.VMEM((LATW, NR * QROWS), F32),
            pltpu.VMEM((1, NR * QROWS), F32),
            pltpu.VMEM((1, NR * QROWS), F32),
            pltpu.VMEM((NR, 4, 2, 64, QROWS), I16),
            pltpu.VMEM((NR, 2, 1, QROWS), F32),
            pltpu.VMEM((NR, 6, 64, QROWS), I16),
            pltpu.VMEM((NR, 6, 2, 1, QROWS), F32),
            pltpu.VMEM((NR, 2, 64, QROWS), I16),
            pltpu.VMEM((NR, 2, 2, 1, QROWS), F32),
            pltpu.VMEM((NR, 2, 2, 32, QROWS), I16),
            pltpu.VMEM((NR, 2, 2, 1, QROWS), F32),
            pltpu.VMEM((NR, 3, 32, QROWS), I16),
            pltpu.VMEM((NR, 3, 2, 1, QROWS), F32),
            pltpu.SemaphoreType.DMA((13 + 2 * NR,)),
            pltpu.SemaphoreType.DMA((LINKS,)),
            pltpu.SemaphoreType.DMA((LINKS,)),
        ],
        compiler_params=pltpu.CompilerParams(
            collective_id=0, has_side_effects=True, vmem_limit_bytes=56 * 1024 * 1024
        ),
        cost_estimate=pl.CostEstimate(flops=7_500_000_000, bytes_accessed=12_000_000, transcendentals=3_000_000),
    )(
        hidden, kv_down.T, kv_gain.reshape(1, LATW), page_owner.T, page_request, queries, cache.transpose(0, 2, 1), lengths,
        jnp.asarray(cosine), jnp.asarray(sine),
    )
    return sums.transpose(0, 1, 3, 2)


def solution(mesh):
    return jax.shard_map(
        on_device,
        mesh=mesh,
        in_specs=(
            P(("seq", "batch"), "mp"),
            P("mp", "batch"),
            P(),
            P(("seq", "batch"), None),
            P(("seq", "batch")),
            P(None, "batch", "mp", None),
            P("batch", "seq", None),
            P("batch"),
        ),
        out_specs=P(None, "batch", "mp", "seq"),
        check_vma=False,
    )
```

```python
import jax
import jax.numpy as jnp
import numpy as np
from jax import lax
from jax.experimental import pallas as pl
from jax.experimental.pallas import tpu as pltpu
from jax.sharding import PartitionSpec as P

MESH = pl.DeviceIdType.MESH
F32, BF16, I32, I16 = jnp.float32, jnp.bfloat16, jnp.int32, jnp.int16

eps_norm = 1e-06
score_scale = 192.0 ** (-0.5)
log2_e = 1.4426950408889634
log2_scale = score_scale * log2_e
rope_base = 10000.0
masked_value = -1e30
floor_value = -1e29
code_top = 32767.0

TOK, HALF_D, KVW, LATW, ROPEW = 384, 3584, 576, 512, 64
USED = 16
LABELS = 64
KVX = KVW + LABELS
BLK = 144
SHARE, DIRECT = 256, 384
CAPTOK = 192
HALF = CAPTOK // 2
PAGES, PAGE, CAP = 24, 16, 12
QROWS = 256
CTXD = 512
NR = 4


def nt(a, b):
    return lax.dot_general(a, b, (((1,), (1,)), ((), ())), preferred_element_type=F32)


def nn(a, b):
    return jnp.dot(a, b, preferred_element_type=F32)


def kernel(
    hidden, kv_down, gain_in, owner_in, request_in, queries, cache, lengths_in, cosine_in, sine_in,
    out_hbm, inverse_hbm,
    gain, owner, request, lengths, cosine, sine, out, inverses,
    hid, kvt, lat, mps, mpr, mss, msr, rows, packed, relay, arr, tok,
    vt, qraw, qbuf, kbuf, acc, ms, ls, osend, ostat, ybuf, ystat, rsend, rstat, mbuf, mstat, fbuf, fstat,
    loc, send, recv,
):
    s, b, p = lax.axis_index("seq"), lax.axis_index("batch"), lax.axis_index("mp")
    c = lax.rem(s, 2)
    sib = s + 1 - 2 * c
    y = lax.div(s, 4)
    in_y = lax.rem(s, 4)
    xh = lax.rem(lax.div(s, 2), 2)
    dev_zp = (s, lax.rem(b + 1, 4), p)
    dev_zm = (s, lax.rem(b + 3, 4), p)
    dev_zz = (s, lax.rem(b + 2, 4), p)
    dev_mp = (s, b, 1 - p)
    dev_sib = (sib, b, p)
    dev_yp = (lax.rem(y + 1, 4) * 4 + in_y, b, p)
    dev_ym = (lax.rem(y + 3, 4) * 4 + in_y, b, p)
    dev_x = (s + 2 - 4 * xh, b, p)
    dev_x_sib = (sib + 2 - 4 * xh, b, p)

    used = [0]
    started = []

    def link(src, dst, dev):
        used[0] += 1
        return link_at(used[0] - 1, src, dst, dev)

    def link_at(i, src, dst, dev):
        return pltpu.make_async_remote_copy(
            src_ref=src, dst_ref=dst, send_sem=send.at[i], recv_sem=recv.at[i],
            device_id=dev, device_id_type=MESH,
        )

    def go(copy):
        copy.start()
        started.append(copy)

    def code(value, axis):
        most = jnp.max(jnp.abs(value), axis=axis, keepdims=True)
        most = jnp.maximum(most, 1e-25)
        return jnp.round(value * (code_top / most)), most * (1.0 / code_top)

    def to_code(value):
        return value.astype(I32).astype(I16)

    def from_code(coded):
        return coded.astype(I32).astype(F32)

    def go_pair(pair):
        go(pair[0])
        go(pair[1])

    def wait_pair(pair):
        pair[0].wait_recv()
        pair[1].wait_recv()

    barrier = pltpu.get_barrier_semaphore()
    for dev in (dev_zp, dev_zm, dev_zz, dev_mp, dev_sib, dev_yp, dev_ym, dev_x, dev_x_sib):
        pl.semaphore_signal(barrier, inc=1, device_id=dev, device_id_type=MESH)

    small = [
        pltpu.make_async_copy(src, dst, loc.at[7 + i])
        for i, (src, dst) in enumerate((
            (owner_in, owner), (request_in, request), (lengths_in, lengths), (gain_in, gain), (cosine_in, cosine),
            (sine_in, sine),
        ))
    ]
    load_kv = pltpu.make_async_copy(kv_down, kvt.at[0], loc.at[0])
    load_hid = pltpu.make_async_copy(hidden, hid, loc.at[1])
    load_q = [pltpu.make_async_copy(queries.at[step, pl.ds(c * NR, NR)], qraw.at[:, step], loc.at[2 + step]) for step in range(4)]
    load_cache = pltpu.make_async_copy(cache.at[pl.ds(c * NR, NR)], kbuf.at[0], loc.at[6])
    for copy in [load_hid, load_kv] + small:
        copy.start()

    pl.semaphore_wait(barrier, 9)

    base = c * (HALF_D // 2)

    def lanes(start, size):
        return pl.ds(pl.multiple_of(base + start, 128), size)

    def kv_link(slot, to_slot, at, dev):
        return link(kvt.at[slot, :, at], kvt.at[to_slot, :, at], dev)

    def first_link(to_slot, at, dev):
        return link(kv_down.at[:, at], kvt.at[to_slot, :, at], dev)

    def part_of(k, first=0, size=SHARE):
        return lanes(lax.rem(y + k, 4) * SHARE + first, size)

    low, high = lanes(4 * SHARE, DIRECT), lanes(4 * SHARE + DIRECT, DIRECT)
    mine = part_of(0)
    s_p, s_m = first_link(1, mine, dev_zp), first_link(2, mine, dev_zm)
    d_p0, d_m1 = first_link(1, low, dev_zp), first_link(2, high, dev_zm)
    d_p1, d_m0 = first_link(1, high, dev_zp), first_link(2, low, dev_zm)
    for copy in (s_p, s_m, d_p0, d_m1):
        go(copy)
    for copy in load_q + [load_cache]:
        copy.start()
    cache_out = link(cache.at[pl.ds((1 - c) * NR, NR)], kbuf.at[1], dev_sib)
    go(cache_out)
    sf_p, sf_m = (
        kv_link(1, 3, part_of(0, 0, SHARE // 2), dev_zp),
        kv_link(2, 3, part_of(0, SHARE // 2, SHARE // 2), dev_zm),
    )
    df_p, df_m = kv_link(1, 3, low, dev_zp), kv_link(2, 3, high, dev_zm)
    near_p = [None] + [kv_link(slot, slot, mine, dev_yp) for slot in (1, 2, 3)]
    near_m = [None] + [kv_link(slot, slot, mine, dev_ym) for slot in (1, 2, 3)]
    far = [None] + [
        (
            kv_link(slot, slot, part_of(3, 0, SHARE // 2), dev_yp),
            kv_link(slot, slot, part_of(1, SHARE // 2, SHARE // 2), dev_ym),
        )
        for slot in (1, 2, 3)
    ]
    share_s = [None] + [kv_link(slot, slot, lanes(0, 4 * SHARE), dev_sib) for slot in (1, 2, 3)]
    share_d = [None] + [kv_link(slot, slot, lanes(4 * SHARE, 2 * DIRECT), dev_sib) for slot in (1, 2, 3)]

    origin = [lax.rem(b + ahead, 4) for ahead in (0, 3, 1, 2)]
    m_copies = [
        (link(mps.at[slot], mpr.at[slot], dev_mp), link(mss.at[slot], msr.at[slot], dev_mp)) for slot in range(3)
    ]
    tails = (slice(0, 256), slice(256, TOK))
    for at in tails:
        at = pl.ds(at.start, at.stop - at.start)
        m_copies.append((
            link(mps.at[3, :, at], mpr.at[3, :, at], dev_mp), link(mss.at[3, :, at], msr.at[3, :, at], dev_mp),
        ))

    def send_part(slot, part, copies, at=slice(None)):
        lat[origin[slot], :, at] = part
        coded, scale = code(part, 0)
        mps[slot, :, at] = to_code(coded)
        mss[slot, :, at] = scale
        go_pair(copies)

    def weigh(score, top):
        return jnp.exp2(score * log2_scale - top * log2_scale)

    def fold(w):
        total = w[:, :128]
        for j in range(1, w.shape[1] // 128):
            total = total + w[:, j * 128:j * 128 + 128]
        return total

    def peak(score):
        most = score[:, :128]
        for j in range(1, score.shape[1] // 128):
            most = jnp.maximum(most, score[:, j * 128:j * 128 + 128])
        return most

    def columns(first, count=1):
        return slice(first * QROWS, (first + count) * QROWS)

    def resident(requests):
        at = lax.broadcasted_iota(I32, (1, CTXD), 1)
        scores = [
            [
                jnp.where(at + place * CTXD < lengths[c * NR + r], nn(qbuf[r, :, :KVW], kbuf[part, r]), masked_value)
                for part, place in enumerate((s, sib))
            ]
            for r in requests
        ]
        weights = []
        for r, (score0, score1) in zip(requests, scores):
            top = jnp.max(jnp.maximum(peak(score0), peak(score1)), axis=1, keepdims=True)
            top = jnp.maximum(top, floor_value)
            w0, w1 = weigh(score0, top), weigh(score1, top)
            ms[:, columns(r)] = jnp.transpose(jnp.broadcast_to(top, (QROWS, 128)))[0:1]
            ls[:, columns(r)] = jnp.sum(jnp.transpose(fold(w0) + fold(w1)), axis=0, keepdims=True)
            weights.append((w0.astype(BF16), w1.astype(BF16)))
        for r, (w0, w1) in zip(requests, weights):
            acc[:, columns(r)] = nt(kbuf[0, r, :LATW, :], w0) + nt(kbuf[1, r, :LATW, :], w1)

    load_hid.wait()
    load_kv.wait()
    send_part(0, nt(kvt[0], hid[...]), m_copies[0])
    s_p.wait_recv()
    go(sf_p)
    go(near_p[1])
    go(near_m[1])
    s_m.wait_recv()
    go(sf_m)
    go(near_p[2])
    go(near_m[2])
    go(d_p1)
    go(d_m0)

    for copy in small:
        copy.wait()
    token = lax.broadcasted_iota(I32, (1, TOK), 1)
    token_page = lax.shift_right_logical(token, 4)
    dest = jnp.zeros((1, TOK), I32)
    asked = jnp.zeros((1, TOK), I32)
    counts = [jnp.int32(0)] * 4
    for page in range(PAGES):
        to = owner[0, page]
        rank = jnp.where(to == 0, counts[0], jnp.where(to == 1, counts[1], jnp.where(to == 2, counts[2], counts[3])))
        counts = [counts[o] + (to == o).astype(I32) for o in range(4)]
        dest = jnp.where(token_page == page, (to * CAP + rank) * PAGE, dest)
        asked = jnp.where(token_page == page, request[page] + 1, asked)
    dest = dest + lax.bitwise_and(token, 15)
    tok[...] = dest

    label_row = lax.broadcasted_iota(I32, (LABELS, TOK), 0)
    rows[KVW:, :] = ((label_row == asked) | (label_row == USED)).astype(F32).astype(BF16)

    d_p0.wait_recv()
    go(df_p)
    d_m1.wait_recv()
    go(df_m)

    def pass_on(slot):
        near_p[slot].wait_recv()
        go(far[slot][0])
        near_m[slot].wait_recv()
        go(far[slot][1])

    def swap_shared(slot):
        far[slot][0].wait_recv()
        far[slot][1].wait_recv()
        go(share_s[slot])

    pass_on(1)
    sf_p.wait_recv()
    sf_m.wait_recv()
    go(near_p[3])
    go(near_m[3])

    for copy in load_q:
        copy.wait()
    load_cache.wait()
    label_at = lax.broadcasted_iota(I32, (QROWS, LABELS), 1)

    def fill(r, carry):
        qbuf[r, :, :KVW] = qraw[r].reshape(QROWS, KVW)
        opened = (label_at == c * NR + r + 1) | (label_at == USED)
        qbuf[r, :, KVW:] = jnp.where(opened, 0.0, masked_value).astype(BF16)
        return carry

    lax.fori_loop(0, NR, fill, 0)
    cache_out.wait_recv()
    resident((0,))

    pass_on(2)
    d_p1.wait_recv()
    go(share_d[1])
    d_m0.wait_recv()
    go(share_d[2])
    swap_shared(1)
    resident((1,))

    pass_on(3)
    swap_shared(2)
    share_d[1].wait_recv()
    share_s[1].wait_recv()
    send_part(1, nt(kvt[1], hid[...]), m_copies[1])
    df_p.wait_recv()
    df_m.wait_recv()
    go(share_d[3])
    swap_shared(3)
    share_d[2].wait_recv()
    share_s[2].wait_recv()
    send_part(2, nt(kvt[2], hid[...]), m_copies[2])

    def over_lanes(starts, size, at):
        return sum(nt(kvt[3, :, start:start + size], hid[at, start:start + size]) for start in starts)

    share_d[3].wait_recv()
    lat[origin[3]] = over_lanes((4 * SHARE, HALF_D // 2 + 4 * SHARE), 2 * DIRECT, slice(None))
    share_s[3].wait_recv()
    for i, at in enumerate(tails):
        send_part(
            3, lat[origin[3], :, at] + over_lanes((0, HALF_D // 2), 4 * SHARE, at), m_copies[3 + i], at
        )
    resident((2, 3))

    for slot in range(4):
        for pair in m_copies[slot:] if slot == 3 else m_copies[slot:slot + 1]:
            wait_pair(pair)
        lat[origin[slot]] = lat[origin[slot]] + from_code(mpr[slot]) * msr[slot]
    whole = lat[...].reshape(KVW, TOK)
    latent = whole[:LATW]
    inverse = lax.rsqrt(jnp.sum(latent * latent, axis=0, keepdims=True) / LATW + eps_norm)
    gain_cols = jnp.transpose(jnp.broadcast_to(gain[...], (128, LATW)))
    for j in range(TOK // 128):
        at = slice(j * 128, j * 128 + 128)
        rows[:LATW, at] = (latent[:, at] * inverse[:, at] * gain_cols).astype(BF16)
    first, second = whole[LATW:LATW + ROPEW // 2], whole[LATW + ROPEW // 2:]
    rows[LATW:LATW + ROPEW // 2, :] = (first * cosine[...] - second * sine[...]).astype(BF16)
    rows[LATW + ROPEW // 2:KVW, :] = (first * sine[...] + second * cosine[...]).astype(BF16)

    slot_at = lax.broadcasted_iota(I32, (CAPTOK, TOK), 0)

    def pack_for(to):
        chosen = ((slot_at + to * CAPTOK) == tok[...]).astype(F32).astype(BF16)
        page_rows = nt(chosen, rows[...])
        empty = page_rows[:, KVW + USED:KVW + USED + 1] < 0.5
        column = lax.broadcasted_iota(I32, (CAPTOK, KVX), 1)
        return jnp.where((column == KVW) & empty, 1.0, page_rows).astype(BF16)

    first, second = pl.ds(0, HALF), pl.ds(HALF, HALF)
    a_p = [link(packed.at[0, at], arr.at[part, c], dev_zp) for at, part in ((first, 2), (second, 4))]
    a_m = [link(packed.at[1, at], arr.at[part, c], dev_zm) for at, part in ((first, 3), (second, 5))]
    a_r0 = link(packed.at[2, first], relay.at[0], dev_zp)
    a_r1 = link(packed.at[2, second], relay.at[1], dev_zm)
    a_f0 = link(relay.at[0], arr.at[6, c], dev_zp)
    a_f1 = link(relay.at[1], arr.at[7, c], dev_zm)
    a_share = [link(arr.at[part, c], arr.at[part, c], dev_sib) for part in range(8)]
    packed[0] = pack_for(lax.rem(b + 1, 4))
    go(a_p[0])
    packed[1] = pack_for(lax.rem(b + 3, 4))
    go(a_m[0])
    packed[2] = pack_for(lax.rem(b + 2, 4))
    go(a_r0)
    go(a_r1)
    go(a_p[1])
    go(a_m[1])
    own_pages = pack_for(b)
    arr[0, c] = own_pages[:HALF]
    go(a_share[0])
    arr[1, c] = own_pages[HALF:]
    go(a_share[1])

    def swap(copies, parts):
        for copy, part in zip(copies, parts):
            copy.wait_recv()
            go(a_share[part])

    def ready(parts):
        for part in parts:
            a_share[part].wait_recv()

    def turn_values(first, last):
        size = (last + 1 - first) * CAPTOK
        values = arr[first:last + 1].reshape(size, KVX)[:, :LATW]
        vt[:, first * CAPTOK:first * CAPTOK + size] = jnp.transpose(values)

    def pages_step(request, count, first, last):
        size, at = (last + 1 - first) * CAPTOK, columns(request, count)
        keys = arr[first:last + 1].reshape(size, KVX)
        score = nt(keys, qbuf[request:request + count].reshape(count * QROWS, KVX))
        old = ms[:, at]
        top = jnp.maximum(old, jnp.max(score, axis=0, keepdims=True))
        shrink = jnp.exp2((old - top) * log2_scale)
        w = weigh(score, top)
        total = ls[:, at] * shrink + jnp.sum(w, axis=0, keepdims=True)
        value = acc[:, at] * shrink + nn(vt[:, first * CAPTOK:first * CAPTOK + size], w.astype(BF16))
        return value, top, total

    def pages_of(request, count, first, last):
        at = columns(request, count)
        acc[:, at], ms[:, at], ls[:, at] = pages_step(request, count, first, last)

    ready((0, 1))
    turn_values(0, 1)
    pages_of(0, 4, 0, 1)
    swap((a_p[0], a_m[0]), (2, 3))
    a_r0.wait_recv()
    go(a_f0)
    a_r1.wait_recv()
    go(a_f1)
    ready((2, 3))
    turn_values(2, 3)
    pages_of(0, 4, 2, 3)
    swap((a_p[1], a_m[1]), (4, 5))
    ready((4, 5))
    turn_values(4, 5)
    swap((a_f0, a_f1), (6, 7))
    pages_of(0, 2, 4, 5)
    ready((6, 7))
    turn_values(6, 7)

    def merge(parts):
        top = parts[0][1][0]
        for _, stat in parts[1:]:
            top = jnp.maximum(top, stat[0])
        value, total = 0.0, 0.0
        for coded, stat in parts:
            factor = jnp.exp2(stat[0] - top)
            value = value + from_code(coded) * factor
            total = total + factor * stat[1]
        return value, top, total

    def put(coded_ref, stat_ref, value, top, total):
        coded, scale = code(value, 0)
        coded_ref[...] = to_code(coded).reshape(coded_ref.shape)
        stat_ref[0] = top + jnp.log(scale) * log2_e
        stat_ref[1] = total / scale

    yp, ym, yy = lax.rem(y + 1, 4), lax.rem(y + 3, 4), lax.rem(y + 2, 4)
    first_y = used[0]

    def y_pair(r, k):
        pairs = (
            (osend.at[r, yy, 0], ostat.at[r], 0, dev_yp),
            (osend.at[r, yy, 1], ostat.at[r], 1, dev_ym),
            (osend.at[r, yp, 1], ostat.at[r], 2, dev_yp),
            (osend.at[r, ym, 0], ostat.at[r], 3, dev_ym),
            (rsend.at[r, 0], rstat.at[r, 0], 4, dev_yp),
            (rsend.at[r, 1], rstat.at[r, 1], 5, dev_ym),
        )
        data, stat, _, dev = pairs[k]
        return (
            link_at(first_y + 18 * r + 2 * k, data, ybuf.at[r, k], dev),
            link_at(first_y + 18 * r + 2 * k + 1, stat, ystat.at[r, k], dev),
        )

    def last_pair(r, k):
        half, core, dev = ((1 - xh, c, dev_x), (1 - xh, 1 - c, dev_x_sib), (xh, 1 - c, dev_sib))[k]
        return (
            link_at(first_y + 18 * r + 12 + 2 * k, mbuf.at[r, half, core], fbuf.at[r, k], dev),
            link_at(first_y + 18 * r + 13 + 2 * k, mstat.at[r, half], fstat.at[r, k], dev),
        )

    def start_pair(pair):
        pair[0].start()
        pair[1].start()

    def relay_sums(r, carry):
        for k, to in ((0, yp), (1, ym)):
            wait_pair(y_pair(r, k))
            put(rsend.at[r, k], rstat.at[r, k], *merge([
                (osend[r, to, k], ostat[r]), (ybuf[r, k], ystat[r, k]),
            ]))
            start_pair(y_pair(r, 4 + k))
        return carry

    for first_request, count, first in ((0, 1, 6), (1, 1, 6), (2, 2, 4)):
        value, top, total = pages_step(first_request, count, first, 7)
        coded, scale = code(value, 0)
        coded, top, total = to_code(coded), top * log2_scale + jnp.log(scale) * log2_e, total / scale
        for r in range(first_request, first_request + count):
            at = columns(r - first_request)
            osend[r] = coded[:, at].reshape(4, 2, 64, QROWS)
            ostat[r, 0] = top[:, at]
            ostat[r, 1] = total[:, at]
            for k in range(4):
                start_pair(y_pair(r, k))

    def sums_over_y(r, carry):
        for k in range(2, 6):
            wait_pair(y_pair(r, k))
        for h, (one, two) in enumerate(((3, 4), (2, 5))):
            put(mbuf.at[r, h], mstat.at[r, h], *merge([
                (osend[r, y, h], ostat[r]), (ybuf[r, one], ystat[r, one]), (ybuf[r, two], ystat[r, two]),
            ]))
        for k in (1, 0, 2):
            start_pair(last_pair(r, k))
        return carry

    def out_copy(wanted):
        return pltpu.make_async_copy(out.at[:, wanted], out_hbm.at[:, wanted], loc.at[13 + wanted])

    def last_sums(r, carry):
        for k in range(3):
            wait_pair(last_pair(r, k))
        own, other = c * NR + r, (1 - c) * NR + r
        for wanted, parts in (
            (own, [(mbuf[r, xh, c], mstat[r, xh]), (fbuf[r, 0], fstat[r, 0])]),
            (other, [(fbuf[r, 2], fstat[r, 2]), (fbuf[r, 1], fstat[r, 1])]),
        ):
            value, _, total = merge(parts)
            total = 1.0 / total
            for step in range(4):
                out[step, wanted] = value[:, 64 * step:64 * step + 64]
                inverses[step, wanted] = total[:, 64 * step:64 * step + 64]
            out_copy(wanted).start()
        return carry

    def finish(r, carry):
        for pair in [y_pair(r, k) for k in range(6)] + [last_pair(r, k) for k in range(3)]:
            pair[0].wait_send()
            pair[1].wait_send()
        return carry

    lax.fori_loop(0, NR, relay_sums, 0)
    for stage in (sums_over_y, last_sums):
        lax.fori_loop(0, NR, stage, 0)
    inverse_copy = pltpu.make_async_copy(inverses, inverse_hbm, loc.at[13 + 2 * NR])
    inverse_copy.start()
    for wanted in range(2 * NR):
        out_copy(wanted).wait()
    inverse_copy.wait()
    lax.fori_loop(0, NR, finish, 0)
    for copy in started:
        copy.wait_send()


LINKS = 144


def tables():
    half = ROPEW // 2
    frequency = rope_base ** (-np.arange(half, dtype=np.float32) / np.float32(half))
    angles = np.arange(TOK, dtype=np.float32)[None, :] * frequency.astype(np.float32)[:, None]
    return np.cos(angles).astype(np.float32), np.sin(angles).astype(np.float32)


def on_device(hidden, kv_down, kv_gain, page_owner, page_request, queries, cache, lengths):
    cosine, sine = tables()
    anywhere = pl.BlockSpec(memory_space=pl.ANY)
    sums, inverse = pl.pallas_call(
        kernel,
        out_shape=(
            jax.ShapeDtypeStruct((4, 2 * NR, 32, 64), F32), jax.ShapeDtypeStruct((4, 2 * NR, 1, 64), F32),
        ),
        in_specs=[anywhere] * 10,
        out_specs=(anywhere, anywhere),
        scratch_shapes=[
            pltpu.VMEM((1, LATW), F32),
            pltpu.SMEM((1, PAGES), I32),
            pltpu.SMEM((PAGES,), I32),
            pltpu.SMEM((2 * NR,), I32),
            pltpu.VMEM((ROPEW // 2, TOK), F32),
            pltpu.VMEM((ROPEW // 2, TOK), F32),
            pltpu.VMEM((4, 2 * NR, 32, 64), F32),
            pltpu.VMEM((4, 2 * NR, 1, 64), F32),
            pltpu.VMEM((TOK, HALF_D), BF16),
            pltpu.VMEM((4, BLK, HALF_D), BF16),
            pltpu.VMEM((4, BLK, TOK), F32),
            pltpu.VMEM((4, BLK, TOK), I16),
            pltpu.VMEM((4, BLK, TOK), I16),
            pltpu.VMEM((4, 1, TOK), F32),
            pltpu.VMEM((4, 1, TOK), F32),
            pltpu.VMEM((KVX, TOK), BF16),
            pltpu.VMEM((3, CAPTOK, KVX), BF16),
            pltpu.VMEM((2, HALF, KVX), BF16),
            pltpu.VMEM((8, 2, HALF, KVX), BF16),
            pltpu.VMEM((1, TOK), I32),
            pltpu.VMEM((LATW, 8 * CAPTOK), BF16),
            pltpu.VMEM((NR, 4, 64, KVW), BF16),
            pltpu.VMEM((NR, QROWS, KVX), BF16),
            pltpu.VMEM((2, NR, KVW, CTXD), BF16),
            pltpu.VMEM((LATW, NR * QROWS), F32),
            pltpu.VMEM((1, NR * QROWS), F32),
            pltpu.VMEM((1, NR * QROWS), F32),
            pltpu.VMEM((NR, 4, 2, 64, QROWS), I16),
            pltpu.VMEM((NR, 2, 1, QROWS), F32),
            pltpu.VMEM((NR, 6, 64, QROWS), I16),
            pltpu.VMEM((NR, 6, 2, 1, QROWS), F32),
            pltpu.VMEM((NR, 2, 64, QROWS), I16),
            pltpu.VMEM((NR, 2, 2, 1, QROWS), F32),
            pltpu.VMEM((NR, 2, 2, 32, QROWS), I16),
            pltpu.VMEM((NR, 2, 2, 1, QROWS), F32),
            pltpu.VMEM((NR, 3, 32, QROWS), I16),
            pltpu.VMEM((NR, 3, 2, 1, QROWS), F32),
            pltpu.SemaphoreType.DMA((14 + 2 * NR,)),
            pltpu.SemaphoreType.DMA((LINKS,)),
            pltpu.SemaphoreType.DMA((LINKS,)),
        ],
        compiler_params=pltpu.CompilerParams(
            collective_id=0, has_side_effects=True, vmem_limit_bytes=56 * 1024 * 1024
        ),
        cost_estimate=pl.CostEstimate(flops=7_500_000_000, bytes_accessed=12_000_000, transcendentals=3_000_000),
    )(
        hidden, kv_down.T, kv_gain.reshape(1, LATW), page_owner.T, page_request, queries, cache.transpose(0, 2, 1), lengths,
        jnp.asarray(cosine), jnp.asarray(sine),
    )
    return (sums * inverse).transpose(0, 1, 3, 2)


def solution(mesh):
    return jax.shard_map(
        on_device,
        mesh=mesh,
        in_specs=(
            P(("seq", "batch"), "mp"),
            P("mp", "batch"),
            P(),
            P(("seq", "batch"), None),
            P(("seq", "batch")),
            P(None, "batch", "mp", None),
            P("batch", "seq", None),
            P("batch"),
        ),
        out_specs=P(None, "batch", "mp", "seq"),
        check_vma=False,
    )
```

```python
import jax
import jax.numpy as jnp
import numpy as np
from jax import lax
from jax.experimental import pallas as pl
from jax.experimental.pallas import tpu as pltpu
from jax.sharding import PartitionSpec as P

MESH = pl.DeviceIdType.MESH
F32, BF16, I32, I16 = jnp.float32, jnp.bfloat16, jnp.int32, jnp.int16

eps_norm = 1e-06
score_scale = 192.0 ** (-0.5)
log2_e = 1.4426950408889634
log2_scale = score_scale * log2_e
rope_base = 10000.0
masked_value = -1e30
floor_value = -1e29
code_top = 32767.0

TOK, HALF_D, KVW, LATW, ROPEW = 384, 3584, 576, 512, 64
USED = 16
LABELS = 64
KVX = KVW + LABELS
BLK = 144
SHARE, DIRECT = 256, 384
CAPTOK = 192
HALF = CAPTOK // 2
PAGES, PAGE, CAP = 24, 16, 12
QROWS = 256
CTXD = 512
NR = 4


def nt(a, b):
    return lax.dot_general(a, b, (((1,), (1,)), ((), ())), preferred_element_type=F32)


def nn(a, b):
    return jnp.dot(a, b, preferred_element_type=F32)


def kernel(
    hidden, kv_down, gain_in, owner_in, request_in, queries, cache, lengths_in, cosine_in, sine_in,
    out_hbm,
    gain, owner, request, lengths, cosine, sine, out,
    hid, kvt, lat, mps, mpr, mss, msr, rows, packed, relay, arr, tok,
    vt, qraw, qbuf, kbuf, acc, ms, ls, osend, ostat, ybuf, ystat, rsend, rstat, mbuf, mstat, fbuf, fstat,
    loc, send, recv,
):
    s, b, p = lax.axis_index("seq"), lax.axis_index("batch"), lax.axis_index("mp")
    c = lax.rem(s, 2)
    sib = s + 1 - 2 * c
    y = lax.div(s, 4)
    in_y = lax.rem(s, 4)
    xh = lax.rem(lax.div(s, 2), 2)
    dev_zp = (s, lax.rem(b + 1, 4), p)
    dev_zm = (s, lax.rem(b + 3, 4), p)
    dev_zz = (s, lax.rem(b + 2, 4), p)
    dev_mp = (s, b, 1 - p)
    dev_sib = (sib, b, p)
    dev_yp = (lax.rem(y + 1, 4) * 4 + in_y, b, p)
    dev_ym = (lax.rem(y + 3, 4) * 4 + in_y, b, p)
    dev_x = (s + 2 - 4 * xh, b, p)
    dev_x_sib = (sib + 2 - 4 * xh, b, p)

    used = [0]
    started = []

    def link(src, dst, dev):
        used[0] += 1
        return link_at(used[0] - 1, src, dst, dev)

    def link_at(i, src, dst, dev):
        return pltpu.make_async_remote_copy(
            src_ref=src, dst_ref=dst, send_sem=send.at[i], recv_sem=recv.at[i],
            device_id=dev, device_id_type=MESH,
        )

    def go(copy):
        copy.start()
        started.append(copy)

    def code(value, axis):
        most = jnp.max(jnp.abs(value), axis=axis, keepdims=True)
        most = jnp.maximum(most, 1e-25)
        return jnp.round(value * (code_top / most)), most * (1.0 / code_top)

    def to_code(value):
        return value.astype(I32).astype(I16)

    def from_code(coded):
        return coded.astype(I32).astype(F32)

    def go_pair(pair):
        go(pair[0])
        go(pair[1])

    def wait_pair(pair):
        pair[0].wait_recv()
        pair[1].wait_recv()

    barrier = pltpu.get_barrier_semaphore()
    for dev in (dev_zp, dev_zm, dev_zz, dev_mp, dev_sib, dev_yp, dev_ym, dev_x, dev_x_sib):
        pl.semaphore_signal(barrier, inc=1, device_id=dev, device_id_type=MESH)

    small = [
        pltpu.make_async_copy(src, dst, loc.at[7 + i])
        for i, (src, dst) in enumerate((
            (owner_in, owner), (request_in, request), (lengths_in, lengths), (gain_in, gain), (cosine_in, cosine),
            (sine_in, sine),
        ))
    ]
    load_kv = pltpu.make_async_copy(kv_down, kvt.at[0], loc.at[0])
    load_hid = pltpu.make_async_copy(hidden, hid, loc.at[1])
    load_q = [pltpu.make_async_copy(queries.at[step, pl.ds(c * NR, NR)], qraw.at[:, step], loc.at[2 + step]) for step in range(4)]
    load_cache = pltpu.make_async_copy(cache.at[pl.ds(c * NR, NR)], kbuf.at[0], loc.at[6])
    for copy in [load_hid, load_kv] + small:
        copy.start()

    pl.semaphore_wait(barrier, 9)

    base = c * (HALF_D // 2)

    def lanes(start, size):
        return pl.ds(pl.multiple_of(base + start, 128), size)

    def kv_link(slot, to_slot, at, dev):
        return link(kvt.at[slot, :, at], kvt.at[to_slot, :, at], dev)

    def first_link(to_slot, at, dev):
        return link(kv_down.at[:, at], kvt.at[to_slot, :, at], dev)

    def part_of(k, first=0, size=SHARE):
        return lanes(lax.rem(y + k, 4) * SHARE + first, size)

    low, high = lanes(4 * SHARE, DIRECT), lanes(4 * SHARE + DIRECT, DIRECT)
    mine = part_of(0)
    s_p, s_m = first_link(1, mine, dev_zp), first_link(2, mine, dev_zm)
    d_p0, d_m1 = first_link(1, low, dev_zp), first_link(2, high, dev_zm)
    d_p1, d_m0 = first_link(1, high, dev_zp), first_link(2, low, dev_zm)
    for copy in (s_p, s_m, d_p0, d_m1):
        go(copy)
    for copy in load_q + [load_cache]:
        copy.start()
    cache_out = link(cache.at[pl.ds((1 - c) * NR, NR)], kbuf.at[1], dev_sib)
    go(cache_out)
    sf_p, sf_m = (
        kv_link(1, 3, part_of(0, 0, SHARE // 2), dev_zp),
        kv_link(2, 3, part_of(0, SHARE // 2, SHARE // 2), dev_zm),
    )
    df_p, df_m = kv_link(1, 3, low, dev_zp), kv_link(2, 3, high, dev_zm)
    near_p = [None] + [kv_link(slot, slot, mine, dev_yp) for slot in (1, 2, 3)]
    near_m = [None] + [kv_link(slot, slot, mine, dev_ym) for slot in (1, 2, 3)]
    far = [None] + [
        (
            kv_link(slot, slot, part_of(3, 0, SHARE // 2), dev_yp),
            kv_link(slot, slot, part_of(1, SHARE // 2, SHARE // 2), dev_ym),
        )
        for slot in (1, 2, 3)
    ]
    share_s = [None] + [kv_link(slot, slot, lanes(0, 4 * SHARE), dev_sib) for slot in (1, 2, 3)]
    share_d = [None] + [kv_link(slot, slot, lanes(4 * SHARE, 2 * DIRECT), dev_sib) for slot in (1, 2, 3)]

    origin = [lax.rem(b + ahead, 4) for ahead in (0, 3, 1, 2)]
    m_copies = [
        (link(mps.at[slot], mpr.at[slot], dev_mp), link(mss.at[slot], msr.at[slot], dev_mp)) for slot in range(3)
    ]
    tails = (slice(0, 256), slice(256, TOK))
    for at in tails:
        at = pl.ds(at.start, at.stop - at.start)
        m_copies.append((
            link(mps.at[3, :, at], mpr.at[3, :, at], dev_mp), link(mss.at[3, :, at], msr.at[3, :, at], dev_mp),
        ))

    def send_part(slot, part, copies, at=slice(None)):
        lat[origin[slot], :, at] = part
        coded, scale = code(part, 0)
        mps[slot, :, at] = to_code(coded)
        mss[slot, :, at] = scale
        go_pair(copies)

    def weigh(score, top):
        return jnp.exp2(score * log2_scale - top * log2_scale)

    def fold(w):
        total = w[:, :128]
        for j in range(1, w.shape[1] // 128):
            total = total + w[:, j * 128:j * 128 + 128]
        return total

    def peak(score):
        most = score[:, :128]
        for j in range(1, score.shape[1] // 128):
            most = jnp.maximum(most, score[:, j * 128:j * 128 + 128])
        return most

    def columns(first, count=1):
        return slice(first * QROWS, (first + count) * QROWS)

    def resident(requests):
        at = lax.broadcasted_iota(I32, (1, CTXD), 1)
        scores = [
            [
                jnp.where(at + place * CTXD < lengths[c * NR + r], nn(qbuf[r, :, :KVW], kbuf[part, r]), masked_value)
                for part, place in enumerate((s, sib))
            ]
            for r in requests
        ]
        weights = []
        for r, (score0, score1) in zip(requests, scores):
            top = jnp.max(jnp.maximum(peak(score0), peak(score1)), axis=1, keepdims=True)
            top = jnp.maximum(top, floor_value)
            w0, w1 = weigh(score0, top), weigh(score1, top)
            ms[:, columns(r)] = jnp.transpose(jnp.broadcast_to(top, (QROWS, 128)))[0:1]
            ls[:, columns(r)] = jnp.sum(jnp.transpose(fold(w0) + fold(w1)), axis=0, keepdims=True)
            weights.append((w0.astype(BF16), w1.astype(BF16)))
        for r, (w0, w1) in zip(requests, weights):
            acc[:, columns(r)] = nt(kbuf[0, r, :LATW, :], w0) + nt(kbuf[1, r, :LATW, :], w1)

    load_hid.wait()
    load_kv.wait()
    send_part(0, nt(kvt[0], hid[...]), m_copies[0])
    s_p.wait_recv()
    go(sf_p)
    go(near_p[1])
    go(near_m[1])
    s_m.wait_recv()
    go(sf_m)
    go(near_p[2])
    go(near_m[2])
    go(d_p1)
    go(d_m0)

    for copy in small:
        copy.wait()
    token = lax.broadcasted_iota(I32, (1, TOK), 1)
    token_page = lax.shift_right_logical(token, 4)
    dest = jnp.zeros((1, TOK), I32)
    asked = jnp.zeros((1, TOK), I32)
    counts = [jnp.int32(0)] * 4
    for page in range(PAGES):
        to = owner[0, page]
        rank = jnp.where(to == 0, counts[0], jnp.where(to == 1, counts[1], jnp.where(to == 2, counts[2], counts[3])))
        counts = [counts[o] + (to == o).astype(I32) for o in range(4)]
        dest = jnp.where(token_page == page, (to * CAP + rank) * PAGE, dest)
        asked = jnp.where(token_page == page, request[page] + 1, asked)
    dest = dest + lax.bitwise_and(token, 15)
    tok[...] = dest

    label_row = lax.broadcasted_iota(I32, (LABELS, TOK), 0)
    rows[KVW:, :] = ((label_row == asked) | (label_row == USED)).astype(F32).astype(BF16)

    d_p0.wait_recv()
    go(df_p)
    d_m1.wait_recv()
    go(df_m)

    def pass_on(slot):
        near_p[slot].wait_recv()
        go(far[slot][0])
        near_m[slot].wait_recv()
        go(far[slot][1])

    def swap_shared(slot):
        far[slot][0].wait_recv()
        far[slot][1].wait_recv()
        go(share_s[slot])

    pass_on(1)
    sf_p.wait_recv()
    sf_m.wait_recv()
    go(near_p[3])
    go(near_m[3])

    for copy in load_q:
        copy.wait()
    load_cache.wait()
    label_at = lax.broadcasted_iota(I32, (QROWS, LABELS), 1)

    def fill(r, carry):
        qbuf[r, :, :KVW] = qraw[r].reshape(QROWS, KVW)
        opened = (label_at == c * NR + r + 1) | (label_at == USED)
        qbuf[r, :, KVW:] = jnp.where(opened, 0.0, masked_value).astype(BF16)
        return carry

    lax.fori_loop(0, NR, fill, 0)
    cache_out.wait_recv()
    resident((0,))

    pass_on(2)
    d_p1.wait_recv()
    go(share_d[1])
    d_m0.wait_recv()
    go(share_d[2])
    swap_shared(1)
    resident((1,))

    pass_on(3)
    swap_shared(2)
    share_d[1].wait_recv()
    share_s[1].wait_recv()
    send_part(1, nt(kvt[1], hid[...]), m_copies[1])
    df_p.wait_recv()
    df_m.wait_recv()
    go(share_d[3])
    swap_shared(3)
    share_d[2].wait_recv()
    share_s[2].wait_recv()
    send_part(2, nt(kvt[2], hid[...]), m_copies[2])

    def over_lanes(starts, size, at):
        return sum(nt(kvt[3, :, start:start + size], hid[at, start:start + size]) for start in starts)

    share_d[3].wait_recv()
    lat[origin[3]] = over_lanes((4 * SHARE, HALF_D // 2 + 4 * SHARE), 2 * DIRECT, slice(None))
    share_s[3].wait_recv()
    for i, at in enumerate(tails):
        send_part(
            3, lat[origin[3], :, at] + over_lanes((0, HALF_D // 2), 4 * SHARE, at), m_copies[3 + i], at
        )
    resident((2, 3))

    for slot in range(4):
        for pair in m_copies[slot:] if slot == 3 else m_copies[slot:slot + 1]:
            wait_pair(pair)
        lat[origin[slot]] = lat[origin[slot]] + from_code(mpr[slot]) * msr[slot]
    whole = lat[...].reshape(KVW, TOK)
    latent = whole[:LATW]
    inverse = lax.rsqrt(jnp.sum(latent * latent, axis=0, keepdims=True) / LATW + eps_norm)
    gain_cols = jnp.transpose(jnp.broadcast_to(gain[...], (128, LATW)))
    for j in range(TOK // 128):
        at = slice(j * 128, j * 128 + 128)
        rows[:LATW, at] = (latent[:, at] * inverse[:, at] * gain_cols).astype(BF16)
    first, second = whole[LATW:LATW + ROPEW // 2], whole[LATW + ROPEW // 2:]
    rows[LATW:LATW + ROPEW // 2, :] = (first * cosine[...] - second * sine[...]).astype(BF16)
    rows[LATW + ROPEW // 2:KVW, :] = (first * sine[...] + second * cosine[...]).astype(BF16)

    slot_at = lax.broadcasted_iota(I32, (CAPTOK, TOK), 0)

    def pack_for(to):
        chosen = ((slot_at + to * CAPTOK) == tok[...]).astype(F32).astype(BF16)
        page_rows = nt(chosen, rows[...])
        empty = page_rows[:, KVW + USED:KVW + USED + 1] < 0.5
        column = lax.broadcasted_iota(I32, (CAPTOK, KVX), 1)
        return jnp.where((column == KVW) & empty, 1.0, page_rows).astype(BF16)

    first, second = pl.ds(0, HALF), pl.ds(HALF, HALF)
    a_p = [link(packed.at[0, at], arr.at[part, c], dev_zp) for at, part in ((first, 2), (second, 4))]
    a_m = [link(packed.at[1, at], arr.at[part, c], dev_zm) for at, part in ((first, 3), (second, 5))]
    a_r0 = link(packed.at[2, first], relay.at[0], dev_zp)
    a_r1 = link(packed.at[2, second], relay.at[1], dev_zm)
    a_f0 = link(relay.at[0], arr.at[6, c], dev_zp)
    a_f1 = link(relay.at[1], arr.at[7, c], dev_zm)
    a_share = [link(arr.at[part, c], arr.at[part, c], dev_sib) for part in range(8)]
    packed[0] = pack_for(lax.rem(b + 1, 4))
    go(a_p[0])
    packed[1] = pack_for(lax.rem(b + 3, 4))
    go(a_m[0])
    packed[2] = pack_for(lax.rem(b + 2, 4))
    go(a_r0)
    go(a_r1)
    go(a_p[1])
    go(a_m[1])
    own_pages = pack_for(b)
    arr[0, c] = own_pages[:HALF]
    go(a_share[0])
    arr[1, c] = own_pages[HALF:]
    go(a_share[1])

    def swap(copies, parts):
        for copy, part in zip(copies, parts):
            copy.wait_recv()
            go(a_share[part])

    def ready(parts):
        for part in parts:
            a_share[part].wait_recv()

    def turn_values(first, last):
        size = (last + 1 - first) * CAPTOK
        values = arr[first:last + 1].reshape(size, KVX)[:, :LATW]
        vt[:, first * CAPTOK:first * CAPTOK + size] = jnp.transpose(values)

    def pages_step(request, count, first, last):
        size, at = (last + 1 - first) * CAPTOK, columns(request, count)
        keys = arr[first:last + 1].reshape(size, KVX)
        score = nt(keys, qbuf[request:request + count].reshape(count * QROWS, KVX))
        old = ms[:, at]
        top = jnp.maximum(old, jnp.max(score, axis=0, keepdims=True))
        shrink = jnp.exp2((old - top) * log2_scale)
        w = weigh(score, top)
        total = ls[:, at] * shrink + jnp.sum(w, axis=0, keepdims=True)
        value = acc[:, at] * shrink + nn(vt[:, first * CAPTOK:first * CAPTOK + size], w.astype(BF16))
        return value, top, total

    def pages_of(request, count, first, last):
        at = columns(request, count)
        acc[:, at], ms[:, at], ls[:, at] = pages_step(request, count, first, last)

    ready((0, 1))
    turn_values(0, 1)
    pages_of(0, 4, 0, 1)
    swap((a_p[0], a_m[0]), (2, 3))
    a_r0.wait_recv()
    go(a_f0)
    a_r1.wait_recv()
    go(a_f1)
    ready((2, 3))
    turn_values(2, 3)
    pages_of(0, 2, 2, 3)
    swap((a_p[1], a_m[1]), (4, 5))
    ready((4, 5))
    turn_values(4, 5)
    swap((a_f0, a_f1), (6, 7))
    pages_of(0, 2, 4, 5)
    ready((6, 7))
    turn_values(6, 7)

    def merge(parts):
        top = parts[0][1][0]
        for _, stat in parts[1:]:
            top = jnp.maximum(top, stat[0])
        value, total = 0.0, 0.0
        for coded, stat in parts:
            factor = jnp.exp2(stat[0] - top)
            value = value + from_code(coded) * factor
            total = total + factor * stat[1]
        return value, top, total

    def put(coded_ref, stat_ref, value, top, total):
        coded, scale = code(value, 0)
        coded_ref[...] = to_code(coded).reshape(coded_ref.shape)
        stat_ref[0] = top + jnp.log(scale) * log2_e
        stat_ref[1] = total / scale

    yp, ym, yy = lax.rem(y + 1, 4), lax.rem(y + 3, 4), lax.rem(y + 2, 4)
    first_y = used[0]

    def y_pair(r, k):
        pairs = (
            (osend.at[r, yy, 0], ostat.at[r], 0, dev_yp),
            (osend.at[r, yy, 1], ostat.at[r], 1, dev_ym),
            (osend.at[r, yp, 1], ostat.at[r], 2, dev_yp),
            (osend.at[r, ym, 0], ostat.at[r], 3, dev_ym),
            (rsend.at[r, 0], rstat.at[r, 0], 4, dev_yp),
            (rsend.at[r, 1], rstat.at[r, 1], 5, dev_ym),
        )
        data, stat, _, dev = pairs[k]
        return (
            link_at(first_y + 18 * r + 2 * k, data, ybuf.at[r, k], dev),
            link_at(first_y + 18 * r + 2 * k + 1, stat, ystat.at[r, k], dev),
        )

    def last_pair(r, k):
        half, core, dev = ((1 - xh, c, dev_x), (1 - xh, 1 - c, dev_x_sib), (xh, 1 - c, dev_sib))[k]
        return (
            link_at(first_y + 18 * r + 12 + 2 * k, mbuf.at[r, half, core], fbuf.at[r, k], dev),
            link_at(first_y + 18 * r + 13 + 2 * k, mstat.at[r, half], fstat.at[r, k], dev),
        )

    def start_pair(pair):
        pair[0].start()
        pair[1].start()

    def relay_sums(r, carry):
        for k, to in ((0, yp), (1, ym)):
            wait_pair(y_pair(r, k))
            put(rsend.at[r, k], rstat.at[r, k], *merge([
                (osend[r, to, k], ostat[r]), (ybuf[r, k], ystat[r, k]),
            ]))
            start_pair(y_pair(r, 4 + k))
        return carry

    for first_request, count, first in ((0, 1, 6), (1, 1, 6), (2, 2, 2)):
        value, top, total = pages_step(first_request, count, first, 7)
        coded, scale = code(value, 0)
        coded, top, total = to_code(coded), top * log2_scale + jnp.log(scale) * log2_e, total / scale
        for r in range(first_request, first_request + count):
            at = columns(r - first_request)
            osend[r] = coded[:, at].reshape(4, 2, 64, QROWS)
            ostat[r, 0] = top[:, at]
            ostat[r, 1] = total[:, at]
            for k in range(4):
                start_pair(y_pair(r, k))

    def sums_over_y(r, carry):
        for k in range(2, 6):
            wait_pair(y_pair(r, k))
        for h, (one, two) in enumerate(((3, 4), (2, 5))):
            put(mbuf.at[r, h], mstat.at[r, h], *merge([
                (osend[r, y, h], ostat[r]), (ybuf[r, one], ystat[r, one]), (ybuf[r, two], ystat[r, two]),
            ]))
        for k in (1, 0, 2):
            start_pair(last_pair(r, k))
        return carry

    def out_copy(wanted):
        return pltpu.make_async_copy(out.at[:, wanted], out_hbm.at[:, wanted], loc.at[13 + wanted])

    def last_sums(r, carry):
        for k in range(3):
            wait_pair(last_pair(r, k))
        own, other = c * NR + r, (1 - c) * NR + r
        for wanted, parts in (
            (own, [(mbuf[r, xh, c], mstat[r, xh]), (fbuf[r, 0], fstat[r, 0])]),
            (other, [(fbuf[r, 2], fstat[r, 2]), (fbuf[r, 1], fstat[r, 1])]),
        ):
            value, _, total = merge(parts)
            value = value / total
            for step in range(4):
                out[step, wanted] = value[:, 64 * step:64 * step + 64]
            out_copy(wanted).start()
        return carry

    def finish(r, carry):
        for pair in [y_pair(r, k) for k in range(6)] + [last_pair(r, k) for k in range(3)]:
            pair[0].wait_send()
            pair[1].wait_send()
        return carry

    lax.fori_loop(0, NR, relay_sums, 0)
    for stage in (sums_over_y, last_sums, finish):
        lax.fori_loop(0, NR, stage, 0)
    for wanted in range(2 * NR):
        out_copy(wanted).wait()
    for copy in started:
        copy.wait_send()


LINKS = 144


def tables():
    half = ROPEW // 2
    frequency = rope_base ** (-np.arange(half, dtype=np.float32) / np.float32(half))
    angles = np.arange(TOK, dtype=np.float32)[None, :] * frequency.astype(np.float32)[:, None]
    return np.cos(angles).astype(np.float32), np.sin(angles).astype(np.float32)


def on_device(hidden, kv_down, kv_gain, page_owner, page_request, queries, cache, lengths):
    cosine, sine = tables()
    anywhere = pl.BlockSpec(memory_space=pl.ANY)
    sums = pl.pallas_call(
        kernel,
        out_shape=jax.ShapeDtypeStruct((4, 2 * NR, 32, 64), F32),
        in_specs=[anywhere] * 10,
        out_specs=anywhere,
        scratch_shapes=[
            pltpu.VMEM((1, LATW), F32),
            pltpu.SMEM((1, PAGES), I32),
            pltpu.SMEM((PAGES,), I32),
            pltpu.SMEM((2 * NR,), I32),
            pltpu.VMEM((ROPEW // 2, TOK), F32),
            pltpu.VMEM((ROPEW // 2, TOK), F32),
            pltpu.VMEM((4, 2 * NR, 32, 64), F32),
            pltpu.VMEM((TOK, HALF_D), BF16),
            pltpu.VMEM((4, BLK, HALF_D), BF16),
            pltpu.VMEM((4, BLK, TOK), F32),
            pltpu.VMEM((4, BLK, TOK), I16),
            pltpu.VMEM((4, BLK, TOK), I16),
            pltpu.VMEM((4, 1, TOK), F32),
            pltpu.VMEM((4, 1, TOK), F32),
            pltpu.VMEM((KVX, TOK), BF16),
            pltpu.VMEM((3, CAPTOK, KVX), BF16),
            pltpu.VMEM((2, HALF, KVX), BF16),
            pltpu.VMEM((8, 2, HALF, KVX), BF16),
            pltpu.VMEM((1, TOK), I32),
            pltpu.VMEM((LATW, 8 * CAPTOK), BF16),
            pltpu.VMEM((NR, 4, 64, KVW), BF16),
            pltpu.VMEM((NR, QROWS, KVX), BF16),
            pltpu.VMEM((2, NR, KVW, CTXD), BF16),
            pltpu.VMEM((LATW, NR * QROWS), F32),
            pltpu.VMEM((1, NR * QROWS), F32),
            pltpu.VMEM((1, NR * QROWS), F32),
            pltpu.VMEM((NR, 4, 2, 64, QROWS), I16),
            pltpu.VMEM((NR, 2, 1, QROWS), F32),
            pltpu.VMEM((NR, 6, 64, QROWS), I16),
            pltpu.VMEM((NR, 6, 2, 1, QROWS), F32),
            pltpu.VMEM((NR, 2, 64, QROWS), I16),
            pltpu.VMEM((NR, 2, 2, 1, QROWS), F32),
            pltpu.VMEM((NR, 2, 2, 32, QROWS), I16),
            pltpu.VMEM((NR, 2, 2, 1, QROWS), F32),
            pltpu.VMEM((NR, 3, 32, QROWS), I16),
            pltpu.VMEM((NR, 3, 2, 1, QROWS), F32),
            pltpu.SemaphoreType.DMA((13 + 2 * NR,)),
            pltpu.SemaphoreType.DMA((LINKS,)),
            pltpu.SemaphoreType.DMA((LINKS,)),
        ],
        compiler_params=pltpu.CompilerParams(
            collective_id=0, has_side_effects=True, vmem_limit_bytes=56 * 1024 * 1024
        ),
        cost_estimate=pl.CostEstimate(flops=7_500_000_000, bytes_accessed=12_000_000, transcendentals=3_000_000),
    )(
        hidden, kv_down.T, kv_gain.reshape(1, LATW), page_owner.T, page_request, queries, cache.transpose(0, 2, 1), lengths,
        jnp.asarray(cosine), jnp.asarray(sine),
    )
    return sums.transpose(0, 1, 3, 2)


def solution(mesh):
    return jax.shard_map(
        on_device,
        mesh=mesh,
        in_specs=(
            P(("seq", "batch"), "mp"),
            P("mp", "batch"),
            P(),
            P(("seq", "batch"), None),
            P(("seq", "batch")),
            P(None, "batch", "mp", None),
            P("batch", "seq", None),
            P("batch"),
        ),
        out_specs=P(None, "batch", "mp", "seq"),
        check_vma=False,
    )
```

```python
import jax
import jax.numpy as jnp
import numpy as np
from jax import lax
from jax.experimental import pallas as pl
from jax.experimental.pallas import tpu as pltpu
from jax.sharding import PartitionSpec as P

MESH = pl.DeviceIdType.MESH
F32, BF16, I32, I16 = jnp.float32, jnp.bfloat16, jnp.int32, jnp.int16

eps_norm = 1e-06
score_scale = 192.0 ** (-0.5)
log2_e = 1.4426950408889634
log2_scale = score_scale * log2_e
rope_base = 10000.0
masked_value = -1e30
floor_value = -1e29
code_top = 32767.0

TOK, HALF_D, KVW, LATW, ROPEW = 384, 3584, 576, 512, 64
USED = 16
LABELS = 64
KVX = KVW + LABELS
BLK = 144
SHARE, DIRECT = 256, 384
CAPTOK = 192
HALF = CAPTOK // 2
PAGES, PAGE, CAP = 24, 16, 12
QROWS = 256
CTXD = 512
NR = 4


def nt(a, b):
    return lax.dot_general(a, b, (((1,), (1,)), ((), ())), preferred_element_type=F32)


def nn(a, b):
    return jnp.dot(a, b, preferred_element_type=F32)


def kernel(
    hidden, kv_down, gain_in, owner_in, request_in, queries, cache, lengths_in, cosine_in, sine_in,
    out_hbm,
    gain, owner, request, lengths, cosine, sine, out,
    hid, kvt, lat, mps, mpr, mss, msr, rows, packed, relay, arr, tok,
    vt, qraw, qbuf, kbuf, acc, ms, ls, osend, ostat, ybuf, ystat, rsend, rstat, mbuf, mstat, fbuf, fstat,
    loc, send, recv,
):
    s, b, p = lax.axis_index("seq"), lax.axis_index("batch"), lax.axis_index("mp")
    c = lax.rem(s, 2)
    sib = s + 1 - 2 * c
    y = lax.div(s, 4)
    in_y = lax.rem(s, 4)
    xh = lax.rem(lax.div(s, 2), 2)
    dev_zp = (s, lax.rem(b + 1, 4), p)
    dev_zm = (s, lax.rem(b + 3, 4), p)
    dev_zz = (s, lax.rem(b + 2, 4), p)
    dev_mp = (s, b, 1 - p)
    dev_sib = (sib, b, p)
    dev_yp = (lax.rem(y + 1, 4) * 4 + in_y, b, p)
    dev_ym = (lax.rem(y + 3, 4) * 4 + in_y, b, p)
    dev_x = (s + 2 - 4 * xh, b, p)
    dev_x_sib = (sib + 2 - 4 * xh, b, p)

    used = [0]
    started = []

    def link(src, dst, dev):
        used[0] += 1
        return link_at(used[0] - 1, src, dst, dev)

    def link_at(i, src, dst, dev):
        return pltpu.make_async_remote_copy(
            src_ref=src, dst_ref=dst, send_sem=send.at[i], recv_sem=recv.at[i],
            device_id=dev, device_id_type=MESH,
        )

    def go(copy):
        copy.start()
        started.append(copy)

    def code(value, axis):
        most = jnp.max(jnp.abs(value), axis=axis, keepdims=True)
        most = jnp.maximum(most, 1e-25)
        return jnp.round(value * (code_top / most)), most * (1.0 / code_top)

    def to_code(value):
        return value.astype(I32).astype(I16)

    def from_code(coded):
        return coded.astype(I32).astype(F32)

    def go_pair(pair):
        go(pair[0])
        go(pair[1])

    def wait_pair(pair):
        pair[0].wait_recv()
        pair[1].wait_recv()

    barrier = pltpu.get_barrier_semaphore()
    for dev in (dev_zp, dev_zm, dev_zz, dev_mp, dev_sib, dev_yp, dev_ym, dev_x, dev_x_sib):
        pl.semaphore_signal(barrier, inc=1, device_id=dev, device_id_type=MESH)

    small = [
        pltpu.make_async_copy(src, dst, loc.at[7 + i])
        for i, (src, dst) in enumerate((
            (owner_in, owner), (request_in, request), (lengths_in, lengths), (gain_in, gain), (cosine_in, cosine),
            (sine_in, sine),
        ))
    ]
    load_kv = pltpu.make_async_copy(kv_down, kvt.at[0], loc.at[0])
    load_hid = pltpu.make_async_copy(hidden, hid, loc.at[1])
    load_q = [pltpu.make_async_copy(queries.at[step, pl.ds(c * NR, NR)], qraw.at[:, step], loc.at[2 + step]) for step in range(4)]
    load_cache = pltpu.make_async_copy(cache.at[pl.ds(c * NR, NR)], kbuf.at[0], loc.at[6])
    for copy in [load_hid, load_kv] + small:
        copy.start()

    pl.semaphore_wait(barrier, 9)

    base = c * (HALF_D // 2)

    def lanes(start, size):
        return pl.ds(pl.multiple_of(base + start, 128), size)

    def kv_link(slot, to_slot, at, dev):
        return link(kvt.at[slot, :, at], kvt.at[to_slot, :, at], dev)

    def first_link(to_slot, at, dev):
        return link(kv_down.at[:, at], kvt.at[to_slot, :, at], dev)

    def part_of(k, first=0, size=SHARE):
        return lanes(lax.rem(y + k, 4) * SHARE + first, size)

    low, high = lanes(4 * SHARE, DIRECT), lanes(4 * SHARE + DIRECT, DIRECT)
    mine = part_of(0)
    s_p, s_m = first_link(1, mine, dev_zp), first_link(2, mine, dev_zm)
    d_p0, d_m1 = first_link(1, low, dev_zp), first_link(2, high, dev_zm)
    d_p1, d_m0 = first_link(1, high, dev_zp), first_link(2, low, dev_zm)
    for copy in (s_p, s_m, d_p0, d_m1):
        go(copy)
    for copy in load_q + [load_cache]:
        copy.start()
    cache_out = link(cache.at[pl.ds((1 - c) * NR, NR)], kbuf.at[1], dev_sib)
    go(cache_out)
    sf_p, sf_m = (
        kv_link(1, 3, part_of(0, 0, SHARE // 2), dev_zp),
        kv_link(2, 3, part_of(0, SHARE // 2, SHARE // 2), dev_zm),
    )
    df_p, df_m = kv_link(1, 3, low, dev_zp), kv_link(2, 3, high, dev_zm)
    near_p = [None] + [kv_link(slot, slot, mine, dev_yp) for slot in (1, 2, 3)]
    near_m = [None] + [kv_link(slot, slot, mine, dev_ym) for slot in (1, 2, 3)]
    far = [None] + [
        (
            kv_link(slot, slot, part_of(3, 0, SHARE // 2), dev_yp),
            kv_link(slot, slot, part_of(1, SHARE // 2, SHARE // 2), dev_ym),
        )
        for slot in (1, 2, 3)
    ]
    share_s = [None] + [kv_link(slot, slot, lanes(0, 4 * SHARE), dev_sib) for slot in (1, 2, 3)]
    share_d = [None] + [kv_link(slot, slot, lanes(4 * SHARE, 2 * DIRECT), dev_sib) for slot in (1, 2, 3)]

    origin = [lax.rem(b + ahead, 4) for ahead in (0, 3, 1, 2)]
    m_copies = [
        (link(mps.at[slot], mpr.at[slot], dev_mp), link(mss.at[slot], msr.at[slot], dev_mp)) for slot in range(3)
    ]
    tails = (slice(0, 256), slice(256, TOK))
    for at in tails:
        at = pl.ds(at.start, at.stop - at.start)
        m_copies.append((
            link(mps.at[3, :, at], mpr.at[3, :, at], dev_mp), link(mss.at[3, :, at], msr.at[3, :, at], dev_mp),
        ))

    def send_part(slot, part, copies, at=slice(None)):
        lat[origin[slot], :, at] = part
        coded, scale = code(part, 0)
        mps[slot, :, at] = to_code(coded)
        mss[slot, :, at] = scale
        go_pair(copies)

    def weigh(score, top):
        return jnp.exp2(score * log2_scale - top * log2_scale)

    def fold(w):
        total = w[:, :128]
        for j in range(1, w.shape[1] // 128):
            total = total + w[:, j * 128:j * 128 + 128]
        return total

    def peak(score):
        most = score[:, :128]
        for j in range(1, score.shape[1] // 128):
            most = jnp.maximum(most, score[:, j * 128:j * 128 + 128])
        return most

    def columns(first, count=1):
        return slice(first * QROWS, (first + count) * QROWS)

    def resident(requests):
        at = lax.broadcasted_iota(I32, (1, CTXD), 1)
        scores = [
            [
                jnp.where(at + place * CTXD < lengths[c * NR + r], nn(qbuf[r, :, :KVW], kbuf[part, r]), masked_value)
                for part, place in enumerate((s, sib))
            ]
            for r in requests
        ]
        weights = []
        for r, (score0, score1) in zip(requests, scores):
            top = jnp.max(jnp.maximum(peak(score0), peak(score1)), axis=1, keepdims=True)
            top = jnp.maximum(top, floor_value)
            w0, w1 = weigh(score0, top), weigh(score1, top)
            ms[:, columns(r)] = jnp.transpose(jnp.broadcast_to(top, (QROWS, 128)))[0:1]
            ls[:, columns(r)] = jnp.sum(jnp.transpose(fold(w0) + fold(w1)), axis=0, keepdims=True)
            weights.append((w0.astype(BF16), w1.astype(BF16)))
        for r, (w0, w1) in zip(requests, weights):
            acc[:, columns(r)] = nt(kbuf[0, r, :LATW, :], w0) + nt(kbuf[1, r, :LATW, :], w1)

    load_hid.wait()
    load_kv.wait()
    send_part(0, nt(kvt[0], hid[...]), m_copies[0])
    s_p.wait_recv()
    go(sf_p)
    go(near_p[1])
    go(near_m[1])
    s_m.wait_recv()
    go(sf_m)
    go(near_p[2])
    go(near_m[2])
    go(d_p1)
    go(d_m0)

    for copy in small:
        copy.wait()
    token = lax.broadcasted_iota(I32, (1, TOK), 1)
    token_page = lax.shift_right_logical(token, 4)
    dest = jnp.zeros((1, TOK), I32)
    asked = jnp.zeros((1, TOK), I32)
    counts = [jnp.int32(0)] * 4
    for page in range(PAGES):
        to = owner[0, page]
        rank = jnp.where(to == 0, counts[0], jnp.where(to == 1, counts[1], jnp.where(to == 2, counts[2], counts[3])))
        counts = [counts[o] + (to == o).astype(I32) for o in range(4)]
        dest = jnp.where(token_page == page, (to * CAP + rank) * PAGE, dest)
        asked = jnp.where(token_page == page, request[page] + 1, asked)
    dest = dest + lax.bitwise_and(token, 15)
    tok[...] = dest

    label_row = lax.broadcasted_iota(I32, (LABELS, TOK), 0)
    rows[KVW:, :] = ((label_row == asked) | (label_row == USED)).astype(F32).astype(BF16)

    d_p0.wait_recv()
    go(df_p)
    d_m1.wait_recv()
    go(df_m)

    def pass_on(slot):
        near_p[slot].wait_recv()
        go(far[slot][0])
        near_m[slot].wait_recv()
        go(far[slot][1])

    def swap_shared(slot):
        far[slot][0].wait_recv()
        far[slot][1].wait_recv()
        go(share_s[slot])

    pass_on(1)
    sf_p.wait_recv()
    sf_m.wait_recv()
    go(near_p[3])
    go(near_m[3])

    for copy in load_q:
        copy.wait()
    load_cache.wait()
    label_at = lax.broadcasted_iota(I32, (QROWS, LABELS), 1)

    def fill(r, carry):
        qbuf[r, :, :KVW] = qraw[r].reshape(QROWS, KVW)
        opened = (label_at == c * NR + r + 1) | (label_at == USED)
        qbuf[r, :, KVW:] = jnp.where(opened, 0.0, masked_value).astype(BF16)
        return carry

    lax.fori_loop(0, NR, fill, 0)
    cache_out.wait_recv()
    resident((0,))

    pass_on(2)
    d_p1.wait_recv()
    go(share_d[1])
    d_m0.wait_recv()
    go(share_d[2])
    swap_shared(1)
    resident((1,))

    pass_on(3)
    swap_shared(2)
    share_d[1].wait_recv()
    share_s[1].wait_recv()
    send_part(1, nt(kvt[1], hid[...]), m_copies[1])
    df_p.wait_recv()
    df_m.wait_recv()
    go(share_d[3])
    swap_shared(3)
    share_d[2].wait_recv()
    share_s[2].wait_recv()
    send_part(2, nt(kvt[2], hid[...]), m_copies[2])

    def over_lanes(starts, size, at):
        return sum(nt(kvt[3, :, start:start + size], hid[at, start:start + size]) for start in starts)

    share_d[3].wait_recv()
    lat[origin[3]] = over_lanes((4 * SHARE, HALF_D // 2 + 4 * SHARE), 2 * DIRECT, slice(None))
    share_s[3].wait_recv()
    for i, at in enumerate(tails):
        send_part(
            3, lat[origin[3], :, at] + over_lanes((0, HALF_D // 2), 4 * SHARE, at), m_copies[3 + i], at
        )
    resident((2, 3))

    for slot in range(4):
        for pair in m_copies[slot:] if slot == 3 else m_copies[slot:slot + 1]:
            wait_pair(pair)
        lat[origin[slot]] = lat[origin[slot]] + from_code(mpr[slot]) * msr[slot]
    whole = lat[...].reshape(KVW, TOK)
    latent = whole[:LATW]
    inverse = lax.rsqrt(jnp.sum(latent * latent, axis=0, keepdims=True) / LATW + eps_norm)
    gain_cols = jnp.transpose(jnp.broadcast_to(gain[...], (128, LATW)))
    for j in range(TOK // 128):
        at = slice(j * 128, j * 128 + 128)
        rows[:LATW, at] = (latent[:, at] * inverse[:, at] * gain_cols).astype(BF16)
    first, second = whole[LATW:LATW + ROPEW // 2], whole[LATW + ROPEW // 2:]
    rows[LATW:LATW + ROPEW // 2, :] = (first * cosine[...] - second * sine[...]).astype(BF16)
    rows[LATW + ROPEW // 2:KVW, :] = (first * sine[...] + second * cosine[...]).astype(BF16)

    slot_at = lax.broadcasted_iota(I32, (CAPTOK, TOK), 0)

    def pack_for(to):
        chosen = ((slot_at + to * CAPTOK) == tok[...]).astype(F32).astype(BF16)
        page_rows = nt(chosen, rows[...])
        empty = page_rows[:, KVW + USED:KVW + USED + 1] < 0.5
        column = lax.broadcasted_iota(I32, (CAPTOK, KVX), 1)
        return jnp.where((column == KVW) & empty, 1.0, page_rows).astype(BF16)

    first, second = pl.ds(0, HALF), pl.ds(HALF, HALF)
    a_p = [link(packed.at[0, at], arr.at[part, c], dev_zp) for at, part in ((first, 2), (second, 4))]
    a_m = [link(packed.at[1, at], arr.at[part, c], dev_zm) for at, part in ((first, 3), (second, 5))]
    a_r0 = link(packed.at[2, first], relay.at[0], dev_zp)
    a_r1 = link(packed.at[2, second], relay.at[1], dev_zm)
    a_f0 = link(relay.at[0], arr.at[6, c], dev_zp)
    a_f1 = link(relay.at[1], arr.at[7, c], dev_zm)
    a_share = [link(arr.at[part, c], arr.at[part, c], dev_sib) for part in range(8)]
    packed[0] = pack_for(lax.rem(b + 1, 4))
    go(a_p[0])
    packed[1] = pack_for(lax.rem(b + 3, 4))
    go(a_m[0])
    packed[2] = pack_for(lax.rem(b + 2, 4))
    go(a_r0)
    go(a_r1)
    go(a_p[1])
    go(a_m[1])
    own_pages = pack_for(b)
    arr[0, c] = own_pages[:HALF]
    go(a_share[0])
    arr[1, c] = own_pages[HALF:]
    go(a_share[1])

    def swap(copies, parts):
        for copy, part in zip(copies, parts):
            copy.wait_recv()
            go(a_share[part])

    def ready(parts):
        for part in parts:
            a_share[part].wait_recv()

    def turn_values(first, last):
        size = (last + 1 - first) * CAPTOK
        values = arr[first:last + 1].reshape(size, KVX)[:, :LATW]
        vt[:, first * CAPTOK:first * CAPTOK + size] = jnp.transpose(values)

    def pages_step(request, count, first, last, between=lambda: None):
        size, at = (last + 1 - first) * CAPTOK, columns(request, count)
        keys = arr[first:last + 1].reshape(size, KVX)
        score = nt(keys, qbuf[request:request + count].reshape(count * QROWS, KVX))
        old = ms[:, at]
        top = jnp.maximum(old, jnp.max(score, axis=0, keepdims=True))
        shrink = jnp.exp2((old - top) * log2_scale)
        w = weigh(score, top)
        total = ls[:, at] * shrink + jnp.sum(w, axis=0, keepdims=True)
        between()
        value = acc[:, at] * shrink + nn(vt[:, first * CAPTOK:first * CAPTOK + size], w.astype(BF16))
        return value, top, total

    def pages_of(request, count, first, last):
        at = columns(request, count)
        acc[:, at], ms[:, at], ls[:, at] = pages_step(request, count, first, last)

    ready((0, 1))
    turn_values(0, 1)
    pages_of(0, 4, 0, 1)
    swap((a_p[0], a_m[0]), (2, 3))
    a_r0.wait_recv()
    go(a_f0)
    a_r1.wait_recv()
    go(a_f1)
    ready((2, 3))
    turn_values(2, 3)
    pages_of(0, 4, 2, 3)
    swap((a_p[1], a_m[1]), (4, 5))
    ready((4, 5))
    turn_values(4, 5)
    swap((a_f0, a_f1), (6, 7))
    pages_of(0, 2, 4, 5)
    ready((6, 7))
    turn_values(6, 7)

    def merge(parts):
        top = parts[0][1][0]
        for _, stat in parts[1:]:
            top = jnp.maximum(top, stat[0])
        value, total = 0.0, 0.0
        for coded, stat in parts:
            factor = jnp.exp2(stat[0] - top)
            value = value + from_code(coded) * factor
            total = total + factor * stat[1]
        return value, top, total

    def put(coded_ref, stat_ref, value, top, total):
        coded, scale = code(value, 0)
        coded_ref[...] = to_code(coded).reshape(coded_ref.shape)
        stat_ref[0] = top + jnp.log(scale) * log2_e
        stat_ref[1] = total / scale

    yp, ym, yy = lax.rem(y + 1, 4), lax.rem(y + 3, 4), lax.rem(y + 2, 4)
    first_y = used[0]

    def y_pair(r, k):
        pairs = (
            (osend.at[r, yy, 0], ostat.at[r], 0, dev_yp),
            (osend.at[r, yy, 1], ostat.at[r], 1, dev_ym),
            (osend.at[r, yp, 1], ostat.at[r], 2, dev_yp),
            (osend.at[r, ym, 0], ostat.at[r], 3, dev_ym),
            (rsend.at[r, 0], rstat.at[r, 0], 4, dev_yp),
            (rsend.at[r, 1], rstat.at[r, 1], 5, dev_ym),
        )
        data, stat, _, dev = pairs[k]
        return (
            link_at(first_y + 18 * r + 2 * k, data, ybuf.at[r, k], dev),
            link_at(first_y + 18 * r + 2 * k + 1, stat, ystat.at[r, k], dev),
        )

    def last_pair(r, k):
        half, core, dev = ((1 - xh, c, dev_x), (1 - xh, 1 - c, dev_x_sib), (xh, 1 - c, dev_sib))[k]
        return (
            link_at(first_y + 18 * r + 12 + 2 * k, mbuf.at[r, half, core], fbuf.at[r, k], dev),
            link_at(first_y + 18 * r + 13 + 2 * k, mstat.at[r, half], fstat.at[r, k], dev),
        )

    def start_pair(pair):
        pair[0].start()
        pair[1].start()

    def relay_sums(r, carry):
        for k, to in ((0, yp), (1, ym)):
            wait_pair(y_pair(r, k))
            put(rsend.at[r, k], rstat.at[r, k], *merge([
                (osend[r, to, k], ostat[r]), (ybuf[r, k], ystat[r, k]),
            ]))
            start_pair(y_pair(r, 4 + k))
        return carry

    for first_request, count, first in ((0, 1, 6), (1, 1, 6), (2, 2, 4)):
        relay = (lambda: lax.fori_loop(0, 2, relay_sums, 0)) if first_request == 2 else (lambda: None)
        value, top, total = pages_step(first_request, count, first, 7, relay)
        coded, scale = code(value, 0)
        coded, top, total = to_code(coded), top * log2_scale + jnp.log(scale) * log2_e, total / scale
        for r in range(first_request, first_request + count):
            at = columns(r - first_request)
            osend[r] = coded[:, at].reshape(4, 2, 64, QROWS)
            ostat[r, 0] = top[:, at]
            ostat[r, 1] = total[:, at]
            for k in range(4):
                start_pair(y_pair(r, k))

    def sums_over_y(r, carry):
        for k in range(2, 6):
            wait_pair(y_pair(r, k))
        for h, (one, two) in enumerate(((3, 4), (2, 5))):
            put(mbuf.at[r, h], mstat.at[r, h], *merge([
                (osend[r, y, h], ostat[r]), (ybuf[r, one], ystat[r, one]), (ybuf[r, two], ystat[r, two]),
            ]))
        for k in (1, 0, 2):
            start_pair(last_pair(r, k))
        return carry

    def out_copy(wanted):
        return pltpu.make_async_copy(out.at[:, wanted], out_hbm.at[:, wanted], loc.at[13 + wanted])

    def last_sums(r, carry):
        for k in range(3):
            wait_pair(last_pair(r, k))
        own, other = c * NR + r, (1 - c) * NR + r
        for wanted, parts in (
            (own, [(mbuf[r, xh, c], mstat[r, xh]), (fbuf[r, 0], fstat[r, 0])]),
            (other, [(fbuf[r, 2], fstat[r, 2]), (fbuf[r, 1], fstat[r, 1])]),
        ):
            value, _, total = merge(parts)
            value = value / total
            for step in range(4):
                out[step, wanted] = value[:, 64 * step:64 * step + 64]
            out_copy(wanted).start()
        return carry

    def finish(r, carry):
        for pair in [y_pair(r, k) for k in range(6)] + [last_pair(r, k) for k in range(3)]:
            pair[0].wait_send()
            pair[1].wait_send()
        return carry

    lax.fori_loop(2, NR, relay_sums, 0)
    for stage in (sums_over_y, last_sums, finish):
        lax.fori_loop(0, NR, stage, 0)
    for wanted in range(2 * NR):
        out_copy(wanted).wait()
    for copy in started:
        copy.wait_send()


LINKS = 144


def tables():
    half = ROPEW // 2
    frequency = rope_base ** (-np.arange(half, dtype=np.float32) / np.float32(half))
    angles = np.arange(TOK, dtype=np.float32)[None, :] * frequency.astype(np.float32)[:, None]
    return np.cos(angles).astype(np.float32), np.sin(angles).astype(np.float32)


def on_device(hidden, kv_down, kv_gain, page_owner, page_request, queries, cache, lengths):
    cosine, sine = tables()
    anywhere = pl.BlockSpec(memory_space=pl.ANY)
    sums = pl.pallas_call(
        kernel,
        out_shape=jax.ShapeDtypeStruct((4, 2 * NR, 32, 64), F32),
        in_specs=[anywhere] * 10,
        out_specs=anywhere,
        scratch_shapes=[
            pltpu.VMEM((1, LATW), F32),
            pltpu.SMEM((1, PAGES), I32),
            pltpu.SMEM((PAGES,), I32),
            pltpu.SMEM((2 * NR,), I32),
            pltpu.VMEM((ROPEW // 2, TOK), F32),
            pltpu.VMEM((ROPEW // 2, TOK), F32),
            pltpu.VMEM((4, 2 * NR, 32, 64), F32),
            pltpu.VMEM((TOK, HALF_D), BF16),
            pltpu.VMEM((4, BLK, HALF_D), BF16),
            pltpu.VMEM((4, BLK, TOK), F32),
            pltpu.VMEM((4, BLK, TOK), I16),
            pltpu.VMEM((4, BLK, TOK), I16),
            pltpu.VMEM((4, 1, TOK), F32),
            pltpu.VMEM((4, 1, TOK), F32),
            pltpu.VMEM((KVX, TOK), BF16),
            pltpu.VMEM((3, CAPTOK, KVX), BF16),
            pltpu.VMEM((2, HALF, KVX), BF16),
            pltpu.VMEM((8, 2, HALF, KVX), BF16),
            pltpu.VMEM((1, TOK), I32),
            pltpu.VMEM((LATW, 8 * CAPTOK), BF16),
            pltpu.VMEM((NR, 4, 64, KVW), BF16),
            pltpu.VMEM((NR, QROWS, KVX), BF16),
            pltpu.VMEM((2, NR, KVW, CTXD), BF16),
            pltpu.VMEM((LATW, NR * QROWS), F32),
            pltpu.VMEM((1, NR * QROWS), F32),
            pltpu.VMEM((1, NR * QROWS), F32),
            pltpu.VMEM((NR, 4, 2, 64, QROWS), I16),
            pltpu.VMEM((NR, 2, 1, QROWS), F32),
            pltpu.VMEM((NR, 6, 64, QROWS), I16),
            pltpu.VMEM((NR, 6, 2, 1, QROWS), F32),
            pltpu.VMEM((NR, 2, 64, QROWS), I16),
            pltpu.VMEM((NR, 2, 2, 1, QROWS), F32),
            pltpu.VMEM((NR, 2, 2, 32, QROWS), I16),
            pltpu.VMEM((NR, 2, 2, 1, QROWS), F32),
            pltpu.VMEM((NR, 3, 32, QROWS), I16),
            pltpu.VMEM((NR, 3, 2, 1, QROWS), F32),
            pltpu.SemaphoreType.DMA((13 + 2 * NR,)),
            pltpu.SemaphoreType.DMA((LINKS,)),
            pltpu.SemaphoreType.DMA((LINKS,)),
        ],
        compiler_params=pltpu.CompilerParams(
            collective_id=0, has_side_effects=True, vmem_limit_bytes=56 * 1024 * 1024
        ),
        cost_estimate=pl.CostEstimate(flops=7_500_000_000, bytes_accessed=12_000_000, transcendentals=3_000_000),
    )(
        hidden, kv_down.T, kv_gain.reshape(1, LATW), page_owner.T, page_request, queries, cache.transpose(0, 2, 1), lengths,
        jnp.asarray(cosine), jnp.asarray(sine),
    )
    return sums.transpose(0, 1, 3, 2)


def solution(mesh):
    return jax.shard_map(
        on_device,
        mesh=mesh,
        in_specs=(
            P(("seq", "batch"), "mp"),
            P("mp", "batch"),
            P(),
            P(("seq", "batch"), None),
            P(("seq", "batch")),
            P(None, "batch", "mp", None),
            P("batch", "seq", None),
            P("batch"),
        ),
        out_specs=P(None, "batch", "mp", "seq"),
        check_vma=False,
    )
```

```python
import jax
import jax.numpy as jnp
import numpy as np
from jax import lax
from jax.experimental import pallas as pl
from jax.experimental.pallas import tpu as pltpu
from jax.sharding import PartitionSpec as P

MESH = pl.DeviceIdType.MESH
F32, BF16, I32, I16 = jnp.float32, jnp.bfloat16, jnp.int32, jnp.int16

eps_norm = 1e-06
score_scale = 192.0 ** (-0.5)
log2_e = 1.4426950408889634
log2_scale = score_scale * log2_e
rope_base = 10000.0
masked_value = -1e30
floor_value = -1e29
code_top = 32767.0

TOK, HALF_D, KVW, LATW, ROPEW = 384, 3584, 576, 512, 64
USED = 16
LABELS = 64
KVX = KVW + LABELS
BLK = 144
SHARE, DIRECT = 256, 384
CAPTOK = 192
HALF = CAPTOK // 2
PAGES, PAGE, CAP = 24, 16, 12
QROWS = 256
CTXD = 512
NR = 4


def nt(a, b):
    return lax.dot_general(a, b, (((1,), (1,)), ((), ())), preferred_element_type=F32)


def nn(a, b):
    return jnp.dot(a, b, preferred_element_type=F32)


def kernel(
    hidden, kv_down, gain_in, owner_in, request_in, queries, cache, lengths_in, cosine_in, sine_in,
    out_hbm,
    gain, owner, request, lengths, cosine, sine, out,
    hid, kvt, lat, mps, mpr, mss, msr, rows, packed, relay, arr, tok,
    vt, qraw, qbuf, kbuf, acc, ms, ls, osend, ostat, ybuf, ystat, rsend, rstat, mbuf, mstat, fbuf, fstat,
    loc, send, recv,
):
    s, b, p = lax.axis_index("seq"), lax.axis_index("batch"), lax.axis_index("mp")
    c = lax.rem(s, 2)
    sib = s + 1 - 2 * c
    y = lax.div(s, 4)
    in_y = lax.rem(s, 4)
    xh = lax.rem(lax.div(s, 2), 2)
    dev_zp = (s, lax.rem(b + 1, 4), p)
    dev_zm = (s, lax.rem(b + 3, 4), p)
    dev_zz = (s, lax.rem(b + 2, 4), p)
    dev_mp = (s, b, 1 - p)
    dev_sib = (sib, b, p)
    dev_yp = (lax.rem(y + 1, 4) * 4 + in_y, b, p)
    dev_ym = (lax.rem(y + 3, 4) * 4 + in_y, b, p)
    dev_x = (s + 2 - 4 * xh, b, p)
    dev_x_sib = (sib + 2 - 4 * xh, b, p)

    used = [0]
    started = []

    def link(src, dst, dev):
        used[0] += 1
        return link_at(used[0] - 1, src, dst, dev)

    def link_at(i, src, dst, dev):
        return pltpu.make_async_remote_copy(
            src_ref=src, dst_ref=dst, send_sem=send.at[i], recv_sem=recv.at[i],
            device_id=dev, device_id_type=MESH,
        )

    def go(copy):
        copy.start()
        started.append(copy)

    def code(value, axis):
        most = jnp.max(jnp.abs(value), axis=axis, keepdims=True)
        most = jnp.maximum(most, 1e-25)
        return jnp.round(value * (code_top / most)), most * (1.0 / code_top)

    def to_code(value):
        return value.astype(I32).astype(I16)

    def from_code(coded):
        return coded.astype(I32).astype(F32)

    def go_pair(pair):
        go(pair[0])
        go(pair[1])

    def wait_pair(pair):
        pair[0].wait_recv()
        pair[1].wait_recv()

    barrier = pltpu.get_barrier_semaphore()
    for dev in (dev_zp, dev_zm, dev_zz, dev_mp, dev_sib, dev_yp, dev_ym, dev_x, dev_x_sib):
        pl.semaphore_signal(barrier, inc=1, device_id=dev, device_id_type=MESH)

    small = [
        pltpu.make_async_copy(src, dst, loc.at[7 + i])
        for i, (src, dst) in enumerate((
            (owner_in, owner), (request_in, request), (lengths_in, lengths), (gain_in, gain), (cosine_in, cosine),
            (sine_in, sine),
        ))
    ]
    load_kv = pltpu.make_async_copy(kv_down, kvt.at[0], loc.at[0])
    load_hid = pltpu.make_async_copy(hidden, hid, loc.at[1])
    load_q = [pltpu.make_async_copy(queries.at[step, pl.ds(c * NR, NR)], qraw.at[:, step], loc.at[2 + step]) for step in range(4)]
    load_cache = pltpu.make_async_copy(cache.at[pl.ds(c * NR, NR)], kbuf.at[0], loc.at[6])
    for copy in [load_hid, load_kv] + small:
        copy.start()

    pl.semaphore_wait(barrier, 9)

    base = c * (HALF_D // 2)

    def lanes(start, size):
        return pl.ds(pl.multiple_of(base + start, 128), size)

    def kv_link(slot, to_slot, at, dev):
        return link(kvt.at[slot, :, at], kvt.at[to_slot, :, at], dev)

    def first_link(to_slot, at, dev):
        return link(kv_down.at[:, at], kvt.at[to_slot, :, at], dev)

    def part_of(k, first=0, size=SHARE):
        return lanes(lax.rem(y + k, 4) * SHARE + first, size)

    low, high = lanes(4 * SHARE, DIRECT), lanes(4 * SHARE + DIRECT, DIRECT)
    mine = part_of(0)
    s_p, s_m = first_link(1, mine, dev_zp), first_link(2, mine, dev_zm)
    d_p0, d_m1 = first_link(1, low, dev_zp), first_link(2, high, dev_zm)
    d_p1, d_m0 = first_link(1, high, dev_zp), first_link(2, low, dev_zm)
    for copy in (s_p, s_m, d_p0, d_m1):
        go(copy)
    for copy in load_q + [load_cache]:
        copy.start()
    cache_out = link(cache.at[pl.ds((1 - c) * NR, NR)], kbuf.at[1], dev_sib)
    go(cache_out)
    sf_p, sf_m = (
        kv_link(1, 3, part_of(0, 0, SHARE // 2), dev_zp),
        kv_link(2, 3, part_of(0, SHARE // 2, SHARE // 2), dev_zm),
    )
    df_p, df_m = kv_link(1, 3, low, dev_zp), kv_link(2, 3, high, dev_zm)
    near_p = [None] + [kv_link(slot, slot, mine, dev_yp) for slot in (1, 2, 3)]
    near_m = [None] + [kv_link(slot, slot, mine, dev_ym) for slot in (1, 2, 3)]
    far = [None] + [
        (
            kv_link(slot, slot, part_of(3, 0, SHARE // 2), dev_yp),
            kv_link(slot, slot, part_of(1, SHARE // 2, SHARE // 2), dev_ym),
        )
        for slot in (1, 2, 3)
    ]
    share_s = [None] + [kv_link(slot, slot, lanes(0, 4 * SHARE), dev_sib) for slot in (1, 2, 3)]
    share_d = [None] + [kv_link(slot, slot, lanes(4 * SHARE, 2 * DIRECT), dev_sib) for slot in (1, 2, 3)]

    origin = [lax.rem(b + ahead, 4) for ahead in (0, 3, 1, 2)]
    m_copies = [
        (link(mps.at[slot], mpr.at[slot], dev_mp), link(mss.at[slot], msr.at[slot], dev_mp)) for slot in range(3)
    ]
    tails = (slice(0, 256), slice(256, TOK))
    for at in tails:
        at = pl.ds(at.start, at.stop - at.start)
        m_copies.append((
            link(mps.at[3, :, at], mpr.at[3, :, at], dev_mp), link(mss.at[3, :, at], msr.at[3, :, at], dev_mp),
        ))

    def send_part(slot, part, copies, at=slice(None)):
        lat[origin[slot], :, at] = part
        coded, scale = code(part, 0)
        mps[slot, :, at] = to_code(coded)
        mss[slot, :, at] = scale
        go_pair(copies)

    def weigh(score, top):
        return jnp.exp2(score * log2_scale - top * log2_scale)

    def fold(w):
        total = w[:, :128]
        for j in range(1, w.shape[1] // 128):
            total = total + w[:, j * 128:j * 128 + 128]
        return total

    def peak(score):
        most = score[:, :128]
        for j in range(1, score.shape[1] // 128):
            most = jnp.maximum(most, score[:, j * 128:j * 128 + 128])
        return most

    def columns(first, count=1):
        return slice(first * QROWS, (first + count) * QROWS)

    def resident(requests):
        at = lax.broadcasted_iota(I32, (1, CTXD), 1)
        scores = [
            [
                jnp.where(at + place * CTXD < lengths[c * NR + r], nn(qbuf[r, :, :KVW], kbuf[part, r]), masked_value)
                for part, place in enumerate((s, sib))
            ]
            for r in requests
        ]
        weights = []
        for r, (score0, score1) in zip(requests, scores):
            top = jnp.max(jnp.maximum(peak(score0), peak(score1)), axis=1, keepdims=True)
            top = jnp.maximum(top, floor_value)
            w0, w1 = weigh(score0, top), weigh(score1, top)
            ms[:, columns(r)] = jnp.transpose(jnp.broadcast_to(top, (QROWS, 128)))[0:1]
            ls[:, columns(r)] = jnp.sum(jnp.transpose(fold(w0) + fold(w1)), axis=0, keepdims=True)
            weights.append((w0.astype(BF16), w1.astype(BF16)))
        for r, (w0, w1) in zip(requests, weights):
            acc[:, columns(r)] = nt(kbuf[0, r, :LATW, :], w0) + nt(kbuf[1, r, :LATW, :], w1)

    load_hid.wait()
    load_kv.wait()
    send_part(0, nt(kvt[0], hid[...]), m_copies[0])
    s_p.wait_recv()
    go(sf_p)
    go(near_p[1])
    go(near_m[1])
    s_m.wait_recv()
    go(sf_m)
    go(near_p[2])
    go(near_m[2])
    go(d_p1)
    go(d_m0)

    for copy in small:
        copy.wait()
    token = lax.broadcasted_iota(I32, (1, TOK), 1)
    token_page = lax.shift_right_logical(token, 4)
    dest = jnp.zeros((1, TOK), I32)
    asked = jnp.zeros((1, TOK), I32)
    counts = [jnp.int32(0)] * 4
    for page in range(PAGES):
        to = owner[0, page]
        rank = jnp.where(to == 0, counts[0], jnp.where(to == 1, counts[1], jnp.where(to == 2, counts[2], counts[3])))
        counts = [counts[o] + (to == o).astype(I32) for o in range(4)]
        dest = jnp.where(token_page == page, (to * CAP + rank) * PAGE, dest)
        asked = jnp.where(token_page == page, request[page] + 1, asked)
    dest = dest + lax.bitwise_and(token, 15)
    tok[...] = dest

    label_row = lax.broadcasted_iota(I32, (LABELS, TOK), 0)
    rows[KVW:, :] = ((label_row == asked) | (label_row == USED)).astype(F32).astype(BF16)

    d_p0.wait_recv()
    go(df_p)
    d_m1.wait_recv()
    go(df_m)

    def pass_on(slot):
        near_p[slot].wait_recv()
        go(far[slot][0])
        near_m[slot].wait_recv()
        go(far[slot][1])

    def swap_shared(slot):
        far[slot][0].wait_recv()
        far[slot][1].wait_recv()
        go(share_s[slot])

    pass_on(1)
    sf_p.wait_recv()
    sf_m.wait_recv()
    go(near_p[3])
    go(near_m[3])

    for copy in load_q:
        copy.wait()
    load_cache.wait()
    label_at = lax.broadcasted_iota(I32, (QROWS, LABELS), 1)

    def fill(r, carry):
        qbuf[r, :, :KVW] = qraw[r].reshape(QROWS, KVW)
        opened = (label_at == c * NR + r + 1) | (label_at == USED)
        qbuf[r, :, KVW:] = jnp.where(opened, 0.0, masked_value).astype(BF16)
        return carry

    lax.fori_loop(0, NR, fill, 0)
    cache_out.wait_recv()
    resident((0,))

    pass_on(2)
    d_p1.wait_recv()
    go(share_d[1])
    d_m0.wait_recv()
    go(share_d[2])
    swap_shared(1)
    resident((1,))

    pass_on(3)
    swap_shared(2)
    share_d[1].wait_recv()
    share_s[1].wait_recv()
    send_part(1, nt(kvt[1], hid[...]), m_copies[1])
    df_p.wait_recv()
    df_m.wait_recv()
    go(share_d[3])
    swap_shared(3)
    share_d[2].wait_recv()
    share_s[2].wait_recv()
    send_part(2, nt(kvt[2], hid[...]), m_copies[2])

    def over_lanes(starts, size, at):
        return sum(nt(kvt[3, :, start:start + size], hid[at, start:start + size]) for start in starts)

    share_d[3].wait_recv()
    lat[origin[3]] = over_lanes((4 * SHARE, HALF_D // 2 + 4 * SHARE), 2 * DIRECT, slice(None))
    share_s[3].wait_recv()
    for i, at in enumerate(tails):
        send_part(
            3, lat[origin[3], :, at] + over_lanes((0, HALF_D // 2), 4 * SHARE, at), m_copies[3 + i], at
        )
    resident((2, 3))

    for slot in range(4):
        for pair in m_copies[slot:] if slot == 3 else m_copies[slot:slot + 1]:
            wait_pair(pair)
        lat[origin[slot]] = lat[origin[slot]] + from_code(mpr[slot]) * msr[slot]
    whole = lat[...].reshape(KVW, TOK)
    latent = whole[:LATW]
    inverse = lax.rsqrt(jnp.sum(latent * latent, axis=0, keepdims=True) / LATW + eps_norm)
    gain_cols = jnp.transpose(jnp.broadcast_to(gain[...], (128, LATW)))
    for j in range(TOK // 128):
        at = slice(j * 128, j * 128 + 128)
        rows[:LATW, at] = (latent[:, at] * inverse[:, at] * gain_cols).astype(BF16)
    first, second = whole[LATW:LATW + ROPEW // 2], whole[LATW + ROPEW // 2:]
    rows[LATW:LATW + ROPEW // 2, :] = (first * cosine[...] - second * sine[...]).astype(BF16)
    rows[LATW + ROPEW // 2:KVW, :] = (first * sine[...] + second * cosine[...]).astype(BF16)

    slot_at = lax.broadcasted_iota(I32, (CAPTOK, TOK), 0)

    def pack_for(to):
        chosen = ((slot_at + to * CAPTOK) == tok[...]).astype(F32).astype(BF16)
        page_rows = nt(chosen, rows[...])
        empty = page_rows[:, KVW + USED:KVW + USED + 1] < 0.5
        column = lax.broadcasted_iota(I32, (CAPTOK, KVX), 1)
        return jnp.where((column == KVW) & empty, 1.0, page_rows).astype(BF16)

    first, second = pl.ds(0, HALF), pl.ds(HALF, HALF)
    a_p = [link(packed.at[0, at], arr.at[part, c], dev_zp) for at, part in ((first, 2), (second, 4))]
    a_m = [link(packed.at[1, at], arr.at[part, c], dev_zm) for at, part in ((first, 3), (second, 5))]
    a_r0 = link(packed.at[2, first], relay.at[0], dev_zp)
    a_r1 = link(packed.at[2, second], relay.at[1], dev_zm)
    a_f0 = link(relay.at[0], arr.at[6, c], dev_zp)
    a_f1 = link(relay.at[1], arr.at[7, c], dev_zm)
    a_share = [link(arr.at[part, c], arr.at[part, c], dev_sib) for part in range(8)]
    packed[0] = pack_for(lax.rem(b + 1, 4))
    go(a_p[0])
    packed[1] = pack_for(lax.rem(b + 3, 4))
    go(a_m[0])
    packed[2] = pack_for(lax.rem(b + 2, 4))
    go(a_r0)
    go(a_r1)
    go(a_p[1])
    go(a_m[1])
    own_pages = pack_for(b)
    arr[0, c] = own_pages[:HALF]
    go(a_share[0])
    arr[1, c] = own_pages[HALF:]
    go(a_share[1])

    def swap(copies, parts):
        for copy, part in zip(copies, parts):
            copy.wait_recv()
            go(a_share[part])

    def ready(parts):
        for part in parts:
            a_share[part].wait_recv()

    def turn_values(first, last):
        size = (last + 1 - first) * CAPTOK
        values = arr[first:last + 1].reshape(size, KVX)[:, :LATW]
        vt[:, first * CAPTOK:first * CAPTOK + size] = jnp.transpose(values)

    def pages_step(request, count, first, last):
        size, at = (last + 1 - first) * CAPTOK, columns(request, count)
        keys = arr[first:last + 1].reshape(size, KVX)
        score = nt(keys, qbuf[request:request + count].reshape(count * QROWS, KVX))
        old = ms[:, at]
        top = jnp.maximum(old, jnp.max(score, axis=0, keepdims=True))
        shrink = jnp.exp2((old - top) * log2_scale)
        w = weigh(score, top)
        total = ls[:, at] * shrink + jnp.sum(w, axis=0, keepdims=True)
        value = acc[:, at] * shrink + nn(vt[:, first * CAPTOK:first * CAPTOK + size], w.astype(BF16))
        return value, top, total

    def pages_of(request, count, first, last):
        at = columns(request, count)
        acc[:, at], ms[:, at], ls[:, at] = pages_step(request, count, first, last)

    ready((0, 1))
    turn_values(0, 1)
    pages_of(0, 4, 0, 1)
    swap((a_p[0], a_m[0]), (2, 3))
    a_r0.wait_recv()
    go(a_f0)
    a_r1.wait_recv()
    go(a_f1)
    ready((2, 3))
    turn_values(2, 3)
    pages_of(0, 4, 2, 3)
    swap((a_p[1], a_m[1]), (4, 5))
    ready((4, 5))
    turn_values(4, 5)
    swap((a_f0, a_f1), (6, 7))
    pages_of(0, 2, 4, 5)
    ready((6, 7))
    turn_values(6, 7)

    def merge(parts):
        top = parts[0][1][0]
        for _, stat in parts[1:]:
            top = jnp.maximum(top, stat[0])
        value, total = 0.0, 0.0
        for coded, stat in parts:
            factor = jnp.exp2(stat[0] - top)
            value = value + from_code(coded) * factor
            total = total + factor * stat[1]
        return value, top, total

    def put(coded_ref, stat_ref, value, top, total):
        coded, scale = code(value, 0)
        coded_ref[...] = to_code(coded).reshape(coded_ref.shape)
        stat_ref[0] = top + jnp.log(scale) * log2_e
        stat_ref[1] = total / scale

    yp, ym, yy = lax.rem(y + 1, 4), lax.rem(y + 3, 4), lax.rem(y + 2, 4)
    first_y = used[0]

    def y_pair(r, k):
        pairs = (
            (osend.at[r, yy, 0], ostat.at[r], 0, dev_yp),
            (osend.at[r, yy, 1], ostat.at[r], 1, dev_ym),
            (osend.at[r, yp, 1], ostat.at[r], 2, dev_yp),
            (osend.at[r, ym, 0], ostat.at[r], 3, dev_ym),
            (rsend.at[r, 0], rstat.at[r, 0], 4, dev_yp),
            (rsend.at[r, 1], rstat.at[r, 1], 5, dev_ym),
        )
        data, stat, _, dev = pairs[k]
        return (
            link_at(first_y + 18 * r + 2 * k, data, ybuf.at[r, k], dev),
            link_at(first_y + 18 * r + 2 * k + 1, stat, ystat.at[r, k], dev),
        )

    def last_pair(r, k):
        half, core, dev = ((1 - xh, c, dev_x), (1 - xh, 1 - c, dev_x_sib), (xh, 1 - c, dev_sib))[k]
        return (
            link_at(first_y + 18 * r + 12 + 2 * k, mbuf.at[r, half, core], fbuf.at[r, k], dev),
            link_at(first_y + 18 * r + 13 + 2 * k, mstat.at[r, half], fstat.at[r, k], dev),
        )

    def start_pair(pair):
        pair[0].start()
        pair[1].start()

    def relay_sums(r, carry):
        for k, to in ((0, yp), (1, ym)):
            wait_pair(y_pair(r, k))
            put(rsend.at[r, k], rstat.at[r, k], *merge([
                (osend[r, to, k], ostat[r]), (ybuf[r, k], ystat[r, k]),
            ]))
            start_pair(y_pair(r, 4 + k))
        return carry

    for first_request, count, first in ((0, 2, 6), (2, 2, 4)):
        value, top, total = pages_step(first_request, count, first, 7)
        coded, scale = code(value, 0)
        coded, top, total = to_code(coded), top * log2_scale + jnp.log(scale) * log2_e, total / scale
        for r in range(first_request, first_request + count):
            at = columns(r - first_request)
            osend[r] = coded[:, at].reshape(4, 2, 64, QROWS)
            ostat[r, 0] = top[:, at]
            ostat[r, 1] = total[:, at]
            for k in range(4):
                start_pair(y_pair(r, k))

    def sums_over_y(r, carry):
        for k in range(2, 6):
            wait_pair(y_pair(r, k))
        for h, (one, two) in enumerate(((3, 4), (2, 5))):
            put(mbuf.at[r, h], mstat.at[r, h], *merge([
                (osend[r, y, h], ostat[r]), (ybuf[r, one], ystat[r, one]), (ybuf[r, two], ystat[r, two]),
            ]))
        for k in (1, 0, 2):
            start_pair(last_pair(r, k))
        return carry

    def out_copy(wanted):
        return pltpu.make_async_copy(out.at[:, wanted], out_hbm.at[:, wanted], loc.at[13 + wanted])

    def last_sums(r, carry):
        for k in range(3):
            wait_pair(last_pair(r, k))
        own, other = c * NR + r, (1 - c) * NR + r
        for wanted, parts in (
            (own, [(mbuf[r, xh, c], mstat[r, xh]), (fbuf[r, 0], fstat[r, 0])]),
            (other, [(fbuf[r, 2], fstat[r, 2]), (fbuf[r, 1], fstat[r, 1])]),
        ):
            value, _, total = merge(parts)
            value = value / total
            for step in range(4):
                out[step, wanted] = value[:, 64 * step:64 * step + 64]
            out_copy(wanted).start()
        return carry

    def finish(r, carry):
        for pair in [y_pair(r, k) for k in range(6)] + [last_pair(r, k) for k in range(3)]:
            pair[0].wait_send()
            pair[1].wait_send()
        return carry

    lax.fori_loop(0, NR, relay_sums, 0)
    for stage in (sums_over_y, last_sums, finish):
        lax.fori_loop(0, NR, stage, 0)
    for wanted in range(2 * NR):
        out_copy(wanted).wait()
    for copy in started:
        copy.wait_send()


LINKS = 144


def tables():
    half = ROPEW // 2
    frequency = rope_base ** (-np.arange(half, dtype=np.float32) / np.float32(half))
    angles = np.arange(TOK, dtype=np.float32)[None, :] * frequency.astype(np.float32)[:, None]
    return np.cos(angles).astype(np.float32), np.sin(angles).astype(np.float32)


def on_device(hidden, kv_down, kv_gain, page_owner, page_request, queries, cache, lengths):
    cosine, sine = tables()
    anywhere = pl.BlockSpec(memory_space=pl.ANY)
    sums = pl.pallas_call(
        kernel,
        out_shape=jax.ShapeDtypeStruct((4, 2 * NR, 32, 64), F32),
        in_specs=[anywhere] * 10,
        out_specs=anywhere,
        scratch_shapes=[
            pltpu.VMEM((1, LATW), F32),
            pltpu.SMEM((1, PAGES), I32),
            pltpu.SMEM((PAGES,), I32),
            pltpu.SMEM((2 * NR,), I32),
            pltpu.VMEM((ROPEW // 2, TOK), F32),
            pltpu.VMEM((ROPEW // 2, TOK), F32),
            pltpu.VMEM((4, 2 * NR, 32, 64), F32),
            pltpu.VMEM((TOK, HALF_D), BF16),
            pltpu.VMEM((4, BLK, HALF_D), BF16),
            pltpu.VMEM((4, BLK, TOK), F32),
            pltpu.VMEM((4, BLK, TOK), I16),
            pltpu.VMEM((4, BLK, TOK), I16),
            pltpu.VMEM((4, 1, TOK), F32),
            pltpu.VMEM((4, 1, TOK), F32),
            pltpu.VMEM((KVX, TOK), BF16),
            pltpu.VMEM((3, CAPTOK, KVX), BF16),
            pltpu.VMEM((2, HALF, KVX), BF16),
            pltpu.VMEM((8, 2, HALF, KVX), BF16),
            pltpu.VMEM((1, TOK), I32),
            pltpu.VMEM((LATW, 8 * CAPTOK), BF16),
            pltpu.VMEM((NR, 4, 64, KVW), BF16),
            pltpu.VMEM((NR, QROWS, KVX), BF16),
            pltpu.VMEM((2, NR, KVW, CTXD), BF16),
            pltpu.VMEM((LATW, NR * QROWS), F32),
            pltpu.VMEM((1, NR * QROWS), F32),
            pltpu.VMEM((1, NR * QROWS), F32),
            pltpu.VMEM((NR, 4, 2, 64, QROWS), I16),
            pltpu.VMEM((NR, 2, 1, QROWS), F32),
            pltpu.VMEM((NR, 6, 64, QROWS), I16),
            pltpu.VMEM((NR, 6, 2, 1, QROWS), F32),
            pltpu.VMEM((NR, 2, 64, QROWS), I16),
            pltpu.VMEM((NR, 2, 2, 1, QROWS), F32),
            pltpu.VMEM((NR, 2, 2, 32, QROWS), I16),
            pltpu.VMEM((NR, 2, 2, 1, QROWS), F32),
            pltpu.VMEM((NR, 3, 32, QROWS), I16),
            pltpu.VMEM((NR, 3, 2, 1, QROWS), F32),
            pltpu.SemaphoreType.DMA((13 + 2 * NR,)),
            pltpu.SemaphoreType.DMA((LINKS,)),
            pltpu.SemaphoreType.DMA((LINKS,)),
        ],
        compiler_params=pltpu.CompilerParams(
            collective_id=0, has_side_effects=True, vmem_limit_bytes=56 * 1024 * 1024
        ),
        cost_estimate=pl.CostEstimate(flops=7_500_000_000, bytes_accessed=12_000_000, transcendentals=3_000_000),
    )(
        hidden, kv_down.T, kv_gain.reshape(1, LATW), page_owner.T, page_request, queries, cache.transpose(0, 2, 1), lengths,
        jnp.asarray(cosine), jnp.asarray(sine),
    )
    return sums.transpose(0, 1, 3, 2)


def solution(mesh):
    return jax.shard_map(
        on_device,
        mesh=mesh,
        in_specs=(
            P(("seq", "batch"), "mp"),
            P("mp", "batch"),
            P(),
            P(("seq", "batch"), None),
            P(("seq", "batch")),
            P(None, "batch", "mp", None),
            P("batch", "seq", None),
            P("batch"),
        ),
        out_specs=P(None, "batch", "mp", "seq"),
        check_vma=False,
    )
```

```python
import jax
import jax.numpy as jnp
import numpy as np
from jax import lax
from jax.experimental import pallas as pl
from jax.experimental.pallas import tpu as pltpu
from jax.sharding import PartitionSpec as P

MESH = pl.DeviceIdType.MESH
F32, BF16, I32, I16 = jnp.float32, jnp.bfloat16, jnp.int32, jnp.int16

eps_norm = 1e-06
score_scale = 192.0 ** (-0.5)
log2_e = 1.4426950408889634
log2_scale = score_scale * log2_e
rope_base = 10000.0
masked_value = -1e30
floor_value = -1e29
code_top = 32767.0

TOK, HALF_D, KVW, LATW, ROPEW = 384, 3584, 576, 512, 64
USED = 16
LABELS = 64
KVX = KVW + LABELS
BLK = 144
SHARE, DIRECT = 256, 384
CAPTOK = 192
HALF = CAPTOK // 2
PAGES, PAGE, CAP = 24, 16, 12
QROWS = 256
CTXD = 512
NR = 4


def nt(a, b):
    return lax.dot_general(a, b, (((1,), (1,)), ((), ())), preferred_element_type=F32)


def nn(a, b):
    return jnp.dot(a, b, preferred_element_type=F32)


def kernel(
    hidden, kv_down, gain_in, owner_in, request_in, queries, cache, lengths_in, cosine_in, sine_in,
    out_hbm,
    gain, owner, request, lengths, cosine, sine, out,
    hid, kvt, lat, mps, mpr, mss, msr, rows, packed, relay, arr, tok,
    vt, qraw, qbuf, kbuf, acc, ms, ls, osend, ostat, ybuf, ystat, rsend, rstat, mbuf, mstat, fbuf, fstat,
    loc, send, recv,
):
    s, b, p = lax.axis_index("seq"), lax.axis_index("batch"), lax.axis_index("mp")
    c = lax.rem(s, 2)
    sib = s + 1 - 2 * c
    y = lax.div(s, 4)
    in_y = lax.rem(s, 4)
    xh = lax.rem(lax.div(s, 2), 2)
    dev_zp = (s, lax.rem(b + 1, 4), p)
    dev_zm = (s, lax.rem(b + 3, 4), p)
    dev_zz = (s, lax.rem(b + 2, 4), p)
    dev_mp = (s, b, 1 - p)
    dev_sib = (sib, b, p)
    dev_yp = (lax.rem(y + 1, 4) * 4 + in_y, b, p)
    dev_ym = (lax.rem(y + 3, 4) * 4 + in_y, b, p)
    dev_x = (s + 2 - 4 * xh, b, p)
    dev_x_sib = (sib + 2 - 4 * xh, b, p)

    used = [0]
    started = []

    def link(src, dst, dev):
        used[0] += 1
        return link_at(used[0] - 1, src, dst, dev)

    def link_at(i, src, dst, dev):
        return pltpu.make_async_remote_copy(
            src_ref=src, dst_ref=dst, send_sem=send.at[i], recv_sem=recv.at[i],
            device_id=dev, device_id_type=MESH,
        )

    def go(copy):
        copy.start()
        started.append(copy)

    def code(value, axis):
        most = jnp.max(jnp.abs(value), axis=axis, keepdims=True)
        most = jnp.maximum(most, 1e-25)
        return jnp.round(value * (code_top / most)), most * (1.0 / code_top)

    def to_code(value):
        return value.astype(I32).astype(I16)

    def from_code(coded):
        return coded.astype(I32).astype(F32)

    def go_pair(pair):
        go(pair[0])
        go(pair[1])

    def wait_pair(pair):
        pair[0].wait_recv()
        pair[1].wait_recv()

    barrier = pltpu.get_barrier_semaphore()
    for dev in (dev_zp, dev_zm, dev_zz, dev_mp, dev_sib, dev_yp, dev_ym, dev_x, dev_x_sib):
        pl.semaphore_signal(barrier, inc=1, device_id=dev, device_id_type=MESH)

    small = [
        pltpu.make_async_copy(src, dst, loc.at[7 + i])
        for i, (src, dst) in enumerate((
            (owner_in, owner), (request_in, request), (lengths_in, lengths), (gain_in, gain), (cosine_in, cosine),
            (sine_in, sine),
        ))
    ]
    load_kv = pltpu.make_async_copy(kv_down, kvt.at[0], loc.at[0])
    load_hid = pltpu.make_async_copy(hidden, hid, loc.at[1])
    load_q = [pltpu.make_async_copy(queries.at[step, pl.ds(c * NR, NR)], qraw.at[:, step], loc.at[2 + step]) for step in range(4)]
    load_cache = pltpu.make_async_copy(cache.at[pl.ds(c * NR, NR)], kbuf.at[0], loc.at[6])
    for copy in [load_hid, load_kv] + small:
        copy.start()

    pl.semaphore_wait(barrier, 9)

    base = c * (HALF_D // 2)

    def lanes(start, size):
        return pl.ds(pl.multiple_of(base + start, 128), size)

    def kv_link(slot, to_slot, at, dev):
        return link(kvt.at[slot, :, at], kvt.at[to_slot, :, at], dev)

    def first_link(to_slot, at, dev):
        return link(kv_down.at[:, at], kvt.at[to_slot, :, at], dev)

    def part_of(k, first=0, size=SHARE):
        return lanes(lax.rem(y + k, 4) * SHARE + first, size)

    low, high = lanes(4 * SHARE, DIRECT), lanes(4 * SHARE + DIRECT, DIRECT)
    mine = part_of(0)
    s_p, s_m = first_link(1, mine, dev_zp), first_link(2, mine, dev_zm)
    d_p0, d_m1 = first_link(1, low, dev_zp), first_link(2, high, dev_zm)
    d_p1, d_m0 = first_link(1, high, dev_zp), first_link(2, low, dev_zm)
    for copy in (s_p, s_m, d_p0, d_m1):
        go(copy)
    for copy in load_q + [load_cache]:
        copy.start()
    cache_out = link(cache.at[pl.ds((1 - c) * NR, NR)], kbuf.at[1], dev_sib)
    go(cache_out)
    sf_p, sf_m = (
        kv_link(1, 3, part_of(0, 0, SHARE // 2), dev_zp),
        kv_link(2, 3, part_of(0, SHARE // 2, SHARE // 2), dev_zm),
    )
    df_p, df_m = kv_link(1, 3, low, dev_zp), kv_link(2, 3, high, dev_zm)
    near_p = [None] + [kv_link(slot, slot, mine, dev_yp) for slot in (1, 2, 3)]
    near_m = [None] + [kv_link(slot, slot, mine, dev_ym) for slot in (1, 2, 3)]
    far = [None] + [
        (
            kv_link(slot, slot, part_of(3, 0, SHARE // 2), dev_yp),
            kv_link(slot, slot, part_of(1, SHARE // 2, SHARE // 2), dev_ym),
        )
        for slot in (1, 2, 3)
    ]
    share_s = [None] + [kv_link(slot, slot, lanes(0, 4 * SHARE), dev_sib) for slot in (1, 2, 3)]
    share_d = [None] + [kv_link(slot, slot, lanes(4 * SHARE, 2 * DIRECT), dev_sib) for slot in (1, 2, 3)]

    origin = [lax.rem(b + ahead, 4) for ahead in (0, 3, 1, 2)]
    m_copies = [
        (link(mps.at[slot], mpr.at[slot], dev_mp), link(mss.at[slot], msr.at[slot], dev_mp)) for slot in range(3)
    ]
    tails = (slice(0, 256), slice(256, TOK))
    for at in tails:
        at = pl.ds(at.start, at.stop - at.start)
        m_copies.append((
            link(mps.at[3, :, at], mpr.at[3, :, at], dev_mp), link(mss.at[3, :, at], msr.at[3, :, at], dev_mp),
        ))

    def send_part(slot, part, copies, at=slice(None)):
        lat[origin[slot], :, at] = part
        coded, scale = code(part, 0)
        mps[slot, :, at] = to_code(coded)
        mss[slot, :, at] = scale
        go_pair(copies)

    def weigh(score, top):
        return jnp.exp2(score * log2_scale - top * log2_scale)

    def fold(w):
        total = w[:, :128]
        for j in range(1, w.shape[1] // 128):
            total = total + w[:, j * 128:j * 128 + 128]
        return total

    def peak(score):
        most = score[:, :128]
        for j in range(1, score.shape[1] // 128):
            most = jnp.maximum(most, score[:, j * 128:j * 128 + 128])
        return most

    def columns(first, count=1):
        return slice(first * QROWS, (first + count) * QROWS)

    def resident(requests):
        at = lax.broadcasted_iota(I32, (1, CTXD), 1)
        scores = [
            [
                jnp.where(at + place * CTXD < lengths[c * NR + r], nn(qbuf[r, :, :KVW], kbuf[part, r]), masked_value)
                for part, place in enumerate((s, sib))
            ]
            for r in requests
        ]
        weights = []
        for r, (score0, score1) in zip(requests, scores):
            top = jnp.max(jnp.maximum(peak(score0), peak(score1)), axis=1, keepdims=True)
            top = jnp.maximum(top, floor_value)
            w0, w1 = weigh(score0, top), weigh(score1, top)
            ms[:, columns(r)] = jnp.transpose(jnp.broadcast_to(top, (QROWS, 128)))[0:1]
            ls[:, columns(r)] = jnp.sum(jnp.transpose(fold(w0) + fold(w1)), axis=0, keepdims=True)
            weights.append((w0.astype(BF16), w1.astype(BF16)))
        for r, (w0, w1) in zip(requests, weights):
            acc[:, columns(r)] = nt(kbuf[0, r, :LATW, :], w0) + nt(kbuf[1, r, :LATW, :], w1)

    load_hid.wait()
    load_kv.wait()
    send_part(0, nt(kvt[0], hid[...]), m_copies[0])
    s_p.wait_recv()
    go(sf_p)
    go(near_p[1])
    go(near_m[1])
    s_m.wait_recv()
    go(sf_m)
    go(near_p[2])
    go(near_m[2])
    go(d_p1)
    go(d_m0)

    for copy in small:
        copy.wait()
    token = lax.broadcasted_iota(I32, (1, TOK), 1)
    token_page = lax.shift_right_logical(token, 4)
    dest = jnp.zeros((1, TOK), I32)
    asked = jnp.zeros((1, TOK), I32)
    counts = [jnp.int32(0)] * 4
    for page in range(PAGES):
        to = owner[0, page]
        rank = jnp.where(to == 0, counts[0], jnp.where(to == 1, counts[1], jnp.where(to == 2, counts[2], counts[3])))
        counts = [counts[o] + (to == o).astype(I32) for o in range(4)]
        dest = jnp.where(token_page == page, (to * CAP + rank) * PAGE, dest)
        asked = jnp.where(token_page == page, request[page] + 1, asked)
    dest = dest + lax.bitwise_and(token, 15)
    tok[...] = dest

    label_row = lax.broadcasted_iota(I32, (LABELS, TOK), 0)
    rows[KVW:, :] = ((label_row == asked) | (label_row == USED)).astype(F32).astype(BF16)

    d_p0.wait_recv()
    go(df_p)
    d_m1.wait_recv()
    go(df_m)

    def pass_on(slot):
        near_p[slot].wait_recv()
        go(far[slot][0])
        near_m[slot].wait_recv()
        go(far[slot][1])

    def swap_shared(slot):
        far[slot][0].wait_recv()
        far[slot][1].wait_recv()
        go(share_s[slot])

    pass_on(1)
    sf_p.wait_recv()
    sf_m.wait_recv()
    go(near_p[3])
    go(near_m[3])

    for copy in load_q:
        copy.wait()
    load_cache.wait()
    label_at = lax.broadcasted_iota(I32, (QROWS, LABELS), 1)

    def fill(r, carry):
        qbuf[r, :, :KVW] = qraw[r].reshape(QROWS, KVW)
        opened = (label_at == c * NR + r + 1) | (label_at == USED)
        qbuf[r, :, KVW:] = jnp.where(opened, 0.0, masked_value).astype(BF16)
        return carry

    lax.fori_loop(0, NR, fill, 0)
    cache_out.wait_recv()
    resident((0,))

    pass_on(2)
    d_p1.wait_recv()
    go(share_d[1])
    d_m0.wait_recv()
    go(share_d[2])
    swap_shared(1)
    resident((1,))

    pass_on(3)
    swap_shared(2)
    share_d[1].wait_recv()
    share_s[1].wait_recv()
    send_part(1, nt(kvt[1], hid[...]), m_copies[1])
    df_p.wait_recv()
    df_m.wait_recv()
    go(share_d[3])
    swap_shared(3)
    share_d[2].wait_recv()
    share_s[2].wait_recv()
    send_part(2, nt(kvt[2], hid[...]), m_copies[2])

    def over_lanes(starts, size, at):
        return sum(nt(kvt[3, :, start:start + size], hid[at, start:start + size]) for start in starts)

    share_d[3].wait_recv()
    lat[origin[3]] = over_lanes((4 * SHARE, HALF_D // 2 + 4 * SHARE), 2 * DIRECT, slice(None))
    share_s[3].wait_recv()
    for i, at in enumerate(tails):
        send_part(
            3, lat[origin[3], :, at] + over_lanes((0, HALF_D // 2), 4 * SHARE, at), m_copies[3 + i], at
        )
    resident((2, 3))

    for slot in range(4):
        for pair in m_copies[slot:] if slot == 3 else m_copies[slot:slot + 1]:
            wait_pair(pair)
        lat[origin[slot]] = lat[origin[slot]] + from_code(mpr[slot]) * msr[slot]
    whole = lat[...].reshape(KVW, TOK)
    latent = whole[:LATW]
    inverse = lax.rsqrt(jnp.sum(latent * latent, axis=0, keepdims=True) / LATW + eps_norm)
    gain_cols = jnp.transpose(jnp.broadcast_to(gain[...], (128, LATW)))
    for j in range(TOK // 128):
        at = slice(j * 128, j * 128 + 128)
        rows[:LATW, at] = (latent[:, at] * inverse[:, at] * gain_cols).astype(BF16)
    first, second = whole[LATW:LATW + ROPEW // 2], whole[LATW + ROPEW // 2:]
    rows[LATW:LATW + ROPEW // 2, :] = (first * cosine[...] - second * sine[...]).astype(BF16)
    rows[LATW + ROPEW // 2:KVW, :] = (first * sine[...] + second * cosine[...]).astype(BF16)

    slot_at = lax.broadcasted_iota(I32, (CAPTOK, TOK), 0)

    def pack_for(to):
        chosen = ((slot_at + to * CAPTOK) == tok[...]).astype(F32).astype(BF16)
        page_rows = nt(chosen, rows[...])
        empty = page_rows[:, KVW + USED:KVW + USED + 1] < 0.5
        column = lax.broadcasted_iota(I32, (CAPTOK, KVX), 1)
        return jnp.where((column == KVW) & empty, 1.0, page_rows).astype(BF16)

    first, second = pl.ds(0, HALF), pl.ds(HALF, HALF)
    a_p = [link(packed.at[0, at], arr.at[part, c], dev_zp) for at, part in ((first, 2), (second, 4))]
    a_m = [link(packed.at[1, at], arr.at[part, c], dev_zm) for at, part in ((first, 3), (second, 5))]
    a_r0 = link(packed.at[2, first], relay.at[0], dev_zp)
    a_r1 = link(packed.at[2, second], relay.at[1], dev_zm)
    a_f0 = link(relay.at[0], arr.at[6, c], dev_zp)
    a_f1 = link(relay.at[1], arr.at[7, c], dev_zm)
    a_share = [link(arr.at[part, c], arr.at[part, c], dev_sib) for part in range(8)]
    packed[0] = pack_for(lax.rem(b + 1, 4))
    go(a_p[0])
    packed[1] = pack_for(lax.rem(b + 3, 4))
    go(a_m[0])
    packed[2] = pack_for(lax.rem(b + 2, 4))
    go(a_r0)
    go(a_r1)
    go(a_p[1])
    go(a_m[1])
    own_pages = pack_for(b)
    arr[0, c] = own_pages[:HALF]
    go(a_share[0])
    arr[1, c] = own_pages[HALF:]
    go(a_share[1])

    def swap(copies, parts):
        for copy, part in zip(copies, parts):
            copy.wait_recv()
            go(a_share[part])

    def ready(parts):
        for part in parts:
            a_share[part].wait_recv()

    def turn_values(first, last):
        size = (last + 1 - first) * CAPTOK
        values = arr[first:last + 1].reshape(size, KVX)[:, :LATW]
        vt[:, first * CAPTOK:first * CAPTOK + size] = jnp.transpose(values)

    def pages_step(request, count, first, last):
        size, at = (last + 1 - first) * CAPTOK, columns(request, count)
        keys = arr[first:last + 1].reshape(size, KVX)
        score = nt(keys, qbuf[request:request + count].reshape(count * QROWS, KVX))
        old = ms[:, at]
        top = jnp.maximum(old, jnp.max(score, axis=0, keepdims=True))
        shrink = jnp.exp2((old - top) * log2_scale)
        w = weigh(score, top)
        total = ls[:, at] * shrink + jnp.sum(w, axis=0, keepdims=True)
        value = acc[:, at] * shrink + nn(vt[:, first * CAPTOK:first * CAPTOK + size], w.astype(BF16))
        return value, top, total

    def pages_of(request, count, first, last):
        at = columns(request, count)
        acc[:, at], ms[:, at], ls[:, at] = pages_step(request, count, first, last)

    ready((0, 1))
    turn_values(0, 1)
    pages_of(0, 4, 0, 1)
    swap((a_p[0], a_m[0]), (2, 3))
    a_r0.wait_recv()
    go(a_f0)
    a_r1.wait_recv()
    go(a_f1)
    ready((2, 3))
    turn_values(2, 3)
    pages_of(0, 4, 2, 3)
    swap((a_p[1], a_m[1]), (4, 5))
    ready((4, 5))
    turn_values(4, 5)
    swap((a_f0, a_f1), (6, 7))
    pages_of(0, 4, 4, 5)
    ready((6, 7))
    turn_values(6, 7)

    def merge(parts):
        top = parts[0][1][0]
        for _, stat in parts[1:]:
            top = jnp.maximum(top, stat[0])
        value, total = 0.0, 0.0
        for coded, stat in parts:
            factor = jnp.exp2(stat[0] - top)
            value = value + from_code(coded) * factor
            total = total + factor * stat[1]
        return value, top, total

    def put(coded_ref, stat_ref, value, top, total):
        coded, scale = code(value, 0)
        coded_ref[...] = to_code(coded).reshape(coded_ref.shape)
        stat_ref[0] = top + jnp.log(scale) * log2_e
        stat_ref[1] = total / scale

    yp, ym, yy = lax.rem(y + 1, 4), lax.rem(y + 3, 4), lax.rem(y + 2, 4)
    first_y = used[0]

    def y_pair(r, k):
        pairs = (
            (osend.at[r, yy, 0], ostat.at[r], 0, dev_yp),
            (osend.at[r, yy, 1], ostat.at[r], 1, dev_ym),
            (osend.at[r, yp, 1], ostat.at[r], 2, dev_yp),
            (osend.at[r, ym, 0], ostat.at[r], 3, dev_ym),
            (rsend.at[r, 0], rstat.at[r, 0], 4, dev_yp),
            (rsend.at[r, 1], rstat.at[r, 1], 5, dev_ym),
        )
        data, stat, _, dev = pairs[k]
        return (
            link_at(first_y + 18 * r + 2 * k, data, ybuf.at[r, k], dev),
            link_at(first_y + 18 * r + 2 * k + 1, stat, ystat.at[r, k], dev),
        )

    def last_pair(r, k):
        half, core, dev = ((1 - xh, c, dev_x), (1 - xh, 1 - c, dev_x_sib), (xh, 1 - c, dev_sib))[k]
        return (
            link_at(first_y + 18 * r + 12 + 2 * k, mbuf.at[r, half, core], fbuf.at[r, k], dev),
            link_at(first_y + 18 * r + 13 + 2 * k, mstat.at[r, half], fstat.at[r, k], dev),
        )

    def start_pair(pair):
        pair[0].start()
        pair[1].start()

    def relay_sums(r, carry):
        for k, to in ((0, yp), (1, ym)):
            wait_pair(y_pair(r, k))
            put(rsend.at[r, k], rstat.at[r, k], *merge([
                (osend[r, to, k], ostat[r]), (ybuf[r, k], ystat[r, k]),
            ]))
            start_pair(y_pair(r, 4 + k))
        return carry

    for first_request, count, first in ((0, 2, 6), (2, 2, 6)):
        value, top, total = pages_step(first_request, count, first, 7)
        coded, scale = code(value, 0)
        coded, top, total = to_code(coded), top * log2_scale + jnp.log(scale) * log2_e, total / scale
        for r in range(first_request, first_request + count):
            at = columns(r - first_request)
            osend[r] = coded[:, at].reshape(4, 2, 64, QROWS)
            ostat[r, 0] = top[:, at]
            ostat[r, 1] = total[:, at]
            for k in range(4):
                start_pair(y_pair(r, k))

    def sums_over_y(r, carry):
        for k in range(2, 6):
            wait_pair(y_pair(r, k))
        for h, (one, two) in enumerate(((3, 4), (2, 5))):
            put(mbuf.at[r, h], mstat.at[r, h], *merge([
                (osend[r, y, h], ostat[r]), (ybuf[r, one], ystat[r, one]), (ybuf[r, two], ystat[r, two]),
            ]))
        for k in (1, 0, 2):
            start_pair(last_pair(r, k))
        return carry

    def out_copy(wanted):
        return pltpu.make_async_copy(out.at[:, wanted], out_hbm.at[:, wanted], loc.at[13 + wanted])

    def last_sums(r, carry):
        for k in range(3):
            wait_pair(last_pair(r, k))
        own, other = c * NR + r, (1 - c) * NR + r
        for wanted, parts in (
            (own, [(mbuf[r, xh, c], mstat[r, xh]), (fbuf[r, 0], fstat[r, 0])]),
            (other, [(fbuf[r, 2], fstat[r, 2]), (fbuf[r, 1], fstat[r, 1])]),
        ):
            value, _, total = merge(parts)
            value = value / total
            for step in range(4):
                out[step, wanted] = value[:, 64 * step:64 * step + 64]
            out_copy(wanted).start()
        return carry

    def finish(r, carry):
        for pair in [y_pair(r, k) for k in range(6)] + [last_pair(r, k) for k in range(3)]:
            pair[0].wait_send()
            pair[1].wait_send()
        return carry

    lax.fori_loop(0, NR, relay_sums, 0)
    for stage in (sums_over_y, last_sums, finish):
        lax.fori_loop(0, NR, stage, 0)
    for wanted in range(2 * NR):
        out_copy(wanted).wait()
    for copy in started:
        copy.wait_send()


LINKS = 144


def tables():
    half = ROPEW // 2
    frequency = rope_base ** (-np.arange(half, dtype=np.float32) / np.float32(half))
    angles = np.arange(TOK, dtype=np.float32)[None, :] * frequency.astype(np.float32)[:, None]
    return np.cos(angles).astype(np.float32), np.sin(angles).astype(np.float32)


def on_device(hidden, kv_down, kv_gain, page_owner, page_request, queries, cache, lengths):
    cosine, sine = tables()
    anywhere = pl.BlockSpec(memory_space=pl.ANY)
    sums = pl.pallas_call(
        kernel,
        out_shape=jax.ShapeDtypeStruct((4, 2 * NR, 32, 64), F32),
        in_specs=[anywhere] * 10,
        out_specs=anywhere,
        scratch_shapes=[
            pltpu.VMEM((1, LATW), F32),
            pltpu.SMEM((1, PAGES), I32),
            pltpu.SMEM((PAGES,), I32),
            pltpu.SMEM((2 * NR,), I32),
            pltpu.VMEM((ROPEW // 2, TOK), F32),
            pltpu.VMEM((ROPEW // 2, TOK), F32),
            pltpu.VMEM((4, 2 * NR, 32, 64), F32),
            pltpu.VMEM((TOK, HALF_D), BF16),
            pltpu.VMEM((4, BLK, HALF_D), BF16),
            pltpu.VMEM((4, BLK, TOK), F32),
            pltpu.VMEM((4, BLK, TOK), I16),
            pltpu.VMEM((4, BLK, TOK), I16),
            pltpu.VMEM((4, 1, TOK), F32),
            pltpu.VMEM((4, 1, TOK), F32),
            pltpu.VMEM((KVX, TOK), BF16),
            pltpu.VMEM((3, CAPTOK, KVX), BF16),
            pltpu.VMEM((2, HALF, KVX), BF16),
            pltpu.VMEM((8, 2, HALF, KVX), BF16),
            pltpu.VMEM((1, TOK), I32),
            pltpu.VMEM((LATW, 8 * CAPTOK), BF16),
            pltpu.VMEM((NR, 4, 64, KVW), BF16),
            pltpu.VMEM((NR, QROWS, KVX), BF16),
            pltpu.VMEM((2, NR, KVW, CTXD), BF16),
            pltpu.VMEM((LATW, NR * QROWS), F32),
            pltpu.VMEM((1, NR * QROWS), F32),
            pltpu.VMEM((1, NR * QROWS), F32),
            pltpu.VMEM((NR, 4, 2, 64, QROWS), I16),
            pltpu.VMEM((NR, 2, 1, QROWS), F32),
            pltpu.VMEM((NR, 6, 64, QROWS), I16),
            pltpu.VMEM((NR, 6, 2, 1, QROWS), F32),
            pltpu.VMEM((NR, 2, 64, QROWS), I16),
            pltpu.VMEM((NR, 2, 2, 1, QROWS), F32),
            pltpu.VMEM((NR, 2, 2, 32, QROWS), I16),
            pltpu.VMEM((NR, 2, 2, 1, QROWS), F32),
            pltpu.VMEM((NR, 3, 32, QROWS), I16),
            pltpu.VMEM((NR, 3, 2, 1, QROWS), F32),
            pltpu.SemaphoreType.DMA((13 + 2 * NR,)),
            pltpu.SemaphoreType.DMA((LINKS,)),
            pltpu.SemaphoreType.DMA((LINKS,)),
        ],
        compiler_params=pltpu.CompilerParams(
            collective_id=0, has_side_effects=True, vmem_limit_bytes=56 * 1024 * 1024
        ),
        cost_estimate=pl.CostEstimate(flops=7_500_000_000, bytes_accessed=12_000_000, transcendentals=3_000_000),
    )(
        hidden, kv_down.T, kv_gain.reshape(1, LATW), page_owner.T, page_request, queries, cache.transpose(0, 2, 1), lengths,
        jnp.asarray(cosine), jnp.asarray(sine),
    )
    return sums.transpose(0, 1, 3, 2)


def solution(mesh):
    return jax.shard_map(
        on_device,
        mesh=mesh,
        in_specs=(
            P(("seq", "batch"), "mp"),
            P("mp", "batch"),
            P(),
            P(("seq", "batch"), None),
            P(("seq", "batch")),
            P(None, "batch", "mp", None),
            P("batch", "seq", None),
            P("batch"),
        ),
        out_specs=P(None, "batch", "mp", "seq"),
        check_vma=False,
    )
```
